32 devices in a mesh: grp: 2 (over y), ctx: 4 (over z), tp: 4 (over x, core).
Axes of the slice: x: 2, y: 2, z: 4, core: 2. Of those that a mesh axis runs over, the one named last changes fastest.
Arguments:
- queries: bfloat16 [16, 128, 4096], P(('grp', 'ctx'), None, 'tp'), parts along dimension 0, may hold values from -31 to 31
- cont_keys: bfloat16 [16, 128, 256], P(('grp', 'ctx')), parts along dimension 0, may hold values from -10 to 10
- cont_values: bfloat16 [16, 128, 256], P(('grp', 'ctx')), parts along dimension 0, may hold values from -6 to 6
- prompt_keys: bfloat16 [8192, 256], P(('grp', 'ctx')), parts along dimension 0, may hold values from -9.5625 to 9.5625
- prompt_values: bfloat16 [8192, 256], P(('grp', 'ctx')), parts along dimension 0, may hold values from -6 to 6
- block_lists: int32 [32, 16, 4, 8], P('tp', ('grp', 'ctx')), parts along dimension 1, may hold values from 0 to 15, as said below
- tile_counts: int32 [32, 16, 4], P('tp', ('grp', 'ctx')), parts along dimension 1, may hold values from 0 to 8, as said below
- out_weight: bfloat16 [4096, 4096], P('tp'), may hold values from -0.09375 to 0.09375
- residual: bfloat16 [16, 128, 4096], P(('grp', 'ctx')), parts along dimension 0, may hold values from -5 to 5
- norm_gain: bfloat16 [4096], P('tp'), may hold values from 0.5 to 1.5
Outputs:
- stream: bfloat16 [16, 128, 4096], P(('grp', 'ctx'), None, 'tp'), parts along dimension 0
- normed: bfloat16 [16, 128, 4096], P(('grp', 'ctx'), None, 'tp'), parts along dimension 0
The draws below stay inside these ranges and needn't reach their ends.
There are 2 independent parts, one for each index of `grp`. The reference program is written for one: setup_inputs(seed, part) draws one part's arguments, and reference() takes and returns one part's arrays. A program takes and returns all parts, laid end to end along the dimension named above; an argument that names none is the same for every part. Nothing has to cross between parts.
Inputs may be any that keep to these rules, and one draw needn't show every extreme that they name: `block_lists`: block numbers within one source shard of 1024 rows; the 8 entries of one list are distinct, and entries past the list's count are valid numbers that are not used. `tile_counts`: for every head and continuation some source has all 8 entries used; a count may be 0.
All inputs are finite; a program needn't handle non-finite values.
Results may differ from the reference program's by a relative error of at most 0.013.
Values may be sent and summed in bfloat16 or wider, within the bound.
No kernel may reach another device: no remote copies, remote signals or barrier semaphores. Data moves between devices by JAX's collectives and lax.ppermute only.
A program may use at most 64 MiB of HBM per device.

```python
import math
import jax
import jax.numpy as jnp
from jax import lax

D = 4096
HEADS = 32
KVH = 2
HD = 128
CLEN = 128
BLK = 64
TILES = 8
BLOCKS_DEV = 16
CONTS = 8
PROMPT = 4096
N_CTX = 4


def draw_queries(key, part):
    key = jax.random.fold_in(key, 1)
    drawn = jax.random.truncated_normal(key, -6.0, 6.0, (CONTS, CLEN, HEADS, HD), jnp.float32) * 1.6
    return drawn.reshape(CONTS, CLEN, HEADS * HD).astype(jnp.bfloat16)


def draw_cont_keys(key, part):
    key = jax.random.fold_in(key, 2)
    drawn = jax.random.truncated_normal(key, -6.0, 6.0, (CONTS, CLEN, KVH, HD), jnp.float32) * 1.6
    return drawn.reshape(CONTS, CLEN, KVH * HD).astype(jnp.bfloat16)


def draw_residual(key, part):
    key = jax.random.fold_in(key, 3)
    column_scale = 0.25 + 0.5 * jnp.arange(D, dtype=jnp.float32) / D
    drawn = jax.random.truncated_normal(key, -6.0, 6.0, (CONTS, CLEN, D), jnp.float32) * column_scale
    return drawn.astype(jnp.bfloat16)


def draw_block_lists(key, part):
    key = jax.random.fold_in(key, 11)
    ranking = jax.random.randint(key, (HEADS, CONTS, N_CTX, BLOCKS_DEV), 0, 2 ** 20) * BLOCKS_DEV
    ranking = ranking + jnp.arange(BLOCKS_DEV, dtype=jnp.int32)
    ordering = jnp.argsort(ranking, axis=-1, stable=True)
    return ordering[..., :TILES].astype(jnp.int32)


def draw_tile_counts(key, part):
    key = jax.random.fold_in(key, 12)
    key_main, key_heads = jax.random.split(key)
    base_count = jax.random.randint(key_main, (HEADS, CONTS, N_CTX), 0, TILES + 1)
    head_level = jax.random.randint(key_heads, (HEADS, 1, 1), 0, TILES // 2 + 1)
    counted = jnp.minimum(base_count + head_level, TILES)
    heads_pos = jnp.arange(HEADS)[:, None, None]
    conts_pos = jnp.arange(CONTS)[None, :, None]
    source_pos = jnp.arange(N_CTX)[None, None, :]
    forced = (heads_pos + conts_pos + source_pos) % 3 == 0
    return jnp.where(forced, TILES, counted).astype(jnp.int32)


def steps_of(key, extent, shards, smallest, high):
    factor_of, own = 1.0, jax.random.fold_in(key, 6)
    for position, blocks in shards:
        heights = jnp.exp(jax.random.uniform(jax.random.fold_in(own, position), (blocks,), jnp.float32, smallest / len(shards), high / len(shards)))
        factor_of = factor_of * jnp.repeat(heights, extent[position] // blocks).reshape([-1 if axis == position else 1 for axis in range(len(extent))])
    return factor_of


def scatter_about(key, dims, scale, bound, cuts=(), held_as=jnp.bfloat16):
    entries = jax.random.normal(key, dims, jnp.float32) * scale
    if len(cuts) > 0:
        entries = steps_of(key, dims, cuts, -0.22, 0.18) * entries
    return jnp.clip(entries, min=-bound, max=bound).astype(held_as)


def setup_inputs(seed: int = 0, part: int = 0) -> dict:
    keys = jax.random.split(jax.random.key(seed), 11)
    part_splits = jax.random.split(jax.random.fold_in(keys[10], part), 11)
    queries = draw_queries(jax.random.fold_in(jax.random.fold_in(keys[10], part), 71), part)
    cont_keys = draw_cont_keys(jax.random.fold_in(jax.random.fold_in(keys[10], part), 71), part)
    cont_values = scatter_about(part_splits[2], (CONTS, CLEN, KVH * HD), 1.0, 6.0, ((0, 4),))
    prompt_keys = scatter_about(part_splits[3], (PROMPT, KVH * HD), 1.6, 9.5625, ((0, 4),))
    prompt_values = scatter_about(part_splits[4], (PROMPT, KVH * HD), 1.0, 6.0, ((0, 4),))
    block_lists = draw_block_lists(jax.random.fold_in(jax.random.fold_in(keys[10], part), 71), part)
    tile_counts = draw_tile_counts(jax.random.fold_in(jax.random.fold_in(keys[10], part), 71), part)
    out_weight = scatter_about(keys[7], (HEADS * HD, D), (HEADS * HD) ** -0.5, 0.09375, ((0, 4),))
    residual = draw_residual(jax.random.fold_in(jax.random.fold_in(keys[10], part), 71), part)
    norm_gain = jnp.clip(1.0 + 0.1 * jax.random.normal(keys[9], (D,), jnp.float32), 0.5, 1.5).astype(jnp.bfloat16)
    return {"queries": queries, "cont_keys": cont_keys, "cont_values": cont_values, "prompt_keys": prompt_keys, "prompt_values": prompt_values, "block_lists": block_lists, "tile_counts": tile_counts, "out_weight": out_weight, "residual": residual, "norm_gain": norm_gain}


def reference(queries, cont_keys, cont_values, prompt_keys, prompt_values, block_lists, tile_counts, out_weight, residual, norm_gain):
    scaling = 1.0 / math.sqrt(HD)
    block_total = PROMPT // BLK
    prompt_key_blocks = prompt_keys.reshape(block_total, BLK, KVH, HD)
    prompt_value_blocks = prompt_values.reshape(block_total, BLK, KVH, HD)
    query_heads = queries.reshape(CONTS, CLEN, HEADS, HD)
    cont_key_heads = cont_keys.reshape(CONTS, CLEN, KVH, HD)
    cont_value_heads = cont_values.reshape(CONTS, CLEN, KVH, HD)
    positions = jnp.arange(CLEN, dtype=jnp.int32)
    causal = (positions[:, None] >= positions[None, :])[None]
    tile_index = jnp.arange(TILES, dtype=jnp.int32)
    offsets = (jnp.arange(N_CTX, dtype=jnp.int32) * BLOCKS_DEV).astype(jnp.int32)

    def one_head(head):
        kv_group = head // (HEADS // KVH)
        lists = (block_lists[head] + offsets[None, :, None]).astype(jnp.int32).reshape(CONTS, N_CTX * TILES)
        usable = (tile_index[None, None, :] < tile_counts[head][:, :, None]).reshape(CONTS, N_CTX * TILES)
        usable = jnp.repeat(usable, BLK, axis=1)[:, None, :]
        head_keys = lax.dynamic_index_in_dim(prompt_key_blocks, kv_group, 2, keepdims=False)
        head_values = lax.dynamic_index_in_dim(prompt_value_blocks, kv_group, 2, keepdims=False)
        key_tiles = head_keys[lists].reshape(CONTS, N_CTX * TILES * BLK, HD).astype(jnp.float32)
        value_tiles = head_values[lists].reshape(CONTS, N_CTX * TILES * BLK, HD).astype(jnp.float32)
        query_rows = lax.dynamic_index_in_dim(query_heads, head, 2, keepdims=False).astype(jnp.float32)
        own_keys = lax.dynamic_index_in_dim(cont_key_heads, kv_group, 2, keepdims=False).astype(jnp.float32)
        own_values = lax.dynamic_index_in_dim(cont_value_heads, kv_group, 2, keepdims=False).astype(jnp.float32)
        prompt_scores = jnp.einsum('cqd,ckd->cqk', query_rows, key_tiles) * scaling
        own_scores = jnp.einsum('cqd,ckd->cqk', query_rows, own_keys) * scaling
        very_low = jnp.float32(-1e+30)
        top = jnp.maximum(lax.optimization_barrier(jnp.max(jnp.where(usable, prompt_scores, very_low), axis=-1)), lax.optimization_barrier(jnp.max(jnp.where(causal, own_scores, very_low), axis=-1)))
        prompt_weights = jnp.where(usable, jnp.exp(prompt_scores - top[..., None]), jnp.float32(0.0))
        own_weights = jnp.where(causal, jnp.exp(own_scores - top[..., None]), jnp.float32(0.0))
        total = lax.optimization_barrier(jnp.sum(prompt_weights, axis=-1)) + lax.optimization_barrier(jnp.sum(own_weights, axis=-1))
        prompt_rounded = lax.optimization_barrier(prompt_weights.astype(jnp.bfloat16)).astype(jnp.float32)
        own_rounded = lax.optimization_barrier(own_weights.astype(jnp.bfloat16)).astype(jnp.float32)
        weighted = jnp.einsum('cqk,ckd->cqd', prompt_rounded, value_tiles) + jnp.einsum('cqk,ckd->cqd', own_rounded, own_values)
        return (weighted / total[..., None]).astype(jnp.bfloat16)
    head_results = lax.map(one_head, jnp.arange(HEADS, dtype=jnp.int32))
    attended = head_results.transpose(1, 2, 0, 3).reshape(CONTS * CLEN, HEADS * HD)
    projected = jnp.dot(attended, out_weight, preferred_element_type=jnp.float32).reshape(CONTS, CLEN, D)
    stream_sum = residual.astype(jnp.float32) + projected
    mean_square = lax.optimization_barrier(jnp.mean(stream_sum * stream_sum, axis=-1, keepdims=True))
    normed = stream_sum * lax.rsqrt(mean_square + 1e-05) * norm_gain.astype(jnp.float32)
    return (stream_sum.astype(jnp.bfloat16), normed.astype(jnp.bfloat16))
```

```python
import functools
import math

import jax
import jax.numpy as jnp
from jax import lax
from jax.experimental import pallas as pl
from jax.experimental.pallas import tpu as pltpu
from jax.sharding import PartitionSpec as P

HEADS = 32
KVH = 2
HD = 128
BLK = 64
TILES = 8
CORES = 2

VERY_LOW = -1e30
TO_LOG2 = math.log2(math.e) / math.sqrt(HD)

VMEM_LIMIT = 40 * 1024 * 1024
NT = (((1,), (1,)), ((), ()))


def absorb(state, scores, values):
    top, total, acc = state
    new_top = jnp.maximum(top, jnp.max(scores, axis=1, keepdims=True))
    weights = jnp.exp2((scores - new_top) * TO_LOG2)
    factor = jnp.exp2((top - new_top) * TO_LOG2)
    total = total * factor + jnp.sum(weights, axis=1, keepdims=True)
    acc = acc * factor + jnp.dot(
        weights.astype(jnp.bfloat16), values, preferred_element_type=jnp.float32
    )
    return new_top, total, acc


def load_state(acc_ref, stat_ref, index):
    return stat_ref[index, :, 0:1], stat_ref[index, :, 64:65], acc_ref[index]


def store_state(acc_ref, stat_ref, index, state):
    top, total, acc = state
    lane = lax.broadcasted_iota(jnp.int32, stat_ref.shape[1:], 1)
    stat_ref[index] = jnp.where(lane < 64, top, total)
    acc_ref[index] = acc


def shard_scores(lists_ref, counts_ref, q_ref, kv_ref, source, sources, head, cont):
    conts = q_ref.shape[0]
    place = (head * conts + cont) * sources + source
    count = counts_ref[place]
    starts = [
        pl.multiple_of(lists_ref[place * TILES + t] * BLK, BLK) for t in range(TILES)
    ]
    query = q_ref[cont, :, pl.ds(pl.multiple_of(head * HD, HD), HD)]
    keys = jnp.concatenate([kv_ref[pl.ds(s, BLK), 0:HD] for s in starts], axis=0)
    values = jnp.concatenate([kv_ref[pl.ds(s, BLK), HD : 2 * HD] for s in starts], axis=0)
    scores = lax.dot_general(query, keys, NT, preferred_element_type=jnp.float32)
    column = lax.broadcasted_iota(jnp.int32, scores.shape, 1)
    return jnp.where(column < count * BLK, scores, VERY_LOW), values


def first_kernel(
    sources, lists_ref, counts_ref, q_ref, kv_ref, ck_ref, cv_ref, acc_ref, stat_ref
):
    conts, length, width = q_ref.shape
    heads = width // HD
    group = lax.axis_index("tp") * heads // (HEADS // KVH)
    lanes = pl.ds(pl.multiple_of(group * HD, HD), HD)
    own = lax.axis_index("ctx")

    def one_head(head, carry):
        made = []
        for cont in range(conts):
            query = q_ref[cont, :, pl.ds(pl.multiple_of(head * HD, HD), HD)]
            scores = lax.dot_general(
                query, ck_ref[cont, :, lanes], NT, preferred_element_type=jnp.float32
            )
            row = lax.broadcasted_iota(jnp.int32, scores.shape, 0)
            column = lax.broadcasted_iota(jnp.int32, scores.shape, 1)
            scores = jnp.where(column <= row, scores, VERY_LOW)
            more, values = shard_scores(
                lists_ref, counts_ref, q_ref, kv_ref, own, sources, head, cont
            )
            made.append((jnp.concatenate([scores, more], axis=1), values))
        states = []
        for cont in range(conts):
            scores, values = made[cont]
            values = jnp.concatenate([cv_ref[cont, :, lanes], values], axis=0)
            start = (
                jnp.full((length, 1), VERY_LOW, jnp.float32),
                jnp.zeros((length, 1), jnp.float32),
                jnp.zeros((length, HD), jnp.float32),
            )
            states.append(absorb(start, scores, values))
        for cont in range(conts):
            store_state(acc_ref, stat_ref, head * conts + cont, states[cont])
        return carry

    lax.fori_loop(0, heads, one_head, 0)


def step_sources(step, sources):
    spot = lax.axis_index("ctx")
    core = lax.axis_index("tp") % CORES
    mine = jnp.where(core == 0, spot - step, spot + step)
    theirs = jnp.where(core == 0, spot + step, spot - step)
    return mine, theirs


def absorb_arrivals(step, sources, lists_ref, counts_ref, q_ref, kv_refs, before, after):
    conts, _, width = q_ref.shape
    heads = width // HD
    for part, source in enumerate(step_sources(step, sources)):
        valid = (source >= 0) & (source < sources)
        held = before if part == 0 else after

        @pl.when(valid)
        def _():
            def one_head(head, carry):
                pairs = [head * conts + cont for cont in range(conts)]
                states = [load_state(*held, pair) for pair in pairs]
                made = [
                    shard_scores(
                        lists_ref, counts_ref, q_ref, kv_refs[part], source, sources, head, cont
                    )
                    for cont in range(conts)
                ]
                states = [absorb(state, *got) for state, got in zip(states, made)]
                for pair, state in zip(pairs, states):
                    store_state(*after, pair, state)
                return carry

            lax.fori_loop(0, heads, one_head, 0)

        if part == 0:

            @pl.when(jnp.logical_not(valid))
            def _():
                for source_ref, target_ref in zip(before, after):
                    target_ref[...] = source_ref[...]


def middle_kernel(
    step,
    sources,
    lists_ref,
    counts_ref,
    q_ref,
    mine_ref,
    theirs_ref,
    acc_in,
    stat_in,
    acc_ref,
    stat_ref,
):
    absorb_arrivals(
        step,
        sources,
        lists_ref,
        counts_ref,
        q_ref,
        (mine_ref, theirs_ref),
        (acc_in, stat_in),
        (acc_ref, stat_ref),
    )


def last_kernel(
    step,
    sources,
    lists_ref,
    counts_ref,
    q_ref,
    mine_ref,
    theirs_ref,
    acc_in,
    stat_in,
    weight_ref,
    attended_ref,
    give_ref,
    acc_ref,
    stat_ref,
    weight_buf,
    sems,
):
    conts, length, width = q_ref.shape
    heads = width // HD
    chips, rows, share = give_ref.shape
    place = lax.axis_index("tp")
    chip, core = place // CORES, place % CORES
    copies = []
    for k in range(chips):
        start = (lax.rem(chip + k, chips) * CORES + 1 - core) * share
        copies.append(
            pltpu.make_async_copy(
                weight_ref.at[:, pl.ds(pl.multiple_of(start, HD), share)],
                weight_buf.at[k],
                sems.at[k],
            )
        )
    for copy in copies:
        copy.start()
    absorb_arrivals(
        step,
        sources,
        lists_ref,
        counts_ref,
        q_ref,
        (mine_ref, theirs_ref),
        (acc_in, stat_in),
        (acc_ref, stat_ref),
    )

    def finish(head, carry):
        for cont in range(conts):
            _, total, acc = load_state(acc_ref, stat_ref, head * conts + cont)
            attended_ref[
                cont * length : (cont + 1) * length,
                pl.ds(pl.multiple_of(head * HD, HD), HD),
            ] = (acc / total).astype(jnp.bfloat16)
        return carry

    lax.fori_loop(0, heads, finish, 0)
    for k in range(chips):
        copies[k].wait()

        def columns(j, carry):
            lanes = pl.ds(pl.multiple_of(j * 256, 256), 256)
            give_ref[k, :, lanes] = jnp.dot(
                attended_ref[...], weight_buf[k, :, lanes], preferred_element_type=jnp.float32
            ).astype(jnp.bfloat16)
            return carry

        lax.fori_loop(0, share // 256, columns, 0)


def keep_kernel(_, attended_ref, weight_ref, keep_ref):
    keep_ref[0] = jnp.dot(
        attended_ref[...], weight_ref[...], preferred_element_type=jnp.float32
    )


def whole(space):
    return pl.BlockSpec(memory_space=space)


def shards(
    queries,
    cont_keys,
    cont_values,
    prompt_keys,
    prompt_values,
    block_lists,
    tile_counts,
    out_weight,
    residual,
    norm_gain,
    *,
    sources,
    members,
):
    conts, length, width = queries.shape
    heads = width // HD
    model_width = residual.shape[2]
    share = norm_gain.shape[0]
    rows = conts * length
    chips = members // CORES
    place = lax.axis_index("tp")
    chip, core = place // CORES, place % CORES
    group = place * heads // (HEADS // KVH)

    payload = jnp.concatenate(
        [
            lax.dynamic_slice_in_dim(prompt_keys, group * HD, HD, 1),
            lax.dynamic_slice_in_dim(prompt_values, group * HD, HD, 1),
        ],
        axis=1,
    )
    along = [
        (z * members + t, (z + (1 if t % CORES == 0 else -1)) * members + t)
        for z in range(sources)
        for t in range(members)
        if 0 <= z + (1 if t % CORES == 0 else -1) < sources
    ]
    sibling = [(t, t ^ 1) for t in range(members)]

    lists = block_lists.reshape(-1)
    counts = tile_counts.reshape(-1)
    pairs = heads * conts
    state_shape = (
        jax.ShapeDtypeStruct((pairs, length, HD), jnp.float32),
        jax.ShapeDtypeStruct((pairs, length, HD), jnp.float32),
    )
    params = pltpu.CompilerParams(vmem_limit_bytes=VMEM_LIMIT)

    def cost(keys):
        return pl.CostEstimate(
            flops=4 * pairs * length * keys * HD,
            bytes_accessed=4 * 2**20,
            transcendentals=pairs * length * keys,
        )

    smem, vmem = whole(pltpu.SMEM), whole(pltpu.VMEM)
    state = pl.pallas_call(
        functools.partial(first_kernel, sources),
        out_shape=state_shape,
        in_specs=[smem, smem] + [vmem] * 4,
        out_specs=(vmem, vmem),
        compiler_params=params,
        cost_estimate=cost(TILES * BLK + length),
        name="attend_own",
    )(lists, counts, queries, payload, cont_keys, cont_values)

    moving = payload
    for step in range(1, sources):
        moving = lax.ppermute(moving, ("ctx", "tp"), along)
        swapped = lax.ppermute(moving, "tp", sibling)
        if step < sources - 1:
            state = pl.pallas_call(
                functools.partial(middle_kernel, step, sources),
                out_shape=state_shape,
                in_specs=[smem, smem] + [vmem] * 5,
                out_specs=(vmem, vmem),
                input_output_aliases={5: 0, 6: 1},
                compiler_params=params,
                cost_estimate=cost(TILES * BLK),
                name="attend_step",
            )(lists, counts, queries, moving, swapped, *state)

    attended, give = pl.pallas_call(
        functools.partial(last_kernel, sources - 1, sources),
        out_shape=(
            jax.ShapeDtypeStruct((rows, width), jnp.bfloat16),
            jax.ShapeDtypeStruct((chips, rows, share), jnp.bfloat16),
        ),
        in_specs=[smem, smem] + [vmem] * 5 + [whole(pl.ANY)],
        out_specs=(vmem, vmem),
        scratch_shapes=[
            pltpu.VMEM((pairs, length, HD), jnp.float32),
            pltpu.VMEM((pairs, length, HD), jnp.float32),
            pltpu.VMEM((chips, width, share), jnp.bfloat16),
            pltpu.SemaphoreType.DMA((chips,)),
        ],
        compiler_params=params,
        cost_estimate=cost(TILES * BLK),
        name="attend_last",
    )(lists, counts, queries, moving, swapped, *state, out_weight)

    got = lax.ppermute(give, "tp", sibling)
    tile = 512
    tiles = share // tile
    order = ((chip + jnp.arange(chips)) % chips * CORES + core).astype(jnp.int32)
    keep = pl.pallas_call(
        keep_kernel,
        out_shape=jax.ShapeDtypeStruct((chips, rows, share), jnp.float32),
        grid_spec=pltpu.PrefetchScalarGridSpec(
            num_scalar_prefetch=1,
            grid=(chips * tiles,),
            in_specs=[
                pl.BlockSpec((rows, width), lambda i, order: (0, 0)),
                pl.BlockSpec(
                    (width, tile), lambda i, order: (0, order[i // tiles] * tiles + i % tiles)
                ),
            ],
            out_specs=pl.BlockSpec((1, rows, tile), lambda i, order: (i // tiles, 0, i % tiles)),
        ),
        compiler_params=params,
        cost_estimate=pl.CostEstimate(
            flops=2 * rows * width * share * chips,
            bytes_accessed=2 * width * share * chips,
            transcendentals=0,
        ),
        name="project_keep",
    )(order, attended, out_weight)

    total = jnp.zeros((rows, share), jnp.float32)
    for k in range(1, chips):
        onward = (keep[k] + got[k].astype(jnp.float32)).astype(jnp.bfloat16)
        to_chip = [
            (t, (t // CORES + k) % chips * CORES + t % CORES) for t in range(members)
        ]
        total = total + lax.ppermute(onward, "tp", to_chip).astype(jnp.float32)
    flat_residual = residual.reshape(rows, model_width)
    own_residual = lax.dynamic_slice_in_dim(flat_residual, place * share, share, 1)
    near = own_residual.astype(jnp.float32) + (keep[0] + got[0].astype(jnp.float32))
    stream_sum = near + total
    squares = jnp.sum(stream_sum * stream_sum, axis=-1)
    all_squares = squares
    for k in range(1, members):
        shift = [(t, (t + k) % members) for t in range(members)]
        all_squares = all_squares + lax.ppermute(squares, "tp", shift)
    scale = lax.rsqrt(all_squares / model_width + 1e-05)[:, None]
    normed = stream_sum * scale * norm_gain.astype(jnp.float32)
    shape = (conts, length, share)
    return (
        stream_sum.astype(jnp.bfloat16).reshape(shape),
        normed.astype(jnp.bfloat16).reshape(shape),
    )


def solution(mesh):
    placed = (
        P(("grp", "ctx"), None, "tp"),
        P(("grp", "ctx"), None, None),
        P(("grp", "ctx"), None, None),
        P(("grp", "ctx"), None),
        P(("grp", "ctx"), None),
        P("tp", ("grp", "ctx"), None, None),
        P("tp", ("grp", "ctx"), None),
        P("tp", None),
        P(("grp", "ctx"), None, None),
        P("tp"),
    )
    return jax.shard_map(
        functools.partial(
            shards, sources=mesh.shape["ctx"], members=mesh.shape["tp"]
        ),
        mesh=mesh,
        in_specs=placed,
        out_specs=(P(("grp", "ctx"), None, "tp"), P(("grp", "ctx"), None, "tp")),
        check_vma=False,
    )
```

```python
import functools
import math

import jax
import jax.numpy as jnp
from jax import lax
from jax.experimental import pallas as pl
from jax.experimental.pallas import tpu as pltpu
from jax.sharding import PartitionSpec as P

HEADS = 32
KVH = 2
HD = 128
BLK = 64
TILES = 8
CORES = 2
TOKENS = TILES * BLK

VERY_LOW = -1e30
TO_LOG2 = math.log2(math.e) / math.sqrt(HD)

VMEM_LIMIT = 24 * 1024 * 1024
NT = (((1,), (1,)), ((), ()))


def key_group(heads):
    return lax.axis_index("tp") * heads // (HEADS // KVH)


def group_lanes(heads):
    return pl.ds(pl.multiple_of(key_group(heads) * HD, HD), HD)


def pack_kernel(heads, keys_ref, values_ref, packed_ref, values_buf, sems):
    rows = keys_ref.shape[0]
    lanes = group_lanes(heads)
    keys_copy = pltpu.make_async_copy(
        keys_ref.at[:, lanes], packed_ref.at[pl.ds(0, rows)], sems.at[0]
    )
    values_copy = pltpu.make_async_copy(values_ref.at[:, lanes], values_buf, sems.at[1])
    values_copy.start()
    keys_copy.start()
    values_copy.wait()
    for p in range(rows // HD):
        packed_ref[rows + p * HD : rows + (p + 1) * HD, :] = values_buf[
            p * HD : (p + 1) * HD, :
        ].T
    keys_copy.wait()


def both_ways(kv_ref, flipped_ref):
    rows = kv_ref.shape[0] // 2
    for p in range(rows // HD):
        pair = kv_ref[rows + p * HD : rows + (p + 1) * HD, :]
        flipped_ref[p * HD : (p + 1) * HD, :] = pair
        flipped_ref[rows + p * HD : rows + (p + 1) * HD, :] = jnp.concatenate(
            [pair[:, BLK:], pair[:, :BLK]], axis=1
        )


def shard_scores(lists_ref, counts_ref, q_ref, kv_ref, flipped_ref, source, sources, head, cont):
    conts = q_ref.shape[0]
    pairs = kv_ref.shape[0] // 2 // HD
    place = (head * conts + cont) * sources + source
    count = counts_ref[place]
    blocks = [lists_ref[place * TILES + t] for t in range(TILES)]
    query = q_ref[cont, :, pl.ds(pl.multiple_of(head * HD, HD), HD)]
    keys = jnp.concatenate(
        [kv_ref[pl.ds(pl.multiple_of(b * BLK, BLK), BLK), :] for b in blocks], axis=0
    )
    scores = lax.dot_general(keys, query, NT, preferred_element_type=jnp.float32)
    lane = lax.broadcasted_iota(jnp.int32, (HD, HD), 1)
    halves = []
    for t, b in enumerate(blocks):
        spot = ((b + t) % 2 * pairs + b // 2) * HD
        halves.append(flipped_ref[pl.ds(pl.multiple_of(spot, HD), HD), :])
    values = jnp.concatenate(
        [jnp.where(lane < BLK, a, b) for a, b in zip(halves[::2], halves[1::2])], axis=1
    )
    tiles = [
        (scores[t * BLK : (t + 1) * BLK], t < count) for t in range(TILES)
    ]
    return tiles, values


def fold(op, tile):
    return functools.reduce(op, [tile[i : i + 8] for i in range(0, tile.shape[0], 8)])


def absorb(state, tiles, values):
    top, total, acc = state
    tops = [
        jnp.where(live, fold(jnp.maximum, tile), VERY_LOW) for tile, live in tiles
    ]
    best = jnp.max(functools.reduce(jnp.maximum, tops), axis=0, keepdims=True)
    new_top = jnp.maximum(top, best)
    weights = [
        jnp.exp2((tile - jnp.where(live, new_top, -VERY_LOW)) * TO_LOG2) for tile, live in tiles
    ]
    factor = jnp.exp2((top - new_top) * TO_LOG2)
    sums = functools.reduce(jnp.add, [fold(jnp.add, w) for w in weights])
    total = total * factor + jnp.sum(sums, axis=0, keepdims=True)
    rounded = jnp.concatenate([w.astype(jnp.bfloat16) for w in weights], axis=0)
    acc = acc * factor + jnp.dot(values, rounded, preferred_element_type=jnp.float32)
    return new_top, total, acc


def load_state(acc_ref, stat_ref, index):
    both = stat_ref[index]
    return both[0:1], both[1:2], acc_ref[index]


def store_state(acc_ref, stat_ref, index, state):
    top, total, acc = state
    stat_ref[index] = jnp.concatenate([top, total] + [total] * 6, axis=0)
    acc_ref[index] = acc


def first_kernel(
    sources,
    lists_ref,
    counts_ref,
    q_ref,
    kv_ref,
    ck_ref,
    cv_ref,
    weight_ref,
    acc_ref,
    stat_ref,
    give_ref,
    keep_ref,
    flipped_ref,
    own_ref,
    sems,
):
    conts, length, width = q_ref.shape
    heads = width // HD
    chips, _, share = give_ref.shape
    place = lax.axis_index("tp")
    chip, core = place // CORES, place % CORES
    copies = []
    for which, target in enumerate((give_ref, keep_ref)):
        held = core if which else 1 - core
        for k in range(chips):
            start = (lax.rem(chip + k, chips) * CORES + held) * share
            copies.append(
                pltpu.make_async_copy(
                    weight_ref.at[:, pl.ds(pl.multiple_of(start, HD), share)],
                    target.at[k],
                    sems.at[which, k],
                )
            )
    for copy in copies:
        copy.start()
    lanes = group_lanes(heads)
    own = lax.axis_index("ctx")
    both_ways(kv_ref, flipped_ref)
    for cont in range(conts):
        own_ref[cont] = cv_ref[cont, :, lanes].T

    def one_head(head, carry):
        made = []
        for cont in range(conts):
            query = q_ref[cont, :, pl.ds(pl.multiple_of(head * HD, HD), HD)]
            scores = lax.dot_general(
                ck_ref[cont, :, lanes], query, NT, preferred_element_type=jnp.float32
            )
            key = lax.broadcasted_iota(jnp.int32, scores.shape, 0)
            row = lax.broadcasted_iota(jnp.int32, scores.shape, 1)
            scores = jnp.where(key <= row, scores, VERY_LOW)
            tiles, values = shard_scores(
                lists_ref, counts_ref, q_ref, kv_ref, flipped_ref, own, sources, head, cont
            )
            made.append(
                ([(scores, True)] + tiles, jnp.concatenate([own_ref[cont], values], axis=1))
            )
        states = []
        for cont in range(conts):
            start = (
                jnp.full((1, length), VERY_LOW, jnp.float32),
                jnp.zeros((1, length), jnp.float32),
                jnp.zeros((HD, length), jnp.float32),
            )
            states.append(absorb(start, *made[cont]))
        for cont in range(conts):
            store_state(acc_ref, stat_ref, head * conts + cont, states[cont])
        return carry

    lax.fori_loop(0, heads, one_head, 0)
    for copy in copies:
        copy.wait()


def arrivals(step, sources):
    spot = lax.axis_index("ctx")
    core = lax.axis_index("tp") % CORES
    if sources == 4:
        if step == 1:
            mine = jnp.bitwise_xor(spot, 1 + core)
            return ((mine, True), (jnp.bitwise_xor(mine, 3), True))
        far = jnp.bitwise_xor(spot, 3)
        return ((far, core == 1), (far, core == 0))
    mine = jnp.where(core == 0, spot - step, spot + step)
    theirs = jnp.where(core == 0, spot + step, spot - step)
    return tuple((s, (s >= 0) & (s < sources)) for s in (mine, theirs))


def steps_of(sources):
    return 2 if sources == 4 else sources - 1


def absorb_arrivals(
    step, sources, chosen, lists_ref, counts_ref, q_ref, kv_refs, flipped_ref, before, after
):
    conts, _, width = q_ref.shape
    heads = width // HD
    together = 2 // len(chosen)
    one_of_two = sources == 4 and step == 2
    for part, (source, valid) in enumerate(arrivals(step, sources)):
        held = before if part == 0 or one_of_two else after

        def absorb_part():
            both_ways(kv_refs[part], flipped_ref)

            def some_heads(index, carry):
                work = [
                    (index * together + j, cont) for j in range(together) for cont in chosen
                ]
                pairs = [head * conts + cont for head, cont in work]
                states = [load_state(*held, pair) for pair in pairs]
                made = [
                    shard_scores(
                        lists_ref,
                        counts_ref,
                        q_ref,
                        kv_refs[part],
                        flipped_ref,
                        source,
                        sources,
                        head,
                        cont,
                    )
                    for head, cont in work
                ]
                states = [absorb(state, *got) for state, got in zip(states, made)]
                for pair, state in zip(pairs, states):
                    store_state(*after, pair, state)
                return carry

            lax.fori_loop(0, heads // together, some_heads, 0)

        if valid is True:
            absorb_part()
            continue
        pl.when(valid)(absorb_part)
        if part == 0 and not one_of_two:

            @pl.when(jnp.logical_not(valid))
            def _():
                for source_ref, target_ref in zip(before, after):
                    target_ref[...] = source_ref[...]


def middle_kernel(
    step,
    sources,
    lists_ref,
    counts_ref,
    q_ref,
    mine_ref,
    theirs_ref,
    acc_in,
    stat_in,
    acc_ref,
    stat_ref,
    flipped_ref,
):
    absorb_arrivals(
        step,
        sources,
        tuple(range(q_ref.shape[0])),
        lists_ref,
        counts_ref,
        q_ref,
        (mine_ref, theirs_ref),
        flipped_ref,
        (acc_in, stat_in),
        (acc_ref, stat_ref),
    )


def last_kernel(
    step,
    sources,
    cont,
    lists_ref,
    counts_ref,
    q_ref,
    mine_ref,
    theirs_ref,
    acc_in,
    stat_in,
    weight_ref,
    attended_ref,
    give_ref,
    acc_ref,
    stat_ref,
    flipped_ref,
):
    conts, length, width = q_ref.shape
    heads = width // HD
    absorb_arrivals(
        step,
        sources,
        (cont,),
        lists_ref,
        counts_ref,
        q_ref,
        (mine_ref, theirs_ref),
        flipped_ref,
        (acc_in, stat_in),
        (acc_ref, stat_ref),
    )
    for head in range(heads):
        _, total, acc = load_state(acc_ref, stat_ref, head * conts + cont)
        attended_ref[:, head * HD : (head + 1) * HD] = (acc / total).T.astype(jnp.bfloat16)
    project(attended_ref, weight_ref, give_ref)


def project(attended_ref, weight_ref, out_ref):
    chips, _, share = weight_ref.shape
    for k in range(chips):
        out_ref[k] = jnp.dot(
            attended_ref[...], weight_ref[k], preferred_element_type=jnp.float32
        ).astype(out_ref.dtype)


def onward_kernel(attended_ref, weight_ref, got_ref, *onward_refs):
    for k, onward_ref in enumerate(onward_refs, 1):
        onward_ref[...] = (
            jnp.dot(attended_ref[...], weight_ref[k], preferred_element_type=jnp.float32)
            + got_ref[k].astype(jnp.float32)
        ).astype(jnp.bfloat16)


def near_kernel(attended_ref, weight_ref, got_ref, residual_ref, near_ref):
    near_ref[...] = (
        residual_ref[...].astype(jnp.float32)
        + jnp.dot(attended_ref[...], weight_ref[0], preferred_element_type=jnp.float32)
        + got_ref[0].astype(jnp.float32)
    )


def shards(
    queries,
    cont_keys,
    cont_values,
    prompt_keys,
    prompt_values,
    block_lists,
    tile_counts,
    out_weight,
    residual,
    norm_gain,
    *,
    sources,
    members,
):
    conts, length, width = queries.shape
    heads = width // HD
    rows_dev = prompt_keys.shape[0]
    model_width = residual.shape[2]
    share = norm_gain.shape[0]
    chips = members // CORES
    place = lax.axis_index("tp")
    pairs = heads * conts
    params = pltpu.CompilerParams(vmem_limit_bytes=VMEM_LIMIT)
    smem = pl.BlockSpec(memory_space=pltpu.SMEM)
    vmem = pl.BlockSpec(memory_space=pltpu.VMEM)
    anywhere = pl.BlockSpec(memory_space=pltpu.HBM)

    def array(shape, dtype):
        return jax.ShapeDtypeStruct(shape, dtype)

    def cost(keys=0, flops=0, pairs=pairs):
        return pl.CostEstimate(flops=1024, bytes_accessed=1024, transcendentals=0)

    packed = pl.pallas_call(
        functools.partial(pack_kernel, heads),
        out_shape=array((2 * rows_dev, HD), jnp.bfloat16),
        in_specs=[anywhere] * 2,
        out_specs=vmem,
        scratch_shapes=[
            pltpu.VMEM((rows_dev, HD), jnp.bfloat16),
            pltpu.SemaphoreType.DMA((2,)),
        ],
        compiler_params=params,
        cost_estimate=cost(flops=2**20),
        name="pack",
    )(prompt_keys, prompt_values)

    def across(step):
        def target(z, t):
            if sources == 4 and step == 1:
                return z ^ (1 + t % CORES)
            if sources == 4:
                return z ^ 1 if t % CORES == 1 else None
            to = z + step if t % CORES == 0 else z - step
            return to if 0 <= to < sources else None

        return [
            (z * members + t, target(z, t) * members + t)
            for z in range(sources)
            for t in range(members)
            if target(z, t) is not None
        ]

    sibling = [(t, t ^ 1) for t in range(members)]
    steps = steps_of(sources)
    lists = block_lists.reshape(-1)
    counts = tile_counts.reshape(-1)
    state_shape = (
        array((pairs, HD, length), jnp.float32),
        array((pairs, 8, length), jnp.float32),
    )
    state_scratch = [pltpu.VMEM(s.shape, s.dtype) for s in state_shape]
    flipped = pltpu.VMEM((2 * rows_dev, HD), jnp.bfloat16)
    weight_shape = array((chips, width, share), jnp.bfloat16)

    *state, give_weight, keep_weight = pl.pallas_call(
        functools.partial(first_kernel, sources),
        out_shape=state_shape + (weight_shape, weight_shape),
        in_specs=[smem, smem] + [vmem] * 4 + [anywhere],
        out_specs=(vmem,) * 4,
        scratch_shapes=[
            flipped,
            pltpu.VMEM((conts, HD, length), jnp.bfloat16),
            pltpu.SemaphoreType.DMA((2, chips)),
        ],
        compiler_params=params,
        cost_estimate=cost(TOKENS + length),
        name="attend_own",
    )(lists, counts, queries, packed, cont_keys, cont_values, out_weight)

    mine = None
    for step in range(1, steps + 1):
        sent = mine if sources == 4 and step == 2 else packed
        mine = lax.ppermute(sent, ("ctx", "tp"), across(step))
        mine, state = lax.optimization_barrier((mine, tuple(state)))
        theirs = lax.ppermute(mine, "tp", sibling)
        if step < steps:
            state = pl.pallas_call(
                functools.partial(middle_kernel, step, sources),
                out_shape=state_shape,
                in_specs=[smem, smem] + [vmem] * 5,
                out_specs=(vmem, vmem),
                scratch_shapes=[flipped],
                compiler_params=params,
                cost_estimate=cost(TOKENS),
                name="attend_step",
            )(lists, counts, queries, mine, theirs, *state)

    attended, given, got = [], [], []
    for cont in range(conts):
        if cont > 0:
            state, given[-1] = lax.optimization_barrier((state, given[-1]))
        made, give = pl.pallas_call(
            functools.partial(last_kernel, steps, sources, cont),
            out_shape=(
                array((length, width), jnp.bfloat16),
                array((chips, length, share), jnp.bfloat16),
            ),
            in_specs=[smem, smem] + [vmem] * 6,
            out_specs=(vmem, vmem),
            scratch_shapes=state_scratch + [flipped],
            compiler_params=params,
            cost_estimate=cost(TOKENS, 2 * length * width * share * chips, heads),
            name="attend_last",
        )(lists, counts, queries, mine, theirs, *state, give_weight)
        attended.append(made)
        given.append(give)
    got = [lax.ppermute(give, "tp", sibling) for give in given]

    far = [[] for _ in range(conts)]
    for cont in range(conts):
        onward = pl.pallas_call(
            onward_kernel,
            out_shape=(array((length, share), jnp.bfloat16),) * (chips - 1),
            in_specs=[vmem] * 3,
            out_specs=(vmem,) * (chips - 1),
            compiler_params=params,
            cost_estimate=cost(flops=2 * length * width * share * (chips - 1)),
            name="project_onward",
        )(attended[cont], keep_weight, got[cont])
        for k in range(1, chips):
            to_chip = [
                (t, (t // CORES + k) % chips * CORES + t % CORES) for t in range(members)
            ]
            far[cont].append(lax.ppermute(onward[k - 1], "tp", to_chip))

    streams, norms = [], []
    gain = norm_gain.astype(jnp.float32)
    for cont in range(conts):
        own_residual = lax.dynamic_slice_in_dim(residual[cont], place * share, share, 1)
        near = pl.pallas_call(
            near_kernel,
            out_shape=array((length, share), jnp.float32),
            in_specs=[vmem] * 4,
            out_specs=vmem,
            compiler_params=params,
            cost_estimate=cost(flops=2 * length * width * share),
            name="project_near",
        )(attended[cont], keep_weight, got[cont], own_residual)
        stream_sum = near
        for part in far[cont]:
            stream_sum = stream_sum + part.astype(jnp.float32)
        squares = jnp.sum(stream_sum * stream_sum, axis=-1)
        all_squares = squares
        for k in range(1, members):
            shift = [(t, (t + k) % members) for t in range(members)]
            all_squares = all_squares + lax.ppermute(squares, "tp", shift)
        scale = lax.rsqrt(all_squares / model_width + 1e-05)[:, None]
        streams.append(stream_sum.astype(jnp.bfloat16))
        norms.append((stream_sum * scale * gain).astype(jnp.bfloat16))
    return jnp.stack(streams), jnp.stack(norms)


def solution(mesh):
    placed = (
        P(("grp", "ctx"), None, "tp"),
        P(("grp", "ctx"), None, None),
        P(("grp", "ctx"), None, None),
        P(("grp", "ctx"), None),
        P(("grp", "ctx"), None),
        P("tp", ("grp", "ctx"), None, None),
        P("tp", ("grp", "ctx"), None),
        P("tp", None),
        P(("grp", "ctx"), None, None),
        P("tp"),
    )
    return jax.shard_map(
        functools.partial(
            shards, sources=mesh.shape["ctx"], members=mesh.shape["tp"]
        ),
        mesh=mesh,
        in_specs=placed,
        out_specs=(P(("grp", "ctx"), None, "tp"), P(("grp", "ctx"), None, "tp")),
        check_vma=False,
    )
```

```python
import functools
import math

import jax
import jax.numpy as jnp
from jax import lax
from jax.experimental import pallas as pl
from jax.experimental.pallas import tpu as pltpu
from jax.sharding import PartitionSpec as P

HEADS = 32
KVH = 2
HD = 128
BLK = 64
TILES = 8
CORES = 2
TOKENS = TILES * BLK

VERY_LOW = -1e30
TO_LOG2 = math.log2(math.e) / math.sqrt(HD)

VMEM_LIMIT = 24 * 1024 * 1024
NT = (((1,), (1,)), ((), ()))


def key_group(heads):
    return lax.axis_index("tp") * heads // (HEADS // KVH)


def group_lanes(heads):
    return pl.ds(pl.multiple_of(key_group(heads) * HD, HD), HD)


def pack_kernel(heads, keys_ref, values_ref, packed_ref, values_buf, sems):
    rows = keys_ref.shape[0]
    lanes = group_lanes(heads)
    keys_copy = pltpu.make_async_copy(
        keys_ref.at[:, lanes], packed_ref.at[pl.ds(0, rows)], sems.at[0]
    )
    values_copy = pltpu.make_async_copy(values_ref.at[:, lanes], values_buf, sems.at[1])
    values_copy.start()
    keys_copy.start()
    values_copy.wait()
    for p in range(rows // HD):
        packed_ref[rows + p * HD : rows + (p + 1) * HD, :] = values_buf[
            p * HD : (p + 1) * HD, :
        ].T
    keys_copy.wait()


def both_ways(kv_ref, flipped_ref):
    rows = kv_ref.shape[0] // 2
    for p in range(rows // HD):
        pair = kv_ref[rows + p * HD : rows + (p + 1) * HD, :]
        flipped_ref[p * HD : (p + 1) * HD, :] = pair
        flipped_ref[rows + p * HD : rows + (p + 1) * HD, :] = jnp.concatenate(
            [pair[:, BLK:], pair[:, :BLK]], axis=1
        )


def shard_scores(lists_ref, counts_ref, q_ref, kv_ref, flipped_ref, source, sources, head, cont):
    conts = q_ref.shape[0]
    pairs = kv_ref.shape[0] // 2 // HD
    place = (head * conts + cont) * sources + source
    count = counts_ref[place]
    blocks = [lists_ref[place * TILES + t] for t in range(TILES)]
    query = q_ref[cont, :, pl.ds(pl.multiple_of(head * HD, HD), HD)]
    keys = jnp.concatenate(
        [kv_ref[pl.ds(pl.multiple_of(b * BLK, BLK), BLK), :] for b in blocks], axis=0
    )
    scores = lax.dot_general(keys, query, NT, preferred_element_type=jnp.float32)
    lane = lax.broadcasted_iota(jnp.int32, (HD, HD), 1)
    halves = []
    for t, b in enumerate(blocks):
        spot = ((b + t) % 2 * pairs + b // 2) * HD
        halves.append(flipped_ref[pl.ds(pl.multiple_of(spot, HD), HD), :])
    values = jnp.concatenate(
        [jnp.where(lane < BLK, a, b) for a, b in zip(halves[::2], halves[1::2])], axis=1
    )
    tiles = [
        (scores[t * BLK : (t + 1) * BLK], t < count) for t in range(TILES)
    ]
    return tiles, values


def fold(op, tile):
    return functools.reduce(op, [tile[i : i + 8] for i in range(0, tile.shape[0], 8)])


def absorb(state, tiles, values):
    top, total, acc = state
    tops = [
        jnp.where(live, fold(jnp.maximum, tile), VERY_LOW) for tile, live in tiles
    ]
    best = jnp.max(functools.reduce(jnp.maximum, tops), axis=0, keepdims=True)
    new_top = jnp.maximum(top, best)
    weights = [
        jnp.exp2((tile - jnp.where(live, new_top, -VERY_LOW)) * TO_LOG2) for tile, live in tiles
    ]
    factor = jnp.exp2((top - new_top) * TO_LOG2)
    sums = functools.reduce(jnp.add, [fold(jnp.add, w) for w in weights])
    total = total * factor + jnp.sum(sums, axis=0, keepdims=True)
    rounded = jnp.concatenate([w.astype(jnp.bfloat16) for w in weights], axis=0)
    acc = acc * factor + jnp.dot(values, rounded, preferred_element_type=jnp.float32)
    return new_top, total, acc


def load_state(acc_ref, stat_ref, index):
    both = stat_ref[index]
    return both[0:1], both[1:2], acc_ref[index]


def store_state(acc_ref, stat_ref, index, state):
    top, total, acc = state
    stat_ref[index] = jnp.concatenate([top, total] + [total] * 6, axis=0)
    acc_ref[index] = acc


def start_all(copies):
    for copy in copies:
        copy.start()
    return copies


def weight_copies(weight_ref, target, sems, sibling):
    chips, _, share = target.shape
    place = lax.axis_index("tp")
    chip, core = place // CORES, place % CORES
    held = 1 - core if sibling else core
    copies = []
    for k in range(chips):
        start = (lax.rem(chip + k, chips) * CORES + held) * share
        copies.append(
            pltpu.make_async_copy(
                weight_ref.at[:, pl.ds(pl.multiple_of(start, HD), share)],
                target.at[k],
                sems.at[k],
            )
        )
    return copies


def first_kernel(
    sources,
    lists_ref,
    counts_ref,
    kv_ref,
    queries_ref,
    cont_keys_ref,
    cont_values_ref,
    acc_ref,
    stat_ref,
    q_ref,
    flipped_ref,
    ck_ref,
    cv_ref,
    own_ref,
    sems,
):
    conts, length, width = q_ref.shape
    heads = width // HD
    lanes = group_lanes(heads)
    copies = start_all(
        [
            pltpu.make_async_copy(cont_values_ref.at[:, :, lanes], cv_ref, sems.at[0]),
            pltpu.make_async_copy(cont_keys_ref.at[:, :, lanes], ck_ref, sems.at[1]),
            pltpu.make_async_copy(queries_ref, q_ref, sems.at[2]),
        ]
    )
    own = lax.axis_index("ctx")
    both_ways(kv_ref, flipped_ref)
    copies[0].wait()
    for cont in range(conts):
        own_ref[cont] = cv_ref[cont].T
    copies[1].wait()
    copies[2].wait()

    def one_head(head, carry):
        made = []
        for cont in range(conts):
            query = q_ref[cont, :, pl.ds(pl.multiple_of(head * HD, HD), HD)]
            scores = lax.dot_general(
                ck_ref[cont], query, NT, preferred_element_type=jnp.float32
            )
            key = lax.broadcasted_iota(jnp.int32, scores.shape, 0)
            row = lax.broadcasted_iota(jnp.int32, scores.shape, 1)
            scores = jnp.where(key <= row, scores, VERY_LOW)
            tiles, values = shard_scores(
                lists_ref, counts_ref, q_ref, kv_ref, flipped_ref, own, sources, head, cont
            )
            made.append(
                ([(scores, True)] + tiles, jnp.concatenate([own_ref[cont], values], axis=1))
            )
        states = []
        for cont in range(conts):
            start = (
                jnp.full((1, length), VERY_LOW, jnp.float32),
                jnp.zeros((1, length), jnp.float32),
                jnp.zeros((HD, length), jnp.float32),
            )
            states.append(absorb(start, *made[cont]))
        for cont in range(conts):
            store_state(acc_ref, stat_ref, head * conts + cont, states[cont])
        return carry

    lax.fori_loop(0, heads, one_head, 0)


def arrivals(step, sources):
    spot = lax.axis_index("ctx")
    core = lax.axis_index("tp") % CORES
    if sources == 4:
        if step == 1:
            mine = jnp.bitwise_xor(spot, 1 + core)
            return ((mine, True), (jnp.bitwise_xor(mine, 3), True))
        far = jnp.bitwise_xor(spot, 3)
        return ((far, core == 1), (far, core == 0))
    mine = jnp.where(core == 0, spot - step, spot + step)
    theirs = jnp.where(core == 0, spot + step, spot - step)
    return tuple((s, (s >= 0) & (s < sources)) for s in (mine, theirs))


def steps_of(sources):
    return 2 if sources == 4 else sources - 1


def absorb_arrivals(
    step, sources, chosen, lists_ref, counts_ref, q_ref, kv_refs, flipped_ref, before, after
):
    conts, _, width = q_ref.shape
    heads = width // HD
    together = 2 // len(chosen)
    one_of_two = sources == 4 and step == 2
    for part, (source, valid) in enumerate(arrivals(step, sources)):
        held = before if part == 0 or one_of_two else after

        def absorb_part():
            both_ways(kv_refs[part], flipped_ref)

            def some_heads(index, carry):
                work = [
                    (index * together + j, cont) for j in range(together) for cont in chosen
                ]
                pairs = [head * conts + cont for head, cont in work]
                states = [load_state(*held, pair) for pair in pairs]
                made = [
                    shard_scores(
                        lists_ref,
                        counts_ref,
                        q_ref,
                        kv_refs[part],
                        flipped_ref,
                        source,
                        sources,
                        head,
                        cont,
                    )
                    for head, cont in work
                ]
                states = [absorb(state, *got) for state, got in zip(states, made)]
                for pair, state in zip(pairs, states):
                    store_state(*after, pair, state)
                return carry

            lax.fori_loop(0, heads // together, some_heads, 0)

        if valid is True:
            absorb_part()
            continue
        pl.when(valid)(absorb_part)
        if part == 0 and not one_of_two:

            @pl.when(jnp.logical_not(valid))
            def _():
                for source_ref, target_ref in zip(before, after):
                    target_ref[...] = source_ref[...]


def middle_kernel(
    step,
    sources,
    chosen,
    with_weight,
    lists_ref,
    counts_ref,
    q_ref,
    mine_ref,
    theirs_ref,
    acc_in,
    stat_in,
    *refs,
):
    if with_weight:
        weight_ref, acc_ref, stat_ref, give_ref, flipped_ref, sems = refs
        copies = start_all(weight_copies(weight_ref, give_ref, sems, True))
    else:
        acc_ref, stat_ref, flipped_ref = refs
    absorb_arrivals(
        step,
        sources,
        chosen,
        lists_ref,
        counts_ref,
        q_ref,
        (mine_ref, theirs_ref),
        flipped_ref,
        (acc_in, stat_in),
        (acc_ref, stat_ref),
    )
    if with_weight:
        for copy in copies:
            copy.wait()


def finish_and_give(cont, conts, acc_ref, stat_ref, weight_ref, attended_ref, give_ref):
    for head in range(attended_ref.shape[1] // HD):
        _, total, acc = load_state(acc_ref, stat_ref, head * conts + cont)
        attended_ref[:, head * HD : (head + 1) * HD] = (acc / total).T.astype(jnp.bfloat16)
    for k in range(weight_ref.shape[0]):
        give_ref[k] = jnp.dot(
            attended_ref[...], weight_ref[k], preferred_element_type=jnp.float32
        ).astype(give_ref.dtype)


def last_kernel(
    step,
    sources,
    cont,
    lists_ref,
    counts_ref,
    q_ref,
    mine_ref,
    theirs_ref,
    acc_in,
    stat_in,
    give_weight_ref,
    weight_ref,
    attended_ref,
    give_ref,
    keep_weight_ref,
    acc_ref,
    stat_ref,
    flipped_ref,
    sems,
):
    copies = start_all(weight_copies(weight_ref, keep_weight_ref, sems, False))
    absorb_arrivals(
        step,
        sources,
        (cont,),
        lists_ref,
        counts_ref,
        q_ref,
        (mine_ref, theirs_ref),
        flipped_ref,
        (acc_in, stat_in),
        (acc_ref, stat_ref),
    )
    finish_and_give(
        cont, q_ref.shape[0], acc_ref, stat_ref, give_weight_ref, attended_ref, give_ref
    )
    for copy in copies:
        copy.wait()


def finish_kernel(cont, conts, acc_ref, stat_ref, weight_ref, attended_ref, give_ref):
    finish_and_give(cont, conts, acc_ref, stat_ref, weight_ref, attended_ref, give_ref)


def onward_kernel(attended_ref, weight_ref, got_ref, *onward_refs):
    for k, onward_ref in enumerate(onward_refs, 1):
        onward_ref[...] = (
            jnp.dot(attended_ref[...], weight_ref[k], preferred_element_type=jnp.float32)
            + got_ref[k].astype(jnp.float32)
        ).astype(jnp.bfloat16)


def near_kernel(cont, attended_ref, weight_ref, got_ref, residual_ref, near_ref, own_ref, sem):
    share = near_ref.shape[1]
    start = pl.multiple_of(lax.axis_index("tp") * share, HD)
    copy = pltpu.make_async_copy(
        residual_ref.at[cont, :, pl.ds(start, share)], own_ref, sem.at[0]
    )
    copy.start()
    near_ref[...] = jnp.dot(
        attended_ref[...], weight_ref[0], preferred_element_type=jnp.float32
    ) + got_ref[0].astype(jnp.float32)
    copy.wait()
    near_ref[...] += own_ref[...].astype(jnp.float32)


def sum_kernel(count, *refs):
    near_ref, fars, (total_ref, squares_ref) = refs[0], refs[1 : 1 + count], refs[1 + count :]
    total = near_ref[...]
    for far_ref in fars:
        total = total + far_ref[...].astype(jnp.float32)
    total_ref[...] = total
    sums = jnp.sum(total * total, axis=1, keepdims=True)
    squares_ref[...] = jnp.broadcast_to(sums, (sums.shape[0], HD)).T[:8]


def norm_kernel(conts, members, model_width, *refs):
    totals, squares = refs[:conts], refs[conts : conts + members]
    gain_ref, stream_ref, normed_ref = refs[conts + members :]
    gain = gain_ref[...].astype(jnp.float32)
    for cont in range(conts):
        row = functools.reduce(jnp.add, [ref[cont * 8 : cont * 8 + 1, :] for ref in squares])
        scale = lax.rsqrt(row / model_width + 1e-05)
        scale = jnp.broadcast_to(scale, (HD, scale.shape[1])).T[:, 0:1]
        total = totals[cont][...]
        stream_ref[cont] = total.astype(jnp.bfloat16)
        normed_ref[cont] = (total * scale * gain).astype(jnp.bfloat16)


def shards(
    queries,
    cont_keys,
    cont_values,
    prompt_keys,
    prompt_values,
    block_lists,
    tile_counts,
    out_weight,
    residual,
    norm_gain,
    *,
    sources,
    members,
):
    conts, length, width = queries.shape
    heads = width // HD
    rows_dev = prompt_keys.shape[0]
    model_width = residual.shape[2]
    share = norm_gain.shape[0]
    chips = members // CORES
    place = lax.axis_index("tp")
    pairs = heads * conts
    params = pltpu.CompilerParams(vmem_limit_bytes=VMEM_LIMIT)
    smem = pl.BlockSpec(memory_space=pltpu.SMEM)
    vmem = pl.BlockSpec(memory_space=pltpu.VMEM)
    hbm = pl.BlockSpec(memory_space=pltpu.HBM)

    def array(shape, dtype):
        return jax.ShapeDtypeStruct(shape, dtype)

    def cost(flops=1024):
        return pl.CostEstimate(flops=flops, bytes_accessed=1024, transcendentals=0)

    def in_hbm(x):
        return pltpu.with_memory_space_constraint(x, pltpu.HBM)

    packed = pl.pallas_call(
        functools.partial(pack_kernel, heads),
        out_shape=array((2 * rows_dev, HD), jnp.bfloat16),
        in_specs=[hbm] * 2,
        out_specs=vmem,
        scratch_shapes=[
            pltpu.VMEM((rows_dev, HD), jnp.bfloat16),
            pltpu.SemaphoreType.DMA((2,)),
        ],
        compiler_params=params,
        cost_estimate=cost(),
        name="pack",
    )(in_hbm(prompt_keys), in_hbm(prompt_values))

    def across(step):
        def target(z, t):
            if sources == 4 and step == 1:
                return z ^ (1 + t % CORES)
            if sources == 4:
                return z ^ 1 if t % CORES == 1 else None
            to = z + step if t % CORES == 0 else z - step
            return to if 0 <= to < sources else None

        return [
            (z * members + t, target(z, t) * members + t)
            for z in range(sources)
            for t in range(members)
            if target(z, t) is not None
        ]

    sibling = [(t, t ^ 1) for t in range(members)]
    steps = steps_of(sources)
    lists = block_lists.reshape(-1)
    counts = tile_counts.reshape(-1)
    state_shape = (
        array((pairs, HD, length), jnp.float32),
        array((pairs, 8, length), jnp.float32),
    )
    state_scratch = [pltpu.VMEM(s.shape, s.dtype) for s in state_shape]
    flipped = pltpu.VMEM((2 * rows_dev, HD), jnp.bfloat16)
    weight_shape = array((chips, width, share), jnp.bfloat16)

    *state, q = pl.pallas_call(
        functools.partial(first_kernel, sources),
        out_shape=state_shape + (array(queries.shape, jnp.bfloat16),),
        in_specs=[smem, smem, vmem] + [hbm] * 3,
        out_specs=(vmem,) * 3,
        scratch_shapes=[
            flipped,
            pltpu.VMEM((conts, length, HD), jnp.bfloat16),
            pltpu.VMEM((conts, length, HD), jnp.bfloat16),
            pltpu.VMEM((conts, HD, length), jnp.bfloat16),
            pltpu.SemaphoreType.DMA((3,)),
        ],
        compiler_params=params,
        cost_estimate=cost(),
        name="attend_own",
    )(lists, counts, packed, in_hbm(queries), in_hbm(cont_keys), in_hbm(cont_values))

    def attend_step(step, chosen, with_weight, state):
        return pl.pallas_call(
            functools.partial(middle_kernel, step, sources, chosen, with_weight),
            out_shape=state_shape + ((weight_shape,) if with_weight else ()),
            in_specs=[smem, smem] + [vmem] * 5 + [hbm] * with_weight,
            out_specs=(vmem,) * (2 + with_weight),
            scratch_shapes=[flipped] + [pltpu.SemaphoreType.DMA((chips,))] * with_weight,
            compiler_params=params,
            cost_estimate=cost(),
            name="attend_step",
        )(lists, counts, q, mine, theirs, *state, *([in_hbm(out_weight)] * with_weight))

    mine = None
    for step in range(1, steps + 1):
        sent = mine if sources == 4 and step == 2 else packed
        mine = lax.ppermute(sent, ("ctx", "tp"), across(step))
        mine, state = lax.optimization_barrier((mine, tuple(state)))
        theirs = lax.ppermute(mine, "tp", sibling)
        if step < steps:
            *state, give_weight = attend_step(step, tuple(range(conts)), True, state)

    attended, give, keep_weight = pl.pallas_call(
        functools.partial(last_kernel, steps, sources, 0),
        out_shape=(
            array((length, width), jnp.bfloat16),
            array((chips, length, share), jnp.bfloat16),
            weight_shape,
        ),
        in_specs=[smem, smem] + [vmem] * 6 + [hbm],
        out_specs=(vmem,) * 3,
        scratch_shapes=[pltpu.VMEM(a.shape, a.dtype) for a in state_shape]
        + [flipped, pltpu.SemaphoreType.DMA((chips,))],
        compiler_params=params,
        cost_estimate=cost(),
        name="attend_last",
    )(lists, counts, q, mine, theirs, *state, give_weight, in_hbm(out_weight))

    def onward(attended, got):
        parts = pl.pallas_call(
            onward_kernel,
            out_shape=(array((length, share), jnp.bfloat16),) * (chips - 1),
            in_specs=[vmem] * 3,
            out_specs=(vmem,) * (chips - 1),
            compiler_params=params,
            cost_estimate=cost(),
            name="project_onward",
        )(attended, keep_weight, got)
        far = []
        for k in range(1, chips):
            to_chip = [
                (t, (t // CORES + k) % chips * CORES + t % CORES) for t in range(members)
            ]
            far.append(lax.ppermute(parts[k - 1], "tp", to_chip))
        return parts, far

    def near(cont, attended, got):
        return pl.pallas_call(
            functools.partial(near_kernel, cont),
            out_shape=array((length, share), jnp.float32),
            in_specs=[vmem] * 3 + [hbm],
            out_specs=vmem,
            scratch_shapes=[
                pltpu.VMEM((length, share), jnp.bfloat16),
                pltpu.SemaphoreType.DMA((1,)),
            ],
            compiler_params=params,
            cost_estimate=cost(),
            name="project_near",
        )(attended, keep_weight, got, in_hbm(residual))

    got = lax.ppermute(give, "tp", sibling)
    rest = state
    nears, fars = [], []
    for cont in range(conts):
        if cont > 0:
            rest = attend_step(steps, (cont,), False, state)
            rest, got, parts = lax.optimization_barrier((rest, got, parts))
            attended, give = pl.pallas_call(
                functools.partial(finish_kernel, cont, conts),
                out_shape=(
                    array((length, width), jnp.bfloat16),
                    array((chips, length, share), jnp.bfloat16),
                ),
                in_specs=[vmem] * 3,
                out_specs=(vmem,) * 2,
                compiler_params=params,
                cost_estimate=cost(),
                name="finish",
            )(*rest, give_weight)
            got = lax.ppermute(give, "tp", sibling)
        parts, far = onward(attended, got)
        fars.append(far)
        nears.append(near(cont, attended, got))

    totals, squares = [], []
    for cont in range(conts):
        total, square = pl.pallas_call(
            functools.partial(sum_kernel, chips - 1),
            out_shape=(array((length, share), jnp.float32), array((8, length), jnp.float32)),
            in_specs=[vmem] * chips,
            out_specs=(vmem,) * 2,
            compiler_params=params,
            cost_estimate=cost(),
            name="add_up",
        )(nears[cont], *fars[cont])
        totals.append(total)
        squares.append(square)
    squares = jnp.concatenate(squares, axis=0)
    all_squares = [squares] + [
        lax.ppermute(squares, "tp", [(t, (t + k) % members) for t in range(members)])
        for k in range(1, members)
    ]
    out = array((conts, length, share), jnp.bfloat16)
    return pl.pallas_call(
        functools.partial(norm_kernel, conts, members, model_width),
        out_shape=(out, out),
        in_specs=[vmem] * (conts + members + 1),
        out_specs=(vmem, vmem),
        compiler_params=params,
        cost_estimate=cost(),
        name="norm",
    )(*totals, *all_squares, norm_gain.reshape(1, share))


def solution(mesh):
    placed = (
        P(("grp", "ctx"), None, "tp"),
        P(("grp", "ctx"), None, None),
        P(("grp", "ctx"), None, None),
        P(("grp", "ctx"), None),
        P(("grp", "ctx"), None),
        P("tp", ("grp", "ctx"), None, None),
        P("tp", ("grp", "ctx"), None),
        P("tp", None),
        P(("grp", "ctx"), None, None),
        P("tp"),
    )
    return jax.shard_map(
        functools.partial(
            shards, sources=mesh.shape["ctx"], members=mesh.shape["tp"]
        ),
        mesh=mesh,
        in_specs=placed,
        out_specs=(P(("grp", "ctx"), None, "tp"), P(("grp", "ctx"), None, "tp")),
        check_vma=False,
    )
```

```python
import functools
import math

import jax
import jax.numpy as jnp
from jax import lax
from jax.experimental import pallas as pl
from jax.experimental.pallas import tpu as pltpu
from jax.sharding import PartitionSpec as P

HEADS = 32
KVH = 2
HD = 128
BLK = 64
TILES = 8
CORES = 2
TOKENS = TILES * BLK

VERY_LOW = -1e30
TO_LOG2 = math.log2(math.e) / math.sqrt(HD)

VMEM_LIMIT = 24 * 1024 * 1024


def key_group(heads):
    return lax.axis_index("tp") * heads // (HEADS // KVH)


def group_lanes(heads):
    return pl.ds(pl.multiple_of(key_group(heads) * HD, HD), HD)


def pack_kernel(heads, keys_ref, values_ref, packed_ref, values_buf, sems):
    rows = keys_ref.shape[0]
    lanes = group_lanes(heads)
    keys_copy = pltpu.make_async_copy(
        keys_ref.at[:, lanes], packed_ref.at[pl.ds(0, rows)], sems.at[0]
    )
    values_copy = pltpu.make_async_copy(values_ref.at[:, lanes], values_buf, sems.at[1])
    values_copy.start()
    keys_copy.start()
    values_copy.wait()
    for p in range(rows // HD):
        packed_ref[rows + p * HD : rows + (p + 1) * HD, :] = values_buf[
            p * HD : (p + 1) * HD, :
        ].T
    keys_copy.wait()


def both_ways(kv_ref, flipped_ref):
    rows = kv_ref.shape[0] // 2
    for p in range(rows // HD):
        pair = kv_ref[rows + p * HD : rows + (p + 1) * HD, :]
        flipped_ref[p * HD : (p + 1) * HD, :] = pair
        flipped_ref[rows + p * HD : rows + (p + 1) * HD, :] = jnp.concatenate(
            [pair[:, BLK:], pair[:, :BLK]], axis=1
        )


def shard_scores(lists_ref, counts_ref, q_ref, kv_ref, flipped_ref, source, sources, head, cont):
    conts = q_ref.shape[1]
    pairs = kv_ref.shape[0] // 2 // HD
    place = (head * conts + cont) * sources + source
    count = counts_ref[place]
    blocks = [lists_ref[place * TILES + t] for t in range(TILES)]
    keys = jnp.concatenate(
        [kv_ref[pl.ds(pl.multiple_of(b * BLK, BLK), BLK), :] for b in blocks], axis=0
    )
    scores = jnp.dot(keys, q_ref[head, cont], preferred_element_type=jnp.float32)
    lane = lax.broadcasted_iota(jnp.int32, (HD, HD), 1)
    halves = []
    for t, b in enumerate(blocks):
        spot = ((b + t) % 2 * pairs + b // 2) * HD
        halves.append(flipped_ref[pl.ds(pl.multiple_of(spot, HD), HD), :])
    values = jnp.concatenate(
        [jnp.where(lane < BLK, a, b) for a, b in zip(halves[::2], halves[1::2])], axis=1
    )
    tiles = [
        (scores[t * BLK : (t + 1) * BLK], t < count) for t in range(TILES)
    ]
    return tiles, values


def fold(op, tile):
    return functools.reduce(op, [tile[i : i + 8] for i in range(0, tile.shape[0], 8)])


def absorb(state, tiles, values):
    top, total, acc = state
    tops = [
        jnp.where(live, fold(jnp.maximum, tile), VERY_LOW) for tile, live in tiles
    ]
    best = jnp.max(functools.reduce(jnp.maximum, tops), axis=0, keepdims=True)
    new_top = jnp.maximum(top, best)
    weights = [
        jnp.exp2((tile - jnp.where(live, new_top, -VERY_LOW)) * TO_LOG2) for tile, live in tiles
    ]
    factor = jnp.exp2((top - new_top) * TO_LOG2)
    sums = functools.reduce(jnp.add, [fold(jnp.add, w) for w in weights])
    total = total * factor + jnp.sum(sums, axis=0, keepdims=True)
    rounded = jnp.concatenate([w.astype(jnp.bfloat16) for w in weights], axis=0)
    acc = acc * factor + jnp.dot(values, rounded, preferred_element_type=jnp.float32)
    return new_top, total, acc


def load_state(acc_ref, stat_ref, index):
    both = stat_ref[index]
    return both[0:1], both[1:2], acc_ref[index]


def store_state(acc_ref, stat_ref, index, state):
    top, total, acc = state
    stat_ref[index] = jnp.concatenate([top, total] + [total] * 6, axis=0)
    acc_ref[index] = acc


def start_all(copies):
    for copy in copies:
        copy.start()
    return copies


def weight_copies(weight_ref, target, sems, sibling):
    chips, _, share = target.shape
    place = lax.axis_index("tp")
    chip, core = place // CORES, place % CORES
    held = 1 - core if sibling else core
    copies = []
    for k in range(chips):
        start = (lax.rem(chip + k, chips) * CORES + held) * share
        copies.append(
            pltpu.make_async_copy(
                weight_ref.at[:, pl.ds(pl.multiple_of(start, HD), share)],
                target.at[k],
                sems.at[k],
            )
        )
    return copies


def first_kernel(
    sources,
    lists_ref,
    counts_ref,
    kv_ref,
    queries_ref,
    cont_keys_ref,
    cont_values_ref,
    acc_ref,
    stat_ref,
    q_ref,
    flipped_ref,
    rows_ref,
    ck_ref,
    cv_ref,
    own_ref,
    sems,
):
    heads, conts, _, length = q_ref.shape
    lanes = group_lanes(heads)
    copies = start_all(
        [
            pltpu.make_async_copy(cont_values_ref.at[:, :, lanes], cv_ref, sems.at[0]),
            pltpu.make_async_copy(cont_keys_ref.at[:, :, lanes], ck_ref, sems.at[1]),
            pltpu.make_async_copy(queries_ref, rows_ref, sems.at[2]),
        ]
    )
    own = lax.axis_index("ctx")
    both_ways(kv_ref, flipped_ref)
    copies[0].wait()
    for cont in range(conts):
        own_ref[cont] = cv_ref[cont].T
    copies[1].wait()
    copies[2].wait()

    for head in range(heads):
        for cont in range(conts):
            q_ref[head, cont] = rows_ref[cont, :, head * HD : (head + 1) * HD].T

    together = 4 // conts

    def some_heads(index, carry):
        work = [(index * together + j, cont) for j in range(together) for cont in range(conts)]
        made = []
        for head, cont in work:
            scores = jnp.dot(ck_ref[cont], q_ref[head, cont], preferred_element_type=jnp.float32)
            key = lax.broadcasted_iota(jnp.int32, scores.shape, 0)
            row = lax.broadcasted_iota(jnp.int32, scores.shape, 1)
            scores = jnp.where(key <= row, scores, VERY_LOW)
            tiles, values = shard_scores(
                lists_ref, counts_ref, q_ref, kv_ref, flipped_ref, own, sources, head, cont
            )
            made.append(
                ([(scores, True)] + tiles, jnp.concatenate([own_ref[cont], values], axis=1))
            )
        states = []
        for got in made:
            start = (
                jnp.full((1, length), VERY_LOW, jnp.float32),
                jnp.zeros((1, length), jnp.float32),
                jnp.zeros((HD, length), jnp.float32),
            )
            states.append(absorb(start, *got))
        for (head, cont), state in zip(work, states):
            store_state(acc_ref, stat_ref, head * conts + cont, state)
        return carry

    lax.fori_loop(0, heads // together, some_heads, 0)


def arrivals(step, sources):
    spot = lax.axis_index("ctx")
    core = lax.axis_index("tp") % CORES
    if sources == 4:
        if step == 1:
            mine = jnp.bitwise_xor(spot, 1 + core)
            return ((mine, True), (jnp.bitwise_xor(mine, 3), True))
        far = jnp.bitwise_xor(spot, 3)
        return ((far, core == 1), (far, core == 0))
    mine = jnp.where(core == 0, spot - step, spot + step)
    theirs = jnp.where(core == 0, spot + step, spot - step)
    return tuple((s, (s >= 0) & (s < sources)) for s in (mine, theirs))


def steps_of(sources):
    return 2 if sources == 4 else sources - 1


def absorb_arrivals(
    step, sources, chosen, lists_ref, counts_ref, q_ref, kv_refs, flipped_ref, before, after
):
    heads, conts = q_ref.shape[:2]
    together = 4 // len(chosen)
    one_of_two = sources == 4 and step == 2
    for part, (source, valid) in enumerate(arrivals(step, sources)):
        held = before if part == 0 or one_of_two else after

        def absorb_part():
            both_ways(kv_refs[part], flipped_ref)

            def some_heads(index, carry):
                work = [
                    (index * together + j, cont) for j in range(together) for cont in chosen
                ]
                pairs = [head * conts + cont for head, cont in work]
                states = [load_state(*held, pair) for pair in pairs]
                made = [
                    shard_scores(
                        lists_ref,
                        counts_ref,
                        q_ref,
                        kv_refs[part],
                        flipped_ref,
                        source,
                        sources,
                        head,
                        cont,
                    )
                    for head, cont in work
                ]
                states = [absorb(state, *got) for state, got in zip(states, made)]
                for pair, state in zip(pairs, states):
                    store_state(*after, pair, state)
                return carry

            lax.fori_loop(0, heads // together, some_heads, 0)

        if valid is True:
            absorb_part()
            continue
        pl.when(valid)(absorb_part)
        if part == 0 and not one_of_two:

            @pl.when(jnp.logical_not(valid))
            def _():
                for source_ref, target_ref in zip(before, after):
                    target_ref[...] = source_ref[...]


def middle_kernel(
    step,
    sources,
    chosen,
    with_weight,
    lists_ref,
    counts_ref,
    q_ref,
    mine_ref,
    theirs_ref,
    acc_in,
    stat_in,
    *refs,
):
    if with_weight:
        weight_ref, acc_ref, stat_ref, give_ref, flipped_ref, sems = refs
        copies = start_all(weight_copies(weight_ref, give_ref, sems, True))
    else:
        acc_ref, stat_ref, flipped_ref = refs
    absorb_arrivals(
        step,
        sources,
        chosen,
        lists_ref,
        counts_ref,
        q_ref,
        (mine_ref, theirs_ref),
        flipped_ref,
        (acc_in, stat_in),
        (acc_ref, stat_ref),
    )
    if with_weight:
        for copy in copies:
            copy.wait()


def finish_and_give(cont, conts, acc_ref, stat_ref, weight_ref, attended_ref, give_ref):
    for head in range(attended_ref.shape[1] // HD):
        _, total, acc = load_state(acc_ref, stat_ref, head * conts + cont)
        attended_ref[:, head * HD : (head + 1) * HD] = (acc / total).T.astype(jnp.bfloat16)
    for k in range(weight_ref.shape[0]):
        give_ref[k] = jnp.dot(
            attended_ref[...], weight_ref[k], preferred_element_type=jnp.float32
        ).astype(give_ref.dtype)


def last_kernel(
    step,
    sources,
    cont,
    lists_ref,
    counts_ref,
    q_ref,
    mine_ref,
    theirs_ref,
    acc_in,
    stat_in,
    give_weight_ref,
    weight_ref,
    attended_ref,
    give_ref,
    keep_weight_ref,
    acc_ref,
    stat_ref,
    flipped_ref,
    sems,
):
    copies = start_all(weight_copies(weight_ref, keep_weight_ref, sems, False))
    absorb_arrivals(
        step,
        sources,
        (cont,),
        lists_ref,
        counts_ref,
        q_ref,
        (mine_ref, theirs_ref),
        flipped_ref,
        (acc_in, stat_in),
        (acc_ref, stat_ref),
    )
    finish_and_give(
        cont, q_ref.shape[1], acc_ref, stat_ref, give_weight_ref, attended_ref, give_ref
    )
    for copy in copies:
        copy.wait()


def finish_kernel(cont, conts, acc_ref, stat_ref, weight_ref, attended_ref, give_ref):
    finish_and_give(cont, conts, acc_ref, stat_ref, weight_ref, attended_ref, give_ref)


def onward_kernel(attended_ref, weight_ref, got_ref, *onward_refs):
    for k, onward_ref in enumerate(onward_refs, 1):
        onward_ref[...] = (
            jnp.dot(attended_ref[...], weight_ref[k], preferred_element_type=jnp.float32)
            + got_ref[k].astype(jnp.float32)
        ).astype(jnp.bfloat16)


def near_kernel(cont, attended_ref, weight_ref, got_ref, residual_ref, near_ref, own_ref, sem):
    share = near_ref.shape[1]
    start = pl.multiple_of(lax.axis_index("tp") * share, HD)
    copy = pltpu.make_async_copy(
        residual_ref.at[cont, :, pl.ds(start, share)], own_ref, sem.at[0]
    )
    copy.start()
    near_ref[...] = jnp.dot(
        attended_ref[...], weight_ref[0], preferred_element_type=jnp.float32
    ) + got_ref[0].astype(jnp.float32)
    copy.wait()
    near_ref[...] += own_ref[...].astype(jnp.float32)


def sum_kernel(count, *refs):
    near_ref, fars, (total_ref, squares_ref) = refs[0], refs[1 : 1 + count], refs[1 + count :]
    total = near_ref[...]
    for far_ref in fars:
        total = total + far_ref[...].astype(jnp.float32)
    total_ref[...] = total
    sums = jnp.sum(total * total, axis=1, keepdims=True)
    squares_ref[...] = jnp.broadcast_to(sums, (sums.shape[0], HD)).T[:8]


def norm_kernel(conts, members, model_width, *refs):
    totals, squares = refs[:conts], refs[conts : conts + members]
    gain_ref, stream_ref, normed_ref = refs[conts + members :]
    gain = gain_ref[...].astype(jnp.float32)
    for cont in range(conts):
        row = functools.reduce(jnp.add, [ref[cont * 8 : cont * 8 + 1, :] for ref in squares])
        scale = lax.rsqrt(row / model_width + 1e-05)
        scale = jnp.broadcast_to(scale, (HD, scale.shape[1])).T[:, 0:1]
        total = totals[cont][...]
        stream_ref[cont] = total.astype(jnp.bfloat16)
        normed_ref[cont] = (total * scale * gain).astype(jnp.bfloat16)


def shards(
    queries,
    cont_keys,
    cont_values,
    prompt_keys,
    prompt_values,
    block_lists,
    tile_counts,
    out_weight,
    residual,
    norm_gain,
    *,
    sources,
    members,
):
    conts, length, width = queries.shape
    heads = width // HD
    rows_dev = prompt_keys.shape[0]
    model_width = residual.shape[2]
    share = norm_gain.shape[0]
    chips = members // CORES
    place = lax.axis_index("tp")
    pairs = heads * conts
    params = pltpu.CompilerParams(vmem_limit_bytes=VMEM_LIMIT)
    smem = pl.BlockSpec(memory_space=pltpu.SMEM)
    vmem = pl.BlockSpec(memory_space=pltpu.VMEM)
    hbm = pl.BlockSpec(memory_space=pltpu.HBM)

    def array(shape, dtype):
        return jax.ShapeDtypeStruct(shape, dtype)

    def cost(flops=1024):
        return pl.CostEstimate(flops=flops, bytes_accessed=1024, transcendentals=0)

    def in_hbm(x):
        return pltpu.with_memory_space_constraint(x, pltpu.HBM)

    packed = pl.pallas_call(
        functools.partial(pack_kernel, heads),
        out_shape=array((2 * rows_dev, HD), jnp.bfloat16),
        in_specs=[hbm] * 2,
        out_specs=vmem,
        scratch_shapes=[
            pltpu.VMEM((rows_dev, HD), jnp.bfloat16),
            pltpu.SemaphoreType.DMA((2,)),
        ],
        compiler_params=params,
        cost_estimate=cost(),
        name="pack",
    )(in_hbm(prompt_keys), in_hbm(prompt_values))

    def across(step):
        def target(z, t):
            if sources == 4 and step == 1:
                return z ^ (1 + t % CORES)
            if sources == 4:
                return z ^ 1 if t % CORES == 1 else None
            to = z + step if t % CORES == 0 else z - step
            return to if 0 <= to < sources else None

        return [
            (z * members + t, target(z, t) * members + t)
            for z in range(sources)
            for t in range(members)
            if target(z, t) is not None
        ]

    sibling = [(t, t ^ 1) for t in range(members)]
    steps = steps_of(sources)
    lists = block_lists.reshape(-1)
    counts = tile_counts.reshape(-1)
    state_shape = (
        array((pairs, HD, length), jnp.float32),
        array((pairs, 8, length), jnp.float32),
    )
    state_scratch = [pltpu.VMEM(s.shape, s.dtype) for s in state_shape]
    flipped = pltpu.VMEM((2 * rows_dev, HD), jnp.bfloat16)
    weight_shape = array((chips, width, share), jnp.bfloat16)

    *state, q = pl.pallas_call(
        functools.partial(first_kernel, sources),
        out_shape=state_shape + (array((heads, conts, HD, length), jnp.bfloat16),),
        in_specs=[smem, smem, vmem] + [hbm] * 3,
        out_specs=(vmem,) * 3,
        scratch_shapes=[
            flipped,
            pltpu.VMEM(queries.shape, jnp.bfloat16),
            pltpu.VMEM((conts, length, HD), jnp.bfloat16),
            pltpu.VMEM((conts, length, HD), jnp.bfloat16),
            pltpu.VMEM((conts, HD, length), jnp.bfloat16),
            pltpu.SemaphoreType.DMA((3,)),
        ],
        compiler_params=params,
        cost_estimate=cost(),
        name="attend_own",
    )(lists, counts, packed, in_hbm(queries), in_hbm(cont_keys), in_hbm(cont_values))

    def attend_step(step, chosen, with_weight, state):
        return pl.pallas_call(
            functools.partial(middle_kernel, step, sources, chosen, with_weight),
            out_shape=state_shape + ((weight_shape,) if with_weight else ()),
            in_specs=[smem, smem] + [vmem] * 5 + [hbm] * with_weight,
            out_specs=(vmem,) * (2 + with_weight),
            scratch_shapes=[flipped] + [pltpu.SemaphoreType.DMA((chips,))] * with_weight,
            compiler_params=params,
            cost_estimate=cost(),
            name="attend_step",
        )(lists, counts, q, mine, theirs, *state, *([in_hbm(out_weight)] * with_weight))

    mine = None
    for step in range(1, steps + 1):
        sent = mine if sources == 4 and step == 2 else packed
        mine = lax.ppermute(sent, ("ctx", "tp"), across(step))
        mine, state = lax.optimization_barrier((mine, tuple(state)))
        theirs = lax.ppermute(mine, "tp", sibling)
        if step < steps:
            *state, give_weight = attend_step(step, tuple(range(conts)), True, state)

    attended, give, keep_weight = pl.pallas_call(
        functools.partial(last_kernel, steps, sources, 0),
        out_shape=(
            array((length, width), jnp.bfloat16),
            array((chips, length, share), jnp.bfloat16),
            weight_shape,
        ),
        in_specs=[smem, smem] + [vmem] * 6 + [hbm],
        out_specs=(vmem,) * 3,
        scratch_shapes=[pltpu.VMEM(a.shape, a.dtype) for a in state_shape]
        + [flipped, pltpu.SemaphoreType.DMA((chips,))],
        compiler_params=params,
        cost_estimate=cost(),
        name="attend_last",
    )(lists, counts, q, mine, theirs, *state, give_weight, in_hbm(out_weight))

    def onward(attended, got):
        parts = pl.pallas_call(
            onward_kernel,
            out_shape=(array((length, share), jnp.bfloat16),) * (chips - 1),
            in_specs=[vmem] * 3,
            out_specs=(vmem,) * (chips - 1),
            compiler_params=params,
            cost_estimate=cost(),
            name="project_onward",
        )(attended, keep_weight, got)
        far = []
        for k in range(1, chips):
            to_chip = [
                (t, (t // CORES + k) % chips * CORES + t % CORES) for t in range(members)
            ]
            far.append(lax.ppermute(parts[k - 1], "tp", to_chip))
        return parts, far

    def near(cont, attended, got):
        return pl.pallas_call(
            functools.partial(near_kernel, cont),
            out_shape=array((length, share), jnp.float32),
            in_specs=[vmem] * 3 + [hbm],
            out_specs=vmem,
            scratch_shapes=[
                pltpu.VMEM((length, share), jnp.bfloat16),
                pltpu.SemaphoreType.DMA((1,)),
            ],
            compiler_params=params,
            cost_estimate=cost(),
            name="project_near",
        )(attended, keep_weight, got, in_hbm(residual))

    got = lax.ppermute(give, "tp", sibling)
    rest = state
    nears, fars = [], []
    for cont in range(conts):
        if cont > 0:
            rest = attend_step(steps, (cont,), False, state)
            rest, got, parts = lax.optimization_barrier((rest, got, parts))
            attended, give = pl.pallas_call(
                functools.partial(finish_kernel, cont, conts),
                out_shape=(
                    array((length, width), jnp.bfloat16),
                    array((chips, length, share), jnp.bfloat16),
                ),
                in_specs=[vmem] * 3,
                out_specs=(vmem,) * 2,
                compiler_params=params,
                cost_estimate=cost(),
                name="finish",
            )(*rest, give_weight)
            got = lax.ppermute(give, "tp", sibling)
        parts, far = onward(attended, got)
        fars.append(far)
        nears.append(near(cont, attended, got))

    totals, squares = [], []
    for cont in range(conts):
        total, square = pl.pallas_call(
            functools.partial(sum_kernel, chips - 1),
            out_shape=(array((length, share), jnp.float32), array((8, length), jnp.float32)),
            in_specs=[vmem] * chips,
            out_specs=(vmem,) * 2,
            compiler_params=params,
            cost_estimate=cost(),
            name="add_up",
        )(nears[cont], *fars[cont])
        totals.append(total)
        squares.append(square)
    squares = jnp.concatenate(squares, axis=0)
    all_squares = [squares] + [
        lax.ppermute(squares, "tp", [(t, (t + k) % members) for t in range(members)])
        for k in range(1, members)
    ]
    out = array((conts, length, share), jnp.bfloat16)
    return pl.pallas_call(
        functools.partial(norm_kernel, conts, members, model_width),
        out_shape=(out, out),
        in_specs=[vmem] * (conts + members + 1),
        out_specs=(vmem, vmem),
        compiler_params=params,
        cost_estimate=cost(),
        name="norm",
    )(*totals, *all_squares, norm_gain.reshape(1, share))


def solution(mesh):
    placed = (
        P(("grp", "ctx"), None, "tp"),
        P(("grp", "ctx"), None, None),
        P(("grp", "ctx"), None, None),
        P(("grp", "ctx"), None),
        P(("grp", "ctx"), None),
        P("tp", ("grp", "ctx"), None, None),
        P("tp", ("grp", "ctx"), None),
        P("tp", None),
        P(("grp", "ctx"), None, None),
        P("tp"),
    )
    return jax.shard_map(
        functools.partial(
            shards, sources=mesh.shape["ctx"], members=mesh.shape["tp"]
        ),
        mesh=mesh,
        in_specs=placed,
        out_specs=(P(("grp", "ctx"), None, "tp"), P(("grp", "ctx"), None, "tp")),
        check_vma=False,
    )
```

```python
import functools
import math

import jax
import jax.numpy as jnp
from jax import lax
from jax.experimental import pallas as pl
from jax.experimental.pallas import tpu as pltpu
from jax.sharding import PartitionSpec as P

HEADS = 32
KVH = 2
HD = 128
BLK = 64
TILES = 8
CORES = 2
TOGETHER = 4

VERY_LOW = -1e30
TO_LOG2 = math.log2(math.e) / math.sqrt(HD)

VMEM_LIMIT = 24 * 1024 * 1024


def key_group(heads):
    return lax.axis_index("tp") * heads // (HEADS // KVH)


def group_lanes(heads):
    return pl.ds(pl.multiple_of(key_group(heads) * HD, HD), HD)


def pack_keys_kernel(heads, keys_ref, packed_ref, sems):
    copy = pltpu.make_async_copy(keys_ref.at[:, group_lanes(heads)], packed_ref, sems.at[0])
    copy.start()
    copy.wait()


def pack_values_kernel(heads, values_ref, packed_ref, values_buf, sems):
    copy = pltpu.make_async_copy(values_ref.at[:, group_lanes(heads)], values_buf, sems.at[0])
    copy.start()
    copy.wait()
    for p in range(packed_ref.shape[0] // HD):
        rows = slice(p * HD, (p + 1) * HD)
        packed_ref[rows, :] = values_buf[rows, :].T


def both_ways(values_refs, flipped_ref):
    total = flipped_ref.shape[0] // 2
    for part, values_ref in enumerate(values_refs):
        rows = values_ref.shape[0]
        for p in range(rows // HD):
            pair = values_ref[p * HD : (p + 1) * HD, :]
            at = part * rows + p * HD
            flipped_ref[at : at + HD, :] = pair
            flipped_ref[total + at : total + at + HD, :] = jnp.concatenate(
                [pair[:, BLK:], pair[:, :BLK]], axis=1
            )


def shard_scores(lists_ref, counts_ref, q_refs, keys_ref, flipped_ref, source, head, cont):
    pairs = keys_ref.shape[0] // HD
    count = counts_ref[cont, source, head]
    blocks = [lists_ref[head, cont, source, t] for t in range(TILES)]
    keys = jnp.concatenate(
        [keys_ref[pl.ds(pl.multiple_of(b * BLK, BLK), BLK), :] for b in blocks], axis=0
    )
    scores = jnp.dot(keys, q_refs[cont][head], preferred_element_type=jnp.float32)
    lane = lax.broadcasted_iota(jnp.int32, (HD, HD), 1)
    halves = []
    for t, b in enumerate(blocks):
        spot = ((b + t) % 2 * pairs + b // 2) * HD
        halves.append(flipped_ref[pl.ds(pl.multiple_of(spot, HD), HD), :])
    values = jnp.concatenate(
        [jnp.where(lane < BLK, a, b) for a, b in zip(halves[::2], halves[1::2])], axis=1
    )
    tiles = [
        (scores[t * BLK : (t + 1) * BLK], t < count) for t in range(TILES)
    ]
    return tiles, values


def fold(op, tile):
    return functools.reduce(op, [tile[i : i + 8] for i in range(0, tile.shape[0], 8)])


def absorb(state, tiles, values):
    top, total, acc = state
    tops = [
        jnp.where(live, fold(jnp.maximum, tile), VERY_LOW) for tile, live in tiles
    ]
    best = jnp.max(functools.reduce(jnp.maximum, tops), axis=0, keepdims=True)
    new_top = jnp.maximum(top, best)
    weights = [
        jnp.exp2((tile - jnp.where(live, new_top, -VERY_LOW)) * TO_LOG2) for tile, live in tiles
    ]
    factor = jnp.exp2((top - new_top) * TO_LOG2)
    sums = functools.reduce(jnp.add, [fold(jnp.add, w) for w in weights])
    total = total * factor + jnp.sum(sums, axis=0, keepdims=True)
    rounded = jnp.concatenate([w.astype(jnp.bfloat16) for w in weights], axis=0)
    acc = acc * factor + jnp.dot(values, rounded, preferred_element_type=jnp.float32)
    return new_top, total, acc


def load_state(acc_ref, stat_ref, index):
    both = stat_ref[index]
    return both[0:1], both[1:2], acc_ref[index]


def store_state(acc_ref, stat_ref, index, state):
    top, total, acc = state
    stat_ref[index] = jnp.concatenate([top, total] + [total] * 6, axis=0)
    acc_ref[index] = acc


def start_all(copies):
    for copy in copies:
        copy.start()
    return copies


def weight_copies(weight_ref, target, sems, sibling):
    chips, _, share = target.shape
    place = lax.axis_index("tp")
    chip, core = place // CORES, place % CORES
    held = 1 - core if sibling else core
    copies = []
    for k in range(chips):
        start = (lax.rem(chip + k, chips) * CORES + held) * share
        copies.append(
            pltpu.make_async_copy(
                weight_ref.at[:, pl.ds(pl.multiple_of(start, HD), share)],
                target.at[k],
                sems.at[k],
            )
        )
    return copies


def first_kernel(
    cont,
    lists_ref,
    counts_ref,
    keys_ref,
    values_ref,
    queries_ref,
    cont_keys_ref,
    cont_values_ref,
    acc_ref,
    stat_ref,
    q_ref,
    flipped_ref,
    rows_ref,
    ck_ref,
    cv_ref,
    own_ref,
    sems,
):
    heads, _, length = q_ref.shape
    lanes = group_lanes(heads)
    copies = start_all(
        [
            pltpu.make_async_copy(cont_values_ref.at[cont, :, lanes], cv_ref, sems.at[0]),
            pltpu.make_async_copy(cont_keys_ref.at[cont, :, lanes], ck_ref, sems.at[1]),
            pltpu.make_async_copy(queries_ref.at[cont], rows_ref, sems.at[2]),
        ]
    )
    own = lax.axis_index("ctx")
    both_ways([values_ref], flipped_ref)
    copies[0].wait()
    own_ref[...] = cv_ref[...].T
    copies[1].wait()
    copies[2].wait()
    for head in range(heads):
        q_ref[head] = rows_ref[:, head * HD : (head + 1) * HD].T

    def some_heads(index, carry):
        work = [index * TOGETHER + j for j in range(TOGETHER)]
        made = []
        for head in work:
            scores = jnp.dot(ck_ref[...], q_ref[head], preferred_element_type=jnp.float32)
            key = lax.broadcasted_iota(jnp.int32, scores.shape, 0)
            row = lax.broadcasted_iota(jnp.int32, scores.shape, 1)
            scores = jnp.where(key <= row, scores, VERY_LOW)
            tiles, values = shard_scores(
                lists_ref, counts_ref, {cont: q_ref}, keys_ref, flipped_ref, own, head, cont
            )
            made.append(
                ([(scores, True)] + tiles, jnp.concatenate([own_ref[...], values], axis=1))
            )
        states = []
        for got in made:
            start = (
                jnp.full((1, length), VERY_LOW, jnp.float32),
                jnp.zeros((1, length), jnp.float32),
                jnp.zeros((HD, length), jnp.float32),
            )
            states.append(absorb(start, *got))
        for head, state in zip(work, states):
            store_state(acc_ref, stat_ref, head, state)
        return carry

    lax.fori_loop(0, heads // TOGETHER, some_heads, 0)


def arrivals(step, sources):
    spot = lax.axis_index("ctx")
    core = lax.axis_index("tp") % CORES
    if sources == 4:
        if step == 1:
            mine = jnp.bitwise_xor(spot, 1 + core)
            return ((mine, True), (jnp.bitwise_xor(mine, 3), True))
        far = jnp.bitwise_xor(spot, 3)
        return ((far, core == 1), (far, core == 0))
    mine = jnp.where(core == 0, spot - step, spot + step)
    theirs = jnp.where(core == 0, spot + step, spot - step)
    return tuple((s, (s >= 0) & (s < sources)) for s in (mine, theirs))


def steps_of(sources):
    return 2 if sources == 4 else sources - 1


def absorb_shard(
    source, lists_ref, counts_ref, q_refs, keys_ref, values_refs, flipped_ref, before, after
):
    heads = next(iter(q_refs.values())).shape[0]
    together = TOGETHER // len(q_refs)
    both_ways(values_refs, flipped_ref)

    def some_heads(index, carry):
        work = [(index * together + j, cont) for j in range(together) for cont in q_refs]
        states = [load_state(*before[cont], head) for head, cont in work]
        made = [
            shard_scores(lists_ref, counts_ref, q_refs, keys_ref, flipped_ref, source, head, cont)
            for head, cont in work
        ]
        states = [absorb(state, *got) for state, got in zip(states, made)]
        for (head, cont), state in zip(work, states):
            store_state(*after[cont], head, state)
        return carry

    lax.fori_loop(0, heads // together, some_heads, 0)


def hand_on(before, after):
    for source_ref, target_ref in zip(before, after):
        target_ref[...] = source_ref[...]


def by_cont(refs):
    return {cont: refs[2 * cont : 2 * cont + 2] for cont in range(len(refs) // 2)}


def middle_kernel(
    step, part, sources, conts, pieces, with_weight, lists_ref, counts_ref, *refs
):
    q_refs, refs = dict(enumerate(refs[:conts])), refs[conts:]
    keys_ref, values_refs, refs = refs[0], refs[1 : 1 + pieces], refs[1 + pieces :]
    before, refs = refs[: 2 * conts], refs[2 * conts :]
    if with_weight:
        weight_ref, *refs = refs
    after, refs = refs[: 2 * conts], refs[2 * conts :]
    if with_weight:
        give_ref, flipped_ref, sems = refs
        copies = start_all(weight_copies(weight_ref, give_ref, sems, True))
    else:
        (flipped_ref,) = refs
    source, valid = arrivals(step, sources)[part]

    def absorb_part():
        shard = (source, lists_ref, counts_ref, q_refs, keys_ref, values_refs, flipped_ref)
        absorb_shard(*shard, by_cont(before), by_cont(after))

    if valid is True:
        absorb_part()
    else:
        pl.when(valid)(absorb_part)
        pl.when(jnp.logical_not(valid))(lambda: hand_on(before, after))
    if with_weight:
        for copy in copies:
            copy.wait()


def finish_and_give(acc_ref, stat_ref, weight_ref, attended_ref, give_ref):
    for head in range(attended_ref.shape[1] // HD):
        _, total, acc = load_state(acc_ref, stat_ref, head)
        attended_ref[:, head * HD : (head + 1) * HD] = (acc / total).T.astype(jnp.bfloat16)
    for k in range(weight_ref.shape[0]):
        give_ref[k] = jnp.dot(
            attended_ref[...], weight_ref[k], preferred_element_type=jnp.float32
        ).astype(give_ref.dtype)


def last_kernel(
    step,
    sources,
    cont,
    lists_ref,
    counts_ref,
    q_ref,
    mine_keys_ref,
    mine_values_ref,
    their_keys_ref,
    their_values_ref,
    acc_in,
    stat_in,
    give_weight_ref,
    *refs,
):
    if cont == 0:
        weight_ref, attended_ref, give_ref, keep_weight_ref, *refs, sems = refs
        copies = start_all(weight_copies(weight_ref, keep_weight_ref, sems, False))
    else:
        attended_ref, give_ref, *refs = refs
    acc_ref, stat_ref, flipped_ref = refs
    before, after = (acc_in, stat_in), (acc_ref, stat_ref)
    held = (mine_keys_ref, [mine_values_ref]), (their_keys_ref, [their_values_ref])
    parts = arrivals(step, sources)
    one_of_two = sources == 4
    for part, (source, valid) in enumerate(parts):

        def absorb_part():
            shard = (source, lists_ref, counts_ref, {cont: q_ref}, *held[part], flipped_ref)
            first = part == 0 or one_of_two
            absorb_shard(*shard, {cont: before if first else after}, {cont: after})

        pl.when(valid)(absorb_part)
        if part == 0 and not one_of_two:
            pl.when(jnp.logical_not(valid))(lambda: hand_on(before, after))
    finish_and_give(acc_ref, stat_ref, give_weight_ref, attended_ref, give_ref)
    if cont == 0:
        for copy in copies:
            copy.wait()


def onward_kernel(attended_ref, weight_ref, got_ref, *onward_refs):
    for k, onward_ref in enumerate(onward_refs, 1):
        onward_ref[...] = (
            jnp.dot(attended_ref[...], weight_ref[k], preferred_element_type=jnp.float32)
            + got_ref[k].astype(jnp.float32)
        ).astype(jnp.bfloat16)


def near_kernel(cont, attended_ref, weight_ref, got_ref, residual_ref, near_ref, own_ref, sem):
    share = near_ref.shape[1]
    start = pl.multiple_of(lax.axis_index("tp") * share, HD)
    copy = pltpu.make_async_copy(
        residual_ref.at[cont, :, pl.ds(start, share)], own_ref, sem.at[0]
    )
    copy.start()
    near_ref[...] = jnp.dot(
        attended_ref[...], weight_ref[0], preferred_element_type=jnp.float32
    ) + got_ref[0].astype(jnp.float32)
    copy.wait()
    near_ref[...] += own_ref[...].astype(jnp.float32)


def sum_kernel(count, *refs):
    near_ref, fars, (total_ref, squares_ref) = refs[0], refs[1 : 1 + count], refs[1 + count :]
    total = near_ref[...]
    for far_ref in fars:
        total = total + far_ref[...].astype(jnp.float32)
    total_ref[...] = total
    sums = jnp.sum(total * total, axis=1, keepdims=True)
    squares_ref[...] = jnp.broadcast_to(sums, (sums.shape[0], HD)).T[:8]


def norm_kernel(conts, members, model_width, *refs):
    totals, squares = refs[:conts], refs[conts : conts + members]
    gain_ref, stream_ref, normed_ref = refs[conts + members :]
    gain = gain_ref[...].astype(jnp.float32)
    for cont in range(conts):
        row = functools.reduce(jnp.add, [ref[cont * 8 : cont * 8 + 1, :] for ref in squares])
        scale = lax.rsqrt(row / model_width + 1e-05)
        scale = jnp.broadcast_to(scale, (HD, scale.shape[1])).T[:, 0:1]
        total = totals[cont][...]
        stream_ref[cont] = total.astype(jnp.bfloat16)
        normed_ref[cont] = (total * scale * gain).astype(jnp.bfloat16)


def shards(
    queries,
    cont_keys,
    cont_values,
    prompt_keys,
    prompt_values,
    block_lists,
    tile_counts,
    out_weight,
    residual,
    norm_gain,
    *,
    sources,
    members,
):
    conts, length, width = queries.shape
    heads = width // HD
    rows_dev = prompt_keys.shape[0]
    model_width = residual.shape[2]
    share = norm_gain.shape[0]
    chips = members // CORES
    place = lax.axis_index("tp")
    pairs = heads * conts
    params = pltpu.CompilerParams(vmem_limit_bytes=VMEM_LIMIT)
    smem = pl.BlockSpec(memory_space=pltpu.SMEM)
    vmem = pl.BlockSpec(memory_space=pltpu.VMEM)
    hbm = pl.BlockSpec(memory_space=pltpu.HBM)

    def array(shape, dtype):
        return jax.ShapeDtypeStruct(shape, dtype)

    def cost(flops=1024):
        return pl.CostEstimate(flops=flops, bytes_accessed=1024, transcendentals=0)

    def in_hbm(x):
        return pltpu.with_memory_space_constraint(x, pltpu.HBM)

    kept = array((rows_dev, HD), jnp.bfloat16)
    keys = pl.pallas_call(
        functools.partial(pack_keys_kernel, heads),
        out_shape=kept,
        in_specs=[hbm],
        out_specs=vmem,
        scratch_shapes=[pltpu.SemaphoreType.DMA((1,))],
        compiler_params=params,
        cost_estimate=cost(),
        name="pack_keys",
    )(in_hbm(prompt_keys))
    values = pl.pallas_call(
        functools.partial(pack_values_kernel, heads),
        out_shape=kept,
        in_specs=[hbm],
        out_specs=vmem,
        scratch_shapes=[
            pltpu.VMEM((rows_dev, HD), jnp.bfloat16),
            pltpu.SemaphoreType.DMA((1,)),
        ],
        compiler_params=params,
        cost_estimate=cost(),
        name="pack_values",
    )(in_hbm(prompt_values))

    def across(step):
        def target(z, t):
            if sources == 4 and step == 1:
                return z ^ (1 + t % CORES)
            if sources == 4:
                return z ^ 1 if t % CORES == 1 else None
            to = z + step if t % CORES == 0 else z - step
            return to if 0 <= to < sources else None

        return [
            (z * members + t, target(z, t) * members + t)
            for z in range(sources)
            for t in range(members)
            if target(z, t) is not None
        ]

    sibling = [(t, t ^ 1) for t in range(members)]
    steps = steps_of(sources)
    lists = in_hbm(block_lists)
    counts = in_hbm(tile_counts.transpose(1, 2, 0))
    state_shape = (
        array((heads, HD, length), jnp.float32),
        array((heads, 8, length), jnp.float32),
    )
    flipped = pltpu.VMEM((2 * rows_dev, HD), jnp.bfloat16)
    weight_shape = array((chips, width, share), jnp.bfloat16)

    def attend_own(cont, keys):
        *state, q = pl.pallas_call(
            functools.partial(first_kernel, cont),
            out_shape=state_shape + (array((heads, HD, length), jnp.bfloat16),),
            in_specs=[smem, smem, vmem, vmem] + [hbm] * 3,
            out_specs=(vmem,) * 3,
            scratch_shapes=[
                flipped,
                pltpu.VMEM((length, width), jnp.bfloat16),
                pltpu.VMEM((length, HD), jnp.bfloat16),
                pltpu.VMEM((length, HD), jnp.bfloat16),
                pltpu.VMEM((HD, length), jnp.bfloat16),
                pltpu.SemaphoreType.DMA((3,)),
            ],
            compiler_params=params,
            cost_estimate=cost(),
            name="attend_own",
        )(
            lists,
            counts,
            keys,
            values,
            in_hbm(queries),
            in_hbm(cont_keys),
            in_hbm(cont_values),
        )
        return tuple(state), q

    def attend_step(step, part, with_weight, states, held):
        flat = [x for state in states for x in state]
        made = pl.pallas_call(
            functools.partial(
                middle_kernel, step, part, sources, conts, len(held) - 1, with_weight
            ),
            out_shape=state_shape * conts + ((weight_shape,) if with_weight else ()),
            in_specs=[smem, smem] + [vmem] * (3 * conts + len(held)) + [hbm] * with_weight,
            out_specs=(vmem,) * (2 * conts + with_weight),
            scratch_shapes=[flipped] + [pltpu.SemaphoreType.DMA((chips,))] * with_weight,
            compiler_params=params,
            cost_estimate=cost(),
            name="attend_step",
        )(lists, counts, *qs, *held, *flat, *([in_hbm(out_weight)] * with_weight))
        return tuple(made[2 * c : 2 * c + 2] for c in range(conts)), made[2 * conts :]

    states, qs = [], []
    for step in range(1, steps + 1):
        sent = mine if sources == 4 and step == 2 else (keys, values)
        mine_keys, mine_values = [lax.ppermute(x, ("ctx", "tp"), across(step)) for x in sent]
        own_keys = keys
        if step == 1:
            state, q = attend_own(0, keys)
            states.append(state)
            qs.append(q)
        mine_keys, own_keys, states = lax.optimization_barrier(
            (mine_keys, own_keys, tuple(states))
        )
        if step == 1:
            states = list(states)
            for cont in range(1, conts):
                state, q = attend_own(cont, own_keys)
                states.append(state)
                qs.append(q)
        their_keys = lax.ppermute(mine_keys, "tp", sibling)
        mine_values, states = lax.optimization_barrier((mine_values, tuple(states)))
        their_values = [
            lax.ppermute(x, "tp", sibling)
            for x in jnp.split(mine_values, 2 if step < steps else 1)
        ]
        mine, theirs = (mine_keys, mine_values), (their_keys, *their_values)
        if step < steps:
            states, (give_weight,) = attend_step(step, 0, True, states, mine)
            states, _ = attend_step(step, 1, False, states, theirs)

    def attend_last(cont):
        fetch = cont == 0
        return pl.pallas_call(
            functools.partial(last_kernel, steps, sources, cont),
            out_shape=(
                array((length, width), jnp.bfloat16),
                array((chips, length, share), jnp.bfloat16),
            )
            + (weight_shape,) * fetch,
            in_specs=[smem, smem] + [vmem] * 8 + [hbm] * fetch,
            out_specs=(vmem,) * (2 + fetch),
            scratch_shapes=[pltpu.VMEM(a.shape, a.dtype) for a in state_shape]
            + [flipped]
            + [pltpu.SemaphoreType.DMA((chips,))] * fetch,
            compiler_params=params,
            cost_estimate=cost(),
            name="attend_last",
        )(
            lists,
            counts,
            qs[cont],
            *mine,
            *theirs,
            *states[cont],
            give_weight,
            *([in_hbm(out_weight)] * fetch),
        )

    def onward(attended, got):
        parts = pl.pallas_call(
            onward_kernel,
            out_shape=(array((length, share), jnp.bfloat16),) * (chips - 1),
            in_specs=[vmem] * 3,
            out_specs=(vmem,) * (chips - 1),
            compiler_params=params,
            cost_estimate=cost(),
            name="project_onward",
        )(attended, keep_weight, got)
        far = []
        for k in range(1, chips):
            to_chip = [
                (t, (t // CORES + k) % chips * CORES + t % CORES) for t in range(members)
            ]
            far.append(lax.ppermute(parts[k - 1], "tp", to_chip))
        return parts, far

    def near(cont, attended, got):
        return pl.pallas_call(
            functools.partial(near_kernel, cont),
            out_shape=array((length, share), jnp.float32),
            in_specs=[vmem] * 3 + [hbm],
            out_specs=vmem,
            scratch_shapes=[
                pltpu.VMEM((length, share), jnp.bfloat16),
                pltpu.SemaphoreType.DMA((1,)),
            ],
            compiler_params=params,
            cost_estimate=cost(),
            name="project_near",
        )(attended, keep_weight, got, in_hbm(residual))

    attended, give, keep_weight = attend_last(0)
    nears, fars = [], []
    for cont in range(conts):
        got = lax.ppermute(give, "tp", sibling)
        here = attended
        if cont + 1 < conts:
            attended, give = attend_last(cont + 1)
            got, give = lax.optimization_barrier((got, give))
        _, far = onward(here, got)
        fars.append(far)
        nears.append(near(cont, here, got))

    totals, squares = [], []
    for cont in range(conts):
        total, square = pl.pallas_call(
            functools.partial(sum_kernel, chips - 1),
            out_shape=(array((length, share), jnp.float32), array((8, length), jnp.float32)),
            in_specs=[vmem] * chips,
            out_specs=(vmem,) * 2,
            compiler_params=params,
            cost_estimate=cost(),
            name="add_up",
        )(nears[cont], *fars[cont])
        totals.append(total)
        squares.append(square)
    squares = jnp.concatenate(squares, axis=0)
    all_squares = [squares] + [
        lax.ppermute(squares, "tp", [(t, (t + k) % members) for t in range(members)])
        for k in range(1, members)
    ]
    out = array((conts, length, share), jnp.bfloat16)
    return pl.pallas_call(
        functools.partial(norm_kernel, conts, members, model_width),
        out_shape=(out, out),
        in_specs=[vmem] * (conts + members + 1),
        out_specs=(vmem, vmem),
        compiler_params=params,
        cost_estimate=cost(),
        name="norm",
    )(*totals, *all_squares, norm_gain.reshape(1, share))


def solution(mesh):
    placed = (
        P(("grp", "ctx"), None, "tp"),
        P(("grp", "ctx"), None, None),
        P(("grp", "ctx"), None, None),
        P(("grp", "ctx"), None),
        P(("grp", "ctx"), None),
        P("tp", ("grp", "ctx"), None, None),
        P("tp", ("grp", "ctx"), None),
        P("tp", None),
        P(("grp", "ctx"), None, None),
        P("tp"),
    )
    return jax.shard_map(
        functools.partial(
            shards, sources=mesh.shape["ctx"], members=mesh.shape["tp"]
        ),
        mesh=mesh,
        in_specs=placed,
        out_specs=(P(("grp", "ctx"), None, "tp"), P(("grp", "ctx"), None, "tp")),
        check_vma=False,
    )
```

```python
import functools
import math

import jax
import jax.numpy as jnp
from jax import lax
from jax.experimental import pallas as pl
from jax.experimental.pallas import tpu as pltpu
from jax.sharding import PartitionSpec as P

HEADS = 32
KVH = 2
HD = 128
BLK = 64
TILES = 8
CORES = 2
TOGETHER = 8

VERY_LOW = -1e30
TO_LOG2 = math.log2(math.e) / math.sqrt(HD)

VMEM_LIMIT = 24 * 1024 * 1024


def key_group(heads):
    return lax.axis_index("tp") * heads // (HEADS // KVH)


def group_lanes(heads):
    return pl.ds(pl.multiple_of(key_group(heads) * HD, HD), HD)


def pack_keys_kernel(heads, keys_ref, packed_ref, sems):
    copy = pltpu.make_async_copy(keys_ref.at[:, group_lanes(heads)], packed_ref, sems.at[0])
    copy.start()
    copy.wait()


def pack_values_kernel(heads, values_ref, packed_ref, values_buf, sems):
    copy = pltpu.make_async_copy(values_ref.at[:, group_lanes(heads)], values_buf, sems.at[0])
    copy.start()
    copy.wait()
    for p in range(packed_ref.shape[0] // HD):
        rows = slice(p * HD, (p + 1) * HD)
        packed_ref[rows, :] = values_buf[rows, :].T


def both_ways(values_refs, flipped_ref):
    total = flipped_ref.shape[0] // 2
    for part, values_ref in enumerate(values_refs):
        rows = values_ref.shape[0]
        for p in range(rows // HD):
            pair = values_ref[p * HD : (p + 1) * HD, :]
            at = part * rows + p * HD
            flipped_ref[at : at + HD, :] = pair
            flipped_ref[total + at : total + at + HD, :] = jnp.concatenate(
                [pair[:, BLK:], pair[:, :BLK]], axis=1
            )


def shard_scores(lists_ref, counts_ref, q_refs, keys_ref, flipped_ref, source, head, cont):
    pairs = keys_ref.shape[0] // HD
    count = counts_ref[cont, source, head]
    blocks = [lists_ref[head, cont, source, t] for t in range(TILES)]
    keys = jnp.concatenate(
        [keys_ref[pl.ds(pl.multiple_of(b * BLK, BLK), BLK), :] for b in blocks], axis=0
    )
    scores = jnp.dot(keys, q_refs[cont][head], preferred_element_type=jnp.float32)
    lane = lax.broadcasted_iota(jnp.int32, (HD, HD), 1)
    halves = []
    for t, b in enumerate(blocks):
        spot = ((b + t) % 2 * pairs + b // 2) * HD
        halves.append(flipped_ref[pl.ds(pl.multiple_of(spot, HD), HD), :])
    values = jnp.concatenate(
        [jnp.where(lane < BLK, a, b) for a, b in zip(halves[::2], halves[1::2])], axis=1
    )
    tiles = [
        (scores[t * BLK : (t + 1) * BLK], t < count) for t in range(TILES)
    ]
    return tiles, values


def fold(op, tile):
    return functools.reduce(op, [tile[i : i + 8] for i in range(0, tile.shape[0], 8)])


def absorb(state, tiles, values):
    top, total, acc = state
    tops = [
        jnp.where(live, fold(jnp.maximum, tile), VERY_LOW) for tile, live in tiles
    ]
    best = jnp.max(functools.reduce(jnp.maximum, tops), axis=0, keepdims=True)
    new_top = jnp.maximum(top, best)
    weights = [
        jnp.exp2((tile - jnp.where(live, new_top, -VERY_LOW)) * TO_LOG2) for tile, live in tiles
    ]
    factor = jnp.exp2((top - new_top) * TO_LOG2)
    sums = functools.reduce(jnp.add, [fold(jnp.add, w) for w in weights])
    total = total * factor + jnp.sum(sums, axis=0, keepdims=True)
    rounded = jnp.concatenate([w.astype(jnp.bfloat16) for w in weights], axis=0)
    acc = acc * factor + jnp.dot(values, rounded, preferred_element_type=jnp.float32)
    return new_top, total, acc


def load_state(acc_ref, stat_ref, index):
    both = stat_ref[index]
    return both[0:1], both[1:2], acc_ref[index]


def store_state(acc_ref, stat_ref, index, state):
    top, total, acc = state
    stat_ref[index] = jnp.concatenate([top, total] + [total] * 6, axis=0)
    acc_ref[index] = acc


def start_all(copies):
    for copy in copies:
        copy.start()
    return copies


def weight_copies(weight_ref, target, sems, sibling):
    chips, _, share = target.shape
    place = lax.axis_index("tp")
    chip, core = place // CORES, place % CORES
    held = 1 - core if sibling else core
    copies = []
    for k in range(chips):
        start = (lax.rem(chip + k, chips) * CORES + held) * share
        copies.append(
            pltpu.make_async_copy(
                weight_ref.at[:, pl.ds(pl.multiple_of(start, HD), share)],
                target.at[k],
                sems.at[k],
            )
        )
    return copies


def first_kernel(
    conts,
    lists_hbm,
    counts_hbm,
    keys_ref,
    values_ref,
    queries_ref,
    cont_keys_ref,
    cont_values_ref,
    *refs,
):
    states, refs = by_cont(refs[: 2 * conts]), refs[2 * conts :]
    q_refs, refs = refs[:conts], refs[conts:]
    lists_kept, counts_kept, lists_ref, counts_ref, *refs = refs
    flipped_ref, rows_ref, ck_ref, cv_ref, own_ref, sems = refs
    heads, _, length = q_refs[0].shape
    lanes = group_lanes(heads)
    copies = start_all(
        [
            pltpu.make_async_copy(cont_values_ref.at[:, :, lanes], cv_ref, sems.at[0]),
            pltpu.make_async_copy(queries_ref, rows_ref, sems.at[1]),
            pltpu.make_async_copy(cont_keys_ref.at[:, :, lanes], ck_ref, sems.at[2]),
            pltpu.make_async_copy(lists_hbm, lists_ref, sems.at[3]),
            pltpu.make_async_copy(counts_hbm, counts_ref, sems.at[4]),
            pltpu.make_async_copy(lists_hbm, lists_kept, sems.at[5]),
            pltpu.make_async_copy(counts_hbm, counts_kept, sems.at[6]),
        ]
    )
    own = lax.axis_index("ctx")
    both_ways([values_ref], flipped_ref)
    copies[0].wait()
    for cont in range(conts):
        own_ref[cont] = cv_ref[cont].T
    copies[1].wait()
    for cont in range(conts):
        for head in range(heads):
            q_refs[cont][head] = rows_ref[cont, :, head * HD : (head + 1) * HD].T
    for copy in copies[2:]:
        copy.wait()
    together = TOGETHER // conts

    def some_heads(index, carry):
        work = [(index * together + j, cont) for j in range(together) for cont in range(conts)]
        made = []
        for head, cont in work:
            scores = jnp.dot(
                ck_ref[cont], q_refs[cont][head], preferred_element_type=jnp.float32
            )
            key = lax.broadcasted_iota(jnp.int32, scores.shape, 0)
            row = lax.broadcasted_iota(jnp.int32, scores.shape, 1)
            scores = jnp.where(key <= row, scores, VERY_LOW)
            tiles, values = shard_scores(
                lists_ref, counts_ref, q_refs, keys_ref, flipped_ref, own, head, cont
            )
            made.append(
                ([(scores, True)] + tiles, jnp.concatenate([own_ref[cont], values], axis=1))
            )
        after = []
        for got in made:
            start = (
                jnp.full((1, length), VERY_LOW, jnp.float32),
                jnp.zeros((1, length), jnp.float32),
                jnp.zeros((HD, length), jnp.float32),
            )
            after.append(absorb(start, *got))
        for (head, cont), state in zip(work, after):
            store_state(*states[cont], head, state)
        return carry

    lax.fori_loop(0, heads // together, some_heads, 0)


def arrivals(step, sources):
    spot = lax.axis_index("ctx")
    core = lax.axis_index("tp") % CORES
    if sources == 4:
        if step == 1:
            mine = jnp.bitwise_xor(spot, 1 + core)
            return ((mine, True), (jnp.bitwise_xor(mine, 3), True))
        far = jnp.bitwise_xor(spot, 3)
        return ((far, core == 1), (far, core == 0))
    mine = jnp.where(core == 0, spot - step, spot + step)
    theirs = jnp.where(core == 0, spot + step, spot - step)
    return tuple((s, (s >= 0) & (s < sources)) for s in (mine, theirs))


def steps_of(sources):
    return 2 if sources == 4 else sources - 1


def lists_copies(lists_kept, counts_kept, lists_ref, counts_ref, sems):
    return start_all(
        [
            pltpu.make_async_copy(lists_kept, lists_ref, sems.at[0]),
            pltpu.make_async_copy(counts_kept, counts_ref, sems.at[1]),
        ]
    )


def absorb_shard(
    pending,
    source,
    lists_ref,
    counts_ref,
    q_refs,
    keys_ref,
    values_refs,
    flipped_ref,
    before,
    after,
):
    heads = next(iter(q_refs.values())).shape[0]
    together = min(heads, TOGETHER // len(q_refs))
    both_ways(values_refs, flipped_ref)
    for copy in pending:
        copy.wait()

    def some_heads(index, carry):
        work = [(index * together + j, cont) for j in range(together) for cont in q_refs]
        states = [load_state(*before[cont], head) for head, cont in work]
        made = [
            shard_scores(lists_ref, counts_ref, q_refs, keys_ref, flipped_ref, source, head, cont)
            for head, cont in work
        ]
        states = [absorb(state, *got) for state, got in zip(states, made)]
        for (head, cont), state in zip(work, states):
            store_state(*after[cont], head, state)
        return carry

    lax.fori_loop(0, heads // together, some_heads, 0)


def hand_on(before, after):
    for source_ref, target_ref in zip(before, after):
        target_ref[...] = source_ref[...]


def by_cont(refs):
    return {cont: refs[2 * cont : 2 * cont + 2] for cont in range(len(refs) // 2)}


def middle_kernel(
    step, part, sources, conts, pieces, with_weight, lists_kept, counts_kept, *refs
):
    q_refs, refs = dict(enumerate(refs[:conts])), refs[conts:]
    keys_ref, values_refs, refs = refs[0], refs[1 : 1 + pieces], refs[1 + pieces :]
    before, refs = refs[: 2 * conts], refs[2 * conts :]
    if with_weight:
        weight_ref, *refs = refs
    after, refs = refs[: 2 * conts], refs[2 * conts :]
    if with_weight:
        give_ref, *refs, sems = refs
        copies = start_all(weight_copies(weight_ref, give_ref, sems, True))
    flipped_ref, lists_ref, counts_ref, list_sems = refs
    source, valid = arrivals(step, sources)[part]

    def absorb_part():
        pending = lists_copies(lists_kept, counts_kept, lists_ref, counts_ref, list_sems)
        shard = (pending, source, lists_ref, counts_ref, q_refs, keys_ref, values_refs, flipped_ref)
        absorb_shard(*shard, by_cont(before), by_cont(after))

    if valid is True:
        absorb_part()
    else:
        pl.when(valid)(absorb_part)
        pl.when(jnp.logical_not(valid))(lambda: hand_on(before, after))
    if with_weight:
        for copy in copies:
            copy.wait()


def finish_and_give(acc_ref, stat_ref, weight_ref, attended_ref, give_ref):
    for head in range(attended_ref.shape[1] // HD):
        _, total, acc = load_state(acc_ref, stat_ref, head)
        attended_ref[:, head * HD : (head + 1) * HD] = (acc / total).T.astype(jnp.bfloat16)
    for k in range(weight_ref.shape[0]):
        give_ref[k] = jnp.dot(
            attended_ref[...], weight_ref[k], preferred_element_type=jnp.float32
        ).astype(give_ref.dtype)


def last_kernel(
    step,
    sources,
    cont,
    lists_kept,
    counts_kept,
    q_ref,
    mine_keys_ref,
    mine_values_ref,
    their_keys_ref,
    their_values_ref,
    acc_in,
    stat_in,
    give_weight_ref,
    *refs,
):
    if cont == 0:
        weight_ref, attended_ref, give_ref, keep_weight_ref, *refs, sems = refs
        copies = start_all(weight_copies(weight_ref, keep_weight_ref, sems, False))
    else:
        attended_ref, give_ref, *refs = refs
    acc_ref, stat_ref, flipped_ref, lists_ref, counts_ref, list_sems = refs
    before, after = (acc_in, stat_in), (acc_ref, stat_ref)
    held = (mine_keys_ref, [mine_values_ref]), (their_keys_ref, [their_values_ref])
    parts = arrivals(step, sources)
    one_of_two = sources == 4
    for part, (source, valid) in enumerate(parts):

        def absorb_part():
            pending = lists_copies(lists_kept, counts_kept, lists_ref, counts_ref, list_sems)
            shard = (pending, source, lists_ref, counts_ref, {cont: q_ref}, *held[part])
            first = part == 0 or one_of_two
            absorb_shard(
                *shard, flipped_ref, {cont: before if first else after}, {cont: after}
            )

        pl.when(valid)(absorb_part)
        if part == 0 and not one_of_two:
            pl.when(jnp.logical_not(valid))(lambda: hand_on(before, after))
    finish_and_give(acc_ref, stat_ref, give_weight_ref, attended_ref, give_ref)
    if cont == 0:
        for copy in copies:
            copy.wait()


def onward_kernel(attended_ref, weight_ref, got_ref, *onward_refs):
    for k, onward_ref in enumerate(onward_refs, 1):
        onward_ref[...] = (
            jnp.dot(attended_ref[...], weight_ref[k], preferred_element_type=jnp.float32)
            + got_ref[k].astype(jnp.float32)
        ).astype(jnp.bfloat16)


def near_kernel(cont, attended_ref, weight_ref, got_ref, residual_ref, near_ref, own_ref, sem):
    share = near_ref.shape[1]
    start = pl.multiple_of(lax.axis_index("tp") * share, HD)
    copy = pltpu.make_async_copy(
        residual_ref.at[cont, :, pl.ds(start, share)], own_ref, sem.at[0]
    )
    copy.start()
    near_ref[...] = jnp.dot(
        attended_ref[...], weight_ref[0], preferred_element_type=jnp.float32
    ) + got_ref[0].astype(jnp.float32)
    copy.wait()
    near_ref[...] += own_ref[...].astype(jnp.float32)


def sum_kernel(count, *refs):
    near_ref, fars, (total_ref, squares_ref) = refs[0], refs[1 : 1 + count], refs[1 + count :]
    total = near_ref[...]
    for far_ref in fars:
        total = total + far_ref[...].astype(jnp.float32)
    total_ref[...] = total
    sums = jnp.sum(total * total, axis=1, keepdims=True)
    squares_ref[...] = jnp.broadcast_to(sums, (sums.shape[0], HD)).T[:8]


def norm_kernel(conts, members, model_width, *refs):
    totals, squares = refs[:conts], refs[conts : conts + members]
    gain_ref, stream_ref, normed_ref = refs[conts + members :]
    gain = gain_ref[...].astype(jnp.float32)
    for cont in range(conts):
        row = functools.reduce(jnp.add, [ref[cont * 8 : cont * 8 + 1, :] for ref in squares])
        scale = lax.rsqrt(row / model_width + 1e-05)
        scale = jnp.broadcast_to(scale, (HD, scale.shape[1])).T[:, 0:1]
        total = totals[cont][...]
        stream_ref[cont] = total.astype(jnp.bfloat16)
        normed_ref[cont] = (total * scale * gain).astype(jnp.bfloat16)


def shards(
    queries,
    cont_keys,
    cont_values,
    prompt_keys,
    prompt_values,
    block_lists,
    tile_counts,
    out_weight,
    residual,
    norm_gain,
    *,
    sources,
    members,
):
    conts, length, width = queries.shape
    heads = width // HD
    rows_dev = prompt_keys.shape[0]
    model_width = residual.shape[2]
    share = norm_gain.shape[0]
    chips = members // CORES
    place = lax.axis_index("tp")
    pairs = heads * conts
    params = pltpu.CompilerParams(vmem_limit_bytes=VMEM_LIMIT)
    vmem = pl.BlockSpec(memory_space=pltpu.VMEM)
    hbm = pl.BlockSpec(memory_space=pltpu.HBM)

    def array(shape, dtype):
        return jax.ShapeDtypeStruct(shape, dtype)

    def cost(flops=1024):
        return pl.CostEstimate(flops=flops, bytes_accessed=1024, transcendentals=0)

    def in_hbm(x):
        return pltpu.with_memory_space_constraint(x, pltpu.HBM)

    kept = array((rows_dev, HD), jnp.bfloat16)
    keys = pl.pallas_call(
        functools.partial(pack_keys_kernel, heads),
        out_shape=kept,
        in_specs=[hbm],
        out_specs=vmem,
        scratch_shapes=[pltpu.SemaphoreType.DMA((1,))],
        compiler_params=params,
        cost_estimate=cost(),
        name="pack_keys",
    )(in_hbm(prompt_keys))
    values = pl.pallas_call(
        functools.partial(pack_values_kernel, heads),
        out_shape=kept,
        in_specs=[hbm],
        out_specs=vmem,
        scratch_shapes=[
            pltpu.VMEM((rows_dev, HD), jnp.bfloat16),
            pltpu.SemaphoreType.DMA((1,)),
        ],
        compiler_params=params,
        cost_estimate=cost(),
        name="pack_values",
    )(in_hbm(prompt_values))

    def across(step):
        def target(z, t):
            if sources == 4 and step == 1:
                return z ^ (1 + t % CORES)
            if sources == 4:
                return z ^ 1 if t % CORES == 1 else None
            to = z + step if t % CORES == 0 else z - step
            return to if 0 <= to < sources else None

        return [
            (z * members + t, target(z, t) * members + t)
            for z in range(sources)
            for t in range(members)
            if target(z, t) is not None
        ]

    sibling = [(t, t ^ 1) for t in range(members)]
    steps = steps_of(sources)
    lists = in_hbm(block_lists)
    counts = in_hbm(tile_counts.transpose(1, 2, 0))
    state_shape = (
        array((heads, HD, length), jnp.float32),
        array((heads, 8, length), jnp.float32),
    )
    flipped = pltpu.VMEM((2 * rows_dev, HD), jnp.bfloat16)
    weight_shape = array((chips, width, share), jnp.bfloat16)

    list_shapes = (array(lists.shape, jnp.int32), array(counts.shape, jnp.int32))
    list_scratch = [pltpu.SMEM(x.shape, x.dtype) for x in list_shapes]
    with_lists = [flipped] + list_scratch + [pltpu.SemaphoreType.DMA((2,))]
    *made, lists_kept, counts_kept = pl.pallas_call(
        functools.partial(first_kernel, conts),
        out_shape=state_shape * conts
        + (array((heads, HD, length), jnp.bfloat16),) * conts
        + list_shapes,
        in_specs=[hbm, hbm, vmem, vmem] + [hbm] * 3,
        out_specs=(vmem,) * (3 * conts + 2),
        scratch_shapes=list_scratch
        + [
            flipped,
            pltpu.VMEM(queries.shape, jnp.bfloat16),
            pltpu.VMEM((conts, length, HD), jnp.bfloat16),
            pltpu.VMEM((conts, length, HD), jnp.bfloat16),
            pltpu.VMEM((conts, HD, length), jnp.bfloat16),
            pltpu.SemaphoreType.DMA((7,)),
        ],
        compiler_params=params,
        cost_estimate=cost(),
        name="attend_own",
    )(lists, counts, keys, values, in_hbm(queries), in_hbm(cont_keys), in_hbm(cont_values))
    states = tuple(made[2 * c : 2 * c + 2] for c in range(conts))
    qs = made[2 * conts :]

    def attend_step(step, part, with_weight, states, held):
        flat = [x for state in states for x in state]
        made = pl.pallas_call(
            functools.partial(
                middle_kernel, step, part, sources, conts, len(held) - 1, with_weight
            ),
            out_shape=state_shape * conts + ((weight_shape,) if with_weight else ()),
            in_specs=[vmem] * (2 + 3 * conts + len(held)) + [hbm] * with_weight,
            out_specs=(vmem,) * (2 * conts + with_weight),
            scratch_shapes=with_lists + [pltpu.SemaphoreType.DMA((chips,))] * with_weight,
            compiler_params=params,
            cost_estimate=cost(),
            name="attend_step",
        )(lists_kept, counts_kept, *qs, *held, *flat, *([in_hbm(out_weight)] * with_weight))
        return tuple(made[2 * c : 2 * c + 2] for c in range(conts)), made[2 * conts :]

    for step in range(1, steps + 1):
        sent = mine if sources == 4 and step == 2 else (keys, values)
        mine_keys, mine_values = [lax.ppermute(x, ("ctx", "tp"), across(step)) for x in sent]
        mine_keys, states = lax.optimization_barrier((mine_keys, tuple(states)))
        their_keys = lax.ppermute(mine_keys, "tp", sibling)
        mine_values, states = lax.optimization_barrier((mine_values, tuple(states)))
        their_values = [
            lax.ppermute(x, "tp", sibling)
            for x in jnp.split(mine_values, 2 if step < steps else 1)
        ]
        mine, theirs = (mine_keys, mine_values), (their_keys, *their_values)
        if step < steps:
            states, (give_weight,) = attend_step(step, 0, True, states, mine)
            states, _ = attend_step(step, 1, False, states, theirs)

    def attend_last(cont):
        fetch = cont == 0
        return pl.pallas_call(
            functools.partial(last_kernel, steps, sources, cont),
            out_shape=(
                array((length, width), jnp.bfloat16),
                array((chips, length, share), jnp.bfloat16),
            )
            + (weight_shape,) * fetch,
            in_specs=[vmem] * 10 + [hbm] * fetch,
            out_specs=(vmem,) * (2 + fetch),
            scratch_shapes=[pltpu.VMEM(a.shape, a.dtype) for a in state_shape]
            + with_lists
            + [pltpu.SemaphoreType.DMA((chips,))] * fetch,
            compiler_params=params,
            cost_estimate=cost(),
            name="attend_last",
        )(
            lists_kept,
            counts_kept,
            qs[cont],
            *mine,
            *theirs,
            *states[cont],
            give_weight,
            *([in_hbm(out_weight)] * fetch),
        )

    def onward(attended, got):
        parts = pl.pallas_call(
            onward_kernel,
            out_shape=(array((length, share), jnp.bfloat16),) * (chips - 1),
            in_specs=[vmem] * 3,
            out_specs=(vmem,) * (chips - 1),
            compiler_params=params,
            cost_estimate=cost(),
            name="project_onward",
        )(attended, keep_weight, got)
        far = []
        for k in range(1, chips):
            to_chip = [
                (t, (t // CORES + k) % chips * CORES + t % CORES) for t in range(members)
            ]
            far.append(lax.ppermute(parts[k - 1], "tp", to_chip))
        return parts, far

    def near(cont, attended, got):
        return pl.pallas_call(
            functools.partial(near_kernel, cont),
            out_shape=array((length, share), jnp.float32),
            in_specs=[vmem] * 3 + [hbm],
            out_specs=vmem,
            scratch_shapes=[
                pltpu.VMEM((length, share), jnp.bfloat16),
                pltpu.SemaphoreType.DMA((1,)),
            ],
            compiler_params=params,
            cost_estimate=cost(),
            name="project_near",
        )(attended, keep_weight, got, in_hbm(residual))

    attended, give, keep_weight = attend_last(0)
    nears, fars = [], []
    for cont in range(conts):
        got = lax.ppermute(give, "tp", sibling)
        here = attended
        if cont + 1 < conts:
            attended, give = attend_last(cont + 1)
            got, give = lax.optimization_barrier((got, give))
        _, far = onward(here, got)
        fars.append(far)
        nears.append(near(cont, here, got))

    totals, squares = [], []
    for cont in range(conts):
        total, square = pl.pallas_call(
            functools.partial(sum_kernel, chips - 1),
            out_shape=(array((length, share), jnp.float32), array((8, length), jnp.float32)),
            in_specs=[vmem] * chips,
            out_specs=(vmem,) * 2,
            compiler_params=params,
            cost_estimate=cost(),
            name="add_up",
        )(nears[cont], *fars[cont])
        totals.append(total)
        squares.append(square)
    squares = jnp.concatenate(squares, axis=0)
    all_squares = [squares] + [
        lax.ppermute(squares, "tp", [(t, (t + k) % members) for t in range(members)])
        for k in range(1, members)
    ]
    out = array((conts, length, share), jnp.bfloat16)
    return pl.pallas_call(
        functools.partial(norm_kernel, conts, members, model_width),
        out_shape=(out, out),
        in_specs=[vmem] * (conts + members + 1),
        out_specs=(vmem, vmem),
        compiler_params=params,
        cost_estimate=cost(),
        name="norm",
    )(*totals, *all_squares, norm_gain.reshape(1, share))


def solution(mesh):
    placed = (
        P(("grp", "ctx"), None, "tp"),
        P(("grp", "ctx"), None, None),
        P(("grp", "ctx"), None, None),
        P(("grp", "ctx"), None),
        P(("grp", "ctx"), None),
        P("tp", ("grp", "ctx"), None, None),
        P("tp", ("grp", "ctx"), None),
        P("tp", None),
        P(("grp", "ctx"), None, None),
        P("tp"),
    )
    return jax.shard_map(
        functools.partial(
            shards, sources=mesh.shape["ctx"], members=mesh.shape["tp"]
        ),
        mesh=mesh,
        in_specs=placed,
        out_specs=(P(("grp", "ctx"), None, "tp"), P(("grp", "ctx"), None, "tp")),
        check_vma=False,
    )
```

```python
import functools
import math

import jax
import jax.numpy as jnp
from jax import lax
from jax.experimental import pallas as pl
from jax.experimental.pallas import tpu as pltpu
from jax.sharding import PartitionSpec as P

HEADS = 32
KVH = 2
HD = 128
BLK = 64
TILES = 8
CORES = 2
TOGETHER = 8

VERY_LOW = -1e30
TO_LOG2 = math.log2(math.e) / math.sqrt(HD)

VMEM_LIMIT = 24 * 1024 * 1024


def key_group(heads):
    return lax.axis_index("tp") * heads // (HEADS // KVH)


def group_lanes(heads):
    return pl.ds(pl.multiple_of(key_group(heads) * HD, HD), HD)


def pack_keys_kernel(heads, keys_ref, packed_ref, sems):
    copy = pltpu.make_async_copy(keys_ref.at[:, group_lanes(heads)], packed_ref, sems.at[0])
    copy.start()
    copy.wait()


def pack_values_kernel(heads, values_ref, packed_ref, values_buf, sems):
    copy = pltpu.make_async_copy(values_ref.at[:, group_lanes(heads)], values_buf, sems.at[0])
    copy.start()
    copy.wait()
    for p in range(packed_ref.shape[0] // HD):
        rows = slice(p * HD, (p + 1) * HD)
        packed_ref[rows, :] = values_buf[rows, :].T


def both_ways(values_ref, flipped_ref):
    rows = values_ref.shape[0]
    for p in range(rows // HD):
        pair = values_ref[p * HD : (p + 1) * HD, :]
        flipped_ref[p * HD : (p + 1) * HD, :] = pair
        flipped_ref[rows + p * HD : rows + (p + 1) * HD, :] = jnp.concatenate(
            [pair[:, BLK:], pair[:, :BLK]], axis=1
        )


def used_tiles(lists_ref, counts_ref, source, sources, place):
    at = place * sources + source
    return [lists_ref[at * TILES + t] for t in range(TILES)], counts_ref[at]


def shard_scores(blocks, count, query, keys_ref):
    keys = jnp.concatenate(
        [keys_ref[pl.ds(pl.multiple_of(b * BLK, BLK), BLK), :] for b in blocks], axis=0
    )
    scores = jnp.dot(keys, query, preferred_element_type=jnp.float32)
    return [(scores[t * BLK : (t + 1) * BLK], t < count) for t in range(TILES)]


def shard_values(blocks, flipped_ref):
    pairs = flipped_ref.shape[0] // 2 // HD
    lane = lax.broadcasted_iota(jnp.int32, (HD, HD), 1)
    halves = []
    for t, b in enumerate(blocks):
        spot = ((b + t) % 2 * pairs + b // 2) * HD
        halves.append(flipped_ref[pl.ds(pl.multiple_of(spot, HD), HD), :])
    return jnp.concatenate(
        [jnp.where(lane < BLK, a, b) for a, b in zip(halves[::2], halves[1::2])], axis=1
    )


def fold(op, tile):
    return functools.reduce(op, [tile[i : i + 8] for i in range(0, tile.shape[0], 8)])


def weigh(top, total, tiles):
    tops = [
        jnp.where(live, fold(jnp.maximum, tile), VERY_LOW) for tile, live in tiles
    ]
    best = jnp.max(functools.reduce(jnp.maximum, tops), axis=0, keepdims=True)
    new_top = jnp.maximum(top, best)
    weights = [
        jnp.exp2((tile - jnp.where(live, new_top, -VERY_LOW)) * TO_LOG2) for tile, live in tiles
    ]
    factor = jnp.exp2((top - new_top) * TO_LOG2)
    sums = functools.reduce(jnp.add, [fold(jnp.add, w) for w in weights])
    total = total * factor + jnp.sum(sums, axis=0, keepdims=True)
    rounded = jnp.concatenate([w.astype(jnp.bfloat16) for w in weights], axis=0)
    return (new_top, total, factor), rounded


def put_stat(stat_ref, head, stat):
    top, total, factor = stat
    stat_ref[head] = jnp.concatenate([top, total, factor] + [factor] * 5, axis=0)


def start_all(copies):
    for copy in copies:
        copy.start()
    return copies


def weight_copies(weight_ref, target, sems, sibling):
    chips, _, share = target.shape
    place = lax.axis_index("tp")
    chip, core = place // CORES, place % CORES
    held = 1 - core if sibling else core
    copies = []
    for k in range(chips):
        start = (lax.rem(chip + k, chips) * CORES + held) * share
        copies.append(
            pltpu.make_async_copy(
                weight_ref.at[:, pl.ds(pl.multiple_of(start, HD), share)],
                target.at[k],
                sems.at[k],
            )
        )
    return copies


def first_kernel(
    sources,
    conts,
    lists_ref,
    counts_ref,
    keys_ref,
    values_ref,
    queries_ref,
    cont_keys_ref,
    cont_values_ref,
    *refs,
):
    acc_refs, stat_refs, q_refs = refs[:conts], refs[conts : 2 * conts], refs[2 * conts : 3 * conts]
    flipped_ref, rows_ref, ck_ref, cv_ref, own_ref, sems = refs[3 * conts :]
    heads, _, length = q_refs[0].shape
    lanes = group_lanes(heads)
    copies = start_all(
        [
            pltpu.make_async_copy(cont_values_ref.at[:, :, lanes], cv_ref, sems.at[0]),
            pltpu.make_async_copy(queries_ref, rows_ref, sems.at[1]),
            pltpu.make_async_copy(cont_keys_ref.at[:, :, lanes], ck_ref, sems.at[2]),
        ]
    )
    own = lax.axis_index("ctx")
    both_ways(values_ref, flipped_ref)
    copies[0].wait()
    for cont in range(conts):
        own_ref[cont] = cv_ref[cont].T
    copies[1].wait()
    for cont in range(conts):
        for head in range(heads):
            q_refs[cont][head] = rows_ref[cont, :, head * HD : (head + 1) * HD].T
    copies[2].wait()
    together = TOGETHER // conts

    def some_heads(index, carry):
        work = [(index * together + j, cont) for j in range(together) for cont in range(conts)]
        made = []
        for head, cont in work:
            query = q_refs[cont][head]
            scores = jnp.dot(ck_ref[cont], query, preferred_element_type=jnp.float32)
            key = lax.broadcasted_iota(jnp.int32, scores.shape, 0)
            row = lax.broadcasted_iota(jnp.int32, scores.shape, 1)
            scores = jnp.where(key <= row, scores, VERY_LOW)
            blocks, count = used_tiles(
                lists_ref, counts_ref, own, sources, head * conts + cont
            )
            tiles = [(scores, True)] + shard_scores(blocks, count, query, keys_ref)
            values = jnp.concatenate([own_ref[cont], shard_values(blocks, flipped_ref)], axis=1)
            made.append((tiles, values))
        after = []
        for tiles, values in made:
            stat, rounded = weigh(
                jnp.full((1, length), VERY_LOW, jnp.float32),
                jnp.zeros((1, length), jnp.float32),
                tiles,
            )
            after.append((stat, jnp.dot(values, rounded, preferred_element_type=jnp.float32)))
        for (head, cont), (stat, acc) in zip(work, after):
            put_stat(stat_refs[cont], head, stat)
            acc_refs[cont][head] = acc
        return carry

    lax.fori_loop(0, heads // together, some_heads, 0)


def arrivals(step, sources):
    spot = lax.axis_index("ctx")
    core = lax.axis_index("tp") % CORES
    if sources == 4:
        if step == 1:
            mine = jnp.bitwise_xor(spot, 1 + core)
            return ((mine, True), (jnp.bitwise_xor(mine, 3), True))
        far = jnp.bitwise_xor(spot, 3)
        return ((far, core == 1), (far, core == 0))
    mine = jnp.where(core == 0, spot - step, spot + step)
    theirs = jnp.where(core == 0, spot + step, spot - step)
    return tuple((s, (s >= 0) & (s < sources)) for s in (mine, theirs))


def steps_of(sources):
    return 2 if sources == 4 else sources - 1


def terms_of(step, sources):
    parts = [(which, *part) for which, part in enumerate(arrivals(step, sources))]
    return [parts] if sources == 4 and step == 2 else [[part] for part in parts]


def if_there(valid, count, body):
    def work():
        lax.fori_loop(0, count, body, 0)

    if valid is True:
        work()
    else:
        pl.when(valid)(work)


def scores_kernel(step, term, sources, conts, lists_ref, counts_ref, *refs):
    candidates = terms_of(step, sources)[term]
    q_refs, refs = refs[:conts], refs[conts:]
    stat_in, refs = refs[:conts], refs[conts:]
    key_refs, refs = refs[: len(candidates)], refs[len(candidates) :]
    stat_refs, weight_refs = refs[:conts], refs[conts:]
    heads = q_refs[0].shape[0]
    together = TOGETHER // conts
    for (_, source, valid), keys_ref in zip(candidates, key_refs):

        def some_heads(index, carry):
            work = [
                (index * together + j, cont) for j in range(together) for cont in range(conts)
            ]
            made = []
            for head, cont in work:
                blocks, count = used_tiles(
                    lists_ref, counts_ref, source, sources, head * conts + cont
                )
                made.append(shard_scores(blocks, count, q_refs[cont][head], keys_ref))
            after = []
            for (head, cont), tiles in zip(work, made):
                stat = stat_in[cont][head]
                after.append(weigh(stat[0:1], stat[1:2], tiles))
            for (head, cont), (stat, rounded) in zip(work, after):
                put_stat(stat_refs[cont], head, stat)
                weight_refs[cont][head] = rounded
            return carry

        if_there(valid, heads // together, some_heads)
    if len(candidates) == 1 and valid is not True:

        @pl.when(jnp.logical_not(valid))
        def _():
            for before, after in zip(stat_in, stat_refs):
                after[...] = before[...]


def sums_kernel(step, sources, conts, lists_ref, counts_ref, *refs):
    terms = terms_of(step, sources)
    acc_in, refs = refs[:conts], refs[conts:]
    value_refs, refs = refs[: len(terms)], refs[len(terms) :]
    held = []
    for _ in terms:
        held.append((refs[:conts], refs[conts : 2 * conts]))
        refs = refs[2 * conts :]
    weight_ref, refs = refs[0], refs[1:]
    acc_refs, (give_ref, *flipped_refs, sems) = refs[:conts], refs[conts:]
    copies = start_all(weight_copies(weight_ref, give_ref, sems, True))
    heads = acc_refs[0].shape[0]
    together = TOGETHER // conts
    groups = [[0, 1]] if all(t[0][2] is True for t in terms) else [[t] for t in range(len(terms))]
    for values_ref, flipped_ref in zip(value_refs, flipped_refs):
        both_ways(values_ref, flipped_ref)
    for group in groups:
        before = acc_in if group[0] == 0 else acc_refs

        def some_heads(index, carry):
            work = [
                (index * together + j, cont) for j in range(together) for cont in range(conts)
            ]
            after = []
            for head, cont in work:
                acc = before[cont][head]
                for term in group:
                    _, source, _ = terms[term][0]
                    stat_refs, weight_refs = held[term]
                    blocks, _ = used_tiles(
                        lists_ref, counts_ref, source, sources, head * conts + cont
                    )
                    acc = acc * stat_refs[cont][head, 2:3, :] + jnp.dot(
                        shard_values(blocks, flipped_refs[term]),
                        weight_refs[cont][head],
                        preferred_element_type=jnp.float32,
                    )
                after.append(acc)
            for (head, cont), acc in zip(work, after):
                acc_refs[cont][head] = acc
            return carry

        valid = terms[group[0]][0][2]
        if_there(valid, heads // together, some_heads)
        if valid is not True and group[0] == 0:

            @pl.when(jnp.logical_not(valid))
            def _():
                for source_ref, target_ref in zip(acc_in, acc_refs):
                    target_ref[...] = source_ref[...]

    for copy in copies:
        copy.wait()


def last_kernel(step, sources, conts, cont, fetch, lists_ref, counts_ref, *refs):
    terms = terms_of(step, sources)
    acc_in, refs = refs[0], refs[1:]
    value_refs, refs = refs[:2], refs[2:]
    held = [refs[2 * t : 2 * t + 2] for t in range(len(terms))]
    give_weight_ref, *refs = refs[2 * len(terms) :]
    if fetch:
        weight_ref, attended_ref, give_ref, keep_weight_ref, acc_ref, flipped_ref, sems = refs
        copies = start_all(weight_copies(weight_ref, keep_weight_ref, sems, False))
    else:
        attended_ref, give_ref, acc_ref, flipped_ref = refs
    heads = acc_in.shape[0]
    together = min(heads, TOGETHER)
    before = acc_in
    for number, (candidates, (stat_ref, weights_ref)) in enumerate(zip(terms, held)):
        for which, source, valid in candidates:

            def absorb():
                both_ways(value_refs[which], flipped_ref)

                def some_heads(index, carry):
                    work = [index * together + j for j in range(together)]
                    after = []
                    for head in work:
                        blocks, _ = used_tiles(
                            lists_ref, counts_ref, source, sources, head * conts + cont
                        )
                        after.append(
                            before[head] * stat_ref[head, 2:3, :]
                            + jnp.dot(
                                shard_values(blocks, flipped_ref),
                                weights_ref[head],
                                preferred_element_type=jnp.float32,
                            )
                        )
                    for head, acc in zip(work, after):
                        acc_ref[head] = acc
                    return carry

                lax.fori_loop(0, heads // together, some_heads, 0)

            pl.when(valid)(absorb)
        if len(candidates) == 1 and number == 0:

            @pl.when(jnp.logical_not(valid))
            def _():
                acc_ref[...] = acc_in[...]

        before = acc_ref
    stat_ref = held[-1][0]
    for head in range(heads):
        attended_ref[:, head * HD : (head + 1) * HD] = (
            (acc_ref[head] / stat_ref[head, 1:2, :]).T.astype(jnp.bfloat16)
        )
    for k in range(give_weight_ref.shape[0]):
        give_ref[k] = jnp.dot(
            attended_ref[...], give_weight_ref[k], preferred_element_type=jnp.float32
        ).astype(give_ref.dtype)
    if fetch:
        for copy in copies:
            copy.wait()


def onward_kernel(attended_ref, weight_ref, got_ref, *onward_refs):
    for k, onward_ref in enumerate(onward_refs, 1):
        onward_ref[...] = (
            jnp.dot(attended_ref[...], weight_ref[k], preferred_element_type=jnp.float32)
            + got_ref[k].astype(jnp.float32)
        ).astype(jnp.bfloat16)


def near_kernel(cont, attended_ref, weight_ref, got_ref, residual_ref, near_ref, own_ref, sem):
    share = near_ref.shape[1]
    start = pl.multiple_of(lax.axis_index("tp") * share, HD)
    copy = pltpu.make_async_copy(
        residual_ref.at[cont, :, pl.ds(start, share)], own_ref, sem.at[0]
    )
    copy.start()
    near_ref[...] = jnp.dot(
        attended_ref[...], weight_ref[0], preferred_element_type=jnp.float32
    ) + got_ref[0].astype(jnp.float32)
    copy.wait()
    near_ref[...] += own_ref[...].astype(jnp.float32)


def sum_kernel(count, *refs):
    near_ref, fars, (total_ref, squares_ref) = refs[0], refs[1 : 1 + count], refs[1 + count :]
    total = near_ref[...]
    for far_ref in fars:
        total = total + far_ref[...].astype(jnp.float32)
    total_ref[...] = total
    sums = jnp.sum(total * total, axis=1, keepdims=True)
    squares_ref[...] = jnp.broadcast_to(sums, (sums.shape[0], HD)).T[:8]


def stream_kernel(conts, *refs):
    for cont in range(conts):
        refs[conts][cont] = refs[cont][...].astype(jnp.bfloat16)


def norm_kernel(conts, model_width, *refs):
    totals, squares = refs[:conts], refs[conts:-2]
    gain_ref, normed_ref = refs[-2:]
    gain = gain_ref[...].astype(jnp.float32)
    for cont in range(conts):
        row = functools.reduce(jnp.add, [ref[cont * 8 : cont * 8 + 1, :] for ref in squares])
        scale = lax.rsqrt(row / model_width + 1e-05)
        scale = jnp.broadcast_to(scale, (HD, scale.shape[1])).T[:, 0:1]
        total = totals[cont][...]
        normed_ref[cont] = (total * scale * gain).astype(jnp.bfloat16)


def shards(
    queries,
    cont_keys,
    cont_values,
    prompt_keys,
    prompt_values,
    block_lists,
    tile_counts,
    out_weight,
    residual,
    norm_gain,
    *,
    sources,
    members,
):
    conts, length, width = queries.shape
    heads = width // HD
    rows_dev = prompt_keys.shape[0]
    model_width = residual.shape[2]
    share = norm_gain.shape[0]
    chips = members // CORES
    place = lax.axis_index("tp")
    pairs = heads * conts
    params = pltpu.CompilerParams(vmem_limit_bytes=VMEM_LIMIT)
    vmem = pl.BlockSpec(memory_space=pltpu.VMEM)
    hbm = pl.BlockSpec(memory_space=pltpu.HBM)

    def array(shape, dtype):
        return jax.ShapeDtypeStruct(shape, dtype)

    def cost(flops=1024):
        return pl.CostEstimate(flops=flops, bytes_accessed=1024, transcendentals=0)

    def in_hbm(x):
        return pltpu.with_memory_space_constraint(x, pltpu.HBM)

    kept = array((rows_dev, HD), jnp.bfloat16)
    keys = pl.pallas_call(
        functools.partial(pack_keys_kernel, heads),
        out_shape=kept,
        in_specs=[hbm],
        out_specs=vmem,
        scratch_shapes=[pltpu.SemaphoreType.DMA((1,))],
        compiler_params=params,
        cost_estimate=cost(),
        name="pack_keys",
    )(in_hbm(prompt_keys))
    values = pl.pallas_call(
        functools.partial(pack_values_kernel, heads),
        out_shape=kept,
        in_specs=[hbm],
        out_specs=vmem,
        scratch_shapes=[
            pltpu.VMEM((rows_dev, HD), jnp.bfloat16),
            pltpu.SemaphoreType.DMA((1,)),
        ],
        compiler_params=params,
        cost_estimate=cost(),
        name="pack_values",
    )(in_hbm(prompt_values))

    def across(step):
        def target(z, t):
            if sources == 4 and step == 1:
                return z ^ (1 + t % CORES)
            if sources == 4:
                return z ^ 1 if t % CORES == 1 else None
            to = z + step if t % CORES == 0 else z - step
            return to if 0 <= to < sources else None

        return [
            (z * members + t, target(z, t) * members + t)
            for z in range(sources)
            for t in range(members)
            if target(z, t) is not None
        ]

    sibling = [(t, t ^ 1) for t in range(members)]
    steps = steps_of(sources)
    smem = pl.BlockSpec(memory_space=pltpu.SMEM)
    lists = block_lists.reshape(-1)
    counts = tile_counts.reshape(-1)
    flipped = pltpu.VMEM((2 * rows_dev, HD), jnp.bfloat16)
    weight_shape = array((chips, width, share), jnp.bfloat16)
    accs_shape = (array((heads, HD, length), jnp.float32),) * conts
    stats_shape = (array((heads, 8, length), jnp.float32),) * conts
    qs_shape = (array((heads, HD, length), jnp.bfloat16),) * conts
    rounded_shape = (array((heads, TILES * BLK, length), jnp.bfloat16),) * conts

    made = pl.pallas_call(
        functools.partial(first_kernel, sources, conts),
        out_shape=accs_shape + stats_shape + qs_shape,
        in_specs=[smem, smem, vmem, vmem] + [hbm] * 3,
        out_specs=(vmem,) * (3 * conts),
        scratch_shapes=[
            flipped,
            pltpu.VMEM(queries.shape, jnp.bfloat16),
            pltpu.VMEM((conts, length, HD), jnp.bfloat16),
            pltpu.VMEM((conts, length, HD), jnp.bfloat16),
            pltpu.VMEM((conts, HD, length), jnp.bfloat16),
            pltpu.SemaphoreType.DMA((3,)),
        ],
        compiler_params=params,
        cost_estimate=cost(),
        name="attend_own",
    )(lists, counts, keys, values, in_hbm(queries), in_hbm(cont_keys), in_hbm(cont_values))
    accs, stats, qs = (tuple(made[i * conts : (i + 1) * conts]) for i in range(3))

    def scores(step, term, stats, keys):
        made = pl.pallas_call(
            functools.partial(scores_kernel, step, term, sources, conts),
            out_shape=stats_shape + rounded_shape,
            in_specs=[smem, smem] + [vmem] * (2 * conts + len(keys)),
            out_specs=(vmem,) * (2 * conts),
            compiler_params=params,
            cost_estimate=cost(),
            name="scores",
        )(lists, counts, *qs, *stats, *keys)
        return tuple(made[:conts]), tuple(made[conts:])

    def weighted_sums(step, accs, values, held):
        *accs, give_weight = pl.pallas_call(
            functools.partial(sums_kernel, step, sources, conts),
            out_shape=accs_shape + (weight_shape,),
            in_specs=[smem, smem] + [vmem] * (conts + 2 + 4 * conts) + [hbm],
            out_specs=(vmem,) * (conts + 1),
            scratch_shapes=[flipped, flipped, pltpu.SemaphoreType.DMA((chips,))],
            compiler_params=params,
            cost_estimate=cost(),
            name="weighted_sums",
        )(
            lists,
            counts,
            *accs,
            *values,
            *[x for stats, rounded in held for x in (*stats, *rounded)],
            in_hbm(out_weight),
        )
        return tuple(accs), give_weight

    for step in range(1, steps + 1):
        sent = mine if sources == 4 and step == 2 else (keys, values)
        mine_keys, mine_values = [lax.ppermute(x, ("ctx", "tp"), across(step)) for x in sent]
        mine_keys, accs, stats = lax.optimization_barrier((mine_keys, accs, stats))
        their_keys = jnp.concatenate(
            [lax.ppermute(x, "tp", sibling) for x in jnp.split(mine_keys, 2)]
        )
        held = []
        if sources == 4 and step == 2:
            held.append(scores(step, 0, stats, (mine_keys, their_keys)))
        else:
            held.append(scores(step, 0, stats, (mine_keys,)))
            held.append(scores(step, 1, held[0][0], (their_keys,)))
        stats = held[-1][0]
        mine_keys, mine_values, held, stats = lax.optimization_barrier(
            (mine_keys, mine_values, held, stats)
        )
        their_values = lax.ppermute(mine_values, "tp", sibling)
        mine = (mine_keys, mine_values)
        if step < steps:
            accs, give_weight = weighted_sums(step, accs, (mine_values, their_values), held)

    def attend_last(cont):
        fetch = cont == 0
        terms = [x for stats, rounded in held for x in (stats[cont], rounded[cont])]
        return pl.pallas_call(
            functools.partial(last_kernel, steps, sources, conts, cont, fetch),
            out_shape=(
                array((length, width), jnp.bfloat16),
                array((chips, length, share), jnp.bfloat16),
            )
            + (weight_shape,) * fetch,
            in_specs=[smem, smem] + [vmem] * (4 + len(terms)) + [hbm] * fetch,
            out_specs=(vmem,) * (2 + fetch),
            scratch_shapes=[pltpu.VMEM((heads, HD, length), jnp.float32), flipped]
            + [pltpu.SemaphoreType.DMA((chips,))] * fetch,
            compiler_params=params,
            cost_estimate=cost(),
            name="attend_last",
        )(
            lists,
            counts,
            accs[cont],
            mine_values,
            their_values,
            *terms,
            give_weight,
            *([in_hbm(out_weight)] * fetch),
        )

    def onward(attended, got):
        parts = pl.pallas_call(
            onward_kernel,
            out_shape=(array((length, share), jnp.bfloat16),) * (chips - 1),
            in_specs=[vmem] * 3,
            out_specs=(vmem,) * (chips - 1),
            compiler_params=params,
            cost_estimate=cost(),
            name="project_onward",
        )(attended, keep_weight, got)
        far = []
        for k in range(1, chips):
            to_chip = [
                (t, (t // CORES + k) % chips * CORES + t % CORES) for t in range(members)
            ]
            far.append(lax.ppermute(parts[k - 1], "tp", to_chip))
        return parts, far

    def near(cont, attended, got):
        return pl.pallas_call(
            functools.partial(near_kernel, cont),
            out_shape=array((length, share), jnp.float32),
            in_specs=[vmem] * 3 + [hbm],
            out_specs=vmem,
            scratch_shapes=[
                pltpu.VMEM((length, share), jnp.bfloat16),
                pltpu.SemaphoreType.DMA((1,)),
            ],
            compiler_params=params,
            cost_estimate=cost(),
            name="project_near",
        )(attended, keep_weight, got, in_hbm(residual))

    attended, give, keep_weight = attend_last(0)
    nears, fars = [], []
    for cont in range(conts):
        got = lax.ppermute(give, "tp", sibling)
        here = attended
        if cont + 1 < conts:
            attended, give = attend_last(cont + 1)
            got, give = lax.optimization_barrier((got, give))
        _, far = onward(here, got)
        fars.append(far)
        nears.append(near(cont, here, got))

    totals, squares = [], []
    for cont in range(conts):
        total, square = pl.pallas_call(
            functools.partial(sum_kernel, chips - 1),
            out_shape=(array((length, share), jnp.float32), array((8, length), jnp.float32)),
            in_specs=[vmem] * chips,
            out_specs=(vmem,) * 2,
            compiler_params=params,
            cost_estimate=cost(),
            name="add_up",
        )(nears[cont], *fars[cont])
        totals.append(total)
        squares.append(square)
    squares = jnp.concatenate(squares, axis=0)
    squares = squares + lax.ppermute(squares, "tp", sibling)
    all_squares = [squares] + [
        lax.ppermute(
            squares,
            "tp",
            [(t, (t // CORES + k) % chips * CORES + t % CORES) for t in range(members)],
        )
        for k in range(1, chips)
    ]
    out = array((conts, length, share), jnp.bfloat16)
    stream = pl.pallas_call(
        functools.partial(stream_kernel, conts),
        out_shape=out,
        in_specs=[vmem] * conts,
        out_specs=vmem,
        compiler_params=params,
        cost_estimate=cost(),
        name="stream",
    )(*totals)
    normed = pl.pallas_call(
        functools.partial(norm_kernel, conts, model_width),
        out_shape=out,
        in_specs=[vmem] * (conts + chips + 1),
        out_specs=vmem,
        compiler_params=params,
        cost_estimate=cost(),
        name="norm",
    )(*totals, *all_squares, norm_gain.reshape(1, share))
    return stream, normed


def solution(mesh):
    placed = (
        P(("grp", "ctx"), None, "tp"),
        P(("grp", "ctx"), None, None),
        P(("grp", "ctx"), None, None),
        P(("grp", "ctx"), None),
        P(("grp", "ctx"), None),
        P("tp", ("grp", "ctx"), None, None),
        P("tp", ("grp", "ctx"), None),
        P("tp", None),
        P(("grp", "ctx"), None, None),
        P("tp"),
    )
    return jax.shard_map(
        functools.partial(
            shards, sources=mesh.shape["ctx"], members=mesh.shape["tp"]
        ),
        mesh=mesh,
        in_specs=placed,
        out_specs=(P(("grp", "ctx"), None, "tp"), P(("grp", "ctx"), None, "tp")),
        check_vma=False,
    )
```

```python
import functools
import math

import jax
import jax.numpy as jnp
from jax import lax
from jax.experimental import pallas as pl
from jax.experimental.pallas import tpu as pltpu
from jax.sharding import PartitionSpec as P

HEADS = 32
KVH = 2
HD = 128
BLK = 64
TILES = 8
CORES = 2
TOGETHER = 4

VERY_LOW = -1e30
TO_LOG2 = math.log2(math.e) / math.sqrt(HD)

VMEM_LIMIT = 28 * 1024 * 1024


def key_group(heads):
    return lax.axis_index("tp") * heads // (HEADS // KVH)


def group_lanes(heads):
    return pl.ds(pl.multiple_of(key_group(heads) * HD, HD), HD)


def pack_kernel(heads, transposed, rows_ref, packed_ref, buffer, sems):
    target = buffer if transposed else packed_ref
    copy = pltpu.make_async_copy(rows_ref.at[:, group_lanes(heads)], target, sems.at[0])
    copy.start()
    copy.wait()
    if transposed:
        for p in range(packed_ref.shape[0] // HD):
            rows = slice(p * HD, (p + 1) * HD)
            packed_ref[rows, :] = buffer[rows, :].T


def side_by_side(keys_ref):
    return jnp.concatenate(
        [keys_ref[p : p + HD, :] for p in range(0, keys_ref.shape[0], HD)], axis=1
    )


def with_ones(values):
    return jnp.concatenate([values, jnp.ones_like(values)], axis=1)


def block_bias(mask, width):
    block = lax.broadcasted_iota(jnp.int32, (1, width), 1) // BLK
    used = jnp.bitwise_and(jnp.right_shift(mask, block), 1)
    return jnp.where(used == 1, 0.0, VERY_LOW)


def weigh(top, scores, store):
    best = jnp.max(scores, axis=1, keepdims=True)
    new_top = jnp.maximum(top, best)
    for p in range(0, scores.shape[1], HD):
        store(p, jnp.exp2((scores[:, p : p + HD] - new_top) * TO_LOG2).astype(jnp.bfloat16))
    return new_top, jnp.exp2((top - new_top) * TO_LOG2)


def twice(x):
    return jnp.concatenate([x, x], axis=1)


def start_all(copies):
    for copy in copies:
        copy.start()
    return copies


def weight_copies(weight_ref, target, sems, sibling):
    chips, _, share = target.shape
    place = lax.axis_index("tp")
    chip, core = place // CORES, place % CORES
    held = 1 - core if sibling else core
    copies = []
    for k in range(chips):
        start = (lax.rem(chip + k, chips) * CORES + held) * share
        copies.append(
            pltpu.make_async_copy(
                weight_ref.at[:, pl.ds(pl.multiple_of(start, HD), share)],
                target.at[k],
                sems.at[k],
            )
        )
    return copies


def first_kernel(
    sources,
    conts,
    masks_ref,
    keys_ref,
    values_ref,
    queries_ref,
    cont_keys_ref,
    cont_values_ref,
    *refs,
):
    acc_refs, top_refs, q_refs = refs[:conts], refs[conts : 2 * conts], refs[2 * conts : 3 * conts]
    rows_ref, ck_ref, cv_ref, weights_ref, sems = refs[3 * conts :]
    length = cv_ref.shape[1]
    heads = q_refs[0].shape[0] // length
    shard = keys_ref.shape[0]
    lanes = group_lanes(heads)
    copies = start_all(
        [
            pltpu.make_async_copy(queries_ref, rows_ref, sems.at[0]),
            pltpu.make_async_copy(cont_keys_ref.at[:, :, lanes], ck_ref, sems.at[1]),
            pltpu.make_async_copy(cont_values_ref.at[:, :, lanes], cv_ref, sems.at[2]),
        ]
    )
    own = lax.axis_index("ctx")
    copies[0].wait()
    for cont in range(conts):
        for head in range(heads):
            q_refs[cont][head * length : (head + 1) * length, :] = rows_ref[
                cont, :, head * HD : (head + 1) * HD
            ]
    copies[1].wait()
    own_keys = [ck_ref[cont].T for cont in range(conts)]
    copies[2].wait()
    row = lax.broadcasted_iota(jnp.int32, (length, length), 0)
    column = lax.broadcasted_iota(jnp.int32, (length, length), 1)
    causal = jnp.where(column <= row, 0.0, VERY_LOW)

    def some_heads(index, carry):
        here = pl.ds(pl.multiple_of(index * TOGETHER * length, length), TOGETHER * length)
        keys = side_by_side(keys_ref)
        for cont in range(conts):
            query = q_refs[cont][here, :]
            scores = jnp.dot(query, keys, preferred_element_type=jnp.float32)
            owns = jnp.dot(query, own_keys[cont], preferred_element_type=jnp.float32)
            for j in range(TOGETHER):
                rows = slice(j * length, (j + 1) * length)
                mask = masks_ref[((index * TOGETHER + j) * conts + cont) * sources + own]
                both = jnp.concatenate(
                    [owns[rows] + causal, scores[rows] + block_bias(mask, shard)], axis=1
                )

                def store(p, weights, rows=rows, cont=cont):
                    weights_ref[cont, rows, p : p + HD] = weights

                top, _ = weigh(jnp.full((length, HD), VERY_LOW, jnp.float32), both, store)
                at = pl.ds(pl.multiple_of((index * TOGETHER + j) * length, length), length)
                top_refs[cont][at, :] = top
        for cont in range(conts):
            values = jnp.concatenate([cv_ref[cont], values_ref[...]], axis=0)
            acc_refs[cont][here, :] = jnp.dot(
                weights_ref[cont], with_ones(values), preferred_element_type=jnp.float32
            )
        return carry

    lax.fori_loop(0, heads // TOGETHER, some_heads, 0)


def arrivals(step, sources):
    spot = lax.axis_index("ctx")
    core = lax.axis_index("tp") % CORES
    if sources == 4:
        if step == 1:
            mine = jnp.bitwise_xor(spot, 1 + core)
            return ((mine, True), (jnp.bitwise_xor(mine, 3), True))
        far = jnp.bitwise_xor(spot, 3)
        return ((far, core == 1), (far, core == 0))
    mine = jnp.where(core == 0, spot - step, spot + step)
    theirs = jnp.where(core == 0, spot + step, spot - step)
    return tuple((s, (s >= 0) & (s < sources)) for s in (mine, theirs))


def steps_of(sources):
    return 2 if sources == 4 else sources - 1


def terms_of(step, sources):
    parts = [(which, *part) for which, part in enumerate(arrivals(step, sources))]
    return [parts] if sources == 4 and step == 2 else [[part] for part in parts]


def if_there(valid, work):
    if valid is True:
        work()
    else:
        pl.when(valid)(work)


def scores_kernel(step, term, sources, conts, length, masks_ref, *refs):
    candidates = terms_of(step, sources)[term]
    q_refs, refs = refs[:conts], refs[conts:]
    top_in, refs = refs[:conts], refs[conts:]
    key_refs, refs = refs[: len(candidates)], refs[len(candidates) :]
    top_refs, factor_refs, weight_refs = (refs[i * conts : (i + 1) * conts] for i in range(3))
    heads = q_refs[0].shape[0] // length
    for (_, source, valid), keys_ref in zip(candidates, key_refs):

        def some_heads(index, carry):
            here = pl.ds(pl.multiple_of(index * TOGETHER * length, length), TOGETHER * length)
            keys = side_by_side(keys_ref)
            for cont in range(conts):
                scores = jnp.dot(q_refs[cont][here, :], keys, preferred_element_type=jnp.float32)
                for j in range(TOGETHER):
                    place = index * TOGETHER + j
                    at = pl.ds(pl.multiple_of(place * length, length), length)
                    mask = masks_ref[(place * conts + cont) * sources + source]
                    masked = scores[j * length : (j + 1) * length] + block_bias(
                        mask, keys_ref.shape[0]
                    )

                    def store(p, weights, at=at, cont=cont):
                        weight_refs[cont][at, p : p + HD] = weights

                    top, factor = weigh(top_in[cont][at, :], masked, store)
                    top_refs[cont][at, :] = top
                    factor_refs[cont][at, :] = factor
            return carry

        def work():
            lax.fori_loop(0, heads // TOGETHER, some_heads, 0)

        if_there(valid, work)
    if len(candidates) == 1 and valid is not True:

        @pl.when(jnp.logical_not(valid))
        def _():
            for before, after in zip(top_in, top_refs):
                after[...] = before[...]


def add_term(before, factor_ref, weights_ref, values_ref, after):
    rows, width = after.shape
    values = with_ones(values_ref[...])
    piece = 512

    def some_rows(index, carry):
        at = pl.ds(pl.multiple_of(index * piece, piece), piece)
        after[at, :] = before[at, :] * twice(factor_ref[at, :]) + jnp.dot(
            weights_ref[at, :], values, preferred_element_type=jnp.float32
        )
        return carry

    lax.fori_loop(0, rows // piece, some_rows, 0)


def sums_kernel(step, sources, conts, *refs):
    terms = terms_of(step, sources)
    acc_in, refs = refs[:conts], refs[conts:]
    value_refs, refs = refs[: len(terms)], refs[len(terms) :]
    held = []
    for _ in terms:
        held.append((refs[:conts], refs[conts : 2 * conts]))
        refs = refs[2 * conts :]
    weight_ref, refs = refs[0], refs[1:]
    acc_refs, (give_ref, sems) = refs[:conts], refs[conts:]
    copies = start_all(weight_copies(weight_ref, give_ref, sems, True))
    for number, ([(_, _, valid)], (factor_refs, weight_refs)) in enumerate(zip(terms, held)):
        before = acc_refs if number else acc_in

        def work():
            for cont in range(conts):
                add_term(
                    before[cont],
                    factor_refs[cont],
                    weight_refs[cont],
                    value_refs[number],
                    acc_refs[cont],
                )

        if_there(valid, work)
        if valid is not True and number == 0:

            @pl.when(jnp.logical_not(valid))
            def _():
                for source_ref, target_ref in zip(acc_in, acc_refs):
                    target_ref[...] = source_ref[...]

    for copy in copies:
        copy.wait()


def last_kernel(step, sources, fetch, *refs):
    terms = terms_of(step, sources)
    acc_in, refs = refs[0], refs[1:]
    value_refs, refs = refs[:2], refs[2:]
    held = [refs[2 * t : 2 * t + 2] for t in range(len(terms))]
    give_weight_ref, *refs = refs[2 * len(terms) :]
    if fetch:
        weight_ref, attended_ref, give_ref, keep_weight_ref, acc_ref, sems = refs
        copies = start_all(weight_copies(weight_ref, keep_weight_ref, sems, False))
    else:
        attended_ref, give_ref, acc_ref = refs
    before = acc_in
    for number, (candidates, (factor_ref, weights_ref)) in enumerate(zip(terms, held)):
        for which, _, valid in candidates:

            @pl.when(valid)
            def _():
                add_term(before, factor_ref, weights_ref, value_refs[which], acc_ref)

        if len(candidates) == 1 and number == 0:

            @pl.when(jnp.logical_not(valid))
            def _():
                acc_ref[...] = acc_in[...]

        before = acc_ref
    length = attended_ref.shape[0]
    for head in range(attended_ref.shape[1] // HD):
        at = slice(head * length, (head + 1) * length)
        attended_ref[:, head * HD : (head + 1) * HD] = (
            acc_ref[at, :HD] / acc_ref[at, HD:]
        ).astype(jnp.bfloat16)
    for k in range(give_weight_ref.shape[0]):
        give_ref[k] = jnp.dot(
            attended_ref[...], give_weight_ref[k], preferred_element_type=jnp.float32
        ).astype(give_ref.dtype)
    if fetch:
        for copy in copies:
            copy.wait()


def onward_kernel(attended_ref, weight_ref, got_ref, *onward_refs):
    for k, onward_ref in enumerate(onward_refs, 1):
        onward_ref[...] = (
            jnp.dot(attended_ref[...], weight_ref[k], preferred_element_type=jnp.float32)
            + got_ref[k].astype(jnp.float32)
        ).astype(jnp.bfloat16)


def near_kernel(cont, attended_ref, weight_ref, got_ref, residual_ref, near_ref, own_ref, sem):
    share = near_ref.shape[1]
    start = pl.multiple_of(lax.axis_index("tp") * share, HD)
    copy = pltpu.make_async_copy(
        residual_ref.at[cont, :, pl.ds(start, share)], own_ref, sem.at[0]
    )
    copy.start()
    near_ref[...] = jnp.dot(
        attended_ref[...], weight_ref[0], preferred_element_type=jnp.float32
    ) + got_ref[0].astype(jnp.float32)
    copy.wait()
    near_ref[...] += own_ref[...].astype(jnp.float32)


def sum_kernel(count, *refs):
    near_ref, fars, (total_ref, squares_ref) = refs[0], refs[1 : 1 + count], refs[1 + count :]
    total = near_ref[...]
    for far_ref in fars:
        total = total + far_ref[...].astype(jnp.float32)
    total_ref[...] = total
    sums = jnp.sum(total * total, axis=1, keepdims=True)
    squares_ref[...] = jnp.broadcast_to(sums, (sums.shape[0], HD)).T[:8]


def stream_kernel(conts, *refs):
    for cont in range(conts):
        refs[conts][cont] = refs[cont][...].astype(jnp.bfloat16)


def norm_kernel(conts, model_width, *refs):
    totals, squares = refs[:conts], refs[conts:-2]
    gain_ref, normed_ref = refs[-2:]
    gain = gain_ref[...].astype(jnp.float32)
    for cont in range(conts):
        row = functools.reduce(jnp.add, [ref[cont * 8 : cont * 8 + 1, :] for ref in squares])
        scale = lax.rsqrt(row / model_width + 1e-05)
        scale = jnp.broadcast_to(scale, (HD, scale.shape[1])).T[:, 0:1]
        total = totals[cont][...]
        normed_ref[cont] = (total * scale * gain).astype(jnp.bfloat16)


def shards(
    queries,
    cont_keys,
    cont_values,
    prompt_keys,
    prompt_values,
    block_lists,
    tile_counts,
    out_weight,
    residual,
    norm_gain,
    *,
    sources,
    members,
):
    conts, length, width = queries.shape
    heads = width // HD
    rows_dev = prompt_keys.shape[0]
    model_width = residual.shape[2]
    share = norm_gain.shape[0]
    chips = members // CORES
    place = lax.axis_index("tp")
    pairs = heads * conts
    params = pltpu.CompilerParams(vmem_limit_bytes=VMEM_LIMIT)
    vmem = pl.BlockSpec(memory_space=pltpu.VMEM)
    hbm = pl.BlockSpec(memory_space=pltpu.HBM)

    def array(shape, dtype):
        return jax.ShapeDtypeStruct(shape, dtype)

    def cost(flops=1024):
        return pl.CostEstimate(flops=flops, bytes_accessed=1024, transcendentals=0)

    def in_hbm(x):
        return pltpu.with_memory_space_constraint(x, pltpu.HBM)

    def pack(x, transposed, name):
        shape = (rows_dev, HD)
        return pl.pallas_call(
            functools.partial(pack_kernel, heads, transposed),
            out_shape=array(shape, jnp.bfloat16),
            in_specs=[hbm],
            out_specs=vmem,
            scratch_shapes=[pltpu.VMEM(shape, jnp.bfloat16), pltpu.SemaphoreType.DMA((1,))],
            compiler_params=params,
            cost_estimate=cost(),
            name=name,
        )(in_hbm(x))

    keys = pack(prompt_keys, True, "pack_keys")
    values = pack(prompt_values, False, "pack_values")

    def across(step):
        def target(z, t):
            if sources == 4 and step == 1:
                return z ^ (1 + t % CORES)
            if sources == 4:
                return z ^ 1 if t % CORES == 1 else None
            to = z + step if t % CORES == 0 else z - step
            return to if 0 <= to < sources else None

        return [
            (z * members + t, target(z, t) * members + t)
            for z in range(sources)
            for t in range(members)
            if target(z, t) is not None
        ]

    sibling = [(t, t ^ 1) for t in range(members)]
    steps = steps_of(sources)
    smem = pl.BlockSpec(memory_space=pltpu.SMEM)
    live = jnp.arange(TILES) < tile_counts[..., None]
    masks = jnp.sum(jnp.where(live, jnp.left_shift(1, block_lists), 0), axis=-1).reshape(-1)
    rows = heads * length
    weight_shape = array((chips, width, share), jnp.bfloat16)
    accs_shape = (array((rows, 2 * HD), jnp.float32),) * conts
    tops_shape = (array((rows, HD), jnp.float32),) * conts
    qs_shape = (array((rows, HD), jnp.bfloat16),) * conts
    rounded_shape = (array((rows, rows_dev), jnp.bfloat16),) * conts

    made = pl.pallas_call(
        functools.partial(first_kernel, sources, conts),
        out_shape=accs_shape + tops_shape + qs_shape,
        in_specs=[smem, vmem, vmem] + [hbm] * 3,
        out_specs=(vmem,) * (3 * conts),
        scratch_shapes=[
            pltpu.VMEM(queries.shape, jnp.bfloat16),
            pltpu.VMEM((conts, length, HD), jnp.bfloat16),
            pltpu.VMEM((conts, length, HD), jnp.bfloat16),
            pltpu.VMEM((conts, TOGETHER * length, length + rows_dev), jnp.bfloat16),
            pltpu.SemaphoreType.DMA((3,)),
        ],
        compiler_params=params,
        cost_estimate=cost(),
        name="attend_own",
    )(masks, keys, values, in_hbm(queries), in_hbm(cont_keys), in_hbm(cont_values))
    accs, tops, qs = (tuple(made[i * conts : (i + 1) * conts]) for i in range(3))

    def scores(step, term, tops, keys):
        made = pl.pallas_call(
            functools.partial(scores_kernel, step, term, sources, conts, length),
            out_shape=tops_shape + tops_shape + rounded_shape,
            in_specs=[smem] + [vmem] * (2 * conts + len(keys)),
            out_specs=(vmem,) * (3 * conts),
            compiler_params=params,
            cost_estimate=cost(),
            name="scores",
        )(masks, *qs, *tops, *keys)
        tops, factors, rounded = (tuple(made[i * conts : (i + 1) * conts]) for i in range(3))
        return tops, (factors, rounded)

    def weighted_sums(step, accs, values, held):
        *accs, give_weight = pl.pallas_call(
            functools.partial(sums_kernel, step, sources, conts),
            out_shape=accs_shape + (weight_shape,),
            in_specs=[vmem] * (conts + 2 + 4 * conts) + [hbm],
            out_specs=(vmem,) * (conts + 1),
            scratch_shapes=[pltpu.SemaphoreType.DMA((chips,))],
            compiler_params=params,
            cost_estimate=cost(),
            name="weighted_sums",
        )(
            *accs,
            *values,
            *[x for factors, rounded in held for x in (*factors, *rounded)],
            in_hbm(out_weight),
        )
        return tuple(accs), give_weight

    for step in range(1, steps + 1):
        sent = mine if sources == 4 and step == 2 else (keys, values)
        mine_keys, mine_values = [lax.ppermute(x, ("ctx", "tp"), across(step)) for x in sent]
        mine_keys, accs, tops = lax.optimization_barrier((mine_keys, accs, tops))
        their_keys = jnp.concatenate(
            [lax.ppermute(x, "tp", sibling) for x in jnp.split(mine_keys, 2)]
        )
        held = []
        if sources == 4 and step == 2:
            tops, made = scores(step, 0, tops, (mine_keys, their_keys))
            held.append(made)
        else:
            for term, source_keys in enumerate((mine_keys, their_keys)):
                tops, made = scores(step, term, tops, (source_keys,))
                held.append(made)
        mine_keys, mine_values, held, tops = lax.optimization_barrier(
            (mine_keys, mine_values, held, tops)
        )
        their_values = lax.ppermute(mine_values, "tp", sibling)
        mine = (mine_keys, mine_values)
        if step < steps:
            accs, give_weight = weighted_sums(step, accs, (mine_values, their_values), held)

    def attend_last(cont):
        fetch = cont == 0
        terms = [x for factors, rounded in held for x in (factors[cont], rounded[cont])]
        return pl.pallas_call(
            functools.partial(last_kernel, steps, sources, fetch),
            out_shape=(
                array((length, width), jnp.bfloat16),
                array((chips, length, share), jnp.bfloat16),
            )
            + (weight_shape,) * fetch,
            in_specs=[vmem] * (4 + len(terms)) + [hbm] * fetch,
            out_specs=(vmem,) * (2 + fetch),
            scratch_shapes=[pltpu.VMEM((rows, 2 * HD), jnp.float32)]
            + [pltpu.SemaphoreType.DMA((chips,))] * fetch,
            compiler_params=params,
            cost_estimate=cost(),
            name="attend_last",
        )(
            accs[cont],
            mine_values,
            their_values,
            *terms,
            give_weight,
            *([in_hbm(out_weight)] * fetch),
        )

    def onward(attended, got):
        parts = pl.pallas_call(
            onward_kernel,
            out_shape=(array((length, share), jnp.bfloat16),) * (chips - 1),
            in_specs=[vmem] * 3,
            out_specs=(vmem,) * (chips - 1),
            compiler_params=params,
            cost_estimate=cost(),
            name="project_onward",
        )(attended, keep_weight, got)
        far = []
        for k in range(1, chips):
            to_chip = [
                (t, (t // CORES + k) % chips * CORES + t % CORES) for t in range(members)
            ]
            far.append(lax.ppermute(parts[k - 1], "tp", to_chip))
        return parts, far

    def near(cont, attended, got):
        return pl.pallas_call(
            functools.partial(near_kernel, cont),
            out_shape=array((length, share), jnp.float32),
            in_specs=[vmem] * 3 + [hbm],
            out_specs=vmem,
            scratch_shapes=[
                pltpu.VMEM((length, share), jnp.bfloat16),
                pltpu.SemaphoreType.DMA((1,)),
            ],
            compiler_params=params,
            cost_estimate=cost(),
            name="project_near",
        )(attended, keep_weight, got, in_hbm(residual))

    attended, give, keep_weight = attend_last(0)
    nears, fars = [], []
    for cont in range(conts):
        got = lax.ppermute(give, "tp", sibling)
        here = attended
        if cont + 1 < conts:
            attended, give = attend_last(cont + 1)
            got, give = lax.optimization_barrier((got, give))
        _, far = onward(here, got)
        fars.append(far)
        nears.append(near(cont, here, got))

    totals, squares = [], []
    for cont in range(conts):
        total, square = pl.pallas_call(
            functools.partial(sum_kernel, chips - 1),
            out_shape=(array((length, share), jnp.float32), array((8, length), jnp.float32)),
            in_specs=[vmem] * chips,
            out_specs=(vmem,) * 2,
            compiler_params=params,
            cost_estimate=cost(),
            name="add_up",
        )(nears[cont], *fars[cont])
        totals.append(total)
        squares.append(square)
    squares = jnp.concatenate(squares, axis=0)
    squares = squares + lax.ppermute(squares, "tp", sibling)
    all_squares = [squares] + [
        lax.ppermute(
            squares,
            "tp",
            [(t, (t // CORES + k) % chips * CORES + t % CORES) for t in range(members)],
        )
        for k in range(1, chips)
    ]
    out = array((conts, length, share), jnp.bfloat16)
    stream = pl.pallas_call(
        functools.partial(stream_kernel, conts),
        out_shape=out,
        in_specs=[vmem] * conts,
        out_specs=vmem,
        compiler_params=params,
        cost_estimate=cost(),
        name="stream",
    )(*totals)
    normed = pl.pallas_call(
        functools.partial(norm_kernel, conts, model_width),
        out_shape=out,
        in_specs=[vmem] * (conts + chips + 1),
        out_specs=vmem,
        compiler_params=params,
        cost_estimate=cost(),
        name="norm",
    )(*totals, *all_squares, norm_gain.reshape(1, share))
    return stream, normed


def solution(mesh):
    placed = (
        P(("grp", "ctx"), None, "tp"),
        P(("grp", "ctx"), None, None),
        P(("grp", "ctx"), None, None),
        P(("grp", "ctx"), None),
        P(("grp", "ctx"), None),
        P("tp", ("grp", "ctx"), None, None),
        P("tp", ("grp", "ctx"), None),
        P("tp", None),
        P(("grp", "ctx"), None, None),
        P("tp"),
    )
    return jax.shard_map(
        functools.partial(
            shards, sources=mesh.shape["ctx"], members=mesh.shape["tp"]
        ),
        mesh=mesh,
        in_specs=placed,
        out_specs=(P(("grp", "ctx"), None, "tp"), P(("grp", "ctx"), None, "tp")),
        check_vma=False,
    )
```

```python
import functools
import math

import jax
import jax.numpy as jnp
from jax import lax
from jax.experimental import pallas as pl
from jax.experimental.pallas import tpu as pltpu
from jax.sharding import PartitionSpec as P

HEADS = 32
KVH = 2
HD = 128
BLK = 64
TILES = 8
CORES = 2
TOGETHER = 8

VERY_LOW = -1e30
TO_LOG2 = math.log2(math.e) / math.sqrt(HD)

VMEM_LIMIT = 24 * 1024 * 1024


def key_group(heads):
    return lax.axis_index("tp") * heads // (HEADS // KVH)


def group_lanes(heads):
    return pl.ds(pl.multiple_of(key_group(heads) * HD, HD), HD)


def pack_kernel(heads, transposed, rows_ref, packed_ref, half_ref, buffer, sems):
    target = buffer if transposed else packed_ref
    copy = pltpu.make_async_copy(rows_ref.at[:, group_lanes(heads)], target, sems.at[0])
    copy.start()
    copy.wait()
    if transposed:
        for p in range(packed_ref.shape[0] // HD):
            rows = slice(p * HD, (p + 1) * HD)
            packed_ref[rows, :] = buffer[rows, :].T
    half = half_ref.shape[0]
    start = lax.axis_index("tp") % CORES * half
    half_ref[...] = packed_ref[pl.ds(pl.multiple_of(start, half), half), :]


def of_sibling(both_ref):
    return both_ref.at[1 - lax.axis_index("tp") % CORES]


def both_ways(values_ref, flipped_ref):
    rows = values_ref.shape[0]
    for p in range(rows // HD):
        pair = values_ref[p * HD : (p + 1) * HD, :]
        flipped_ref[p * HD : (p + 1) * HD, :] = pair
        flipped_ref[rows + p * HD : rows + (p + 1) * HD, :] = jnp.concatenate(
            [pair[:, BLK:], pair[:, :BLK]], axis=1
        )


def used_tiles(lists_ref, counts_ref, source, sources, place):
    at = place * sources + source
    return [lists_ref[at * TILES + t] for t in range(TILES)], counts_ref[at]


def shard_scores(blocks, count, query, keys_ref):
    keys = jnp.concatenate(
        [keys_ref[pl.ds(pl.multiple_of(b * BLK, BLK), BLK), :] for b in blocks], axis=0
    )
    scores = jnp.dot(keys, query, preferred_element_type=jnp.float32)
    return [(scores[t * BLK : (t + 1) * BLK], t < count) for t in range(TILES)]


def shard_values(blocks, flipped_ref):
    pairs = flipped_ref.shape[0] // 2 // HD
    lane = lax.broadcasted_iota(jnp.int32, (HD, HD), 1)
    halves = []
    for t, b in enumerate(blocks):
        spot = ((b + t) % 2 * pairs + b // 2) * HD
        halves.append(flipped_ref[pl.ds(pl.multiple_of(spot, HD), HD), :])
    return jnp.concatenate(
        [jnp.where(lane < BLK, a, b) for a, b in zip(halves[::2], halves[1::2])], axis=1
    )


def fold(op, tile):
    return functools.reduce(op, [tile[i : i + 8] for i in range(0, tile.shape[0], 8)])


def weigh(top, total, tiles):
    tops = [
        jnp.where(live, fold(jnp.maximum, tile), VERY_LOW) for tile, live in tiles
    ]
    best = jnp.max(functools.reduce(jnp.maximum, tops), axis=0, keepdims=True)
    new_top = jnp.maximum(top, best)
    weights = [
        jnp.exp2((tile - jnp.where(live, new_top, -VERY_LOW)) * TO_LOG2) for tile, live in tiles
    ]
    factor = jnp.exp2((top - new_top) * TO_LOG2)
    sums = functools.reduce(jnp.add, [fold(jnp.add, w) for w in weights])
    total = total * factor + jnp.sum(sums, axis=0, keepdims=True)
    rounded = jnp.concatenate([w.astype(jnp.bfloat16) for w in weights], axis=0)
    return (new_top, total, factor), rounded


def put_stat(stat_ref, head, stat):
    top, total, factor = stat
    stat_ref[head] = jnp.concatenate([top, total, factor] + [factor] * 5, axis=0)


def start_all(copies):
    for copy in copies:
        copy.start()
    return copies


def weight_copies(weight_ref, target, sems, sibling):
    chips, _, share = target.shape
    place = lax.axis_index("tp")
    chip, core = place // CORES, place % CORES
    held = 1 - core if sibling else core
    copies = []
    for k in range(chips):
        start = (lax.rem(chip + k, chips) * CORES + held) * share
        copies.append(
            pltpu.make_async_copy(
                weight_ref.at[:, pl.ds(pl.multiple_of(start, HD), share)],
                target.at[k],
                sems.at[k],
            )
        )
    return copies


def first_kernel(
    sources,
    conts,
    lists_ref,
    counts_ref,
    keys_ref,
    values_ref,
    queries_ref,
    cont_keys_ref,
    cont_values_ref,
    *refs,
):
    acc_refs, stat_refs, q_refs = refs[:conts], refs[conts : 2 * conts], refs[2 * conts : 3 * conts]
    flipped_ref, rows_ref, ck_ref, cv_ref, own_ref, sems = refs[3 * conts :]
    heads, _, length = q_refs[0].shape
    lanes = group_lanes(heads)
    copies = start_all(
        [
            pltpu.make_async_copy(cont_values_ref.at[:, :, lanes], cv_ref, sems.at[0]),
            pltpu.make_async_copy(queries_ref, rows_ref, sems.at[1]),
            pltpu.make_async_copy(cont_keys_ref.at[:, :, lanes], ck_ref, sems.at[2]),
        ]
    )
    own = lax.axis_index("ctx")
    both_ways(values_ref, flipped_ref)
    copies[0].wait()
    for cont in range(conts):
        own_ref[cont] = cv_ref[cont].T
    copies[1].wait()
    for cont in range(conts):
        for head in range(heads):
            q_refs[cont][head] = rows_ref[cont, :, head * HD : (head + 1) * HD].T
    copies[2].wait()
    together = TOGETHER // conts

    def some_heads(index, carry):
        work = [(index * together + j, cont) for j in range(together) for cont in range(conts)]
        made = []
        for head, cont in work:
            query = q_refs[cont][head]
            scores = jnp.dot(ck_ref[cont], query, preferred_element_type=jnp.float32)
            key = lax.broadcasted_iota(jnp.int32, scores.shape, 0)
            row = lax.broadcasted_iota(jnp.int32, scores.shape, 1)
            scores = jnp.where(key <= row, scores, VERY_LOW)
            blocks, count = used_tiles(
                lists_ref, counts_ref, own, sources, head * conts + cont
            )
            tiles = [(scores, True)] + shard_scores(blocks, count, query, keys_ref)
            values = jnp.concatenate([own_ref[cont], shard_values(blocks, flipped_ref)], axis=1)
            made.append((tiles, values))
        after = []
        for tiles, values in made:
            stat, rounded = weigh(
                jnp.full((1, length), VERY_LOW, jnp.float32),
                jnp.zeros((1, length), jnp.float32),
                tiles,
            )
            after.append((stat, jnp.dot(values, rounded, preferred_element_type=jnp.float32)))
        for (head, cont), (stat, acc) in zip(work, after):
            put_stat(stat_refs[cont], head, stat)
            acc_refs[cont][head] = acc
        return carry

    lax.fori_loop(0, heads // together, some_heads, 0)


def steps_of(sources):
    return 2 if sources == 4 else sources - 1


def far_step(step, sources):
    return sources == 4 and step == 2


def terms_of(step, sources):
    spot = lax.axis_index("ctx")
    core = lax.axis_index("tp") % CORES
    if far_step(step, sources):
        return [(jnp.bitwise_xor(spot, 3), True)]
    if sources == 4:
        mine = jnp.bitwise_xor(spot, 1 + core)
        return [(mine, True), (jnp.bitwise_xor(mine, 3), True)]
    mine = jnp.where(core == 0, spot - step, spot + step)
    theirs = jnp.where(core == 0, spot + step, spot - step)
    return [(s, (s >= 0) & (s < sources)) for s in (mine, theirs)]


def if_there(valid, work):
    if valid is True:
        work()
    else:
        pl.when(valid)(work)


def scores_kernel(step, term, sources, conts, lists_ref, counts_ref, *refs):
    source, valid = terms_of(step, sources)[term]
    q_refs, refs = refs[:conts], refs[conts:]
    stat_in, refs = refs[:conts], refs[conts:]
    keys_ref, *refs = refs
    if term == 1:
        keys_ref = of_sibling(keys_ref)
    stat_refs, weight_refs = refs[:conts], refs[conts:]
    heads = q_refs[0].shape[0]
    together = TOGETHER // conts

    def some_heads(index, carry):
        work = [(index * together + j, cont) for j in range(together) for cont in range(conts)]
        made = []
        for head, cont in work:
            blocks, count = used_tiles(
                lists_ref, counts_ref, source, sources, head * conts + cont
            )
            made.append(shard_scores(blocks, count, q_refs[cont][head], keys_ref))
        after = []
        for (head, cont), tiles in zip(work, made):
            stat = stat_in[cont][head]
            after.append(weigh(stat[0:1], stat[1:2], tiles))
        for (head, cont), (stat, rounded) in zip(work, after):
            put_stat(stat_refs[cont], head, stat)
            weight_refs[cont][head] = rounded
        return carry

    def work():
        lax.fori_loop(0, heads // together, some_heads, 0)

    if_there(valid, work)
    if valid is not True:

        @pl.when(jnp.logical_not(valid))
        def _():
            for before, after in zip(stat_in, stat_refs):
                after[...] = before[...]


def sums_kernel(step, sources, conts, lists_ref, counts_ref, *refs):
    terms = terms_of(step, sources)
    acc_in, refs = refs[:conts], refs[conts:]
    value_refs, refs = (refs[0], of_sibling(refs[1])), refs[2:]
    held = []
    for _ in terms:
        held.append((refs[:conts], refs[conts : 2 * conts]))
        refs = refs[2 * conts :]
    weight_ref, refs = refs[0], refs[1:]
    acc_refs, (give_ref, *flipped_refs, sems) = refs[:conts], refs[conts:]
    copies = start_all(weight_copies(weight_ref, give_ref, sems, True))
    heads = acc_refs[0].shape[0]
    together = TOGETHER // conts
    apart = any(valid is not True for _, valid in terms)
    groups = [[0], [1]] if apart else [[0, 1]]
    for values_ref, flipped_ref in zip(value_refs, flipped_refs):
        both_ways(values_ref, flipped_ref)
    for group in groups:
        before = acc_in if group[0] == 0 else acc_refs

        def some_heads(index, carry):
            work = [
                (index * together + j, cont) for j in range(together) for cont in range(conts)
            ]
            after = []
            for head, cont in work:
                acc = before[cont][head]
                for term in group:
                    stat_refs, weight_refs = held[term]
                    blocks, _ = used_tiles(
                        lists_ref, counts_ref, terms[term][0], sources, head * conts + cont
                    )
                    acc = acc * stat_refs[cont][head, 2:3, :] + jnp.dot(
                        shard_values(blocks, flipped_refs[term]),
                        weight_refs[cont][head],
                        preferred_element_type=jnp.float32,
                    )
                after.append(acc)
            for (head, cont), acc in zip(work, after):
                acc_refs[cont][head] = acc
            return carry

        def work():
            lax.fori_loop(0, heads // together, some_heads, 0)

        valid = terms[group[0]][1]
        if_there(valid, work)
        if valid is not True and group[0] == 0:

            @pl.when(jnp.logical_not(valid))
            def _():
                for source_ref, target_ref in zip(acc_in, acc_refs):
                    target_ref[...] = source_ref[...]

    for copy in copies:
        copy.wait()


def last_kernel(step, sources, conts, cont, fetch, lists_ref, counts_ref, *refs):
    terms = terms_of(step, sources)
    acc_in, refs = refs[0], refs[1:]
    value_refs, refs = refs[: len(terms)], refs[len(terms) :]
    if len(terms) == 2:
        value_refs = (value_refs[0], of_sibling(value_refs[1]))
    held = [refs[2 * t : 2 * t + 2] for t in range(len(terms))]
    give_weight_ref, *refs = refs[2 * len(terms) :]
    if fetch:
        weight_ref, attended_ref, give_ref, keep_weight_ref, acc_ref, flipped_ref, sems = refs
        copies = start_all(weight_copies(weight_ref, keep_weight_ref, sems, False))
    else:
        attended_ref, give_ref, acc_ref, flipped_ref = refs
    heads = acc_in.shape[0]
    together = min(heads, TOGETHER)
    before = acc_in
    for number, ((source, valid), (stat_ref, weights_ref)) in enumerate(zip(terms, held)):

        def absorb():
            both_ways(value_refs[number], flipped_ref)

            def some_heads(index, carry):
                work = [index * together + j for j in range(together)]
                after = []
                for head in work:
                    blocks, _ = used_tiles(
                        lists_ref, counts_ref, source, sources, head * conts + cont
                    )
                    after.append(
                        before[head] * stat_ref[head, 2:3, :]
                        + jnp.dot(
                            shard_values(blocks, flipped_ref),
                            weights_ref[head],
                            preferred_element_type=jnp.float32,
                        )
                    )
                for head, acc in zip(work, after):
                    acc_ref[head] = acc
                return carry

            lax.fori_loop(0, heads // together, some_heads, 0)

        if_there(valid, absorb)
        if valid is not True and number == 0:

            @pl.when(jnp.logical_not(valid))
            def _():
                acc_ref[...] = acc_in[...]

        before = acc_ref
    stat_ref = held[-1][0]
    for head in range(heads):
        attended_ref[:, head * HD : (head + 1) * HD] = (
            (acc_ref[head] / stat_ref[head, 1:2, :]).T.astype(jnp.bfloat16)
        )
    for k in range(give_weight_ref.shape[0]):
        give_ref[k] = jnp.dot(
            attended_ref[...], give_weight_ref[k], preferred_element_type=jnp.float32
        ).astype(give_ref.dtype)
    if fetch:
        for copy in copies:
            copy.wait()


def onward_kernel(attended_ref, weight_ref, got_ref, *onward_refs):
    for k, onward_ref in enumerate(onward_refs, 1):
        onward_ref[...] = (
            jnp.dot(attended_ref[...], weight_ref[k], preferred_element_type=jnp.float32)
            + got_ref[k].astype(jnp.float32)
        ).astype(jnp.bfloat16)


def near_kernel(cont, attended_ref, weight_ref, got_ref, residual_ref, near_ref, own_ref, sem):
    share = near_ref.shape[1]
    start = pl.multiple_of(lax.axis_index("tp") * share, HD)
    copy = pltpu.make_async_copy(
        residual_ref.at[cont, :, pl.ds(start, share)], own_ref, sem.at[0]
    )
    copy.start()
    near_ref[...] = jnp.dot(
        attended_ref[...], weight_ref[0], preferred_element_type=jnp.float32
    ) + got_ref[0].astype(jnp.float32)
    copy.wait()
    near_ref[...] += own_ref[...].astype(jnp.float32)


def sum_kernel(count, *refs):
    near_ref, fars, (total_ref, squares_ref) = refs[0], refs[1 : 1 + count], refs[1 + count :]
    total = near_ref[...]
    for far_ref in fars:
        total = total + far_ref[...].astype(jnp.float32)
    total_ref[...] = total
    sums = jnp.sum(total * total, axis=1, keepdims=True)
    squares_ref[...] = jnp.broadcast_to(sums, (sums.shape[0], HD)).T[:8]


def stream_kernel(conts, *refs):
    for cont in range(conts):
        refs[conts][cont] = refs[cont][...].astype(jnp.bfloat16)


def norm_kernel(conts, model_width, *refs):
    totals, squares = refs[:conts], refs[conts:-2]
    gain_ref, normed_ref = refs[-2:]
    gain = gain_ref[...].astype(jnp.float32)
    for cont in range(conts):
        row = functools.reduce(jnp.add, [ref[cont * 8 : cont * 8 + 1, :] for ref in squares])
        scale = lax.rsqrt(row / model_width + 1e-05)
        scale = jnp.broadcast_to(scale, (HD, scale.shape[1])).T[:, 0:1]
        total = totals[cont][...]
        normed_ref[cont] = (total * scale * gain).astype(jnp.bfloat16)


def shards(
    queries,
    cont_keys,
    cont_values,
    prompt_keys,
    prompt_values,
    block_lists,
    tile_counts,
    out_weight,
    residual,
    norm_gain,
    *,
    sources,
    members,
):
    conts, length, width = queries.shape
    heads = width // HD
    rows_dev = prompt_keys.shape[0]
    model_width = residual.shape[2]
    share = norm_gain.shape[0]
    chips = members // CORES
    place = lax.axis_index("tp")
    pairs = heads * conts
    params = pltpu.CompilerParams(vmem_limit_bytes=VMEM_LIMIT)
    vmem = pl.BlockSpec(memory_space=pltpu.VMEM)
    hbm = pl.BlockSpec(memory_space=pltpu.HBM)

    def array(shape, dtype):
        return jax.ShapeDtypeStruct(shape, dtype)

    def cost(flops=1024):
        return pl.CostEstimate(flops=flops, bytes_accessed=1024, transcendentals=0)

    def in_hbm(x):
        return pltpu.with_memory_space_constraint(x, pltpu.HBM)

    half_dev = rows_dev // CORES

    def pack(x, transposed, name):
        return pl.pallas_call(
            functools.partial(pack_kernel, heads, transposed),
            out_shape=(
                array((rows_dev, HD), jnp.bfloat16),
                array((half_dev, HD), jnp.bfloat16),
            ),
            in_specs=[hbm],
            out_specs=(vmem, vmem),
            scratch_shapes=[
                pltpu.VMEM((rows_dev, HD), jnp.bfloat16),
                pltpu.SemaphoreType.DMA((1,)),
            ],
            compiler_params=params,
            cost_estimate=cost(),
            name=name,
        )(in_hbm(x))

    keys, far_keys = pack(prompt_keys, False, "pack_keys")
    values, far_values = pack(prompt_values, True, "pack_values")

    def across(step):
        def target(z, t):
            if sources == 4 and step == 1:
                return z ^ (1 + t % CORES)
            if sources == 4:
                return z ^ 3
            to = z + step if t % CORES == 0 else z - step
            return to if 0 <= to < sources else None

        return [
            (z * members + t, target(z, t) * members + t)
            for z in range(sources)
            for t in range(members)
            if target(z, t) is not None
        ]

    sibling = [(t, t ^ 1) for t in range(members)]
    steps = steps_of(sources)
    smem = pl.BlockSpec(memory_space=pltpu.SMEM)
    lists = block_lists.reshape(-1)
    counts = tile_counts.reshape(-1)
    flipped = pltpu.VMEM((2 * rows_dev, HD), jnp.bfloat16)
    weight_shape = array((chips, width, share), jnp.bfloat16)
    accs_shape = (array((heads, HD, length), jnp.float32),) * conts
    stats_shape = (array((heads, 8, length), jnp.float32),) * conts
    qs_shape = (array((heads, HD, length), jnp.bfloat16),) * conts
    rounded_shape = (array((heads, TILES * BLK, length), jnp.bfloat16),) * conts

    made = pl.pallas_call(
        functools.partial(first_kernel, sources, conts),
        out_shape=accs_shape + stats_shape + qs_shape,
        in_specs=[smem, smem, vmem, vmem] + [hbm] * 3,
        out_specs=(vmem,) * (3 * conts),
        scratch_shapes=[
            flipped,
            pltpu.VMEM(queries.shape, jnp.bfloat16),
            pltpu.VMEM((conts, length, HD), jnp.bfloat16),
            pltpu.VMEM((conts, length, HD), jnp.bfloat16),
            pltpu.VMEM((conts, HD, length), jnp.bfloat16),
            pltpu.SemaphoreType.DMA((3,)),
        ],
        compiler_params=params,
        cost_estimate=cost(),
        name="attend_own",
    )(lists, counts, keys, values, in_hbm(queries), in_hbm(cont_keys), in_hbm(cont_values))
    accs, stats, qs = (tuple(made[i * conts : (i + 1) * conts]) for i in range(3))

    def scores(step, term, stats, keys):
        made = pl.pallas_call(
            functools.partial(scores_kernel, step, term, sources, conts),
            out_shape=stats_shape + rounded_shape,
            in_specs=[smem, smem] + [vmem] * (2 * conts + 1),
            out_specs=(vmem,) * (2 * conts),
            compiler_params=params,
            cost_estimate=cost(),
            name="scores",
        )(lists, counts, *qs, *stats, keys)
        return tuple(made[:conts]), tuple(made[conts:])

    def weighted_sums(step, accs, values, held):
        *accs, give_weight = pl.pallas_call(
            functools.partial(sums_kernel, step, sources, conts),
            out_shape=accs_shape + (weight_shape,),
            in_specs=[smem, smem] + [vmem] * (conts + 2 + 4 * conts) + [hbm],
            out_specs=(vmem,) * (conts + 1),
            scratch_shapes=[flipped, flipped, pltpu.SemaphoreType.DMA((chips,))],
            compiler_params=params,
            cost_estimate=cost(),
            name="weighted_sums",
        )(
            lists,
            counts,
            *accs,
            *values,
            *[x for stats, rounded in held for x in (*stats, *rounded)],
            in_hbm(out_weight),
        )
        return tuple(accs), give_weight

    pairs = [[t, t + 1] for t in range(0, members, CORES)]

    def both_cores(x):
        return lax.all_to_all(jnp.stack([x] * CORES), "tp", 0, 0, axis_index_groups=pairs)

    for step in range(1, steps + 1):
        far = far_step(step, sources)
        sent = (far_keys, far_values) if far else (keys, values)
        mine_keys, mine_values = [lax.ppermute(x, ("ctx", "tp"), across(step)) for x in sent]
        mine_keys, accs, stats = lax.optimization_barrier((mine_keys, accs, stats))
        both_keys = both_cores(mine_keys)
        if far:
            held = [scores(step, 0, stats, both_keys.reshape(rows_dev, HD))]
        else:
            held = [scores(step, 0, stats, mine_keys)]
            held.append(scores(step, 1, held[0][0], both_keys))
        stats = held[-1][0]
        mine_values, held, stats = lax.optimization_barrier((mine_values, held, stats))
        both_values = both_cores(mine_values)
        if far:
            last_values = (both_values.reshape(rows_dev, HD),)
        else:
            last_values = (mine_values, both_values)
        if step < steps:
            accs, give_weight = weighted_sums(step, accs, last_values, held)

    def attend_last(cont):
        fetch = cont == 0
        terms = [x for stats, rounded in held for x in (stats[cont], rounded[cont])]
        return pl.pallas_call(
            functools.partial(last_kernel, steps, sources, conts, cont, fetch),
            out_shape=(
                array((length, width), jnp.bfloat16),
                array((chips, length, share), jnp.bfloat16),
            )
            + (weight_shape,) * fetch,
            in_specs=[smem, smem]
            + [vmem] * (2 + len(last_values) + len(terms))
            + [hbm] * fetch,
            out_specs=(vmem,) * (2 + fetch),
            scratch_shapes=[pltpu.VMEM((heads, HD, length), jnp.float32), flipped]
            + [pltpu.SemaphoreType.DMA((chips,))] * fetch,
            compiler_params=params,
            cost_estimate=cost(),
            name="attend_last",
        )(
            lists,
            counts,
            accs[cont],
            *last_values,
            *terms,
            give_weight,
            *([in_hbm(out_weight)] * fetch),
        )

    def onward(attended, got):
        parts = pl.pallas_call(
            onward_kernel,
            out_shape=(array((length, share), jnp.bfloat16),) * (chips - 1),
            in_specs=[vmem] * 3,
            out_specs=(vmem,) * (chips - 1),
            compiler_params=params,
            cost_estimate=cost(),
            name="project_onward",
        )(attended, keep_weight, got)
        far = []
        for k in range(1, chips):
            to_chip = [
                (t, (t // CORES + k) % chips * CORES + t % CORES) for t in range(members)
            ]
            far.append(lax.ppermute(parts[k - 1], "tp", to_chip))
        return parts, far

    def near(cont, attended, got):
        return pl.pallas_call(
            functools.partial(near_kernel, cont),
            out_shape=array((length, share), jnp.float32),
            in_specs=[vmem] * 3 + [hbm],
            out_specs=vmem,
            scratch_shapes=[
                pltpu.VMEM((length, share), jnp.bfloat16),
                pltpu.SemaphoreType.DMA((1,)),
            ],
            compiler_params=params,
            cost_estimate=cost(),
            name="project_near",
        )(attended, keep_weight, got, in_hbm(residual))

    attended, give, keep_weight = attend_last(0)
    nears, fars = [], []
    for cont in range(conts):
        got = lax.ppermute(give, "tp", sibling)
        here = attended
        if cont + 1 < conts:
            attended, give = attend_last(cont + 1)
            got, give = lax.optimization_barrier((got, give))
        _, far = onward(here, got)
        fars.append(far)
        nears.append(near(cont, here, got))

    totals, squares = [], []
    for cont in range(conts):
        total, square = pl.pallas_call(
            functools.partial(sum_kernel, chips - 1),
            out_shape=(array((length, share), jnp.float32), array((8, length), jnp.float32)),
            in_specs=[vmem] * chips,
            out_specs=(vmem,) * 2,
            compiler_params=params,
            cost_estimate=cost(),
            name="add_up",
        )(nears[cont], *fars[cont])
        totals.append(total)
        squares.append(square)
    squares = jnp.concatenate(squares, axis=0)
    squares = squares + lax.ppermute(squares, "tp", sibling)
    all_squares = [squares] + [
        lax.ppermute(
            squares,
            "tp",
            [(t, (t // CORES + k) % chips * CORES + t % CORES) for t in range(members)],
        )
        for k in range(1, chips)
    ]
    out = array((conts, length, share), jnp.bfloat16)
    stream = pl.pallas_call(
        functools.partial(stream_kernel, conts),
        out_shape=out,
        in_specs=[vmem] * conts,
        out_specs=vmem,
        compiler_params=params,
        cost_estimate=cost(),
        name="stream",
    )(*totals)
    normed = pl.pallas_call(
        functools.partial(norm_kernel, conts, model_width),
        out_shape=out,
        in_specs=[vmem] * (conts + chips + 1),
        out_specs=vmem,
        compiler_params=params,
        cost_estimate=cost(),
        name="norm",
    )(*totals, *all_squares, norm_gain.reshape(1, share))
    return stream, normed


def solution(mesh):
    placed = (
        P(("grp", "ctx"), None, "tp"),
        P(("grp", "ctx"), None, None),
        P(("grp", "ctx"), None, None),
        P(("grp", "ctx"), None),
        P(("grp", "ctx"), None),
        P("tp", ("grp", "ctx"), None, None),
        P("tp", ("grp", "ctx"), None),
        P("tp", None),
        P(("grp", "ctx"), None, None),
        P("tp"),
    )
    return jax.shard_map(
        functools.partial(
            shards, sources=mesh.shape["ctx"], members=mesh.shape["tp"]
        ),
        mesh=mesh,
        in_specs=placed,
        out_specs=(P(("grp", "ctx"), None, "tp"), P(("grp", "ctx"), None, "tp")),
        check_vma=False,
    )
```

```python
import functools
import math

import jax
import jax.numpy as jnp
from jax import lax
from jax.experimental import pallas as pl
from jax.experimental.pallas import tpu as pltpu
from jax.sharding import PartitionSpec as P

HEADS = 32
KVH = 2
HD = 128
BLK = 64
TILES = 8
CORES = 2
TOGETHER = 8

VERY_LOW = -1e30
TO_LOG2 = math.log2(math.e) / math.sqrt(HD)

VMEM_LIMIT = 24 * 1024 * 1024


def key_group(heads):
    return lax.axis_index("tp") * heads // (HEADS // KVH)


def group_lanes(heads):
    return pl.ds(pl.multiple_of(key_group(heads) * HD, HD), HD)


def pack_kernel(heads, keys_ref, values_ref, packed_ref, values_buf, sems):
    rows = keys_ref.shape[0]
    lanes = group_lanes(heads)
    keys_copy = pltpu.make_async_copy(
        keys_ref.at[:, lanes], packed_ref.at[pl.ds(0, rows)], sems.at[0]
    )
    values_copy = pltpu.make_async_copy(values_ref.at[:, lanes], values_buf, sems.at[1])
    values_copy.start()
    keys_copy.start()
    values_copy.wait()
    for p in range(rows // HD):
        packed_ref[rows + p * HD : rows + (p + 1) * HD, :] = values_buf[
            p * HD : (p + 1) * HD, :
        ].T
    keys_copy.wait()


def split(refs):
    if len(refs) == 2:
        return refs
    rows = refs[0].shape[0] // 2
    return refs[0].at[pl.ds(0, rows)], refs[0].at[pl.ds(rows, rows)]


def both_ways(values_ref, flipped_ref):
    rows = values_ref.shape[0]
    for p in range(rows // HD):
        pair = values_ref[p * HD : (p + 1) * HD, :]
        flipped_ref[p * HD : (p + 1) * HD, :] = pair
        flipped_ref[rows + p * HD : rows + (p + 1) * HD, :] = jnp.concatenate(
            [pair[:, BLK:], pair[:, :BLK]], axis=1
        )


def shard_scores(lists_ref, counts_ref, q_refs, keys_ref, flipped_ref, place, head, cont):
    pairs = keys_ref.shape[0] // HD
    conts, sources, source = place
    at = (head * conts + cont) * sources + source
    count = counts_ref[at]
    blocks = [lists_ref[at * TILES + t] for t in range(TILES)]
    keys = jnp.concatenate(
        [keys_ref[pl.ds(pl.multiple_of(b * BLK, BLK), BLK), :] for b in blocks], axis=0
    )
    scores = jnp.dot(keys, q_refs[cont][head], preferred_element_type=jnp.float32)
    lane = lax.broadcasted_iota(jnp.int32, (HD, HD), 1)
    halves = []
    for t, b in enumerate(blocks):
        spot = ((b + t) % 2 * pairs + b // 2) * HD
        halves.append(flipped_ref[pl.ds(pl.multiple_of(spot, HD), HD), :])
    values = jnp.concatenate(
        [jnp.where(lane < BLK, a, b) for a, b in zip(halves[::2], halves[1::2])], axis=1
    )
    tiles = [
        (scores[t * BLK : (t + 1) * BLK], t < count) for t in range(TILES)
    ]
    return tiles, values


def fold(op, tile):
    return functools.reduce(op, [tile[i : i + 8] for i in range(0, tile.shape[0], 8)])


def absorb(state, tiles, values):
    top, total, acc = state
    tops = [
        jnp.where(live, fold(jnp.maximum, tile), VERY_LOW) for tile, live in tiles
    ]
    best = jnp.max(functools.reduce(jnp.maximum, tops), axis=0, keepdims=True)
    new_top = jnp.maximum(top, best)
    weights = [
        jnp.exp2((tile - jnp.where(live, new_top, -VERY_LOW)) * TO_LOG2) for tile, live in tiles
    ]
    factor = jnp.exp2((top - new_top) * TO_LOG2)
    sums = functools.reduce(jnp.add, [fold(jnp.add, w) for w in weights])
    total = total * factor + jnp.sum(sums, axis=0, keepdims=True)
    rounded = jnp.concatenate([w.astype(jnp.bfloat16) for w in weights], axis=0)
    acc = acc * factor + jnp.dot(values, rounded, preferred_element_type=jnp.float32)
    return new_top, total, acc


def load_state(acc_ref, stat_ref, index):
    both = stat_ref[index]
    return both[0:1], both[1:2], acc_ref[index]


def store_state(acc_ref, stat_ref, index, state):
    top, total, acc = state
    stat_ref[index] = jnp.concatenate([top, total] + [total] * 6, axis=0)
    acc_ref[index] = acc


def start_all(copies):
    for copy in copies:
        copy.start()
    return copies


def weight_copies(weight_ref, target, sems, sibling):
    chips, _, share = target.shape
    place = lax.axis_index("tp")
    chip, core = place // CORES, place % CORES
    held = 1 - core if sibling else core
    copies = []
    for k in range(chips):
        start = (lax.rem(chip + k, chips) * CORES + held) * share
        copies.append(
            pltpu.make_async_copy(
                weight_ref.at[:, pl.ds(pl.multiple_of(start, HD), share)],
                target.at[k],
                sems.at[k],
            )
        )
    return copies


def first_kernel(
    sources,
    conts,
    lists_ref,
    counts_ref,
    packed_ref,
    queries_ref,
    cont_keys_ref,
    cont_values_ref,
    *refs,
):
    states, refs = by_cont(refs[: 2 * conts]), refs[2 * conts :]
    q_refs, refs = refs[:conts], refs[conts:]
    flipped_ref, rows_ref, ck_ref, cv_ref, own_ref, sems = refs
    keys_ref, values_ref = split([packed_ref])
    heads, _, length = q_refs[0].shape
    lanes = group_lanes(heads)
    copies = start_all(
        [
            pltpu.make_async_copy(cont_values_ref.at[:, :, lanes], cv_ref, sems.at[0]),
            pltpu.make_async_copy(queries_ref, rows_ref, sems.at[1]),
            pltpu.make_async_copy(cont_keys_ref.at[:, :, lanes], ck_ref, sems.at[2]),
        ]
    )
    place = conts, sources, lax.axis_index("ctx")
    both_ways(values_ref, flipped_ref)
    copies[0].wait()
    for cont in range(conts):
        own_ref[cont] = cv_ref[cont].T
    copies[1].wait()
    for cont in range(conts):
        for head in range(heads):
            q_refs[cont][head] = rows_ref[cont, :, head * HD : (head + 1) * HD].T
    for copy in copies[2:]:
        copy.wait()
    together = TOGETHER // conts

    def some_heads(index, carry):
        work = [(index * together + j, cont) for j in range(together) for cont in range(conts)]
        made = []
        for head, cont in work:
            scores = jnp.dot(
                ck_ref[cont], q_refs[cont][head], preferred_element_type=jnp.float32
            )
            key = lax.broadcasted_iota(jnp.int32, scores.shape, 0)
            row = lax.broadcasted_iota(jnp.int32, scores.shape, 1)
            scores = jnp.where(key <= row, scores, VERY_LOW)
            tiles, values = shard_scores(
                lists_ref, counts_ref, q_refs, keys_ref, flipped_ref, place, head, cont
            )
            made.append(
                ([(scores, True)] + tiles, jnp.concatenate([own_ref[cont], values], axis=1))
            )
        after = []
        for got in made:
            start = (
                jnp.full((1, length), VERY_LOW, jnp.float32),
                jnp.zeros((1, length), jnp.float32),
                jnp.zeros((HD, length), jnp.float32),
            )
            after.append(absorb(start, *got))
        for (head, cont), state in zip(work, after):
            store_state(*states[cont], head, state)
        return carry

    lax.fori_loop(0, heads // together, some_heads, 0)


def arrivals(step, sources):
    spot = lax.axis_index("ctx")
    core = lax.axis_index("tp") % CORES
    if sources == 4:
        if step == 1:
            mine = jnp.bitwise_xor(spot, 1 + core)
            return ((mine, True), (jnp.bitwise_xor(mine, 3), True))
        far = jnp.bitwise_xor(spot, 3)
        return ((far, core == 1), (far, core == 0))
    mine = jnp.where(core == 0, spot - step, spot + step)
    theirs = jnp.where(core == 0, spot + step, spot - step)
    return tuple((s, (s >= 0) & (s < sources)) for s in (mine, theirs))


def steps_of(sources):
    return 2 if sources == 4 else sources - 1


def absorb_shard(place, lists_ref, counts_ref, q_refs, held, flipped_ref, before, after):
    keys_ref, values_ref = split(held)
    heads = next(iter(q_refs.values())).shape[0]
    together = min(heads, TOGETHER // len(q_refs))
    both_ways(values_ref, flipped_ref)

    def some_heads(index, carry):
        work = [(index * together + j, cont) for j in range(together) for cont in q_refs]
        states = [load_state(*before[cont], head) for head, cont in work]
        made = [
            shard_scores(lists_ref, counts_ref, q_refs, keys_ref, flipped_ref, place, head, cont)
            for head, cont in work
        ]
        states = [absorb(state, *got) for state, got in zip(states, made)]
        for (head, cont), state in zip(work, states):
            store_state(*after[cont], head, state)
        return carry

    lax.fori_loop(0, heads // together, some_heads, 0)


def hand_on(before, after):
    for source_ref, target_ref in zip(before, after):
        target_ref[...] = source_ref[...]


def by_cont(refs, chosen=None):
    chosen = range(len(refs) // 2) if chosen is None else chosen
    return {cont: refs[2 * i : 2 * i + 2] for i, cont in enumerate(chosen)}


def middle_kernel(
    step, part, sources, conts, chosen, pieces, with_weight, lists_ref, counts_ref, *refs
):
    count = len(chosen)
    q_refs, refs = dict(zip(chosen, refs)), refs[count:]
    held, refs = refs[:pieces], refs[pieces:]
    before, refs = refs[: 2 * count], refs[2 * count :]
    if with_weight:
        weight_ref, *refs = refs
    after, refs = refs[: 2 * count], refs[2 * count :]
    if with_weight:
        give_ref, flipped_ref, sems = refs
        copies = start_all(weight_copies(weight_ref, give_ref, sems, True))
    else:
        (flipped_ref,) = refs
    source, valid = arrivals(step, sources)[part]

    def absorb_part():
        shard = ((conts, sources, source), lists_ref, counts_ref, q_refs, held, flipped_ref)
        absorb_shard(*shard, by_cont(before, chosen), by_cont(after, chosen))

    if valid is True:
        absorb_part()
    else:
        pl.when(valid)(absorb_part)
        pl.when(jnp.logical_not(valid))(lambda: hand_on(before, after))
    if with_weight:
        for copy in copies:
            copy.wait()


def finish_and_give(acc_ref, stat_ref, weight_ref, attended_ref, give_ref):
    for head in range(attended_ref.shape[1] // HD):
        _, total, acc = load_state(acc_ref, stat_ref, head)
        attended_ref[:, head * HD : (head + 1) * HD] = (acc / total).T.astype(jnp.bfloat16)
    for k in range(weight_ref.shape[0]):
        give_ref[k] = jnp.dot(
            attended_ref[...], weight_ref[k], preferred_element_type=jnp.float32
        ).astype(give_ref.dtype)


def last_kernel(
    step,
    sources,
    conts,
    cont,
    lists_ref,
    counts_ref,
    q_ref,
    mine_ref,
    theirs_ref,
    acc_in,
    stat_in,
    give_weight_ref,
    *refs,
):
    if cont == 0:
        weight_ref, attended_ref, give_ref, keep_weight_ref, *refs, sems = refs
        copies = start_all(weight_copies(weight_ref, keep_weight_ref, sems, False))
    else:
        attended_ref, give_ref, *refs = refs
    acc_ref, stat_ref, flipped_ref = refs
    before, after = (acc_in, stat_in), (acc_ref, stat_ref)
    one_of_two = sources == 4
    for part, (source, valid) in enumerate(arrivals(step, sources)):

        def absorb_part():
            held = [(mine_ref, theirs_ref)[part]]
            shard = ((conts, sources, source), lists_ref, counts_ref, {cont: q_ref}, held)
            first = part == 0 or one_of_two
            absorb_shard(
                *shard, flipped_ref, {cont: before if first else after}, {cont: after}
            )

        pl.when(valid)(absorb_part)
        if part == 0 and not one_of_two:
            pl.when(jnp.logical_not(valid))(lambda: hand_on(before, after))
    finish_and_give(acc_ref, stat_ref, give_weight_ref, attended_ref, give_ref)
    if cont == 0:
        for copy in copies:
            copy.wait()


def onward_kernel(attended_ref, weight_ref, got_ref, *onward_refs):
    for k, onward_ref in enumerate(onward_refs, 1):
        onward_ref[...] = (
            jnp.dot(attended_ref[...], weight_ref[k], preferred_element_type=jnp.float32)
            + got_ref[k].astype(jnp.float32)
        ).astype(jnp.bfloat16)


def near_kernel(cont, attended_ref, weight_ref, got_ref, residual_ref, near_ref, own_ref, sem):
    share = near_ref.shape[1]
    start = pl.multiple_of(lax.axis_index("tp") * share, HD)
    copy = pltpu.make_async_copy(
        residual_ref.at[cont, :, pl.ds(start, share)], own_ref, sem.at[0]
    )
    copy.start()
    near_ref[...] = jnp.dot(
        attended_ref[...], weight_ref[0], preferred_element_type=jnp.float32
    ) + got_ref[0].astype(jnp.float32)
    copy.wait()
    near_ref[...] += own_ref[...].astype(jnp.float32)


def sum_kernel(count, *refs):
    near_ref, fars, (total_ref, squares_ref) = refs[0], refs[1 : 1 + count], refs[1 + count :]
    total = near_ref[...]
    for far_ref in fars:
        total = total + far_ref[...].astype(jnp.float32)
    total_ref[...] = total
    sums = jnp.sum(total * total, axis=1, keepdims=True)
    squares_ref[...] = jnp.broadcast_to(sums, (sums.shape[0], HD)).T[:8]


def norm_kernel(conts, members, model_width, *refs):
    totals, squares = refs[:conts], refs[conts : conts + members]
    gain_ref, stream_ref, normed_ref = refs[conts + members :]
    gain = gain_ref[...].astype(jnp.float32)
    for cont in range(conts):
        row = functools.reduce(jnp.add, [ref[cont * 8 : cont * 8 + 1, :] for ref in squares])
        scale = lax.rsqrt(row / model_width + 1e-05)
        scale = jnp.broadcast_to(scale, (HD, scale.shape[1])).T[:, 0:1]
        total = totals[cont][...]
        stream_ref[cont] = total.astype(jnp.bfloat16)
        normed_ref[cont] = (total * scale * gain).astype(jnp.bfloat16)


def shards(
    queries,
    cont_keys,
    cont_values,
    prompt_keys,
    prompt_values,
    block_lists,
    tile_counts,
    out_weight,
    residual,
    norm_gain,
    *,
    sources,
    members,
):
    conts, length, width = queries.shape
    heads = width // HD
    rows_dev = prompt_keys.shape[0]
    model_width = residual.shape[2]
    share = norm_gain.shape[0]
    chips = members // CORES
    place = lax.axis_index("tp")
    pairs = heads * conts
    params = pltpu.CompilerParams(vmem_limit_bytes=VMEM_LIMIT)
    vmem = pl.BlockSpec(memory_space=pltpu.VMEM)
    hbm = pl.BlockSpec(memory_space=pltpu.HBM)

    def array(shape, dtype):
        return jax.ShapeDtypeStruct(shape, dtype)

    def cost(flops=1024):
        return pl.CostEstimate(flops=flops, bytes_accessed=1024, transcendentals=0)

    def in_hbm(x):
        return pltpu.with_memory_space_constraint(x, pltpu.HBM)

    packed = pl.pallas_call(
        functools.partial(pack_kernel, heads),
        out_shape=array((2 * rows_dev, HD), jnp.bfloat16),
        in_specs=[hbm] * 2,
        out_specs=vmem,
        scratch_shapes=[
            pltpu.VMEM((rows_dev, HD), jnp.bfloat16),
            pltpu.SemaphoreType.DMA((2,)),
        ],
        compiler_params=params,
        cost_estimate=cost(),
        name="pack",
    )(in_hbm(prompt_keys), in_hbm(prompt_values))

    def across(step):
        def target(z, t):
            if sources == 4 and step == 1:
                return z ^ (1 + t % CORES)
            if sources == 4:
                return z ^ 1 if t % CORES == 1 else None
            to = z + step if t % CORES == 0 else z - step
            return to if 0 <= to < sources else None

        return [
            (z * members + t, target(z, t) * members + t)
            for z in range(sources)
            for t in range(members)
            if target(z, t) is not None
        ]

    sibling = [(t, t ^ 1) for t in range(members)]
    steps = steps_of(sources)
    smem = pl.BlockSpec(memory_space=pltpu.SMEM)
    lists = block_lists.reshape(-1)
    counts = tile_counts.reshape(-1)
    state_shape = (
        array((heads, HD, length), jnp.float32),
        array((heads, 8, length), jnp.float32),
    )
    flipped = pltpu.VMEM((2 * rows_dev, HD), jnp.bfloat16)
    weight_shape = array((chips, width, share), jnp.bfloat16)

    made = pl.pallas_call(
        functools.partial(first_kernel, sources, conts),
        out_shape=state_shape * conts + (array((heads, HD, length), jnp.bfloat16),) * conts,
        in_specs=[smem, smem, vmem] + [hbm] * 3,
        out_specs=(vmem,) * (3 * conts),
        scratch_shapes=[
            flipped,
            pltpu.VMEM(queries.shape, jnp.bfloat16),
            pltpu.VMEM((conts, length, HD), jnp.bfloat16),
            pltpu.VMEM((conts, length, HD), jnp.bfloat16),
            pltpu.VMEM((conts, HD, length), jnp.bfloat16),
            pltpu.SemaphoreType.DMA((3,)),
        ],
        compiler_params=params,
        cost_estimate=cost(),
        name="attend_own",
    )(lists, counts, packed, in_hbm(queries), in_hbm(cont_keys), in_hbm(cont_values))
    states = tuple(made[2 * c : 2 * c + 2] for c in range(conts))
    qs = made[2 * conts :]

    def attend_step(step, part, chosen, with_weight, states, held):
        flat = [x for cont in chosen for x in states[cont]]
        count = len(chosen)
        made = pl.pallas_call(
            functools.partial(
                middle_kernel, step, part, sources, conts, chosen, len(held), with_weight
            ),
            out_shape=state_shape * count + ((weight_shape,) if with_weight else ()),
            in_specs=[smem, smem] + [vmem] * (3 * count + len(held)) + [hbm] * with_weight,
            out_specs=(vmem,) * (2 * count + with_weight),
            scratch_shapes=[flipped] + [pltpu.SemaphoreType.DMA((chips,))] * with_weight,
            compiler_params=params,
            cost_estimate=cost(),
            name="attend_step",
        )(
            lists,
            counts,
            *[qs[cont] for cont in chosen],
            *held,
            *flat,
            *([in_hbm(out_weight)] * with_weight),
        )
        states = list(states)
        for i, cont in enumerate(chosen):
            states[cont] = tuple(made[2 * i : 2 * i + 2])
        return tuple(states), made[2 * count :]

    everyone = tuple(range(conts))
    mine, theirs = packed, None
    for step in range(1, steps + 1):
        sent = mine if sources == 4 and step == 2 else packed
        mine = lax.ppermute(sent, ("ctx", "tp"), across(step))
        mine, states = lax.optimization_barrier((mine, states))
        rest = theirs
        if step < steps:
            theirs = [lax.ppermute(x, "tp", sibling) for x in jnp.split(mine, 2)]
            states, (give_weight,) = attend_step(step, 0, everyone, True, states, [mine])
            states, _ = attend_step(step, 1, everyone[:1], False, states, theirs)
        else:
            theirs = [lax.ppermute(mine, "tp", sibling)]
        if step > 1:
            states, _ = attend_step(step - 1, 1, everyone[1:], False, states, rest)
            theirs, states = lax.optimization_barrier((theirs, states))

    def attend_last(cont, state):
        fetch = cont == 0
        return pl.pallas_call(
            functools.partial(last_kernel, steps, sources, conts, cont),
            out_shape=(
                array((length, width), jnp.bfloat16),
                array((chips, length, share), jnp.bfloat16),
            )
            + (weight_shape,) * fetch,
            in_specs=[smem, smem] + [vmem] * 6 + [hbm] * fetch,
            out_specs=(vmem,) * (2 + fetch),
            scratch_shapes=[pltpu.VMEM(a.shape, a.dtype) for a in state_shape]
            + [flipped]
            + [pltpu.SemaphoreType.DMA((chips,))] * fetch,
            compiler_params=params,
            cost_estimate=cost(),
            name="attend_last",
        )(
            lists,
            counts,
            qs[cont],
            mine,
            *theirs,
            *state,
            give_weight,
            *([in_hbm(out_weight)] * fetch),
        )

    def onward(attended, got):
        parts = pl.pallas_call(
            onward_kernel,
            out_shape=(array((length, share), jnp.bfloat16),) * (chips - 1),
            in_specs=[vmem] * 3,
            out_specs=(vmem,) * (chips - 1),
            compiler_params=params,
            cost_estimate=cost(),
            name="project_onward",
        )(attended, keep_weight, got)
        far = []
        for k in range(1, chips):
            to_chip = [
                (t, (t // CORES + k) % chips * CORES + t % CORES) for t in range(members)
            ]
            far.append(lax.ppermute(parts[k - 1], "tp", to_chip))
        return parts, far

    def near(cont, attended, got):
        return pl.pallas_call(
            functools.partial(near_kernel, cont),
            out_shape=array((length, share), jnp.float32),
            in_specs=[vmem] * 3 + [hbm],
            out_specs=vmem,
            scratch_shapes=[
                pltpu.VMEM((length, share), jnp.bfloat16),
                pltpu.SemaphoreType.DMA((1,)),
            ],
            compiler_params=params,
            cost_estimate=cost(),
            name="project_near",
        )(attended, keep_weight, got, in_hbm(residual))

    attended, give, keep_weight = attend_last(0, states[0])
    nears, fars = [], []
    for cont in range(conts):
        got = lax.ppermute(give, "tp", sibling)
        here = attended
        if cont + 1 < conts:
            attended, give = attend_last(cont + 1, states[cont + 1])
            got, give = lax.optimization_barrier((got, give))
        _, far = onward(here, got)
        fars.append(far)
        nears.append(near(cont, here, got))

    totals, squares = [], []
    for cont in range(conts):
        total, square = pl.pallas_call(
            functools.partial(sum_kernel, chips - 1),
            out_shape=(array((length, share), jnp.float32), array((8, length), jnp.float32)),
            in_specs=[vmem] * chips,
            out_specs=(vmem,) * 2,
            compiler_params=params,
            cost_estimate=cost(),
            name="add_up",
        )(nears[cont], *fars[cont])
        totals.append(total)
        squares.append(square)
    squares = jnp.concatenate(squares, axis=0)
    all_squares = [squares] + [
        lax.ppermute(squares, "tp", [(t, (t + k) % members) for t in range(members)])
        for k in range(1, members)
    ]
    out = array((conts, length, share), jnp.bfloat16)
    return pl.pallas_call(
        functools.partial(norm_kernel, conts, members, model_width),
        out_shape=(out, out),
        in_specs=[vmem] * (conts + members + 1),
        out_specs=(vmem, vmem),
        compiler_params=params,
        cost_estimate=cost(),
        name="norm",
    )(*totals, *all_squares, norm_gain.reshape(1, share))


def solution(mesh):
    placed = (
        P(("grp", "ctx"), None, "tp"),
        P(("grp", "ctx"), None, None),
        P(("grp", "ctx"), None, None),
        P(("grp", "ctx"), None),
        P(("grp", "ctx"), None),
        P("tp", ("grp", "ctx"), None, None),
        P("tp", ("grp", "ctx"), None),
        P("tp", None),
        P(("grp", "ctx"), None, None),
        P("tp"),
    )
    return jax.shard_map(
        functools.partial(
            shards, sources=mesh.shape["ctx"], members=mesh.shape["tp"]
        ),
        mesh=mesh,
        in_specs=placed,
        out_specs=(P(("grp", "ctx"), None, "tp"), P(("grp", "ctx"), None, "tp")),
        check_vma=False,
    )
```

```python
import functools
import math

import jax
import jax.numpy as jnp
from jax import lax
from jax.experimental import pallas as pl
from jax.experimental.pallas import tpu as pltpu
from jax.sharding import PartitionSpec as P

HEADS = 32
KVH = 2
HD = 128
BLK = 64
TILES = 8
CORES = 2
TOGETHER = 8

VERY_LOW = -1e30
TO_LOG2 = math.log2(math.e) / math.sqrt(HD)

VMEM_LIMIT = 24 * 1024 * 1024


def key_group(heads):
    return lax.axis_index("tp") * heads // (HEADS // KVH)


def group_lanes(heads):
    return pl.ds(pl.multiple_of(key_group(heads) * HD, HD), HD)


def pack_keys_kernel(heads, keys_ref, packed_ref, sems):
    copy = pltpu.make_async_copy(keys_ref.at[:, group_lanes(heads)], packed_ref, sems.at[0])
    copy.start()
    copy.wait()


def pack_values_kernel(heads, values_ref, packed_ref, values_buf, sems):
    copy = pltpu.make_async_copy(values_ref.at[:, group_lanes(heads)], values_buf, sems.at[0])
    copy.start()
    copy.wait()
    for p in range(packed_ref.shape[0] // HD):
        rows = slice(p * HD, (p + 1) * HD)
        packed_ref[rows, :] = values_buf[rows, :].T


def both_ways(values_refs, flipped_ref):
    total = flipped_ref.shape[0] // 2
    for part, values_ref in enumerate(values_refs):
        rows = values_ref.shape[0]
        for p in range(rows // HD):
            pair = values_ref[p * HD : (p + 1) * HD, :]
            at = part * rows + p * HD
            flipped_ref[at : at + HD, :] = pair
            flipped_ref[total + at : total + at + HD, :] = jnp.concatenate(
                [pair[:, BLK:], pair[:, :BLK]], axis=1
            )


def shard_scores(lists_ref, counts_ref, q_refs, keys_ref, flipped_ref, place, head, cont):
    pairs = keys_ref.shape[0] // HD
    conts, sources, source = place
    at = (head * conts + cont) * sources + source
    count = counts_ref[at]
    blocks = [lists_ref[at * TILES + t] for t in range(TILES)]
    keys = jnp.concatenate(
        [keys_ref[pl.ds(pl.multiple_of(b * BLK, BLK), BLK), :] for b in blocks], axis=0
    )
    scores = jnp.dot(keys, q_refs[cont][head], preferred_element_type=jnp.float32)
    lane = lax.broadcasted_iota(jnp.int32, (HD, HD), 1)
    halves = []
    for t, b in enumerate(blocks):
        spot = ((b + t) % 2 * pairs + b // 2) * HD
        halves.append(flipped_ref[pl.ds(pl.multiple_of(spot, HD), HD), :])
    values = jnp.concatenate(
        [jnp.where(lane < BLK, a, b) for a, b in zip(halves[::2], halves[1::2])], axis=1
    )
    tiles = [
        (scores[t * BLK : (t + 1) * BLK], t < count) for t in range(TILES)
    ]
    return tiles, values


def fold(op, tile):
    return functools.reduce(op, [tile[i : i + 8] for i in range(0, tile.shape[0], 8)])


def absorb(state, tiles, values):
    top, total, acc = state
    tops = [
        jnp.where(live, fold(jnp.maximum, tile), VERY_LOW) for tile, live in tiles
    ]
    best = jnp.max(functools.reduce(jnp.maximum, tops), axis=0, keepdims=True)
    new_top = jnp.maximum(top, best)
    weights = [
        jnp.exp2((tile - jnp.where(live, new_top, -VERY_LOW)) * TO_LOG2) for tile, live in tiles
    ]
    factor = jnp.exp2((top - new_top) * TO_LOG2)
    sums = functools.reduce(jnp.add, [fold(jnp.add, w) for w in weights])
    total = total * factor + jnp.sum(sums, axis=0, keepdims=True)
    rounded = jnp.concatenate([w.astype(jnp.bfloat16) for w in weights], axis=0)
    acc = acc * factor + jnp.dot(values, rounded, preferred_element_type=jnp.float32)
    return new_top, total, acc


def load_state(acc_ref, stat_ref, index):
    both = stat_ref[index]
    return both[0:1], both[1:2], acc_ref[index]


def store_state(acc_ref, stat_ref, index, state):
    top, total, acc = state
    stat_ref[index] = jnp.concatenate([top, total] + [total] * 6, axis=0)
    acc_ref[index] = acc


def start_all(copies):
    for copy in copies:
        copy.start()
    return copies


def weight_copies(weight_ref, target, sems, sibling):
    chips, _, share = target.shape
    place = lax.axis_index("tp")
    chip, core = place // CORES, place % CORES
    held = 1 - core if sibling else core
    copies = []
    for k in range(chips):
        start = (lax.rem(chip + k, chips) * CORES + held) * share
        copies.append(
            pltpu.make_async_copy(
                weight_ref.at[:, pl.ds(pl.multiple_of(start, HD), share)],
                target.at[k],
                sems.at[k],
            )
        )
    return copies


def first_kernel(
    sources,
    conts,
    lists_ref,
    counts_ref,
    keys_ref,
    values_ref,
    queries_ref,
    cont_keys_ref,
    cont_values_ref,
    *refs,
):
    states, refs = by_cont(refs[: 2 * conts]), refs[2 * conts :]
    q_refs, refs = refs[:conts], refs[conts:]
    flipped_ref, rows_ref, ck_ref, cv_ref, own_ref, sems = refs
    heads, _, length = q_refs[0].shape
    lanes = group_lanes(heads)
    copies = start_all(
        [
            pltpu.make_async_copy(cont_values_ref.at[:, :, lanes], cv_ref, sems.at[0]),
            pltpu.make_async_copy(queries_ref, rows_ref, sems.at[1]),
            pltpu.make_async_copy(cont_keys_ref.at[:, :, lanes], ck_ref, sems.at[2]),
        ]
    )
    place = conts, sources, lax.axis_index("ctx")
    both_ways([values_ref], flipped_ref)
    copies[0].wait()
    for cont in range(conts):
        own_ref[cont] = cv_ref[cont].T
    copies[1].wait()
    for cont in range(conts):
        for head in range(heads):
            q_refs[cont][head] = rows_ref[cont, :, head * HD : (head + 1) * HD].T
    for copy in copies[2:]:
        copy.wait()
    together = TOGETHER // conts

    def some_heads(index, carry):
        work = [(index * together + j, cont) for j in range(together) for cont in range(conts)]
        made = []
        for head, cont in work:
            scores = jnp.dot(
                ck_ref[cont], q_refs[cont][head], preferred_element_type=jnp.float32
            )
            key = lax.broadcasted_iota(jnp.int32, scores.shape, 0)
            row = lax.broadcasted_iota(jnp.int32, scores.shape, 1)
            scores = jnp.where(key <= row, scores, VERY_LOW)
            tiles, values = shard_scores(
                lists_ref, counts_ref, q_refs, keys_ref, flipped_ref, place, head, cont
            )
            made.append(
                ([(scores, True)] + tiles, jnp.concatenate([own_ref[cont], values], axis=1))
            )
        after = []
        for got in made:
            start = (
                jnp.full((1, length), VERY_LOW, jnp.float32),
                jnp.zeros((1, length), jnp.float32),
                jnp.zeros((HD, length), jnp.float32),
            )
            after.append(absorb(start, *got))
        for (head, cont), state in zip(work, after):
            store_state(*states[cont], head, state)
        return carry

    lax.fori_loop(0, heads // together, some_heads, 0)


def arrivals(step, sources):
    spot = lax.axis_index("ctx")
    core = lax.axis_index("tp") % CORES
    if sources == 4:
        if step == 1:
            mine = jnp.bitwise_xor(spot, 1 + core)
            return ((mine, True), (jnp.bitwise_xor(mine, 3), True))
        far = jnp.bitwise_xor(spot, 3)
        return ((far, core == 1), (far, core == 0))
    mine = jnp.where(core == 0, spot - step, spot + step)
    theirs = jnp.where(core == 0, spot + step, spot - step)
    return tuple((s, (s >= 0) & (s < sources)) for s in (mine, theirs))


def steps_of(sources):
    return 2 if sources == 4 else sources - 1


def absorb_shard(place, lists_ref, counts_ref, q_refs, held, flipped_ref, before, after):
    keys_ref, *values_refs = held
    heads = next(iter(q_refs.values())).shape[0]
    together = min(heads, TOGETHER // len(q_refs))
    both_ways(values_refs, flipped_ref)

    def some_heads(index, carry):
        work = [(index * together + j, cont) for j in range(together) for cont in q_refs]
        states = [load_state(*before[cont], head) for head, cont in work]
        made = [
            shard_scores(lists_ref, counts_ref, q_refs, keys_ref, flipped_ref, place, head, cont)
            for head, cont in work
        ]
        states = [absorb(state, *got) for state, got in zip(states, made)]
        for (head, cont), state in zip(work, states):
            store_state(*after[cont], head, state)
        return carry

    lax.fori_loop(0, heads // together, some_heads, 0)


def hand_on(before, after):
    for source_ref, target_ref in zip(before, after):
        target_ref[...] = source_ref[...]


def by_cont(refs, chosen=None):
    chosen = range(len(refs) // 2) if chosen is None else chosen
    return {cont: refs[2 * i : 2 * i + 2] for i, cont in enumerate(chosen)}


def middle_kernel(
    step, part, sources, conts, chosen, pieces, with_weight, lists_ref, counts_ref, *refs
):
    count = len(chosen)
    q_refs, refs = dict(zip(chosen, refs)), refs[count:]
    held, refs = refs[:pieces], refs[pieces:]
    before, refs = refs[: 2 * count], refs[2 * count :]
    if with_weight:
        weight_ref, *refs = refs
    after, refs = refs[: 2 * count], refs[2 * count :]
    if with_weight:
        give_ref, flipped_ref, sems = refs
        copies = start_all(weight_copies(weight_ref, give_ref, sems, True))
    else:
        (flipped_ref,) = refs
    source, valid = arrivals(step, sources)[part]

    def absorb_part():
        shard = ((conts, sources, source), lists_ref, counts_ref, q_refs, held, flipped_ref)
        absorb_shard(*shard, by_cont(before, chosen), by_cont(after, chosen))

    if valid is True:
        absorb_part()
    else:
        pl.when(valid)(absorb_part)
        pl.when(jnp.logical_not(valid))(lambda: hand_on(before, after))
    if with_weight:
        for copy in copies:
            copy.wait()


def finish_and_give(acc_ref, stat_ref, weight_ref, attended_ref, give_ref):
    for head in range(attended_ref.shape[1] // HD):
        _, total, acc = load_state(acc_ref, stat_ref, head)
        attended_ref[:, head * HD : (head + 1) * HD] = (acc / total).T.astype(jnp.bfloat16)
    for k in range(weight_ref.shape[0]):
        give_ref[k] = jnp.dot(
            attended_ref[...], weight_ref[k], preferred_element_type=jnp.float32
        ).astype(give_ref.dtype)


def last_kernel(
    step,
    sources,
    conts,
    cont,
    lists_ref,
    counts_ref,
    q_ref,
    mine_keys_ref,
    mine_values_ref,
    their_keys_ref,
    their_values_ref,
    acc_in,
    stat_in,
    give_weight_ref,
    *refs,
):
    if cont == 0:
        weight_ref, attended_ref, give_ref, keep_weight_ref, *refs, sems = refs
        copies = start_all(weight_copies(weight_ref, keep_weight_ref, sems, False))
    else:
        attended_ref, give_ref, *refs = refs
    acc_ref, stat_ref, flipped_ref = refs
    before, after = (acc_in, stat_in), (acc_ref, stat_ref)
    one_of_two = sources == 4
    for part, (source, valid) in enumerate(arrivals(step, sources)):

        def absorb_part():
            held = (
                (mine_keys_ref, mine_values_ref),
                (their_keys_ref, their_values_ref),
            )[part]
            shard = ((conts, sources, source), lists_ref, counts_ref, {cont: q_ref}, held)
            first = part == 0 or one_of_two
            absorb_shard(
                *shard, flipped_ref, {cont: before if first else after}, {cont: after}
            )

        pl.when(valid)(absorb_part)
        if part == 0 and not one_of_two:
            pl.when(jnp.logical_not(valid))(lambda: hand_on(before, after))
    finish_and_give(acc_ref, stat_ref, give_weight_ref, attended_ref, give_ref)
    if cont == 0:
        for copy in copies:
            copy.wait()


def onward_kernel(attended_ref, weight_ref, got_ref, *onward_refs):
    for k, onward_ref in enumerate(onward_refs, 1):
        onward_ref[...] = (
            jnp.dot(attended_ref[...], weight_ref[k], preferred_element_type=jnp.float32)
            + got_ref[k].astype(jnp.float32)
        ).astype(jnp.bfloat16)


def near_kernel(cont, attended_ref, weight_ref, got_ref, residual_ref, near_ref, own_ref, sem):
    share = near_ref.shape[1]
    start = pl.multiple_of(lax.axis_index("tp") * share, HD)
    copy = pltpu.make_async_copy(
        residual_ref.at[cont, :, pl.ds(start, share)], own_ref, sem.at[0]
    )
    copy.start()
    near_ref[...] = jnp.dot(
        attended_ref[...], weight_ref[0], preferred_element_type=jnp.float32
    ) + got_ref[0].astype(jnp.float32)
    copy.wait()
    near_ref[...] += own_ref[...].astype(jnp.float32)


def sum_kernel(count, *refs):
    near_ref, fars, (total_ref, squares_ref) = refs[0], refs[1 : 1 + count], refs[1 + count :]
    total = near_ref[...]
    for far_ref in fars:
        total = total + far_ref[...].astype(jnp.float32)
    total_ref[...] = total
    sums = jnp.sum(total * total, axis=1, keepdims=True)
    squares_ref[...] = jnp.broadcast_to(sums, (sums.shape[0], HD)).T[:8]


def stream_kernel(conts, *refs):
    for cont in range(conts):
        refs[conts][cont] = refs[cont][...].astype(jnp.bfloat16)


def norm_kernel(conts, model_width, *refs):
    totals, squares = refs[:conts], refs[conts:-2]
    gain_ref, normed_ref = refs[-2:]
    gain = gain_ref[...].astype(jnp.float32)
    for cont in range(conts):
        row = functools.reduce(jnp.add, [ref[cont * 8 : cont * 8 + 1, :] for ref in squares])
        scale = lax.rsqrt(row / model_width + 1e-05)
        scale = jnp.broadcast_to(scale, (HD, scale.shape[1])).T[:, 0:1]
        total = totals[cont][...]
        normed_ref[cont] = (total * scale * gain).astype(jnp.bfloat16)


def shards(
    queries,
    cont_keys,
    cont_values,
    prompt_keys,
    prompt_values,
    block_lists,
    tile_counts,
    out_weight,
    residual,
    norm_gain,
    *,
    sources,
    members,
):
    conts, length, width = queries.shape
    heads = width // HD
    rows_dev = prompt_keys.shape[0]
    model_width = residual.shape[2]
    share = norm_gain.shape[0]
    chips = members // CORES
    place = lax.axis_index("tp")
    pairs = heads * conts
    params = pltpu.CompilerParams(vmem_limit_bytes=VMEM_LIMIT)
    vmem = pl.BlockSpec(memory_space=pltpu.VMEM)
    hbm = pl.BlockSpec(memory_space=pltpu.HBM)

    def array(shape, dtype):
        return jax.ShapeDtypeStruct(shape, dtype)

    def cost(flops=1024):
        return pl.CostEstimate(flops=flops, bytes_accessed=1024, transcendentals=0)

    def in_hbm(x):
        return pltpu.with_memory_space_constraint(x, pltpu.HBM)

    kept = array((rows_dev, HD), jnp.bfloat16)
    keys = pl.pallas_call(
        functools.partial(pack_keys_kernel, heads),
        out_shape=kept,
        in_specs=[hbm],
        out_specs=vmem,
        scratch_shapes=[pltpu.SemaphoreType.DMA((1,))],
        compiler_params=params,
        cost_estimate=cost(),
        name="pack_keys",
    )(in_hbm(prompt_keys))
    values = pl.pallas_call(
        functools.partial(pack_values_kernel, heads),
        out_shape=kept,
        in_specs=[hbm],
        out_specs=vmem,
        scratch_shapes=[
            pltpu.VMEM((rows_dev, HD), jnp.bfloat16),
            pltpu.SemaphoreType.DMA((1,)),
        ],
        compiler_params=params,
        cost_estimate=cost(),
        name="pack_values",
    )(in_hbm(prompt_values))

    def across(step):
        def target(z, t):
            if sources == 4 and step == 1:
                return z ^ (1 + t % CORES)
            if sources == 4:
                return z ^ 1 if t % CORES == 1 else None
            to = z + step if t % CORES == 0 else z - step
            return to if 0 <= to < sources else None

        return [
            (z * members + t, target(z, t) * members + t)
            for z in range(sources)
            for t in range(members)
            if target(z, t) is not None
        ]

    sibling = [(t, t ^ 1) for t in range(members)]
    steps = steps_of(sources)
    smem = pl.BlockSpec(memory_space=pltpu.SMEM)
    lists = block_lists.reshape(-1)
    counts = tile_counts.reshape(-1)
    state_shape = (
        array((heads, HD, length), jnp.float32),
        array((heads, 8, length), jnp.float32),
    )
    flipped = pltpu.VMEM((2 * rows_dev, HD), jnp.bfloat16)
    weight_shape = array((chips, width, share), jnp.bfloat16)

    made = pl.pallas_call(
        functools.partial(first_kernel, sources, conts),
        out_shape=state_shape * conts + (array((heads, HD, length), jnp.bfloat16),) * conts,
        in_specs=[smem, smem, vmem, vmem] + [hbm] * 3,
        out_specs=(vmem,) * (3 * conts),
        scratch_shapes=[
            flipped,
            pltpu.VMEM(queries.shape, jnp.bfloat16),
            pltpu.VMEM((conts, length, HD), jnp.bfloat16),
            pltpu.VMEM((conts, length, HD), jnp.bfloat16),
            pltpu.VMEM((conts, HD, length), jnp.bfloat16),
            pltpu.SemaphoreType.DMA((3,)),
        ],
        compiler_params=params,
        cost_estimate=cost(),
        name="attend_own",
    )(lists, counts, keys, values, in_hbm(queries), in_hbm(cont_keys), in_hbm(cont_values))
    states = tuple(made[2 * c : 2 * c + 2] for c in range(conts))
    qs = made[2 * conts :]

    def attend_step(step, part, chosen, with_weight, states, held):
        flat = [x for cont in chosen for x in states[cont]]
        count = len(chosen)
        made = pl.pallas_call(
            functools.partial(
                middle_kernel, step, part, sources, conts, chosen, len(held), with_weight
            ),
            out_shape=state_shape * count + ((weight_shape,) if with_weight else ()),
            in_specs=[smem, smem] + [vmem] * (3 * count + len(held)) + [hbm] * with_weight,
            out_specs=(vmem,) * (2 * count + with_weight),
            scratch_shapes=[flipped] + [pltpu.SemaphoreType.DMA((chips,))] * with_weight,
            compiler_params=params,
            cost_estimate=cost(),
            name="attend_step",
        )(
            lists,
            counts,
            *[qs[cont] for cont in chosen],
            *held,
            *flat,
            *([in_hbm(out_weight)] * with_weight),
        )
        states = list(states)
        for i, cont in enumerate(chosen):
            states[cont] = tuple(made[2 * i : 2 * i + 2])
        return tuple(states), made[2 * count :]

    everyone = tuple(range(conts))
    mine, theirs = (keys, values), None
    for step in range(1, steps + 1):
        sent = mine if sources == 4 and step == 2 else (keys, values)
        mine_keys, mine_values = [lax.ppermute(x, ("ctx", "tp"), across(step)) for x in sent]
        mine_keys, states = lax.optimization_barrier((mine_keys, states))
        their_keys = lax.ppermute(mine_keys, "tp", sibling)
        mine_values, states = lax.optimization_barrier((mine_values, states))
        their_values = [
            lax.ppermute(x, "tp", sibling)
            for x in jnp.split(mine_values, 2 if step < steps else 1)
        ]
        rest = theirs
        mine, theirs = (mine_keys, mine_values), (their_keys, *their_values)
        if step < steps:
            states, (give_weight,) = attend_step(step, 0, everyone, True, states, mine)
            states, _ = attend_step(step, 1, everyone[:1], False, states, theirs)
        if step > 1:
            states, _ = attend_step(step - 1, 1, everyone[1:], False, states, rest)
            theirs, states = lax.optimization_barrier((theirs, states))

    def attend_last(cont, state):
        fetch = cont == 0
        return pl.pallas_call(
            functools.partial(last_kernel, steps, sources, conts, cont),
            out_shape=(
                array((length, width), jnp.bfloat16),
                array((chips, length, share), jnp.bfloat16),
            )
            + (weight_shape,) * fetch,
            in_specs=[smem, smem] + [vmem] * 8 + [hbm] * fetch,
            out_specs=(vmem,) * (2 + fetch),
            scratch_shapes=[pltpu.VMEM(a.shape, a.dtype) for a in state_shape]
            + [flipped]
            + [pltpu.SemaphoreType.DMA((chips,))] * fetch,
            compiler_params=params,
            cost_estimate=cost(),
            name="attend_last",
        )(
            lists,
            counts,
            qs[cont],
            *mine,
            *theirs,
            *state,
            give_weight,
            *([in_hbm(out_weight)] * fetch),
        )

    def onward(attended, got):
        parts = pl.pallas_call(
            onward_kernel,
            out_shape=(array((length, share), jnp.bfloat16),) * (chips - 1),
            in_specs=[vmem] * 3,
            out_specs=(vmem,) * (chips - 1),
            compiler_params=params,
            cost_estimate=cost(),
            name="project_onward",
        )(attended, keep_weight, got)
        far = []
        for k in range(1, chips):
            to_chip = [
                (t, (t // CORES + k) % chips * CORES + t % CORES) for t in range(members)
            ]
            far.append(lax.ppermute(parts[k - 1], "tp", to_chip))
        return parts, far

    def near(cont, attended, got):
        return pl.pallas_call(
            functools.partial(near_kernel, cont),
            out_shape=array((length, share), jnp.float32),
            in_specs=[vmem] * 3 + [hbm],
            out_specs=vmem,
            scratch_shapes=[
                pltpu.VMEM((length, share), jnp.bfloat16),
                pltpu.SemaphoreType.DMA((1,)),
            ],
            compiler_params=params,
            cost_estimate=cost(),
            name="project_near",
        )(attended, keep_weight, got, in_hbm(residual))

    attended, give, keep_weight = attend_last(0, states[0])
    nears, fars = [], []
    for cont in range(conts):
        got = lax.ppermute(give, "tp", sibling)
        here = attended
        if cont + 1 < conts:
            attended, give = attend_last(cont + 1, states[cont + 1])
            got, give = lax.optimization_barrier((got, give))
        _, far = onward(here, got)
        fars.append(far)
        nears.append(near(cont, here, got))

    totals, squares = [], []
    for cont in range(conts):
        total, square = pl.pallas_call(
            functools.partial(sum_kernel, chips - 1),
            out_shape=(array((length, share), jnp.float32), array((8, length), jnp.float32)),
            in_specs=[vmem] * chips,
            out_specs=(vmem,) * 2,
            compiler_params=params,
            cost_estimate=cost(),
            name="add_up",
        )(nears[cont], *fars[cont])
        totals.append(total)
        squares.append(square)
    squares = jnp.concatenate(squares, axis=0)
    squares = squares + lax.ppermute(squares, "tp", sibling)
    all_squares = [squares] + [
        lax.ppermute(
            squares,
            "tp",
            [(t, (t // CORES + k) % chips * CORES + t % CORES) for t in range(members)],
        )
        for k in range(1, chips)
    ]
    out = array((conts, length, share), jnp.bfloat16)
    stream = pl.pallas_call(
        functools.partial(stream_kernel, conts),
        out_shape=out,
        in_specs=[vmem] * conts,
        out_specs=vmem,
        compiler_params=params,
        cost_estimate=cost(),
        name="stream",
    )(*totals)
    normed = pl.pallas_call(
        functools.partial(norm_kernel, conts, model_width),
        out_shape=out,
        in_specs=[vmem] * (conts + chips + 1),
        out_specs=vmem,
        compiler_params=params,
        cost_estimate=cost(),
        name="norm",
    )(*totals, *all_squares, norm_gain.reshape(1, share))
    return stream, normed


def solution(mesh):
    placed = (
        P(("grp", "ctx"), None, "tp"),
        P(("grp", "ctx"), None, None),
        P(("grp", "ctx"), None, None),
        P(("grp", "ctx"), None),
        P(("grp", "ctx"), None),
        P("tp", ("grp", "ctx"), None, None),
        P("tp", ("grp", "ctx"), None),
        P("tp", None),
        P(("grp", "ctx"), None, None),
        P("tp"),
    )
    return jax.shard_map(
        functools.partial(
            shards, sources=mesh.shape["ctx"], members=mesh.shape["tp"]
        ),
        mesh=mesh,
        in_specs=placed,
        out_specs=(P(("grp", "ctx"), None, "tp"), P(("grp", "ctx"), None, "tp")),
        check_vma=False,
    )
```

```python
import functools
import math

import jax
import jax.numpy as jnp
from jax import lax
from jax.experimental import pallas as pl
from jax.experimental.pallas import tpu as pltpu
from jax.sharding import PartitionSpec as P

HEADS = 32
KVH = 2
HD = 128
BLK = 64
TILES = 8
CORES = 2
TOGETHER = 8

VERY_LOW = -1e30
TO_LOG2 = math.log2(math.e) / math.sqrt(HD)

VMEM_LIMIT = 24 * 1024 * 1024


def key_group(heads):
    return lax.axis_index("tp") * heads // (HEADS // KVH)


def group_lanes(heads):
    return pl.ds(pl.multiple_of(key_group(heads) * HD, HD), HD)


def pack_keys_kernel(heads, keys_ref, packed_ref, sems):
    copy = pltpu.make_async_copy(keys_ref.at[:, group_lanes(heads)], packed_ref, sems.at[0])
    copy.start()
    copy.wait()


def pack_values_kernel(heads, values_ref, packed_ref, values_buf, sems):
    copy = pltpu.make_async_copy(values_ref.at[:, group_lanes(heads)], values_buf, sems.at[0])
    copy.start()
    copy.wait()
    for p in range(packed_ref.shape[0] // HD):
        rows = slice(p * HD, (p + 1) * HD)
        packed_ref[rows, :] = values_buf[rows, :].T


def both_ways(values_refs, flipped_ref):
    total = flipped_ref.shape[0] // 2
    for part, values_ref in enumerate(values_refs):
        rows = values_ref.shape[0]
        for p in range(rows // HD):
            pair = values_ref[p * HD : (p + 1) * HD, :]
            at = part * rows + p * HD
            flipped_ref[at : at + HD, :] = pair
            flipped_ref[total + at : total + at + HD, :] = jnp.concatenate(
                [pair[:, BLK:], pair[:, :BLK]], axis=1
            )


def shard_scores(lists_ref, counts_ref, q_refs, keys_ref, flipped_ref, place, head, cont):
    pairs = keys_ref.shape[0] // HD
    conts, sources, source = place
    at = (head * conts + cont) * sources + source
    count = counts_ref[at]
    blocks = [lists_ref[at * TILES + t] for t in range(TILES)]
    keys = jnp.concatenate(
        [keys_ref[pl.ds(pl.multiple_of(b * BLK, BLK), BLK), :] for b in blocks], axis=0
    )
    scores = jnp.dot(keys, q_refs[cont][head], preferred_element_type=jnp.float32)
    lane = lax.broadcasted_iota(jnp.int32, (HD, HD), 1)
    halves = []
    for t, b in enumerate(blocks):
        spot = ((b + t) % 2 * pairs + b // 2) * HD
        halves.append(flipped_ref[pl.ds(pl.multiple_of(spot, HD), HD), :])
    values = jnp.concatenate(
        [jnp.where(lane < BLK, a, b) for a, b in zip(halves[::2], halves[1::2])], axis=1
    )
    tiles = [
        (scores[t * BLK : (t + 1) * BLK], t < count) for t in range(TILES)
    ]
    return tiles, values


def fold(op, tile):
    return functools.reduce(op, [tile[i : i + 8] for i in range(0, tile.shape[0], 8)])


def absorb(state, tiles, values):
    top, total, acc = state
    tops = [
        jnp.where(live, fold(jnp.maximum, tile), VERY_LOW) for tile, live in tiles
    ]
    best = jnp.max(functools.reduce(jnp.maximum, tops), axis=0, keepdims=True)
    new_top = jnp.maximum(top, best)
    weights = [
        jnp.exp2((tile - jnp.where(live, new_top, -VERY_LOW)) * TO_LOG2) for tile, live in tiles
    ]
    factor = jnp.exp2((top - new_top) * TO_LOG2)
    sums = functools.reduce(jnp.add, [fold(jnp.add, w) for w in weights])
    total = total * factor + jnp.sum(sums, axis=0, keepdims=True)
    rounded = jnp.concatenate([w.astype(jnp.bfloat16) for w in weights], axis=0)
    acc = acc * factor + jnp.dot(values, rounded, preferred_element_type=jnp.float32)
    return new_top, total, acc


def load_state(acc_ref, stat_ref, index):
    both = stat_ref[index]
    return both[0:1], both[1:2], acc_ref[index]


def store_state(acc_ref, stat_ref, index, state):
    top, total, acc = state
    stat_ref[index] = jnp.concatenate([top, total] + [total] * 6, axis=0)
    acc_ref[index] = acc


def start_all(copies):
    for copy in copies:
        copy.start()
    return copies


def weight_copies(weight_ref, target, sems, sibling):
    chips, _, share = target.shape
    place = lax.axis_index("tp")
    chip, core = place // CORES, place % CORES
    held = 1 - core if sibling else core
    copies = []
    for k in range(chips):
        start = (lax.rem(chip + k, chips) * CORES + held) * share
        copies.append(
            pltpu.make_async_copy(
                weight_ref.at[:, pl.ds(pl.multiple_of(start, HD), share)],
                target.at[k],
                sems.at[k],
            )
        )
    return copies


def first_kernel(
    sources,
    conts,
    lists_ref,
    counts_ref,
    keys_ref,
    values_ref,
    queries_ref,
    cont_keys_ref,
    cont_values_ref,
    *refs,
):
    states, refs = by_cont(refs[: 2 * conts]), refs[2 * conts :]
    q_refs, refs = refs[:conts], refs[conts:]
    flipped_ref, rows_ref, ck_ref, cv_ref, own_ref, sems = refs
    heads, _, length = q_refs[0].shape
    lanes = group_lanes(heads)
    copies = start_all(
        [
            pltpu.make_async_copy(cont_values_ref.at[:, :, lanes], cv_ref, sems.at[0]),
            pltpu.make_async_copy(queries_ref, rows_ref, sems.at[1]),
            pltpu.make_async_copy(cont_keys_ref.at[:, :, lanes], ck_ref, sems.at[2]),
        ]
    )
    place = conts, sources, lax.axis_index("ctx")
    both_ways([values_ref], flipped_ref)
    copies[0].wait()
    for cont in range(conts):
        own_ref[cont] = cv_ref[cont].T
    copies[1].wait()
    for cont in range(conts):
        for head in range(heads):
            q_refs[cont][head] = rows_ref[cont, :, head * HD : (head + 1) * HD].T
    for copy in copies[2:]:
        copy.wait()
    together = TOGETHER // conts

    def some_heads(index, carry):
        work = [(index * together + j, cont) for j in range(together) for cont in range(conts)]
        made = []
        for head, cont in work:
            scores = jnp.dot(
                ck_ref[cont], q_refs[cont][head], preferred_element_type=jnp.float32
            )
            key = lax.broadcasted_iota(jnp.int32, scores.shape, 0)
            row = lax.broadcasted_iota(jnp.int32, scores.shape, 1)
            scores = jnp.where(key <= row, scores, VERY_LOW)
            tiles, values = shard_scores(
                lists_ref, counts_ref, q_refs, keys_ref, flipped_ref, place, head, cont
            )
            made.append(
                ([(scores, True)] + tiles, jnp.concatenate([own_ref[cont], values], axis=1))
            )
        after = []
        for got in made:
            start = (
                jnp.full((1, length), VERY_LOW, jnp.float32),
                jnp.zeros((1, length), jnp.float32),
                jnp.zeros((HD, length), jnp.float32),
            )
            after.append(absorb(start, *got))
        for (head, cont), state in zip(work, after):
            store_state(*states[cont], head, state)
        return carry

    lax.fori_loop(0, heads // together, some_heads, 0)


def arrivals(step, sources):
    spot = lax.axis_index("ctx")
    core = lax.axis_index("tp") % CORES
    if sources == 4:
        if step == 1:
            mine = jnp.bitwise_xor(spot, 1 + core)
            return ((mine, True), (jnp.bitwise_xor(mine, 3), True))
        far = jnp.bitwise_xor(spot, 3)
        return ((far, core == 1), (far, core == 0))
    mine = jnp.where(core == 0, spot - step, spot + step)
    theirs = jnp.where(core == 0, spot + step, spot - step)
    return tuple((s, (s >= 0) & (s < sources)) for s in (mine, theirs))


def steps_of(sources):
    return 2 if sources == 4 else sources - 1


def absorb_shard(place, lists_ref, counts_ref, q_refs, held, flipped_ref, before, after):
    keys_ref, *values_refs = held
    heads = next(iter(q_refs.values())).shape[0]
    together = min(heads, TOGETHER // len(q_refs))
    both_ways(values_refs, flipped_ref)

    def some_heads(index, carry):
        work = [(index * together + j, cont) for j in range(together) for cont in q_refs]
        states = [load_state(*before[cont], head) for head, cont in work]
        made = [
            shard_scores(lists_ref, counts_ref, q_refs, keys_ref, flipped_ref, place, head, cont)
            for head, cont in work
        ]
        states = [absorb(state, *got) for state, got in zip(states, made)]
        for (head, cont), state in zip(work, states):
            store_state(*after[cont], head, state)
        return carry

    lax.fori_loop(0, heads // together, some_heads, 0)


def hand_on(before, after):
    for source_ref, target_ref in zip(before, after):
        target_ref[...] = source_ref[...]


def by_cont(refs, chosen=None):
    chosen = range(len(refs) // 2) if chosen is None else chosen
    return {cont: refs[2 * i : 2 * i + 2] for i, cont in enumerate(chosen)}


def middle_kernel(
    step, part, sources, conts, chosen, pieces, with_weight, lists_ref, counts_ref, *refs
):
    count = len(chosen)
    q_refs, refs = dict(zip(chosen, refs)), refs[count:]
    held, refs = refs[:pieces], refs[pieces:]
    before, refs = refs[: 2 * count], refs[2 * count :]
    if with_weight:
        weight_ref, *refs = refs
    after, refs = refs[: 2 * count], refs[2 * count :]
    if with_weight:
        give_ref, flipped_ref, sems = refs
        copies = start_all(weight_copies(weight_ref, give_ref, sems, True))
    else:
        (flipped_ref,) = refs
    source, valid = arrivals(step, sources)[part]

    def absorb_part():
        shard = ((conts, sources, source), lists_ref, counts_ref, q_refs, held, flipped_ref)
        absorb_shard(*shard, by_cont(before, chosen), by_cont(after, chosen))

    if valid is True:
        absorb_part()
    else:
        pl.when(valid)(absorb_part)
        pl.when(jnp.logical_not(valid))(lambda: hand_on(before, after))
    if with_weight:
        for copy in copies:
            copy.wait()


def finish_and_give(acc_ref, stat_ref, weight_ref, attended_ref, give_refs):
    for head in range(attended_ref.shape[1] // HD):
        _, total, acc = load_state(acc_ref, stat_ref, head)
        attended_ref[:, head * HD : (head + 1) * HD] = (acc / total).T.astype(jnp.bfloat16)
    rows = give_refs[0].shape[1]
    for k in range(weight_ref.shape[0]):
        made = jnp.dot(
            attended_ref[...], weight_ref[k], preferred_element_type=jnp.float32
        ).astype(jnp.bfloat16)
        for i, give_ref in enumerate(give_refs):
            give_ref[k] = made[i * rows : (i + 1) * rows]


def last_kernel(
    step,
    sources,
    conts,
    cont,
    pieces,
    lists_ref,
    counts_ref,
    q_ref,
    mine_keys_ref,
    mine_values_ref,
    their_keys_ref,
    their_values_ref,
    acc_in,
    stat_in,
    give_weight_ref,
    *refs,
):
    if cont == 0:
        weight_ref, *refs, sems = refs
    attended_ref, give_refs, refs = refs[0], refs[1 : 1 + pieces], refs[1 + pieces :]
    if cont == 0:
        keep_weight_ref, *refs = refs
        copies = start_all(weight_copies(weight_ref, keep_weight_ref, sems, False))
    acc_ref, stat_ref, flipped_ref = refs
    before, after = (acc_in, stat_in), (acc_ref, stat_ref)
    one_of_two = sources == 4
    for part, (source, valid) in enumerate(arrivals(step, sources)):

        def absorb_part():
            held = (
                (mine_keys_ref, mine_values_ref),
                (their_keys_ref, their_values_ref),
            )[part]
            shard = ((conts, sources, source), lists_ref, counts_ref, {cont: q_ref}, held)
            first = part == 0 or one_of_two
            absorb_shard(
                *shard, flipped_ref, {cont: before if first else after}, {cont: after}
            )

        pl.when(valid)(absorb_part)
        if part == 0 and not one_of_two:
            pl.when(jnp.logical_not(valid))(lambda: hand_on(before, after))
    finish_and_give(acc_ref, stat_ref, give_weight_ref, attended_ref, give_refs)
    if cont == 0:
        for copy in copies:
            copy.wait()


def from_sibling(got_refs, k):
    return jnp.concatenate([ref[k] for ref in got_refs], axis=0).astype(jnp.float32)


def onward_kernel(pieces, cuts, attended_ref, weight_ref, *refs):
    got_refs, onward_refs = refs[:pieces], refs[pieces:]
    for k in range(1, weight_ref.shape[0]):
        made = (
            jnp.dot(attended_ref[...], weight_ref[k], preferred_element_type=jnp.float32)
            + from_sibling(got_refs, k)
        ).astype(jnp.bfloat16)
        for start, end in zip(cuts, cuts[1:]):
            onward_refs[0][...] = made[start:end]
            onward_refs = onward_refs[1:]


def near_kernel(cont, pieces, attended_ref, weight_ref, residual_ref, *refs):
    got_refs, (near_ref, own_ref, sem) = refs[:pieces], refs[pieces:]
    share = near_ref.shape[1]
    start = pl.multiple_of(lax.axis_index("tp") * share, HD)
    copy = pltpu.make_async_copy(
        residual_ref.at[cont, :, pl.ds(start, share)], own_ref, sem.at[0]
    )
    copy.start()
    near_ref[...] = jnp.dot(
        attended_ref[...], weight_ref[0], preferred_element_type=jnp.float32
    ) + from_sibling(got_refs, 0)
    copy.wait()
    near_ref[...] += own_ref[...].astype(jnp.float32)


def sum_kernel(pieces, near_ref, *refs):
    far_refs, (total_ref, squares_ref) = refs[:-2], refs[-2:]
    total = near_ref[...]
    for k in range(0, len(far_refs), pieces):
        parts = [ref[...] for ref in far_refs[k : k + pieces]]
        total = total + jnp.concatenate(parts, axis=0).astype(jnp.float32)
    total_ref[...] = total
    sums = jnp.sum(total * total, axis=1, keepdims=True)
    squares_ref[...] = jnp.broadcast_to(sums, (sums.shape[0], HD)).T[:8]


def stream_kernel(conts, *refs):
    for cont in range(conts):
        refs[conts][cont] = refs[cont][...].astype(jnp.bfloat16)


def norm_kernel(conts, model_width, *refs):
    totals, squares = refs[:conts], refs[conts:-2]
    gain_ref, normed_ref = refs[-2:]
    gain = gain_ref[...].astype(jnp.float32)
    for cont in range(conts):
        row = functools.reduce(jnp.add, [ref[cont * 8 : cont * 8 + 1, :] for ref in squares])
        scale = lax.rsqrt(row / model_width + 1e-05)
        scale = jnp.broadcast_to(scale, (HD, scale.shape[1])).T[:, 0:1]
        total = totals[cont][...]
        normed_ref[cont] = (total * scale * gain).astype(jnp.bfloat16)


def shards(
    queries,
    cont_keys,
    cont_values,
    prompt_keys,
    prompt_values,
    block_lists,
    tile_counts,
    out_weight,
    residual,
    norm_gain,
    *,
    sources,
    members,
):
    conts, length, width = queries.shape
    heads = width // HD
    rows_dev = prompt_keys.shape[0]
    model_width = residual.shape[2]
    share = norm_gain.shape[0]
    chips = members // CORES
    place = lax.axis_index("tp")
    pairs = heads * conts
    params = pltpu.CompilerParams(vmem_limit_bytes=VMEM_LIMIT)
    vmem = pl.BlockSpec(memory_space=pltpu.VMEM)
    hbm = pl.BlockSpec(memory_space=pltpu.HBM)

    def array(shape, dtype):
        return jax.ShapeDtypeStruct(shape, dtype)

    def cost(flops=1024):
        return pl.CostEstimate(flops=flops, bytes_accessed=1024, transcendentals=0)

    def in_hbm(x):
        return pltpu.with_memory_space_constraint(x, pltpu.HBM)

    kept = array((rows_dev, HD), jnp.bfloat16)
    keys = pl.pallas_call(
        functools.partial(pack_keys_kernel, heads),
        out_shape=kept,
        in_specs=[hbm],
        out_specs=vmem,
        scratch_shapes=[pltpu.SemaphoreType.DMA((1,))],
        compiler_params=params,
        cost_estimate=cost(),
        name="pack_keys",
    )(in_hbm(prompt_keys))
    values = pl.pallas_call(
        functools.partial(pack_values_kernel, heads),
        out_shape=kept,
        in_specs=[hbm],
        out_specs=vmem,
        scratch_shapes=[
            pltpu.VMEM((rows_dev, HD), jnp.bfloat16),
            pltpu.SemaphoreType.DMA((1,)),
        ],
        compiler_params=params,
        cost_estimate=cost(),
        name="pack_values",
    )(in_hbm(prompt_values))

    def across(step):
        def target(z, t):
            if sources == 4 and step == 1:
                return z ^ (1 + t % CORES)
            if sources == 4:
                return z ^ 1 if t % CORES == 1 else None
            to = z + step if t % CORES == 0 else z - step
            return to if 0 <= to < sources else None

        return [
            (z * members + t, target(z, t) * members + t)
            for z in range(sources)
            for t in range(members)
            if target(z, t) is not None
        ]

    sibling = [(t, t ^ 1) for t in range(members)]
    steps = steps_of(sources)
    smem = pl.BlockSpec(memory_space=pltpu.SMEM)
    lists = block_lists.reshape(-1)
    counts = tile_counts.reshape(-1)
    state_shape = (
        array((heads, HD, length), jnp.float32),
        array((heads, 8, length), jnp.float32),
    )
    flipped = pltpu.VMEM((2 * rows_dev, HD), jnp.bfloat16)
    weight_shape = array((chips, width, share), jnp.bfloat16)

    made = pl.pallas_call(
        functools.partial(first_kernel, sources, conts),
        out_shape=state_shape * conts + (array((heads, HD, length), jnp.bfloat16),) * conts,
        in_specs=[smem, smem, vmem, vmem] + [hbm] * 3,
        out_specs=(vmem,) * (3 * conts),
        scratch_shapes=[
            flipped,
            pltpu.VMEM(queries.shape, jnp.bfloat16),
            pltpu.VMEM((conts, length, HD), jnp.bfloat16),
            pltpu.VMEM((conts, length, HD), jnp.bfloat16),
            pltpu.VMEM((conts, HD, length), jnp.bfloat16),
            pltpu.SemaphoreType.DMA((3,)),
        ],
        compiler_params=params,
        cost_estimate=cost(),
        name="attend_own",
    )(lists, counts, keys, values, in_hbm(queries), in_hbm(cont_keys), in_hbm(cont_values))
    states = tuple(made[2 * c : 2 * c + 2] for c in range(conts))
    qs = made[2 * conts :]

    def attend_step(step, part, chosen, with_weight, states, held):
        flat = [x for cont in chosen for x in states[cont]]
        count = len(chosen)
        made = pl.pallas_call(
            functools.partial(
                middle_kernel, step, part, sources, conts, chosen, len(held), with_weight
            ),
            out_shape=state_shape * count + ((weight_shape,) if with_weight else ()),
            in_specs=[smem, smem] + [vmem] * (3 * count + len(held)) + [hbm] * with_weight,
            out_specs=(vmem,) * (2 * count + with_weight),
            scratch_shapes=[flipped] + [pltpu.SemaphoreType.DMA((chips,))] * with_weight,
            compiler_params=params,
            cost_estimate=cost(),
            name="attend_step",
        )(
            lists,
            counts,
            *[qs[cont] for cont in chosen],
            *held,
            *flat,
            *([in_hbm(out_weight)] * with_weight),
        )
        states = list(states)
        for i, cont in enumerate(chosen):
            states[cont] = tuple(made[2 * i : 2 * i + 2])
        return tuple(states), made[2 * count :]

    everyone = tuple(range(conts))
    mine, theirs = (keys, values), None
    for step in range(1, steps + 1):
        sent = mine if sources == 4 and step == 2 else (keys, values)
        mine_keys, mine_values = [lax.ppermute(x, ("ctx", "tp"), across(step)) for x in sent]
        mine_keys, states, theirs = lax.optimization_barrier((mine_keys, states, theirs))
        their_keys = lax.ppermute(mine_keys, "tp", sibling)
        mine_values, states = lax.optimization_barrier((mine_values, states))
        their_values = [
            lax.ppermute(x, "tp", sibling)
            for x in jnp.split(mine_values, 2 if step < steps else 1)
        ]
        mine, rest, theirs = (mine_keys, mine_values), theirs, (their_keys, *their_values)
        if rest is not None:
            states, _ = attend_step(step - 1, 1, everyone[:1], False, states, rest)
            theirs, first = lax.optimization_barrier((theirs, states[0]))
            states = (first, *states[1:])
            states, _ = attend_step(step - 1, 1, everyone[1:], False, states, rest)
        if step < steps:
            states, (give_weight,) = attend_step(step, 0, everyone, True, states, mine)

    def attend_last(cont, state):
        fetch, pieces = cont == 0, swap_pieces[cont]
        made = pl.pallas_call(
            functools.partial(last_kernel, steps, sources, conts, cont, pieces),
            out_shape=(array((length, width), jnp.bfloat16),)
            + (array((chips, length // pieces, share), jnp.bfloat16),) * pieces
            + (weight_shape,) * fetch,
            in_specs=[smem, smem] + [vmem] * 8 + [hbm] * fetch,
            out_specs=(vmem,) * (1 + pieces + fetch),
            scratch_shapes=[pltpu.VMEM(a.shape, a.dtype) for a in state_shape]
            + [flipped]
            + [pltpu.SemaphoreType.DMA((chips,))] * fetch,
            compiler_params=params,
            cost_estimate=cost(),
            name="attend_last",
        )(
            lists,
            counts,
            qs[cont],
            *mine,
            *theirs,
            *state,
            give_weight,
            *([in_hbm(out_weight)] * fetch),
        )
        return made[0], made[1 : 1 + pieces], made[1 + pieces :]

    def onward(cuts, attended, got):
        cut_rows = [end - start for start, end in zip(cuts, cuts[1:])]
        parts = pl.pallas_call(
            functools.partial(onward_kernel, len(got), cuts),
            out_shape=tuple(array((n, share), jnp.bfloat16) for n in cut_rows * (chips - 1)),
            in_specs=[vmem] * (2 + len(got)),
            out_specs=(vmem,) * (len(cut_rows) * (chips - 1)),
            compiler_params=params,
            cost_estimate=cost(),
            name="project_onward",
        )(attended, keep_weight, *got)
        far = []
        for k in range(1, chips):
            to_chip = [
                (t, (t // CORES + k) % chips * CORES + t % CORES) for t in range(members)
            ]
            for part in parts[(k - 1) * len(cut_rows) : k * len(cut_rows)]:
                far.append(lax.ppermute(part, "tp", to_chip))
        return parts, far

    def near(cont, attended, got):
        return pl.pallas_call(
            functools.partial(near_kernel, cont, len(got)),
            out_shape=array((length, share), jnp.float32),
            in_specs=[vmem] * 2 + [hbm] + [vmem] * len(got),
            out_specs=vmem,
            scratch_shapes=[
                pltpu.VMEM((length, share), jnp.bfloat16),
                pltpu.SemaphoreType.DMA((1,)),
            ],
            compiler_params=params,
            cost_estimate=cost(),
            name="project_near",
        )(attended, keep_weight, in_hbm(residual), *got)

    swap_pieces = [1] + [4] * (conts - 1)
    attended, give, (keep_weight,) = attend_last(0, states[0])
    nears, fars, cuts = [], [], []
    for cont in range(conts):
        got = [lax.ppermute(x, "tp", sibling) for x in give]
        if cont > 0:
            first = fars[-1][:: len(cuts[-1]) - 1]
            got, first = lax.optimization_barrier((got, first))
            fars[-1][:: len(cuts[-1]) - 1] = first
        cuts.append((0, length))
        parts, far = onward(cuts[-1], attended, got)
        nears.append(near(cont, attended, got))
        fars.append(far)
        if cont + 1 < conts:
            state, parts = lax.optimization_barrier((states[cont + 1], parts))
            attended, give, _ = attend_last(cont + 1, state)

    totals, squares = [], []
    for cont in range(conts):
        total, square = pl.pallas_call(
            functools.partial(sum_kernel, len(cuts[cont]) - 1),
            out_shape=(array((length, share), jnp.float32), array((8, length), jnp.float32)),
            in_specs=[vmem] * (1 + len(fars[cont])),
            out_specs=(vmem,) * 2,
            compiler_params=params,
            cost_estimate=cost(),
            name="add_up",
        )(nears[cont], *fars[cont])
        totals.append(total)
        squares.append(square)
    squares = jnp.concatenate(squares, axis=0)
    squares = squares + lax.ppermute(squares, "tp", sibling)
    all_squares = [squares] + [
        lax.ppermute(
            squares,
            "tp",
            [(t, (t // CORES + k) % chips * CORES + t % CORES) for t in range(members)],
        )
        for k in range(1, chips)
    ]
    out = array((conts, length, share), jnp.bfloat16)
    stream = pl.pallas_call(
        functools.partial(stream_kernel, conts),
        out_shape=out,
        in_specs=[vmem] * conts,
        out_specs=vmem,
        compiler_params=params,
        cost_estimate=cost(),
        name="stream",
    )(*totals)
    normed = pl.pallas_call(
        functools.partial(norm_kernel, conts, model_width),
        out_shape=out,
        in_specs=[vmem] * (conts + chips + 1),
        out_specs=vmem,
        compiler_params=params,
        cost_estimate=cost(),
        name="norm",
    )(*totals, *all_squares, norm_gain.reshape(1, share))
    return stream, normed


def solution(mesh):
    placed = (
        P(("grp", "ctx"), None, "tp"),
        P(("grp", "ctx"), None, None),
        P(("grp", "ctx"), None, None),
        P(("grp", "ctx"), None),
        P(("grp", "ctx"), None),
        P("tp", ("grp", "ctx"), None, None),
        P("tp", ("grp", "ctx"), None),
        P("tp", None),
        P(("grp", "ctx"), None, None),
        P("tp"),
    )
    return jax.shard_map(
        functools.partial(
            shards, sources=mesh.shape["ctx"], members=mesh.shape["tp"]
        ),
        mesh=mesh,
        in_specs=placed,
        out_specs=(P(("grp", "ctx"), None, "tp"), P(("grp", "ctx"), None, "tp")),
        check_vma=False,
    )
```

```python
import functools
import math

import jax
import jax.numpy as jnp
from jax import lax
from jax.experimental import pallas as pl
from jax.experimental.pallas import tpu as pltpu
from jax.sharding import PartitionSpec as P

HEADS = 32
KVH = 2
HD = 128
BLK = 64
TILES = 8
CORES = 2
TOGETHER = 8

VERY_LOW = -1e30
TO_LOG2 = math.log2(math.e) / math.sqrt(HD)

VMEM_LIMIT = 24 * 1024 * 1024


def key_group(heads):
    return lax.axis_index("tp") * heads // (HEADS // KVH)


def group_lanes(heads):
    return pl.ds(pl.multiple_of(key_group(heads) * HD, HD), HD)


def pack_keys_kernel(heads, keys_ref, packed_ref, sems):
    copy = pltpu.make_async_copy(keys_ref.at[:, group_lanes(heads)], packed_ref, sems.at[0])
    copy.start()
    copy.wait()


def pack_values_kernel(heads, values_ref, packed_ref, values_buf, sems):
    copy = pltpu.make_async_copy(values_ref.at[:, group_lanes(heads)], values_buf, sems.at[0])
    copy.start()
    copy.wait()
    for p in range(packed_ref.shape[0] // HD):
        rows = slice(p * HD, (p + 1) * HD)
        packed_ref[rows, :] = values_buf[rows, :].T


def both_ways(values_refs, flipped_ref):
    total = flipped_ref.shape[0] // 2
    for part, values_ref in enumerate(values_refs):
        rows = values_ref.shape[0]
        for p in range(rows // HD):
            pair = values_ref[p * HD : (p + 1) * HD, :]
            at = part * rows + p * HD
            flipped_ref[at : at + HD, :] = pair
            flipped_ref[total + at : total + at + HD, :] = jnp.concatenate(
                [pair[:, BLK:], pair[:, :BLK]], axis=1
            )


def shard_scores(lists_ref, counts_ref, q_refs, keys_ref, flipped_ref, place, head, cont):
    pairs = keys_ref.shape[0] // HD
    conts, sources, source = place
    at = (head * conts + cont) * sources + source
    count = counts_ref[at]
    blocks = [lists_ref[at * TILES + t] for t in range(TILES)]
    keys = jnp.concatenate(
        [keys_ref[pl.ds(pl.multiple_of(b * BLK, BLK), BLK), :] for b in blocks], axis=0
    )
    scores = jnp.dot(keys, q_refs[cont][head], preferred_element_type=jnp.float32)
    lane = lax.broadcasted_iota(jnp.int32, (HD, HD), 1)
    halves = []
    for t, b in enumerate(blocks):
        spot = ((b + t) % 2 * pairs + b // 2) * HD
        halves.append(flipped_ref[pl.ds(pl.multiple_of(spot, HD), HD), :])
    values = jnp.concatenate(
        [jnp.where(lane < BLK, a, b) for a, b in zip(halves[::2], halves[1::2])], axis=1
    )
    tiles = [
        (scores[t * BLK : (t + 1) * BLK], t < count) for t in range(TILES)
    ]
    return tiles, values


def fold(op, tile):
    return functools.reduce(op, [tile[i : i + 8] for i in range(0, tile.shape[0], 8)])


def absorb(state, tiles, values):
    top, total, acc = state
    tops = [
        jnp.where(live, fold(jnp.maximum, tile), VERY_LOW) for tile, live in tiles
    ]
    best = jnp.max(functools.reduce(jnp.maximum, tops), axis=0, keepdims=True)
    new_top = jnp.maximum(top, best)
    weights = [
        jnp.exp2((tile - jnp.where(live, new_top, -VERY_LOW)) * TO_LOG2) for tile, live in tiles
    ]
    factor = jnp.exp2((top - new_top) * TO_LOG2)
    sums = functools.reduce(jnp.add, [fold(jnp.add, w) for w in weights])
    total = total * factor + jnp.sum(sums, axis=0, keepdims=True)
    rounded = jnp.concatenate([w.astype(jnp.bfloat16) for w in weights], axis=0)
    acc = acc * factor + jnp.dot(values, rounded, preferred_element_type=jnp.float32)
    return new_top, total, acc


def load_state(acc_ref, stat_ref, index):
    both = stat_ref[index]
    return both[0:1], both[1:2], acc_ref[index]


def store_state(acc_ref, stat_ref, index, state):
    top, total, acc = state
    stat_ref[index] = jnp.concatenate([top, total] + [total] * 6, axis=0)
    acc_ref[index] = acc


def start_all(copies):
    for copy in copies:
        copy.start()
    return copies


def weight_copies(weight_ref, target, sems, sibling):
    chips, _, share = target.shape
    place = lax.axis_index("tp")
    chip, core = place // CORES, place % CORES
    held = 1 - core if sibling else core
    copies = []
    for k in range(chips):
        start = (lax.rem(chip + k, chips) * CORES + held) * share
        copies.append(
            pltpu.make_async_copy(
                weight_ref.at[:, pl.ds(pl.multiple_of(start, HD), share)],
                target.at[k],
                sems.at[k],
            )
        )
    return copies


def first_kernel(
    sources,
    conts,
    lists_ref,
    counts_ref,
    keys_ref,
    values_ref,
    queries_ref,
    cont_keys_ref,
    cont_values_ref,
    *refs,
):
    states, refs = by_cont(refs[: 2 * conts]), refs[2 * conts :]
    q_refs, refs = refs[:conts], refs[conts:]
    flipped_ref, rows_ref, ck_ref, cv_ref, own_ref, sems = refs
    heads, _, length = q_refs[0].shape
    lanes = group_lanes(heads)
    copies = start_all(
        [
            pltpu.make_async_copy(cont_values_ref.at[:, :, lanes], cv_ref, sems.at[0]),
            pltpu.make_async_copy(queries_ref, rows_ref, sems.at[1]),
            pltpu.make_async_copy(cont_keys_ref.at[:, :, lanes], ck_ref, sems.at[2]),
        ]
    )
    place = conts, sources, lax.axis_index("ctx")
    both_ways([values_ref], flipped_ref)
    copies[0].wait()
    for cont in range(conts):
        own_ref[cont] = cv_ref[cont].T
    copies[1].wait()
    for cont in range(conts):
        for head in range(heads):
            q_refs[cont][head] = rows_ref[cont, :, head * HD : (head + 1) * HD].T
    for copy in copies[2:]:
        copy.wait()
    together = TOGETHER // conts

    def some_heads(index, carry):
        work = [(index * together + j, cont) for j in range(together) for cont in range(conts)]
        made = []
        for head, cont in work:
            scores = jnp.dot(
                ck_ref[cont], q_refs[cont][head], preferred_element_type=jnp.float32
            )
            key = lax.broadcasted_iota(jnp.int32, scores.shape, 0)
            row = lax.broadcasted_iota(jnp.int32, scores.shape, 1)
            scores = jnp.where(key <= row, scores, VERY_LOW)
            tiles, values = shard_scores(
                lists_ref, counts_ref, q_refs, keys_ref, flipped_ref, place, head, cont
            )
            made.append(
                ([(scores, True)] + tiles, jnp.concatenate([own_ref[cont], values], axis=1))
            )
        after = []
        for got in made:
            start = (
                jnp.full((1, length), VERY_LOW, jnp.float32),
                jnp.zeros((1, length), jnp.float32),
                jnp.zeros((HD, length), jnp.float32),
            )
            after.append(absorb(start, *got))
        for (head, cont), state in zip(work, after):
            store_state(*states[cont], head, state)
        return carry

    lax.fori_loop(0, heads // together, some_heads, 0)


def arrivals(step, sources):
    spot = lax.axis_index("ctx")
    core = lax.axis_index("tp") % CORES
    if sources == 4:
        if step == 1:
            mine = jnp.bitwise_xor(spot, 1 + core)
            return ((mine, True), (jnp.bitwise_xor(mine, 3), True))
        far = jnp.bitwise_xor(spot, 3)
        return ((far, core == 1), (far, core == 0))
    mine = jnp.where(core == 0, spot - step, spot + step)
    theirs = jnp.where(core == 0, spot + step, spot - step)
    return tuple((s, (s >= 0) & (s < sources)) for s in (mine, theirs))


def steps_of(sources):
    return 2 if sources == 4 else sources - 1


def absorb_shard(place, lists_ref, counts_ref, q_refs, held, flipped_ref, before, after):
    keys_ref, *values_refs = held
    heads = next(iter(q_refs.values())).shape[0]
    together = min(heads, TOGETHER // len(q_refs))
    both_ways(values_refs, flipped_ref)

    def some_heads(index, carry):
        work = [(index * together + j, cont) for j in range(together) for cont in q_refs]
        states = [load_state(*before[cont], head) for head, cont in work]
        made = [
            shard_scores(lists_ref, counts_ref, q_refs, keys_ref, flipped_ref, place, head, cont)
            for head, cont in work
        ]
        states = [absorb(state, *got) for state, got in zip(states, made)]
        for (head, cont), state in zip(work, states):
            store_state(*after[cont], head, state)
        return carry

    lax.fori_loop(0, heads // together, some_heads, 0)


def hand_on(before, after):
    for source_ref, target_ref in zip(before, after):
        target_ref[...] = source_ref[...]


def by_cont(refs, chosen=None):
    chosen = range(len(refs) // 2) if chosen is None else chosen
    return {cont: refs[2 * i : 2 * i + 2] for i, cont in enumerate(chosen)}


def middle_kernel(
    step, part, sources, conts, chosen, pieces, with_weight, lists_ref, counts_ref, *refs
):
    count = len(chosen)
    q_refs, refs = dict(zip(chosen, refs)), refs[count:]
    held, refs = refs[:pieces], refs[pieces:]
    before, refs = refs[: 2 * count], refs[2 * count :]
    if with_weight:
        weight_ref, *refs = refs
    after, refs = refs[: 2 * count], refs[2 * count :]
    if with_weight:
        give_ref, flipped_ref, sems = refs
        copies = start_all(weight_copies(weight_ref, give_ref, sems, True))
    else:
        (flipped_ref,) = refs
    source, valid = arrivals(step, sources)[part]

    def absorb_part():
        shard = ((conts, sources, source), lists_ref, counts_ref, q_refs, held, flipped_ref)
        absorb_shard(*shard, by_cont(before, chosen), by_cont(after, chosen))

    if valid is True:
        absorb_part()
    else:
        pl.when(valid)(absorb_part)
        pl.when(jnp.logical_not(valid))(lambda: hand_on(before, after))
    if with_weight:
        for copy in copies:
            copy.wait()


def finish_and_give(acc_ref, stat_ref, weight_ref, attended_ref, give_refs):
    for head in range(attended_ref.shape[1] // HD):
        _, total, acc = load_state(acc_ref, stat_ref, head)
        attended_ref[:, head * HD : (head + 1) * HD] = (acc * (1.0 / total)).T.astype(
            jnp.bfloat16
        )
    rows = give_refs[0].shape[1]
    for k in range(weight_ref.shape[0]):
        made = jnp.dot(
            attended_ref[...], weight_ref[k], preferred_element_type=jnp.float32
        ).astype(jnp.bfloat16)
        for i, give_ref in enumerate(give_refs):
            give_ref[k] = made[i * rows : (i + 1) * rows]


def last_kernel(
    step,
    sources,
    conts,
    cont,
    pieces,
    lists_ref,
    counts_ref,
    q_ref,
    mine_keys_ref,
    mine_values_ref,
    their_keys_ref,
    their_values_ref,
    acc_in,
    stat_in,
    give_weight_ref,
    *refs,
):
    if cont == 0:
        weight_ref, *refs, sems = refs
    attended_ref, give_refs, refs = refs[0], refs[1 : 1 + pieces], refs[1 + pieces :]
    if cont == 0:
        keep_weight_ref, *refs = refs
        copies = start_all(weight_copies(weight_ref, keep_weight_ref, sems, False))
    acc_ref, stat_ref, flipped_ref = refs
    before, after = (acc_in, stat_in), (acc_ref, stat_ref)
    one_of_two = sources == 4
    for part, (source, valid) in enumerate(arrivals(step, sources)):

        def absorb_part():
            held = (
                (mine_keys_ref, mine_values_ref),
                (their_keys_ref, their_values_ref),
            )[part]
            shard = ((conts, sources, source), lists_ref, counts_ref, {cont: q_ref}, held)
            first = part == 0 or one_of_two
            absorb_shard(
                *shard, flipped_ref, {cont: before if first else after}, {cont: after}
            )

        pl.when(valid)(absorb_part)
        if part == 0 and not one_of_two:
            pl.when(jnp.logical_not(valid))(lambda: hand_on(before, after))
    finish_and_give(acc_ref, stat_ref, give_weight_ref, attended_ref, give_refs)
    if cont == 0:
        for copy in copies:
            copy.wait()


def from_sibling(got_refs, k):
    return jnp.concatenate([ref[k] for ref in got_refs], axis=0).astype(jnp.float32)


def onward_kernel(pieces, attended_ref, weight_ref, *refs):
    got_refs, onward_refs = refs[:pieces], refs[pieces:]
    for k, onward_ref in enumerate(onward_refs, 1):
        onward_ref[...] = (
            jnp.dot(attended_ref[...], weight_ref[k], preferred_element_type=jnp.float32)
            + from_sibling(got_refs, k)
        ).astype(jnp.bfloat16)


def near_kernel(cont, pieces, attended_ref, weight_ref, residual_ref, *refs):
    got_refs, (near_ref, own_ref, sem) = refs[:pieces], refs[pieces:]
    share = near_ref.shape[1]
    start = pl.multiple_of(lax.axis_index("tp") * share, HD)
    copy = pltpu.make_async_copy(
        residual_ref.at[cont, :, pl.ds(start, share)], own_ref, sem.at[0]
    )
    copy.start()
    near_ref[...] = jnp.dot(
        attended_ref[...], weight_ref[0], preferred_element_type=jnp.float32
    ) + from_sibling(got_refs, 0)
    copy.wait()
    near_ref[...] += own_ref[...].astype(jnp.float32)


def sum_kernel(near_ref, *refs):
    far_refs, (total_ref, squares_ref) = refs[:-2], refs[-2:]
    total = near_ref[...]
    for far_ref in far_refs:
        total = total + far_ref[...].astype(jnp.float32)
    total_ref[...] = total
    sums = jnp.sum(total * total, axis=1, keepdims=True)
    squares_ref[...] = jnp.broadcast_to(sums, (sums.shape[0], HD)).T[:8]


def stream_kernel(conts, *refs):
    for cont in range(conts):
        refs[conts][cont] = refs[cont][...].astype(jnp.bfloat16)


def norm_kernel(conts, model_width, *refs):
    totals, squares = refs[:conts], refs[conts:-2]
    gain_ref, normed_ref = refs[-2:]
    gain = gain_ref[...].astype(jnp.float32)
    for cont in range(conts):
        row = functools.reduce(jnp.add, [ref[cont * 8 : cont * 8 + 1, :] for ref in squares])
        scale = lax.rsqrt(row / model_width + 1e-05)
        scale = jnp.broadcast_to(scale, (HD, scale.shape[1])).T[:, 0:1]
        total = totals[cont][...]
        normed_ref[cont] = (total * scale * gain).astype(jnp.bfloat16)


def shards(
    queries,
    cont_keys,
    cont_values,
    prompt_keys,
    prompt_values,
    block_lists,
    tile_counts,
    out_weight,
    residual,
    norm_gain,
    *,
    sources,
    members,
):
    conts, length, width = queries.shape
    heads = width // HD
    rows_dev = prompt_keys.shape[0]
    model_width = residual.shape[2]
    share = norm_gain.shape[0]
    chips = members // CORES
    place = lax.axis_index("tp")
    pairs = heads * conts
    params = pltpu.CompilerParams(vmem_limit_bytes=VMEM_LIMIT)
    vmem = pl.BlockSpec(memory_space=pltpu.VMEM)
    hbm = pl.BlockSpec(memory_space=pltpu.HBM)

    def array(shape, dtype):
        return jax.ShapeDtypeStruct(shape, dtype)

    def cost(flops=1024):
        return pl.CostEstimate(flops=flops, bytes_accessed=1024, transcendentals=0)

    def in_hbm(x):
        return pltpu.with_memory_space_constraint(x, pltpu.HBM)

    kept = array((rows_dev, HD), jnp.bfloat16)
    keys = pl.pallas_call(
        functools.partial(pack_keys_kernel, heads),
        out_shape=kept,
        in_specs=[hbm],
        out_specs=vmem,
        scratch_shapes=[pltpu.SemaphoreType.DMA((1,))],
        compiler_params=params,
        cost_estimate=cost(),
        name="pack_keys",
    )(in_hbm(prompt_keys))
    values = pl.pallas_call(
        functools.partial(pack_values_kernel, heads),
        out_shape=kept,
        in_specs=[hbm],
        out_specs=vmem,
        scratch_shapes=[
            pltpu.VMEM((rows_dev, HD), jnp.bfloat16),
            pltpu.SemaphoreType.DMA((1,)),
        ],
        compiler_params=params,
        cost_estimate=cost(),
        name="pack_values",
    )(in_hbm(prompt_values))

    def across(step):
        def target(z, t):
            if sources == 4 and step == 1:
                return z ^ (1 + t % CORES)
            if sources == 4:
                return z ^ 1 if t % CORES == 1 else None
            to = z + step if t % CORES == 0 else z - step
            return to if 0 <= to < sources else None

        return [
            (z * members + t, target(z, t) * members + t)
            for z in range(sources)
            for t in range(members)
            if target(z, t) is not None
        ]

    sibling = [(t, t ^ 1) for t in range(members)]
    steps = steps_of(sources)
    smem = pl.BlockSpec(memory_space=pltpu.SMEM)
    lists = block_lists.reshape(-1)
    counts = tile_counts.reshape(-1)
    state_shape = (
        array((heads, HD, length), jnp.float32),
        array((heads, 8, length), jnp.float32),
    )
    flipped = pltpu.VMEM((2 * rows_dev, HD), jnp.bfloat16)
    weight_shape = array((chips, width, share), jnp.bfloat16)

    made = pl.pallas_call(
        functools.partial(first_kernel, sources, conts),
        out_shape=state_shape * conts + (array((heads, HD, length), jnp.bfloat16),) * conts,
        in_specs=[smem, smem, vmem, vmem] + [hbm] * 3,
        out_specs=(vmem,) * (3 * conts),
        scratch_shapes=[
            flipped,
            pltpu.VMEM(queries.shape, jnp.bfloat16),
            pltpu.VMEM((conts, length, HD), jnp.bfloat16),
            pltpu.VMEM((conts, length, HD), jnp.bfloat16),
            pltpu.VMEM((conts, HD, length), jnp.bfloat16),
            pltpu.SemaphoreType.DMA((3,)),
        ],
        compiler_params=params,
        cost_estimate=cost(),
        name="attend_own",
    )(lists, counts, keys, values, in_hbm(queries), in_hbm(cont_keys), in_hbm(cont_values))
    states = tuple(made[2 * c : 2 * c + 2] for c in range(conts))
    qs = made[2 * conts :]

    def attend_step(step, part, chosen, with_weight, states, held):
        flat = [x for cont in chosen for x in states[cont]]
        count = len(chosen)
        made = pl.pallas_call(
            functools.partial(
                middle_kernel, step, part, sources, conts, chosen, len(held), with_weight
            ),
            out_shape=state_shape * count + ((weight_shape,) if with_weight else ()),
            in_specs=[smem, smem] + [vmem] * (3 * count + len(held)) + [hbm] * with_weight,
            out_specs=(vmem,) * (2 * count + with_weight),
            scratch_shapes=[flipped] + [pltpu.SemaphoreType.DMA((chips,))] * with_weight,
            compiler_params=params,
            cost_estimate=cost(),
            name="attend_step",
        )(
            lists,
            counts,
            *[qs[cont] for cont in chosen],
            *held,
            *flat,
            *([in_hbm(out_weight)] * with_weight),
        )
        states = list(states)
        for i, cont in enumerate(chosen):
            states[cont] = tuple(made[2 * i : 2 * i + 2])
        return tuple(states), made[2 * count :]

    everyone = tuple(range(conts))
    mine, theirs = (keys, values), None
    for step in range(1, steps + 1):
        sent = mine if sources == 4 and step == 2 else (keys, values)
        mine_keys, mine_values = [lax.ppermute(x, ("ctx", "tp"), across(step)) for x in sent]
        mine_keys, states, theirs = lax.optimization_barrier((mine_keys, states, theirs))
        their_keys = lax.ppermute(mine_keys, "tp", sibling)
        mine_values, states = lax.optimization_barrier((mine_values, states))
        their_values = [
            lax.ppermute(x, "tp", sibling)
            for x in jnp.split(mine_values, 2 if step < steps else 1)
        ]
        mine, rest, theirs = (mine_keys, mine_values), theirs, (their_keys, *their_values)
        if rest is not None:
            states, _ = attend_step(step - 1, 1, everyone[:1], False, states, rest)
            theirs, first = lax.optimization_barrier((theirs, states[0]))
            states = (first, *states[1:])
            states, _ = attend_step(step - 1, 1, everyone[1:], False, states, rest)
        if step < steps:
            states, (give_weight,) = attend_step(step, 0, everyone, True, states, mine)

    def attend_last(cont, state):
        fetch, pieces = cont == 0, swap_pieces[cont]
        made = pl.pallas_call(
            functools.partial(last_kernel, steps, sources, conts, cont, pieces),
            out_shape=(array((length, width), jnp.bfloat16),)
            + (array((chips, length // pieces, share), jnp.bfloat16),) * pieces
            + (weight_shape,) * fetch,
            in_specs=[smem, smem] + [vmem] * 8 + [hbm] * fetch,
            out_specs=(vmem,) * (1 + pieces + fetch),
            scratch_shapes=[pltpu.VMEM(a.shape, a.dtype) for a in state_shape]
            + [flipped]
            + [pltpu.SemaphoreType.DMA((chips,))] * fetch,
            compiler_params=params,
            cost_estimate=cost(),
            name="attend_last",
        )(
            lists,
            counts,
            qs[cont],
            *mine,
            *theirs,
            *state,
            give_weight,
            *([in_hbm(out_weight)] * fetch),
        )
        return made[0], made[1 : 1 + pieces], made[1 + pieces :]

    def onward(attended, got):
        parts = pl.pallas_call(
            functools.partial(onward_kernel, len(got)),
            out_shape=(array((length, share), jnp.bfloat16),) * (chips - 1),
            in_specs=[vmem] * (2 + len(got)),
            out_specs=(vmem,) * (chips - 1),
            compiler_params=params,
            cost_estimate=cost(),
            name="project_onward",
        )(attended, keep_weight, *got)
        far = []
        for k in range(1, chips):
            to_chip = [
                (t, (t // CORES + k) % chips * CORES + t % CORES) for t in range(members)
            ]
            far.append(lax.ppermute(parts[k - 1], "tp", to_chip))
        return parts, far

    def near(cont, attended, got):
        return pl.pallas_call(
            functools.partial(near_kernel, cont, len(got)),
            out_shape=array((length, share), jnp.float32),
            in_specs=[vmem] * 2 + [hbm] + [vmem] * len(got),
            out_specs=vmem,
            scratch_shapes=[
                pltpu.VMEM((length, share), jnp.bfloat16),
                pltpu.SemaphoreType.DMA((1,)),
            ],
            compiler_params=params,
            cost_estimate=cost(2**35 if cont > 0 else 1024),
            name="project_near",
        )(attended, keep_weight, in_hbm(residual), *got)

    swap_pieces = [1] + [4] * (conts - 1)
    attended, give, (keep_weight,) = attend_last(0, states[0])
    nears, fars = [], []
    for cont in range(conts):
        got = [lax.ppermute(x, "tp", sibling) for x in give]
        if cont + 1 < conts:
            got, state = lax.optimization_barrier((got, states[cont + 1]))
        parts, far = onward(attended, got)
        if cont > 0:
            attended, fars[-1] = lax.optimization_barrier((attended, fars[-1]))
        nears.append(near(cont, attended, got))
        fars.append(far)
        if cont + 1 < conts:
            state, parts = lax.optimization_barrier((state, parts))
            attended, give, _ = attend_last(cont + 1, state)

    totals, squares = [], []
    for cont in range(conts):
        total, square = pl.pallas_call(
            sum_kernel,
            out_shape=(array((length, share), jnp.float32), array((8, length), jnp.float32)),
            in_specs=[vmem] * (1 + len(fars[cont])),
            out_specs=(vmem,) * 2,
            compiler_params=params,
            cost_estimate=cost(),
            name="add_up",
        )(nears[cont], *fars[cont])
        totals.append(total)
        squares.append(square)
    squares = jnp.concatenate(squares, axis=0)
    squares = squares + lax.ppermute(squares, "tp", sibling)
    all_squares = [squares] + [
        lax.ppermute(
            squares,
            "tp",
            [(t, (t // CORES + k) % chips * CORES + t % CORES) for t in range(members)],
        )
        for k in range(1, chips)
    ]
    out = array((conts, length, share), jnp.bfloat16)
    stream = pl.pallas_call(
        functools.partial(stream_kernel, conts),
        out_shape=out,
        in_specs=[vmem] * conts,
        out_specs=vmem,
        compiler_params=params,
        cost_estimate=cost(),
        name="stream",
    )(*totals)
    normed = pl.pallas_call(
        functools.partial(norm_kernel, conts, model_width),
        out_shape=out,
        in_specs=[vmem] * (conts + chips + 1),
        out_specs=vmem,
        compiler_params=params,
        cost_estimate=cost(),
        name="norm",
    )(*totals, *all_squares, norm_gain.reshape(1, share))
    return stream, normed


def solution(mesh):
    placed = (
        P(("grp", "ctx"), None, "tp"),
        P(("grp", "ctx"), None, None),
        P(("grp", "ctx"), None, None),
        P(("grp", "ctx"), None),
        P(("grp", "ctx"), None),
        P("tp", ("grp", "ctx"), None, None),
        P("tp", ("grp", "ctx"), None),
        P("tp", None),
        P(("grp", "ctx"), None, None),
        P("tp"),
    )
    return jax.shard_map(
        functools.partial(
            shards, sources=mesh.shape["ctx"], members=mesh.shape["tp"]
        ),
        mesh=mesh,
        in_specs=placed,
        out_specs=(P(("grp", "ctx"), None, "tp"), P(("grp", "ctx"), None, "tp")),
        check_vma=False,
    )
```

```python
import functools
import math

import jax
import jax.numpy as jnp
from jax import lax
from jax.experimental import pallas as pl
from jax.experimental.pallas import tpu as pltpu
from jax.sharding import PartitionSpec as P

HEADS = 32
KVH = 2
HD = 128
BLK = 64
TILES = 8
CORES = 2
TOGETHER = 8

VERY_LOW = -1e30
TO_LOG2 = math.log2(math.e) / math.sqrt(HD)

VMEM_LIMIT = 24 * 1024 * 1024


def key_group(heads):
    return lax.axis_index("tp") * heads // (HEADS // KVH)


def group_lanes(heads):
    return pl.ds(pl.multiple_of(key_group(heads) * HD, HD), HD)


def pack_keys_kernel(heads, keys_ref, packed_ref, sems):
    copy = pltpu.make_async_copy(keys_ref.at[:, group_lanes(heads)], packed_ref, sems.at[0])
    copy.start()
    copy.wait()


def pack_values_kernel(heads, values_ref, packed_ref, values_buf, sems):
    copy = pltpu.make_async_copy(values_ref.at[:, group_lanes(heads)], values_buf, sems.at[0])
    copy.start()
    copy.wait()
    for p in range(packed_ref.shape[0] // HD):
        rows = slice(p * HD, (p + 1) * HD)
        packed_ref[rows, :] = values_buf[rows, :].T


def both_ways(values_refs, flipped_ref):
    total = flipped_ref.shape[0] // 2
    for part, values_ref in enumerate(values_refs):
        rows = values_ref.shape[0]
        for p in range(rows // HD):
            pair = values_ref[p * HD : (p + 1) * HD, :]
            at = part * rows + p * HD
            flipped_ref[at : at + HD, :] = pair
            flipped_ref[total + at : total + at + HD, :] = jnp.concatenate(
                [pair[:, BLK:], pair[:, :BLK]], axis=1
            )


def shard_scores(lists_ref, counts_ref, q_refs, keys_ref, flipped_ref, place, head, cont):
    pairs = keys_ref.shape[0] // HD
    conts, sources, source = place
    at = (head * conts + cont) * sources + source
    count = counts_ref[at]
    blocks = [lists_ref[at * TILES + t] for t in range(TILES)]
    keys = jnp.concatenate(
        [keys_ref[pl.ds(pl.multiple_of(b * BLK, BLK), BLK), :] for b in blocks], axis=0
    )
    scores = jnp.dot(keys, q_refs[cont][head], preferred_element_type=jnp.float32)
    lane = lax.broadcasted_iota(jnp.int32, (HD, HD), 1)
    halves = []
    for t, b in enumerate(blocks):
        spot = ((b + t) % 2 * pairs + b // 2) * HD
        halves.append(flipped_ref[pl.ds(pl.multiple_of(spot, HD), HD), :])
    values = jnp.concatenate(
        [jnp.where(lane < BLK, a, b) for a, b in zip(halves[::2], halves[1::2])], axis=1
    )
    tiles = [
        (scores[t * BLK : (t + 1) * BLK], t < count) for t in range(TILES)
    ]
    return tiles, values


def fold(op, tile):
    return functools.reduce(op, [tile[i : i + 8] for i in range(0, tile.shape[0], 8)])


def absorb(state, tiles, values):
    top, total, acc = state
    tops = [
        jnp.where(live, fold(jnp.maximum, tile), VERY_LOW) for tile, live in tiles
    ]
    best = jnp.max(functools.reduce(jnp.maximum, tops), axis=0, keepdims=True)
    new_top = jnp.maximum(top, best)
    weights = [
        jnp.exp2((tile - jnp.where(live, new_top, -VERY_LOW)) * TO_LOG2) for tile, live in tiles
    ]
    factor = jnp.exp2((top - new_top) * TO_LOG2)
    sums = functools.reduce(jnp.add, [fold(jnp.add, w) for w in weights])
    total = total * factor + jnp.sum(sums, axis=0, keepdims=True)
    rounded = jnp.concatenate([w.astype(jnp.bfloat16) for w in weights], axis=0)
    acc = acc * factor + jnp.dot(values, rounded, preferred_element_type=jnp.float32)
    return new_top, total, acc


def load_state(acc_ref, stat_ref, index):
    both = stat_ref[index]
    return both[0:1], both[1:2], acc_ref[index]


def store_state(acc_ref, stat_ref, index, state):
    top, total, acc = state
    stat_ref[index] = jnp.concatenate([top, total] + [total] * 6, axis=0)
    acc_ref[index] = acc


def start_all(copies):
    for copy in copies:
        copy.start()
    return copies


def weight_copies(weight_ref, target, sems, sibling):
    chips, _, share = target.shape
    place = lax.axis_index("tp")
    chip, core = place // CORES, place % CORES
    held = 1 - core if sibling else core
    copies = []
    for k in range(chips):
        start = (lax.rem(chip + k, chips) * CORES + held) * share
        copies.append(
            pltpu.make_async_copy(
                weight_ref.at[:, pl.ds(pl.multiple_of(start, HD), share)],
                target.at[k],
                sems.at[k],
            )
        )
    return copies


def first_kernel(
    sources,
    conts,
    lists_ref,
    counts_ref,
    keys_ref,
    values_ref,
    queries_ref,
    cont_keys_ref,
    cont_values_ref,
    *refs,
):
    states, refs = by_cont(refs[: 2 * conts]), refs[2 * conts :]
    q_refs, refs = refs[:conts], refs[conts:]
    flipped_ref, rows_ref, ck_ref, cv_ref, own_ref, sems = refs
    heads, _, length = q_refs[0].shape
    lanes = group_lanes(heads)
    copies = start_all(
        [
            pltpu.make_async_copy(cont_values_ref.at[:, :, lanes], cv_ref, sems.at[0]),
            pltpu.make_async_copy(queries_ref, rows_ref, sems.at[1]),
            pltpu.make_async_copy(cont_keys_ref.at[:, :, lanes], ck_ref, sems.at[2]),
        ]
    )
    place = conts, sources, lax.axis_index("ctx")
    both_ways([values_ref], flipped_ref)
    copies[0].wait()
    for cont in range(conts):
        own_ref[cont] = cv_ref[cont].T
    copies[1].wait()
    for cont in range(conts):
        for head in range(heads):
            q_refs[cont][head] = rows_ref[cont, :, head * HD : (head + 1) * HD].T
    for copy in copies[2:]:
        copy.wait()
    together = TOGETHER // conts

    def some_heads(index, carry):
        work = [(index * together + j, cont) for j in range(together) for cont in range(conts)]
        made = []
        for head, cont in work:
            scores = jnp.dot(
                ck_ref[cont], q_refs[cont][head], preferred_element_type=jnp.float32
            )
            key = lax.broadcasted_iota(jnp.int32, scores.shape, 0)
            row = lax.broadcasted_iota(jnp.int32, scores.shape, 1)
            scores = jnp.where(key <= row, scores, VERY_LOW)
            tiles, values = shard_scores(
                lists_ref, counts_ref, q_refs, keys_ref, flipped_ref, place, head, cont
            )
            made.append(
                ([(scores, True)] + tiles, jnp.concatenate([own_ref[cont], values], axis=1))
            )
        after = []
        for got in made:
            start = (
                jnp.full((1, length), VERY_LOW, jnp.float32),
                jnp.zeros((1, length), jnp.float32),
                jnp.zeros((HD, length), jnp.float32),
            )
            after.append(absorb(start, *got))
        for (head, cont), state in zip(work, after):
            store_state(*states[cont], head, state)
        return carry

    lax.fori_loop(0, heads // together, some_heads, 0)


def arrivals(step, sources):
    spot = lax.axis_index("ctx")
    core = lax.axis_index("tp") % CORES
    if sources == 4:
        if step == 1:
            mine = jnp.bitwise_xor(spot, 1 + core)
            return ((mine, True), (jnp.bitwise_xor(mine, 3), True))
        far = jnp.bitwise_xor(spot, 3)
        return ((far, core == 1), (far, core == 0))
    mine = jnp.where(core == 0, spot - step, spot + step)
    theirs = jnp.where(core == 0, spot + step, spot - step)
    return tuple((s, (s >= 0) & (s < sources)) for s in (mine, theirs))


def steps_of(sources):
    return 2 if sources == 4 else sources - 1


def absorb_shard(place, lists_ref, counts_ref, q_refs, held, flipped_ref, before, after):
    keys_ref, *values_refs = held
    heads = next(iter(q_refs.values())).shape[0]
    together = min(heads, TOGETHER // len(q_refs))
    both_ways(values_refs, flipped_ref)

    def some_heads(index, carry):
        work = [(index * together + j, cont) for j in range(together) for cont in q_refs]
        states = [load_state(*before[cont], head) for head, cont in work]
        made = [
            shard_scores(lists_ref, counts_ref, q_refs, keys_ref, flipped_ref, place, head, cont)
            for head, cont in work
        ]
        states = [absorb(state, *got) for state, got in zip(states, made)]
        for (head, cont), state in zip(work, states):
            store_state(*after[cont], head, state)
        return carry

    lax.fori_loop(0, heads // together, some_heads, 0)


def hand_on(before, after):
    for source_ref, target_ref in zip(before, after):
        target_ref[...] = source_ref[...]


def by_cont(refs, chosen=None):
    chosen = range(len(refs) // 2) if chosen is None else chosen
    return {cont: refs[2 * i : 2 * i + 2] for i, cont in enumerate(chosen)}


def middle_kernel(
    step, part, sources, conts, chosen, pieces, with_weight, lists_ref, counts_ref, *refs
):
    count = len(chosen)
    q_refs, refs = dict(zip(chosen, refs)), refs[count:]
    held, refs = refs[:pieces], refs[pieces:]
    before, refs = refs[: 2 * count], refs[2 * count :]
    if with_weight:
        weight_ref, *refs = refs
    after, refs = refs[: 2 * count], refs[2 * count :]
    if with_weight:
        give_ref, flipped_ref, sems = refs
        copies = start_all(weight_copies(weight_ref, give_ref, sems, True))
    else:
        (flipped_ref,) = refs
    source, valid = arrivals(step, sources)[part]

    def absorb_part():
        shard = ((conts, sources, source), lists_ref, counts_ref, q_refs, held, flipped_ref)
        absorb_shard(*shard, by_cont(before, chosen), by_cont(after, chosen))

    if valid is True:
        absorb_part()
    else:
        pl.when(valid)(absorb_part)
        pl.when(jnp.logical_not(valid))(lambda: hand_on(before, after))
    if with_weight:
        for copy in copies:
            copy.wait()


def finish_and_give(acc_ref, stat_ref, weight_ref, attended_ref, give_refs):
    for head in range(attended_ref.shape[1] // HD):
        _, total, acc = load_state(acc_ref, stat_ref, head)
        attended_ref[:, head * HD : (head + 1) * HD] = (acc * (1.0 / total)).T.astype(
            jnp.bfloat16
        )
    rows = give_refs[0].shape[1]
    for k in range(1, weight_ref.shape[0]):
        made = jnp.dot(
            attended_ref[...], weight_ref[k], preferred_element_type=jnp.float32
        ).astype(jnp.bfloat16)
        for i, give_ref in enumerate(give_refs):
            give_ref[k - 1] = made[i * rows : (i + 1) * rows]


def last_kernel(
    step,
    sources,
    conts,
    cont,
    pieces,
    lists_ref,
    counts_ref,
    q_ref,
    mine_keys_ref,
    mine_values_ref,
    their_keys_ref,
    their_values_ref,
    acc_in,
    stat_in,
    give_weight_ref,
    *refs,
):
    if cont == 0:
        weight_ref, *refs, sems = refs
    attended_ref, give_refs, refs = refs[0], refs[1 : 1 + pieces], refs[1 + pieces :]
    if cont == 0:
        keep_weight_ref, *refs = refs
        copies = start_all(weight_copies(weight_ref, keep_weight_ref, sems, False))
    acc_ref, stat_ref, flipped_ref = refs
    before, after = (acc_in, stat_in), (acc_ref, stat_ref)
    one_of_two = sources == 4
    for part, (source, valid) in enumerate(arrivals(step, sources)):

        def absorb_part():
            held = (
                (mine_keys_ref, mine_values_ref),
                (their_keys_ref, their_values_ref),
            )[part]
            shard = ((conts, sources, source), lists_ref, counts_ref, {cont: q_ref}, held)
            first = part == 0 or one_of_two
            absorb_shard(
                *shard, flipped_ref, {cont: before if first else after}, {cont: after}
            )

        pl.when(valid)(absorb_part)
        if part == 0 and not one_of_two:
            pl.when(jnp.logical_not(valid))(lambda: hand_on(before, after))
    finish_and_give(acc_ref, stat_ref, give_weight_ref, attended_ref, give_refs)
    if cont == 0:
        for copy in copies:
            copy.wait()


def from_sibling(got_refs, k):
    return jnp.concatenate([ref[k] for ref in got_refs], axis=0).astype(jnp.float32)


def onward_kernel(pieces, attended_ref, weight_ref, *refs):
    got_refs, onward_refs = refs[:pieces], refs[pieces:]
    for k, onward_ref in enumerate(onward_refs, 1):
        onward_ref[...] = (
            jnp.dot(attended_ref[...], weight_ref[k], preferred_element_type=jnp.float32)
            + from_sibling(got_refs, k - 1)
        ).astype(jnp.bfloat16)


def attended_rows(refs):
    return jnp.concatenate([ref[...] for ref in refs], axis=0)


def give_near_kernel(conts, *refs):
    attended_refs, weight_ref, give_refs = refs[:conts], refs[conts], refs[conts + 1 :]
    made = jnp.dot(
        attended_rows(attended_refs), weight_ref[0], preferred_element_type=jnp.float32
    ).astype(jnp.bfloat16)
    rows = give_refs[0].shape[0]
    for i, give_ref in enumerate(give_refs):
        give_ref[...] = made[i * rows : (i + 1) * rows]


def near_kernel(conts, pieces, *refs):
    attended_refs, weight_ref, residual_ref = refs[:conts], refs[conts], refs[conts + 1]
    got_refs, refs = refs[conts + 2 : conts + 2 + pieces], refs[conts + 2 + pieces :]
    near_refs, (own_ref, sem) = refs[:conts], refs[conts:]
    length, share = near_refs[0].shape
    start = pl.multiple_of(lax.axis_index("tp") * share, HD)
    copy = pltpu.make_async_copy(
        residual_ref.at[:, :, pl.ds(start, share)], own_ref, sem.at[0]
    )
    copy.start()
    made = jnp.dot(
        attended_rows(attended_refs), weight_ref[0], preferred_element_type=jnp.float32
    ) + attended_rows(got_refs).astype(jnp.float32)
    for cont, near_ref in enumerate(near_refs):
        near_ref[...] = made[cont * length : (cont + 1) * length]
    copy.wait()
    for cont, near_ref in enumerate(near_refs):
        near_ref[...] += own_ref[cont].astype(jnp.float32)


def sum_kernel(near_ref, *refs):
    far_refs, (total_ref, squares_ref) = refs[:-2], refs[-2:]
    total = near_ref[...]
    for far_ref in far_refs:
        total = total + far_ref[...].astype(jnp.float32)
    total_ref[...] = total
    sums = jnp.sum(total * total, axis=1, keepdims=True)
    squares_ref[...] = jnp.broadcast_to(sums, (sums.shape[0], HD)).T[:8]


def stream_kernel(conts, *refs):
    for cont in range(conts):
        refs[conts][cont] = refs[cont][...].astype(jnp.bfloat16)


def norm_kernel(conts, model_width, *refs):
    totals, squares = refs[:conts], refs[conts:-2]
    gain_ref, normed_ref = refs[-2:]
    gain = gain_ref[...].astype(jnp.float32)
    for cont in range(conts):
        row = functools.reduce(jnp.add, [ref[cont * 8 : cont * 8 + 1, :] for ref in squares])
        scale = lax.rsqrt(row / model_width + 1e-05)
        scale = jnp.broadcast_to(scale, (HD, scale.shape[1])).T[:, 0:1]
        total = totals[cont][...]
        normed_ref[cont] = (total * scale * gain).astype(jnp.bfloat16)


def shards(
    queries,
    cont_keys,
    cont_values,
    prompt_keys,
    prompt_values,
    block_lists,
    tile_counts,
    out_weight,
    residual,
    norm_gain,
    *,
    sources,
    members,
):
    conts, length, width = queries.shape
    heads = width // HD
    rows_dev = prompt_keys.shape[0]
    model_width = residual.shape[2]
    share = norm_gain.shape[0]
    chips = members // CORES
    place = lax.axis_index("tp")
    pairs = heads * conts
    params = pltpu.CompilerParams(vmem_limit_bytes=VMEM_LIMIT)
    vmem = pl.BlockSpec(memory_space=pltpu.VMEM)
    hbm = pl.BlockSpec(memory_space=pltpu.HBM)

    def array(shape, dtype):
        return jax.ShapeDtypeStruct(shape, dtype)

    def cost(flops=1024):
        return pl.CostEstimate(flops=flops, bytes_accessed=1024, transcendentals=0)

    def in_hbm(x):
        return pltpu.with_memory_space_constraint(x, pltpu.HBM)

    kept = array((rows_dev, HD), jnp.bfloat16)
    keys = pl.pallas_call(
        functools.partial(pack_keys_kernel, heads),
        out_shape=kept,
        in_specs=[hbm],
        out_specs=vmem,
        scratch_shapes=[pltpu.SemaphoreType.DMA((1,))],
        compiler_params=params,
        cost_estimate=cost(),
        name="pack_keys",
    )(in_hbm(prompt_keys))
    values = pl.pallas_call(
        functools.partial(pack_values_kernel, heads),
        out_shape=kept,
        in_specs=[hbm],
        out_specs=vmem,
        scratch_shapes=[
            pltpu.VMEM((rows_dev, HD), jnp.bfloat16),
            pltpu.SemaphoreType.DMA((1,)),
        ],
        compiler_params=params,
        cost_estimate=cost(),
        name="pack_values",
    )(in_hbm(prompt_values))

    def across(step):
        def target(z, t):
            if sources == 4 and step == 1:
                return z ^ (1 + t % CORES)
            if sources == 4:
                return z ^ 1 if t % CORES == 1 else None
            to = z + step if t % CORES == 0 else z - step
            return to if 0 <= to < sources else None

        return [
            (z * members + t, target(z, t) * members + t)
            for z in range(sources)
            for t in range(members)
            if target(z, t) is not None
        ]

    sibling = [(t, t ^ 1) for t in range(members)]
    steps = steps_of(sources)
    smem = pl.BlockSpec(memory_space=pltpu.SMEM)
    lists = block_lists.reshape(-1)
    counts = tile_counts.reshape(-1)
    state_shape = (
        array((heads, HD, length), jnp.float32),
        array((heads, 8, length), jnp.float32),
    )
    flipped = pltpu.VMEM((2 * rows_dev, HD), jnp.bfloat16)
    weight_shape = array((chips, width, share), jnp.bfloat16)

    made = pl.pallas_call(
        functools.partial(first_kernel, sources, conts),
        out_shape=state_shape * conts + (array((heads, HD, length), jnp.bfloat16),) * conts,
        in_specs=[smem, smem, vmem, vmem] + [hbm] * 3,
        out_specs=(vmem,) * (3 * conts),
        scratch_shapes=[
            flipped,
            pltpu.VMEM(queries.shape, jnp.bfloat16),
            pltpu.VMEM((conts, length, HD), jnp.bfloat16),
            pltpu.VMEM((conts, length, HD), jnp.bfloat16),
            pltpu.VMEM((conts, HD, length), jnp.bfloat16),
            pltpu.SemaphoreType.DMA((3,)),
        ],
        compiler_params=params,
        cost_estimate=cost(),
        name="attend_own",
    )(lists, counts, keys, values, in_hbm(queries), in_hbm(cont_keys), in_hbm(cont_values))
    states = tuple(made[2 * c : 2 * c + 2] for c in range(conts))
    qs = made[2 * conts :]

    def attend_step(step, part, chosen, with_weight, states, held):
        flat = [x for cont in chosen for x in states[cont]]
        count = len(chosen)
        made = pl.pallas_call(
            functools.partial(
                middle_kernel, step, part, sources, conts, chosen, len(held), with_weight
            ),
            out_shape=state_shape * count + ((weight_shape,) if with_weight else ()),
            in_specs=[smem, smem] + [vmem] * (3 * count + len(held)) + [hbm] * with_weight,
            out_specs=(vmem,) * (2 * count + with_weight),
            scratch_shapes=[flipped] + [pltpu.SemaphoreType.DMA((chips,))] * with_weight,
            compiler_params=params,
            cost_estimate=cost(),
            name="attend_step",
        )(
            lists,
            counts,
            *[qs[cont] for cont in chosen],
            *held,
            *flat,
            *([in_hbm(out_weight)] * with_weight),
        )
        states = list(states)
        for i, cont in enumerate(chosen):
            states[cont] = tuple(made[2 * i : 2 * i + 2])
        return tuple(states), made[2 * count :]

    everyone = tuple(range(conts))
    mine, theirs = (keys, values), None
    for step in range(1, steps + 1):
        sent = mine if sources == 4 and step == 2 else (keys, values)
        mine_keys, mine_values = [lax.ppermute(x, ("ctx", "tp"), across(step)) for x in sent]
        mine_keys, states, theirs = lax.optimization_barrier((mine_keys, states, theirs))
        their_keys = lax.ppermute(mine_keys, "tp", sibling)
        mine_values, states = lax.optimization_barrier((mine_values, states))
        their_values = [
            lax.ppermute(x, "tp", sibling)
            for x in jnp.split(mine_values, 2 if step < steps else 1)
        ]
        mine, rest, theirs = (mine_keys, mine_values), theirs, (their_keys, *their_values)
        if rest is not None:
            states, _ = attend_step(step - 1, 1, everyone[:1], False, states, rest)
            theirs, first = lax.optimization_barrier((theirs, states[0]))
            states = (first, *states[1:])
            states, _ = attend_step(step - 1, 1, everyone[1:], False, states, rest)
        if step < steps:
            states, (give_weight,) = attend_step(step, 0, everyone, True, states, mine)

    def attend_last(cont, state):
        fetch, pieces = cont == 0, swap_pieces[cont]
        made = pl.pallas_call(
            functools.partial(last_kernel, steps, sources, conts, cont, pieces),
            out_shape=(array((length, width), jnp.bfloat16),)
            + (array((chips - 1, length // pieces, share), jnp.bfloat16),) * pieces
            + (weight_shape,) * fetch,
            in_specs=[smem, smem] + [vmem] * 8 + [hbm] * fetch,
            out_specs=(vmem,) * (1 + pieces + fetch),
            scratch_shapes=[pltpu.VMEM(a.shape, a.dtype) for a in state_shape]
            + [flipped]
            + [pltpu.SemaphoreType.DMA((chips,))] * fetch,
            compiler_params=params,
            cost_estimate=cost(),
            name="attend_last",
        )(
            lists,
            counts,
            qs[cont],
            *mine,
            *theirs,
            *state,
            give_weight,
            *([in_hbm(out_weight)] * fetch),
        )
        return made[0], made[1 : 1 + pieces], made[1 + pieces :]

    def onward(attended, got):
        parts = pl.pallas_call(
            functools.partial(onward_kernel, len(got)),
            out_shape=(array((length, share), jnp.bfloat16),) * (chips - 1),
            in_specs=[vmem] * (2 + len(got)),
            out_specs=(vmem,) * (chips - 1),
            compiler_params=params,
            cost_estimate=cost(),
            name="project_onward",
        )(attended, keep_weight, *got)
        far = []
        for k in range(1, chips):
            to_chip = [
                (t, (t // CORES + k) % chips * CORES + t % CORES) for t in range(members)
            ]
            far.append(lax.ppermute(parts[k - 1], "tp", to_chip))
        return parts, far

    def give_near(attended, pieces):
        return pl.pallas_call(
            functools.partial(give_near_kernel, conts),
            out_shape=(array((conts * length // pieces, share), jnp.bfloat16),) * pieces,
            in_specs=[vmem] * (conts + 1),
            out_specs=(vmem,) * pieces,
            compiler_params=params,
            cost_estimate=cost(2**35),
            name="give_near",
        )(*attended, give_weight)

    def near(attended, got):
        return pl.pallas_call(
            functools.partial(near_kernel, conts, len(got)),
            out_shape=(array((length, share), jnp.float32),) * conts,
            in_specs=[vmem] * (conts + 1) + [hbm] + [vmem] * len(got),
            out_specs=(vmem,) * conts,
            scratch_shapes=[
                pltpu.VMEM((conts, length, share), jnp.bfloat16),
                pltpu.SemaphoreType.DMA((1,)),
            ],
            compiler_params=params,
            cost_estimate=cost(),
            name="project_near",
        )(*attended, keep_weight, in_hbm(residual), *got)

    swap_pieces = [1] + [2] * (conts - 1)
    attended, give, (keep_weight,) = attend_last(0, states[0])
    all_attended, fars = [], []
    for cont in range(conts):
        got = [lax.ppermute(x, "tp", sibling) for x in give]
        if cont + 1 < conts:
            got, state = lax.optimization_barrier((got, states[cont + 1]))
        parts, far = onward(attended, got)
        all_attended.append(attended)
        fars.append(far)
        if cont + 1 < conts:
            state, parts = lax.optimization_barrier((state, parts))
            attended, give, _ = attend_last(cont + 1, state)
    all_attended, fars[:-1], _ = lax.optimization_barrier((all_attended, fars[:-1], parts))
    got = [lax.ppermute(x, "tp", sibling) for x in give_near(all_attended, 2 * conts)]
    nears = near(all_attended, got)

    totals, squares = [], []
    for cont in range(conts):
        total, square = pl.pallas_call(
            sum_kernel,
            out_shape=(array((length, share), jnp.float32), array((8, length), jnp.float32)),
            in_specs=[vmem] * (1 + len(fars[cont])),
            out_specs=(vmem,) * 2,
            compiler_params=params,
            cost_estimate=cost(),
            name="add_up",
        )(nears[cont], *fars[cont])
        totals.append(total)
        squares.append(square)
    squares = jnp.concatenate(squares, axis=0)
    squares = squares + lax.ppermute(squares, "tp", sibling)
    all_squares = [squares] + [
        lax.ppermute(
            squares,
            "tp",
            [(t, (t // CORES + k) % chips * CORES + t % CORES) for t in range(members)],
        )
        for k in range(1, chips)
    ]
    out = array((conts, length, share), jnp.bfloat16)
    stream = pl.pallas_call(
        functools.partial(stream_kernel, conts),
        out_shape=out,
        in_specs=[vmem] * conts,
        out_specs=vmem,
        compiler_params=params,
        cost_estimate=cost(),
        name="stream",
    )(*totals)
    normed = pl.pallas_call(
        functools.partial(norm_kernel, conts, model_width),
        out_shape=out,
        in_specs=[vmem] * (conts + chips + 1),
        out_specs=vmem,
        compiler_params=params,
        cost_estimate=cost(),
        name="norm",
    )(*totals, *all_squares, norm_gain.reshape(1, share))
    return stream, normed


def solution(mesh):
    placed = (
        P(("grp", "ctx"), None, "tp"),
        P(("grp", "ctx"), None, None),
        P(("grp", "ctx"), None, None),
        P(("grp", "ctx"), None),
        P(("grp", "ctx"), None),
        P("tp", ("grp", "ctx"), None, None),
        P("tp", ("grp", "ctx"), None),
        P("tp", None),
        P(("grp", "ctx"), None, None),
        P("tp"),
    )
    return jax.shard_map(
        functools.partial(
            shards, sources=mesh.shape["ctx"], members=mesh.shape["tp"]
        ),
        mesh=mesh,
        in_specs=placed,
        out_specs=(P(("grp", "ctx"), None, "tp"), P(("grp", "ctx"), None, "tp")),
        check_vma=False,
    )
```

```python
import functools
import math

import jax
import jax.numpy as jnp
from jax import lax
from jax.experimental import pallas as pl
from jax.experimental.pallas import tpu as pltpu
from jax.sharding import PartitionSpec as P

HEADS = 32
KVH = 2
HD = 128
BLK = 64
TILES = 8
CORES = 2
TOGETHER = 8

VERY_LOW = -1e30
TO_LOG2 = math.log2(math.e) / math.sqrt(HD)

VMEM_LIMIT = 24 * 1024 * 1024


def key_group(heads):
    return lax.axis_index("tp") * heads // (HEADS // KVH)


def group_lanes(heads):
    return pl.ds(pl.multiple_of(key_group(heads) * HD, HD), HD)


def pack_keys_kernel(heads, keys_ref, packed_ref, sems):
    copy = pltpu.make_async_copy(keys_ref.at[:, group_lanes(heads)], packed_ref, sems.at[0])
    copy.start()
    copy.wait()


def pack_values_kernel(heads, values_ref, packed_ref, values_buf, sems):
    copy = pltpu.make_async_copy(values_ref.at[:, group_lanes(heads)], values_buf, sems.at[0])
    copy.start()
    copy.wait()
    for p in range(packed_ref.shape[0] // HD):
        rows = slice(p * HD, (p + 1) * HD)
        packed_ref[rows, :] = values_buf[rows, :].T


def both_ways(values_refs, flipped_ref):
    total = flipped_ref.shape[0] // 2
    for part, values_ref in enumerate(values_refs):
        rows = values_ref.shape[0]
        for p in range(rows // HD):
            pair = values_ref[p * HD : (p + 1) * HD, :]
            at = part * rows + p * HD
            flipped_ref[at : at + HD, :] = pair
            flipped_ref[total + at : total + at + HD, :] = jnp.concatenate(
                [pair[:, BLK:], pair[:, :BLK]], axis=1
            )


def shard_scores(lists_ref, counts_ref, q_refs, keys_ref, flipped_ref, place, head, cont):
    pairs = keys_ref.shape[0] // HD
    conts, sources, source = place
    at = (head * conts + cont) * sources + source
    count = counts_ref[at]
    blocks = [lists_ref[at * TILES + t] for t in range(TILES)]
    keys = jnp.concatenate(
        [keys_ref[pl.ds(pl.multiple_of(b * BLK, BLK), BLK), :] for b in blocks], axis=0
    )
    scores = jnp.dot(keys, q_refs[cont][head], preferred_element_type=jnp.float32)
    lane = lax.broadcasted_iota(jnp.int32, (HD, HD), 1)
    halves = []
    for t, b in enumerate(blocks):
        spot = ((b + t) % 2 * pairs + b // 2) * HD
        halves.append(flipped_ref[pl.ds(pl.multiple_of(spot, HD), HD), :])
    values = jnp.concatenate(
        [jnp.where(lane < BLK, a, b) for a, b in zip(halves[::2], halves[1::2])], axis=1
    )
    tiles = [
        (scores[t * BLK : (t + 1) * BLK], t < count) for t in range(TILES)
    ]
    return tiles, values


def fold(op, tile):
    return functools.reduce(op, [tile[i : i + 8] for i in range(0, tile.shape[0], 8)])


def absorb(state, tiles, values):
    top, total, acc = state
    tops = [
        jnp.where(live, fold(jnp.maximum, tile), VERY_LOW) for tile, live in tiles
    ]
    best = jnp.max(functools.reduce(jnp.maximum, tops), axis=0, keepdims=True)
    new_top = jnp.maximum(top, best)
    weights = [
        jnp.exp2((tile - jnp.where(live, new_top, -VERY_LOW)) * TO_LOG2) for tile, live in tiles
    ]
    factor = jnp.exp2((top - new_top) * TO_LOG2)
    sums = functools.reduce(jnp.add, [fold(jnp.add, w) for w in weights])
    total = total * factor + jnp.sum(sums, axis=0, keepdims=True)
    rounded = jnp.concatenate([w.astype(jnp.bfloat16) for w in weights], axis=0)
    acc = acc * factor + jnp.dot(values, rounded, preferred_element_type=jnp.float32)
    return new_top, total, acc


def load_state(acc_ref, stat_ref, index):
    both = stat_ref[index]
    return both[0:1], both[1:2], acc_ref[index]


def store_state(acc_ref, stat_ref, index, state):
    top, total, acc = state
    stat_ref[index] = jnp.concatenate([top, total] + [total] * 6, axis=0)
    acc_ref[index] = acc


def start_all(copies):
    for copy in copies:
        copy.start()
    return copies


def weight_copies(weight_ref, target, sems, sibling, first=0):
    count, _, share = target.shape
    chips = weight_ref.shape[1] // (CORES * share)
    place = lax.axis_index("tp")
    chip, core = place // CORES, place % CORES
    held = 1 - core if sibling else core
    copies = []
    for k in range(count):
        start = (lax.rem(chip + first + k, chips) * CORES + held) * share
        copies.append(
            pltpu.make_async_copy(
                weight_ref.at[:, pl.ds(pl.multiple_of(start, HD), share)],
                target.at[k],
                sems.at[k],
            )
        )
    return copies


def first_kernel(
    sources,
    conts,
    lists_ref,
    counts_ref,
    keys_ref,
    values_ref,
    queries_ref,
    cont_keys_ref,
    cont_values_ref,
    weight_ref,
    *refs,
):
    states, refs = by_cont(refs[: 2 * conts]), refs[2 * conts :]
    q_refs, refs = refs[:conts], refs[conts:]
    give_ref, weight_sems, *refs = refs[0], refs[-1], *refs[1:-1]
    flipped_ref, rows_ref, ck_ref, cv_ref, own_ref, sems = refs
    heads, _, length = q_refs[0].shape
    lanes = group_lanes(heads)
    copies = start_all(
        [
            pltpu.make_async_copy(cont_values_ref.at[:, :, lanes], cv_ref, sems.at[0]),
            pltpu.make_async_copy(queries_ref, rows_ref, sems.at[1]),
            pltpu.make_async_copy(cont_keys_ref.at[:, :, lanes], ck_ref, sems.at[2]),
        ]
    )
    fetched = start_all(weight_copies(weight_ref, give_ref, weight_sems, True))
    place = conts, sources, lax.axis_index("ctx")
    both_ways([values_ref], flipped_ref)
    copies[0].wait()
    for cont in range(conts):
        own_ref[cont] = cv_ref[cont].T
    copies[1].wait()
    for cont in range(conts):
        for head in range(heads):
            q_refs[cont][head] = rows_ref[cont, :, head * HD : (head + 1) * HD].T
    for copy in copies[2:]:
        copy.wait()
    together = TOGETHER // conts

    def some_heads(index, carry):
        work = [(index * together + j, cont) for j in range(together) for cont in range(conts)]
        made = []
        for head, cont in work:
            scores = jnp.dot(
                ck_ref[cont], q_refs[cont][head], preferred_element_type=jnp.float32
            )
            key = lax.broadcasted_iota(jnp.int32, scores.shape, 0)
            row = lax.broadcasted_iota(jnp.int32, scores.shape, 1)
            scores = jnp.where(key <= row, scores, VERY_LOW)
            tiles, values = shard_scores(
                lists_ref, counts_ref, q_refs, keys_ref, flipped_ref, place, head, cont
            )
            made.append(
                ([(scores, True)] + tiles, jnp.concatenate([own_ref[cont], values], axis=1))
            )
        after = []
        for got in made:
            start = (
                jnp.full((1, length), VERY_LOW, jnp.float32),
                jnp.zeros((1, length), jnp.float32),
                jnp.zeros((HD, length), jnp.float32),
            )
            after.append(absorb(start, *got))
        for (head, cont), state in zip(work, after):
            store_state(*states[cont], head, state)
        return carry

    lax.fori_loop(0, heads // together, some_heads, 0)
    for copy in fetched:
        copy.wait()


def arrivals(step, sources):
    spot = lax.axis_index("ctx")
    core = lax.axis_index("tp") % CORES
    if sources == 4:
        if step == 1:
            mine = jnp.bitwise_xor(spot, 1 + core)
            return ((mine, True), (jnp.bitwise_xor(mine, 3), True))
        far = jnp.bitwise_xor(spot, 3)
        return ((far, core == 1), (far, core == 0))
    mine = jnp.where(core == 0, spot - step, spot + step)
    theirs = jnp.where(core == 0, spot + step, spot - step)
    return tuple((s, (s >= 0) & (s < sources)) for s in (mine, theirs))


def steps_of(sources):
    return 2 if sources == 4 else sources - 1


def absorb_shard(place, lists_ref, counts_ref, q_refs, held, flipped_ref, before, after):
    keys_ref, *values_refs = held
    heads = next(iter(q_refs.values())).shape[0]
    together = min(heads, TOGETHER // len(q_refs))
    both_ways(values_refs, flipped_ref)

    def some_heads(index, carry):
        work = [(index * together + j, cont) for j in range(together) for cont in q_refs]
        states = [load_state(*before[cont], head) for head, cont in work]
        made = [
            shard_scores(lists_ref, counts_ref, q_refs, keys_ref, flipped_ref, place, head, cont)
            for head, cont in work
        ]
        states = [absorb(state, *got) for state, got in zip(states, made)]
        for (head, cont), state in zip(work, states):
            store_state(*after[cont], head, state)
        return carry

    lax.fori_loop(0, heads // together, some_heads, 0)


def hand_on(before, after):
    for source_ref, target_ref in zip(before, after):
        target_ref[...] = source_ref[...]


def by_cont(refs, chosen=None):
    chosen = range(len(refs) // 2) if chosen is None else chosen
    return {cont: refs[2 * i : 2 * i + 2] for i, cont in enumerate(chosen)}


def middle_kernel(
    step, part, sources, conts, chosen, pieces, with_weight, lists_ref, counts_ref, *refs
):
    count = len(chosen)
    q_refs, refs = dict(zip(chosen, refs)), refs[count:]
    held, refs = refs[:pieces], refs[pieces:]
    before, refs = refs[: 2 * count], refs[2 * count :]
    if with_weight:
        weight_ref, *refs = refs
    after, refs = refs[: 2 * count], refs[2 * count :]
    if with_weight:
        keep_ref, flipped_ref, sems = refs
        first = 1 if part == 0 else 0
        copies = start_all(weight_copies(weight_ref, keep_ref, sems, False, first))
    else:
        (flipped_ref,) = refs
    source, valid = arrivals(step, sources)[part]

    def absorb_part():
        shard = ((conts, sources, source), lists_ref, counts_ref, q_refs, held, flipped_ref)
        absorb_shard(*shard, by_cont(before, chosen), by_cont(after, chosen))

    if valid is True:
        absorb_part()
    else:
        pl.when(valid)(absorb_part)
        pl.when(jnp.logical_not(valid))(lambda: hand_on(before, after))
    if with_weight:
        for copy in copies:
            copy.wait()


def finish_and_give(acc_ref, stat_ref, weight_ref, attended_ref, give_refs):
    for head in range(attended_ref.shape[1] // HD):
        _, total, acc = load_state(acc_ref, stat_ref, head)
        attended_ref[:, head * HD : (head + 1) * HD] = (acc * (1.0 / total)).T.astype(
            jnp.bfloat16
        )
    rows = give_refs[0].shape[1]
    for k in range(1, weight_ref.shape[0]):
        made = jnp.dot(
            attended_ref[...], weight_ref[k], preferred_element_type=jnp.float32
        ).astype(jnp.bfloat16)
        for i, give_ref in enumerate(give_refs):
            give_ref[k - 1] = made[i * rows : (i + 1) * rows]


def last_kernel(
    step,
    sources,
    conts,
    cont,
    pieces,
    lists_ref,
    counts_ref,
    q_ref,
    mine_keys_ref,
    mine_values_ref,
    their_keys_ref,
    their_values_ref,
    acc_in,
    stat_in,
    give_weight_ref,
    *refs,
):
    attended_ref, give_refs, refs = refs[0], refs[1 : 1 + pieces], refs[1 + pieces :]
    acc_ref, stat_ref, flipped_ref = refs
    before, after = (acc_in, stat_in), (acc_ref, stat_ref)
    one_of_two = sources == 4
    for part, (source, valid) in enumerate(arrivals(step, sources)):

        def absorb_part():
            held = (
                (mine_keys_ref, mine_values_ref),
                (their_keys_ref, their_values_ref),
            )[part]
            shard = ((conts, sources, source), lists_ref, counts_ref, {cont: q_ref}, held)
            first = part == 0 or one_of_two
            absorb_shard(
                *shard, flipped_ref, {cont: before if first else after}, {cont: after}
            )

        pl.when(valid)(absorb_part)
        if part == 0 and not one_of_two:
            pl.when(jnp.logical_not(valid))(lambda: hand_on(before, after))
    finish_and_give(acc_ref, stat_ref, give_weight_ref, attended_ref, give_refs)


def from_sibling(got_refs, k):
    return jnp.concatenate([ref[k] for ref in got_refs], axis=0).astype(jnp.float32)


def onward_kernel(pieces, attended_ref, weight_ref, *refs):
    got_refs, onward_refs = refs[:pieces], refs[pieces:]
    for k, onward_ref in enumerate(onward_refs, 1):
        onward_ref[...] = (
            jnp.dot(attended_ref[...], weight_ref[k - 1], preferred_element_type=jnp.float32)
            + from_sibling(got_refs, k - 1)
        ).astype(jnp.bfloat16)


def attended_rows(refs):
    return jnp.concatenate([ref[...] for ref in refs], axis=0)


def give_near_kernel(conts, *refs):
    attended_refs, weight_ref, give_refs = refs[:conts], refs[conts], refs[conts + 1 :]
    made = jnp.dot(
        attended_rows(attended_refs), weight_ref[0], preferred_element_type=jnp.float32
    ).astype(jnp.bfloat16)
    rows = give_refs[0].shape[0]
    for i, give_ref in enumerate(give_refs):
        give_ref[...] = made[i * rows : (i + 1) * rows]


def near_kernel(conts, pieces, *refs):
    attended_refs, weight_ref, residual_ref = refs[:conts], refs[conts], refs[conts + 1]
    got_refs, refs = refs[conts + 2 : conts + 2 + pieces], refs[conts + 2 + pieces :]
    near_refs, (own_ref, sem) = refs[:conts], refs[conts:]
    length, share = near_refs[0].shape
    start = pl.multiple_of(lax.axis_index("tp") * share, HD)
    copy = pltpu.make_async_copy(
        residual_ref.at[:, :, pl.ds(start, share)], own_ref, sem.at[0]
    )
    copy.start()
    made = jnp.dot(
        attended_rows(attended_refs), weight_ref[0], preferred_element_type=jnp.float32
    ) + attended_rows(got_refs).astype(jnp.float32)
    for cont, near_ref in enumerate(near_refs):
        near_ref[...] = made[cont * length : (cont + 1) * length]
    copy.wait()
    for cont, near_ref in enumerate(near_refs):
        near_ref[...] += own_ref[cont].astype(jnp.float32)


def sum_kernel(near_ref, *refs):
    far_refs, (total_ref, squares_ref) = refs[:-2], refs[-2:]
    total = near_ref[...]
    for far_ref in far_refs:
        total = total + far_ref[...].astype(jnp.float32)
    total_ref[...] = total
    sums = jnp.sum(total * total, axis=1, keepdims=True)
    squares_ref[...] = jnp.broadcast_to(sums, (sums.shape[0], HD)).T[:8]


def stream_kernel(conts, *refs):
    for cont in range(conts):
        refs[conts][cont] = refs[cont][...].astype(jnp.bfloat16)


def norm_kernel(conts, model_width, *refs):
    totals, squares = refs[:conts], refs[conts:-2]
    gain_ref, normed_ref = refs[-2:]
    gain = gain_ref[...].astype(jnp.float32)
    for cont in range(conts):
        row = functools.reduce(jnp.add, [ref[cont * 8 : cont * 8 + 1, :] for ref in squares])
        scale = lax.rsqrt(row / model_width + 1e-05)
        scale = jnp.broadcast_to(scale, (HD, scale.shape[1])).T[:, 0:1]
        total = totals[cont][...]
        normed_ref[cont] = (total * scale * gain).astype(jnp.bfloat16)


def shards(
    queries,
    cont_keys,
    cont_values,
    prompt_keys,
    prompt_values,
    block_lists,
    tile_counts,
    out_weight,
    residual,
    norm_gain,
    *,
    sources,
    members,
):
    conts, length, width = queries.shape
    heads = width // HD
    rows_dev = prompt_keys.shape[0]
    model_width = residual.shape[2]
    share = norm_gain.shape[0]
    chips = members // CORES
    place = lax.axis_index("tp")
    pairs = heads * conts
    params = pltpu.CompilerParams(vmem_limit_bytes=VMEM_LIMIT)
    vmem = pl.BlockSpec(memory_space=pltpu.VMEM)
    hbm = pl.BlockSpec(memory_space=pltpu.HBM)

    def array(shape, dtype):
        return jax.ShapeDtypeStruct(shape, dtype)

    def cost(flops=1024):
        return pl.CostEstimate(flops=flops, bytes_accessed=1024, transcendentals=0)

    def in_hbm(x):
        return pltpu.with_memory_space_constraint(x, pltpu.HBM)

    kept = array((rows_dev, HD), jnp.bfloat16)
    keys = pl.pallas_call(
        functools.partial(pack_keys_kernel, heads),
        out_shape=kept,
        in_specs=[hbm],
        out_specs=vmem,
        scratch_shapes=[pltpu.SemaphoreType.DMA((1,))],
        compiler_params=params,
        cost_estimate=cost(),
        name="pack_keys",
    )(in_hbm(prompt_keys))
    values = pl.pallas_call(
        functools.partial(pack_values_kernel, heads),
        out_shape=kept,
        in_specs=[hbm],
        out_specs=vmem,
        scratch_shapes=[
            pltpu.VMEM((rows_dev, HD), jnp.bfloat16),
            pltpu.SemaphoreType.DMA((1,)),
        ],
        compiler_params=params,
        cost_estimate=cost(),
        name="pack_values",
    )(in_hbm(prompt_values))

    def across(step):
        def target(z, t):
            if sources == 4 and step == 1:
                return z ^ (1 + t % CORES)
            if sources == 4:
                return z ^ 1 if t % CORES == 1 else None
            to = z + step if t % CORES == 0 else z - step
            return to if 0 <= to < sources else None

        return [
            (z * members + t, target(z, t) * members + t)
            for z in range(sources)
            for t in range(members)
            if target(z, t) is not None
        ]

    sibling = [(t, t ^ 1) for t in range(members)]
    steps = steps_of(sources)
    smem = pl.BlockSpec(memory_space=pltpu.SMEM)
    lists = block_lists.reshape(-1)
    counts = tile_counts.reshape(-1)
    state_shape = (
        array((heads, HD, length), jnp.float32),
        array((heads, 8, length), jnp.float32),
    )
    flipped = pltpu.VMEM((2 * rows_dev, HD), jnp.bfloat16)
    weight_shape = array((chips, width, share), jnp.bfloat16)

    made = pl.pallas_call(
        functools.partial(first_kernel, sources, conts),
        out_shape=state_shape * conts
        + (array((heads, HD, length), jnp.bfloat16),) * conts
        + (weight_shape,),
        in_specs=[smem, smem, vmem, vmem] + [hbm] * 4,
        out_specs=(vmem,) * (3 * conts + 1),
        scratch_shapes=[
            flipped,
            pltpu.VMEM(queries.shape, jnp.bfloat16),
            pltpu.VMEM((conts, length, HD), jnp.bfloat16),
            pltpu.VMEM((conts, length, HD), jnp.bfloat16),
            pltpu.VMEM((conts, HD, length), jnp.bfloat16),
            pltpu.SemaphoreType.DMA((3,)),
            pltpu.SemaphoreType.DMA((chips,)),
        ],
        compiler_params=params,
        cost_estimate=cost(),
        name="attend_own",
    )(
        lists,
        counts,
        keys,
        values,
        in_hbm(queries),
        in_hbm(cont_keys),
        in_hbm(cont_values),
        in_hbm(out_weight),
    )
    states = tuple(made[2 * c : 2 * c + 2] for c in range(conts))
    *qs, give_weight = made[2 * conts :]

    def attend_step(step, part, chosen, with_weight, states, held):
        flat = [x for cont in chosen for x in states[cont]]
        count = len(chosen)
        kept = array((chips - 1 if part == 0 else 1, width, share), jnp.bfloat16)
        made = pl.pallas_call(
            functools.partial(
                middle_kernel, step, part, sources, conts, chosen, len(held), with_weight
            ),
            out_shape=state_shape * count + (kept,) * with_weight,
            in_specs=[smem, smem] + [vmem] * (3 * count + len(held)) + [hbm] * with_weight,
            out_specs=(vmem,) * (2 * count + with_weight),
            scratch_shapes=[flipped] + [pltpu.SemaphoreType.DMA(kept.shape[:1])] * with_weight,
            compiler_params=params,
            cost_estimate=cost(),
            name="attend_step",
        )(
            lists,
            counts,
            *[qs[cont] for cont in chosen],
            *held,
            *flat,
            *([in_hbm(out_weight)] * with_weight),
        )
        states = list(states)
        for i, cont in enumerate(chosen):
            states[cont] = tuple(made[2 * i : 2 * i + 2])
        return tuple(states), made[2 * count :]

    everyone = tuple(range(conts))
    mine, theirs = (keys, values), None
    for step in range(1, steps + 1):
        sent = mine if sources == 4 and step == 2 else (keys, values)
        mine_keys, mine_values = [lax.ppermute(x, ("ctx", "tp"), across(step)) for x in sent]
        mine_keys, states, theirs = lax.optimization_barrier((mine_keys, states, theirs))
        their_keys = lax.ppermute(mine_keys, "tp", sibling)
        mine_values, states = lax.optimization_barrier((mine_values, states))
        their_values = [
            lax.ppermute(x, "tp", sibling)
            for x in jnp.split(mine_values, 2 if step < steps else 1)
        ]
        before, mine = mine, (mine_keys, mine_values)
        rest, theirs = theirs, (their_keys, *their_values)
        if step > 1:
            states, _ = attend_step(step - 1, 0, everyone[1:], False, states, before)
            theirs, states = lax.optimization_barrier((theirs, states))
            states, made = attend_step(step - 1, 1, everyone[1:], step == 2, states, rest)
            keep_own = made[0] if step == 2 else keep_own
        if step < steps:
            states, made = attend_step(step, 0, everyone[:1], step == 1, states, mine)
            states, _ = attend_step(step, 1, everyone[:1], False, states, theirs)
            keep_far = made[0] if step == 1 else keep_far

    def attend_last(cont, state):
        pieces = swap_pieces[cont]
        made = pl.pallas_call(
            functools.partial(last_kernel, steps, sources, conts, cont, pieces),
            out_shape=(array((length, width), jnp.bfloat16),)
            + (array((chips - 1, length // pieces, share), jnp.bfloat16),) * pieces,
            in_specs=[smem, smem] + [vmem] * 8,
            out_specs=(vmem,) * (1 + pieces),
            scratch_shapes=[pltpu.VMEM(a.shape, a.dtype) for a in state_shape]
            + [flipped],
            compiler_params=params,
            cost_estimate=cost(),
            name="attend_last",
        )(
            lists,
            counts,
            qs[cont],
            *mine,
            *theirs,
            *state,
            give_weight,
        )
        return made[0], made[1:]

    def onward(attended, got):
        parts = pl.pallas_call(
            functools.partial(onward_kernel, len(got)),
            out_shape=(array((length, share), jnp.bfloat16),) * (chips - 1),
            in_specs=[vmem] * (2 + len(got)),
            out_specs=(vmem,) * (chips - 1),
            compiler_params=params,
            cost_estimate=cost(),
            name="project_onward",
        )(attended, keep_far, *got)
        far = []
        for k in range(1, chips):
            to_chip = [
                (t, (t // CORES + k) % chips * CORES + t % CORES) for t in range(members)
            ]
            far.append(lax.ppermute(parts[k - 1], "tp", to_chip))
        return parts, far

    def give_near(attended, pieces):
        return pl.pallas_call(
            functools.partial(give_near_kernel, conts),
            out_shape=(array((conts * length // pieces, share), jnp.bfloat16),) * pieces,
            in_specs=[vmem] * (conts + 1),
            out_specs=(vmem,) * pieces,
            compiler_params=params,
            cost_estimate=cost(2**35),
            name="give_near",
        )(*attended, give_weight)

    def near(attended, got):
        return pl.pallas_call(
            functools.partial(near_kernel, conts, len(got)),
            out_shape=(array((length, share), jnp.float32),) * conts,
            in_specs=[vmem] * (conts + 1) + [hbm] + [vmem] * len(got),
            out_specs=(vmem,) * conts,
            scratch_shapes=[
                pltpu.VMEM((conts, length, share), jnp.bfloat16),
                pltpu.SemaphoreType.DMA((1,)),
            ],
            compiler_params=params,
            cost_estimate=cost(),
            name="project_near",
        )(*attended, keep_own, in_hbm(residual), *got)

    swap_pieces = [1] + [2] * (conts - 1)
    attended, give = attend_last(0, states[0])
    all_attended, fars = [], []
    for cont in range(conts):
        got = [lax.ppermute(x, "tp", sibling) for x in give]
        if cont + 1 < conts:
            got, state = lax.optimization_barrier((got, states[cont + 1]))
        parts, far = onward(attended, got)
        all_attended.append(attended)
        fars.append(far)
        if cont + 1 < conts:
            state, parts = lax.optimization_barrier((state, parts))
            attended, give = attend_last(cont + 1, state)
    all_attended, fars[:-1], _ = lax.optimization_barrier((all_attended, fars[:-1], parts))
    got = [lax.ppermute(x, "tp", sibling) for x in give_near(all_attended, 2 * conts)]
    nears = near(all_attended, got)

    totals, squares = [], []
    for cont in range(conts):
        total, square = pl.pallas_call(
            sum_kernel,
            out_shape=(array((length, share), jnp.float32), array((8, length), jnp.float32)),
            in_specs=[vmem] * (1 + len(fars[cont])),
            out_specs=(vmem,) * 2,
            compiler_params=params,
            cost_estimate=cost(),
            name="add_up",
        )(nears[cont], *fars[cont])
        totals.append(total)
        squares.append(square)
    squares = jnp.concatenate(squares, axis=0)
    squares = squares + lax.ppermute(squares, "tp", sibling)
    all_squares = [squares] + [
        lax.ppermute(
            squares,
            "tp",
            [(t, (t // CORES + k) % chips * CORES + t % CORES) for t in range(members)],
        )
        for k in range(1, chips)
    ]
    out = array((conts, length, share), jnp.bfloat16)
    stream = pl.pallas_call(
        functools.partial(stream_kernel, conts),
        out_shape=out,
        in_specs=[vmem] * conts,
        out_specs=vmem,
        compiler_params=params,
        cost_estimate=cost(),
        name="stream",
    )(*totals)
    normed = pl.pallas_call(
        functools.partial(norm_kernel, conts, model_width),
        out_shape=out,
        in_specs=[vmem] * (conts + chips + 1),
        out_specs=vmem,
        compiler_params=params,
        cost_estimate=cost(),
        name="norm",
    )(*totals, *all_squares, norm_gain.reshape(1, share))
    return stream, normed


def solution(mesh):
    placed = (
        P(("grp", "ctx"), None, "tp"),
        P(("grp", "ctx"), None, None),
        P(("grp", "ctx"), None, None),
        P(("grp", "ctx"), None),
        P(("grp", "ctx"), None),
        P("tp", ("grp", "ctx"), None, None),
        P("tp", ("grp", "ctx"), None),
        P("tp", None),
        P(("grp", "ctx"), None, None),
        P("tp"),
    )
    return jax.shard_map(
        functools.partial(
            shards, sources=mesh.shape["ctx"], members=mesh.shape["tp"]
        ),
        mesh=mesh,
        in_specs=placed,
        out_specs=(P(("grp", "ctx"), None, "tp"), P(("grp", "ctx"), None, "tp")),
        check_vma=False,
    )
```

```python
import functools
import math

import jax
import jax.numpy as jnp
from jax import lax
from jax.experimental import pallas as pl
from jax.experimental.pallas import tpu as pltpu
from jax.sharding import PartitionSpec as P

HEADS = 32
KVH = 2
HD = 128
BLK = 64
TILES = 8
CORES = 2
TOGETHER = 8

VERY_LOW = -1e30
TO_LOG2 = math.log2(math.e) / math.sqrt(HD)

VMEM_LIMIT = 24 * 1024 * 1024


def key_group(heads):
    return lax.axis_index("tp") * heads // (HEADS // KVH)


def group_lanes(heads):
    return pl.ds(pl.multiple_of(key_group(heads) * HD, HD), HD)


def pack_keys_kernel(heads, keys_ref, packed_ref, sems):
    copy = pltpu.make_async_copy(keys_ref.at[:, group_lanes(heads)], packed_ref, sems.at[0])
    copy.start()
    copy.wait()


def pack_values_kernel(heads, values_ref, packed_ref, values_buf, sems):
    copy = pltpu.make_async_copy(values_ref.at[:, group_lanes(heads)], values_buf, sems.at[0])
    copy.start()
    copy.wait()
    for p in range(packed_ref.shape[0] // HD):
        rows = slice(p * HD, (p + 1) * HD)
        packed_ref[rows, :] = values_buf[rows, :].T


def both_ways(values_refs, flipped_ref):
    total = flipped_ref.shape[0] // 2
    for part, values_ref in enumerate(values_refs):
        rows = values_ref.shape[0]
        for p in range(rows // HD):
            pair = values_ref[p * HD : (p + 1) * HD, :]
            at = part * rows + p * HD
            flipped_ref[at : at + HD, :] = pair
            flipped_ref[total + at : total + at + HD, :] = jnp.concatenate(
                [pair[:, BLK:], pair[:, :BLK]], axis=1
            )


def shard_scores(lists_ref, counts_ref, q_refs, keys_ref, flipped_ref, place, head, cont):
    pairs = keys_ref.shape[0] // HD
    conts, sources, source = place
    at = (head * conts + cont) * sources + source
    count = counts_ref[at]
    blocks = [lists_ref[at * TILES + t] for t in range(TILES)]
    keys = jnp.concatenate(
        [keys_ref[pl.ds(pl.multiple_of(b * BLK, BLK), BLK), :] for b in blocks], axis=0
    )
    scores = jnp.dot(keys, q_refs[cont][head], preferred_element_type=jnp.float32)
    lane = lax.broadcasted_iota(jnp.int32, (HD, HD), 1)
    halves = []
    for t, b in enumerate(blocks):
        spot = ((b + t) % 2 * pairs + b // 2) * HD
        halves.append(flipped_ref[pl.ds(pl.multiple_of(spot, HD), HD), :])
    values = jnp.concatenate(
        [jnp.where(lane < BLK, a, b) for a, b in zip(halves[::2], halves[1::2])], axis=1
    )
    tiles = [
        (scores[t * BLK : (t + 1) * BLK], t < count) for t in range(TILES)
    ]
    return tiles, values


def fold(op, tile):
    return functools.reduce(op, [tile[i : i + 8] for i in range(0, tile.shape[0], 8)])


def absorb(state, tiles, values):
    top, total, acc = state
    tops = [
        jnp.where(live, fold(jnp.maximum, tile), VERY_LOW) for tile, live in tiles
    ]
    best = jnp.max(functools.reduce(jnp.maximum, tops), axis=0, keepdims=True)
    new_top = jnp.maximum(top, best)
    weights = [
        jnp.exp2((tile - jnp.where(live, new_top, -VERY_LOW)) * TO_LOG2) for tile, live in tiles
    ]
    factor = jnp.exp2((top - new_top) * TO_LOG2)
    sums = functools.reduce(jnp.add, [fold(jnp.add, w) for w in weights])
    total = total * factor + jnp.sum(sums, axis=0, keepdims=True)
    rounded = jnp.concatenate([w.astype(jnp.bfloat16) for w in weights], axis=0)
    acc = acc * factor + jnp.dot(values, rounded, preferred_element_type=jnp.float32)
    return new_top, total, acc


def load_state(acc_ref, stat_ref, index):
    both = stat_ref[index]
    return both[0:1], both[1:2], acc_ref[index]


def store_state(acc_ref, stat_ref, index, state):
    top, total, acc = state
    stat_ref[index] = jnp.concatenate([top, total] + [total] * 6, axis=0)
    acc_ref[index] = acc


def start_all(copies):
    for copy in copies:
        copy.start()
    return copies


def weight_copies(weight_ref, target, sems, sibling):
    count, _, share = target.shape
    chips = weight_ref.shape[1] // (CORES * share)
    place = lax.axis_index("tp")
    chip, core = place // CORES, place % CORES
    held = 1 - core if sibling else core
    copies = []
    for k in range(count):
        start = (lax.rem(chip + k, chips) * CORES + held) * share
        copies.append(
            pltpu.make_async_copy(
                weight_ref.at[:, pl.ds(pl.multiple_of(start, HD), share)],
                target.at[k],
                sems.at[k],
            )
        )
    return copies


def first_kernel(
    sources,
    conts,
    lists_ref,
    counts_ref,
    keys_ref,
    values_ref,
    queries_ref,
    cont_keys_ref,
    cont_values_ref,
    weight_ref,
    *refs,
):
    states, refs = by_cont(refs[: 2 * conts]), refs[2 * conts :]
    q_refs, refs = refs[:conts], refs[conts:]
    give_ref, weight_sems, *refs = refs[0], refs[-1], *refs[1:-1]
    flipped_ref, rows_ref, ck_ref, cv_ref, own_ref, sems = refs
    heads, _, length = q_refs[0].shape
    lanes = group_lanes(heads)
    copies = start_all(
        [
            pltpu.make_async_copy(cont_values_ref.at[:, :, lanes], cv_ref, sems.at[0]),
            pltpu.make_async_copy(queries_ref, rows_ref, sems.at[1]),
            pltpu.make_async_copy(cont_keys_ref.at[:, :, lanes], ck_ref, sems.at[2]),
        ]
    )
    fetched = start_all(weight_copies(weight_ref, give_ref, weight_sems, True))
    place = conts, sources, lax.axis_index("ctx")
    both_ways([values_ref], flipped_ref)
    copies[0].wait()
    for cont in range(conts):
        own_ref[cont] = cv_ref[cont].T
    copies[1].wait()
    for cont in range(conts):
        for head in range(heads):
            q_refs[cont][head] = rows_ref[cont, :, head * HD : (head + 1) * HD].T
    for copy in copies[2:]:
        copy.wait()
    together = TOGETHER // conts

    def some_heads(index, carry):
        work = [(index * together + j, cont) for j in range(together) for cont in range(conts)]
        made = []
        for head, cont in work:
            scores = jnp.dot(
                ck_ref[cont], q_refs[cont][head], preferred_element_type=jnp.float32
            )
            key = lax.broadcasted_iota(jnp.int32, scores.shape, 0)
            row = lax.broadcasted_iota(jnp.int32, scores.shape, 1)
            scores = jnp.where(key <= row, scores, VERY_LOW)
            tiles, values = shard_scores(
                lists_ref, counts_ref, q_refs, keys_ref, flipped_ref, place, head, cont
            )
            made.append(
                ([(scores, True)] + tiles, jnp.concatenate([own_ref[cont], values], axis=1))
            )
        after = []
        for got in made:
            start = (
                jnp.full((1, length), VERY_LOW, jnp.float32),
                jnp.zeros((1, length), jnp.float32),
                jnp.zeros((HD, length), jnp.float32),
            )
            after.append(absorb(start, *got))
        for (head, cont), state in zip(work, after):
            store_state(*states[cont], head, state)
        return carry

    lax.fori_loop(0, heads // together, some_heads, 0)
    for copy in fetched:
        copy.wait()


def arrivals(step, sources):
    spot = lax.axis_index("ctx")
    core = lax.axis_index("tp") % CORES
    if sources == 4:
        if step == 1:
            mine = jnp.bitwise_xor(spot, 1 + core)
            return ((mine, True), (jnp.bitwise_xor(mine, 3), True))
        far = jnp.bitwise_xor(spot, 3)
        return ((far, core == 1), (far, core == 0))
    mine = jnp.where(core == 0, spot - step, spot + step)
    theirs = jnp.where(core == 0, spot + step, spot - step)
    return tuple((s, (s >= 0) & (s < sources)) for s in (mine, theirs))


def steps_of(sources):
    return 2 if sources == 4 else sources - 1


def absorb_shard(place, lists_ref, counts_ref, q_refs, held, flipped_ref, before, after):
    keys_ref, *values_refs = held
    heads = next(iter(q_refs.values())).shape[0]
    together = min(heads, TOGETHER // len(q_refs))
    both_ways(values_refs, flipped_ref)

    def some_heads(index, carry):
        work = [(index * together + j, cont) for j in range(together) for cont in q_refs]
        states = [load_state(*before[cont], head) for head, cont in work]
        made = [
            shard_scores(lists_ref, counts_ref, q_refs, keys_ref, flipped_ref, place, head, cont)
            for head, cont in work
        ]
        states = [absorb(state, *got) for state, got in zip(states, made)]
        for (head, cont), state in zip(work, states):
            store_state(*after[cont], head, state)
        return carry

    lax.fori_loop(0, heads // together, some_heads, 0)


def hand_on(before, after):
    for source_ref, target_ref in zip(before, after):
        target_ref[...] = source_ref[...]


def by_cont(refs, chosen=None):
    chosen = range(len(refs) // 2) if chosen is None else chosen
    return {cont: refs[2 * i : 2 * i + 2] for i, cont in enumerate(chosen)}


def middle_kernel(
    step, part, sources, conts, chosen, pieces, with_weight, lists_ref, counts_ref, *refs
):
    count = len(chosen)
    q_refs, refs = dict(zip(chosen, refs)), refs[count:]
    held, refs = refs[:pieces], refs[pieces:]
    before, refs = refs[: 2 * count], refs[2 * count :]
    if with_weight:
        weight_ref, *refs = refs
    after, refs = refs[: 2 * count], refs[2 * count :]
    if with_weight:
        keep_ref, flipped_ref, sems = refs
        copies = start_all(weight_copies(weight_ref, keep_ref, sems, False))
    else:
        (flipped_ref,) = refs
    source, valid = arrivals(step, sources)[part]

    def absorb_part():
        shard = ((conts, sources, source), lists_ref, counts_ref, q_refs, held, flipped_ref)
        absorb_shard(*shard, by_cont(before, chosen), by_cont(after, chosen))

    if valid is True:
        absorb_part()
    else:
        pl.when(valid)(absorb_part)
        pl.when(jnp.logical_not(valid))(lambda: hand_on(before, after))
    if with_weight:
        for copy in copies:
            copy.wait()


def finish_and_give(acc_ref, stat_ref, weight_ref, attended_ref, give_refs):
    for head in range(attended_ref.shape[1] // HD):
        _, total, acc = load_state(acc_ref, stat_ref, head)
        attended_ref[:, head * HD : (head + 1) * HD] = (acc * (1.0 / total)).T.astype(
            jnp.bfloat16
        )
    rows = give_refs[0].shape[1]
    for k in range(1, weight_ref.shape[0]):
        made = jnp.dot(
            attended_ref[...], weight_ref[k], preferred_element_type=jnp.float32
        ).astype(jnp.bfloat16)
        for i, give_ref in enumerate(give_refs):
            give_ref[k - 1] = made[i * rows : (i + 1) * rows]


def last_kernel(
    step,
    sources,
    conts,
    cont,
    pieces,
    lists_ref,
    counts_ref,
    q_ref,
    mine_keys_ref,
    mine_values_ref,
    their_keys_ref,
    their_values_ref,
    acc_in,
    stat_in,
    give_weight_ref,
    *refs,
):
    attended_ref, give_refs, refs = refs[0], refs[1 : 1 + pieces], refs[1 + pieces :]
    acc_ref, stat_ref, flipped_ref = refs
    before, after = (acc_in, stat_in), (acc_ref, stat_ref)
    one_of_two = sources == 4
    for part, (source, valid) in enumerate(arrivals(step, sources)):

        def absorb_part():
            held = (
                (mine_keys_ref, mine_values_ref),
                (their_keys_ref, their_values_ref),
            )[part]
            shard = ((conts, sources, source), lists_ref, counts_ref, {cont: q_ref}, held)
            first = part == 0 or one_of_two
            absorb_shard(
                *shard, flipped_ref, {cont: before if first else after}, {cont: after}
            )

        pl.when(valid)(absorb_part)
        if part == 0 and not one_of_two:
            pl.when(jnp.logical_not(valid))(lambda: hand_on(before, after))
    finish_and_give(acc_ref, stat_ref, give_weight_ref, attended_ref, give_refs)


def from_sibling(got_refs, k):
    return jnp.concatenate([ref[k] for ref in got_refs], axis=0).astype(jnp.float32)


def onward_kernel(pieces, attended_ref, weight_ref, *refs):
    got_refs, onward_refs = refs[:pieces], refs[pieces:]
    for k, onward_ref in enumerate(onward_refs, 1):
        onward_ref[...] = (
            jnp.dot(attended_ref[...], weight_ref[k], preferred_element_type=jnp.float32)
            + from_sibling(got_refs, k - 1)
        ).astype(jnp.bfloat16)


def attended_rows(refs):
    return jnp.concatenate([ref[...] for ref in refs], axis=0)


def give_near_kernel(conts, *refs):
    attended_refs, weight_ref, give_refs = refs[:conts], refs[conts], refs[conts + 1 :]
    made = jnp.dot(
        attended_rows(attended_refs), weight_ref[0], preferred_element_type=jnp.float32
    ).astype(jnp.bfloat16)
    rows = give_refs[0].shape[0]
    for i, give_ref in enumerate(give_refs):
        give_ref[...] = made[i * rows : (i + 1) * rows]


def near_kernel(conts, pieces, *refs):
    attended_refs, weight_ref, residual_ref = refs[:conts], refs[conts], refs[conts + 1]
    got_refs, refs = refs[conts + 2 : conts + 2 + pieces], refs[conts + 2 + pieces :]
    near_refs, (own_ref, sem) = refs[:conts], refs[conts:]
    length, share = near_refs[0].shape
    start = pl.multiple_of(lax.axis_index("tp") * share, HD)
    copy = pltpu.make_async_copy(
        residual_ref.at[:, :, pl.ds(start, share)], own_ref, sem.at[0]
    )
    copy.start()
    made = jnp.dot(
        attended_rows(attended_refs), weight_ref[0], preferred_element_type=jnp.float32
    ) + attended_rows(got_refs).astype(jnp.float32)
    for cont, near_ref in enumerate(near_refs):
        near_ref[...] = made[cont * length : (cont + 1) * length]
    copy.wait()
    for cont, near_ref in enumerate(near_refs):
        near_ref[...] += own_ref[cont].astype(jnp.float32)


def sum_kernel(near_ref, *refs):
    far_refs, (total_ref, squares_ref) = refs[:-2], refs[-2:]
    total = near_ref[...]
    for far_ref in far_refs:
        total = total + far_ref[...].astype(jnp.float32)
    total_ref[...] = total
    sums = jnp.sum(total * total, axis=1, keepdims=True)
    squares_ref[...] = jnp.broadcast_to(sums, (sums.shape[0], HD)).T[:8]


def stream_kernel(conts, *refs):
    for cont in range(conts):
        refs[conts][cont] = refs[cont][...].astype(jnp.bfloat16)


def norm_kernel(conts, model_width, *refs):
    totals, squares = refs[:conts], refs[conts:-2]
    gain_ref, normed_ref = refs[-2:]
    gain = gain_ref[...].astype(jnp.float32)
    for cont in range(conts):
        row = functools.reduce(jnp.add, [ref[cont * 8 : cont * 8 + 1, :] for ref in squares])
        scale = lax.rsqrt(row / model_width + 1e-05)
        scale = jnp.broadcast_to(scale, (HD, scale.shape[1])).T[:, 0:1]
        total = totals[cont][...]
        normed_ref[cont] = (total * scale * gain).astype(jnp.bfloat16)


def shards(
    queries,
    cont_keys,
    cont_values,
    prompt_keys,
    prompt_values,
    block_lists,
    tile_counts,
    out_weight,
    residual,
    norm_gain,
    *,
    sources,
    members,
):
    conts, length, width = queries.shape
    heads = width // HD
    rows_dev = prompt_keys.shape[0]
    model_width = residual.shape[2]
    share = norm_gain.shape[0]
    chips = members // CORES
    place = lax.axis_index("tp")
    pairs = heads * conts
    params = pltpu.CompilerParams(vmem_limit_bytes=VMEM_LIMIT)
    vmem = pl.BlockSpec(memory_space=pltpu.VMEM)
    hbm = pl.BlockSpec(memory_space=pltpu.HBM)

    def array(shape, dtype):
        return jax.ShapeDtypeStruct(shape, dtype)

    def cost(flops=1024):
        return pl.CostEstimate(flops=flops, bytes_accessed=1024, transcendentals=0)

    def in_hbm(x):
        return pltpu.with_memory_space_constraint(x, pltpu.HBM)

    kept = array((rows_dev, HD), jnp.bfloat16)
    keys = pl.pallas_call(
        functools.partial(pack_keys_kernel, heads),
        out_shape=kept,
        in_specs=[hbm],
        out_specs=vmem,
        scratch_shapes=[pltpu.SemaphoreType.DMA((1,))],
        compiler_params=params,
        cost_estimate=cost(),
        name="pack_keys",
    )(in_hbm(prompt_keys))
    values = pl.pallas_call(
        functools.partial(pack_values_kernel, heads),
        out_shape=kept,
        in_specs=[hbm],
        out_specs=vmem,
        scratch_shapes=[
            pltpu.VMEM((rows_dev, HD), jnp.bfloat16),
            pltpu.SemaphoreType.DMA((1,)),
        ],
        compiler_params=params,
        cost_estimate=cost(),
        name="pack_values",
    )(in_hbm(prompt_values))

    def across(step):
        def target(z, t):
            if sources == 4 and step == 1:
                return z ^ (1 + t % CORES)
            if sources == 4:
                return z ^ 1 if t % CORES == 1 else None
            to = z + step if t % CORES == 0 else z - step
            return to if 0 <= to < sources else None

        return [
            (z * members + t, target(z, t) * members + t)
            for z in range(sources)
            for t in range(members)
            if target(z, t) is not None
        ]

    sibling = [(t, t ^ 1) for t in range(members)]
    steps = steps_of(sources)
    smem = pl.BlockSpec(memory_space=pltpu.SMEM)
    lists = block_lists.reshape(-1)
    counts = tile_counts.reshape(-1)
    state_shape = (
        array((heads, HD, length), jnp.float32),
        array((heads, 8, length), jnp.float32),
    )
    flipped = pltpu.VMEM((2 * rows_dev, HD), jnp.bfloat16)
    weight_shape = array((chips, width, share), jnp.bfloat16)

    made = pl.pallas_call(
        functools.partial(first_kernel, sources, conts),
        out_shape=state_shape * conts
        + (array((heads, HD, length), jnp.bfloat16),) * conts
        + (weight_shape,),
        in_specs=[smem, smem, vmem, vmem] + [hbm] * 4,
        out_specs=(vmem,) * (3 * conts + 1),
        scratch_shapes=[
            flipped,
            pltpu.VMEM(queries.shape, jnp.bfloat16),
            pltpu.VMEM((conts, length, HD), jnp.bfloat16),
            pltpu.VMEM((conts, length, HD), jnp.bfloat16),
            pltpu.VMEM((conts, HD, length), jnp.bfloat16),
            pltpu.SemaphoreType.DMA((3,)),
            pltpu.SemaphoreType.DMA((chips,)),
        ],
        compiler_params=params,
        cost_estimate=cost(),
        name="attend_own",
    )(
        lists,
        counts,
        keys,
        values,
        in_hbm(queries),
        in_hbm(cont_keys),
        in_hbm(cont_values),
        in_hbm(out_weight),
    )
    states = tuple(made[2 * c : 2 * c + 2] for c in range(conts))
    *qs, give_weight = made[2 * conts :]

    def attend_step(step, part, chosen, with_weight, states, held):
        flat = [x for cont in chosen for x in states[cont]]
        count = len(chosen)
        made = pl.pallas_call(
            functools.partial(
                middle_kernel, step, part, sources, conts, chosen, len(held), with_weight
            ),
            out_shape=state_shape * count + (weight_shape,) * with_weight,
            in_specs=[smem, smem] + [vmem] * (3 * count + len(held)) + [hbm] * with_weight,
            out_specs=(vmem,) * (2 * count + with_weight),
            scratch_shapes=[flipped] + [pltpu.SemaphoreType.DMA((chips,))] * with_weight,
            compiler_params=params,
            cost_estimate=cost(),
            name="attend_step",
        )(
            lists,
            counts,
            *[qs[cont] for cont in chosen],
            *held,
            *flat,
            *([in_hbm(out_weight)] * with_weight),
        )
        states = list(states)
        for i, cont in enumerate(chosen):
            states[cont] = tuple(made[2 * i : 2 * i + 2])
        return tuple(states), made[2 * count :]

    everyone = tuple(range(conts))
    mine, theirs = (keys, values), None
    for step in range(1, steps + 1):
        sent = mine if sources == 4 and step == 2 else (keys, values)
        mine_keys, mine_values = [lax.ppermute(x, ("ctx", "tp"), across(step)) for x in sent]
        mine_keys, states, theirs = lax.optimization_barrier((mine_keys, states, theirs))
        their_keys = lax.ppermute(mine_keys, "tp", sibling)
        mine_values, states = lax.optimization_barrier((mine_values, states))
        their_values = [
            lax.ppermute(x, "tp", sibling)
            for x in jnp.split(mine_values, 2 if step < steps else 1)
        ]
        mine = (mine_keys, mine_values)
        rest, theirs = theirs, (their_keys, *their_values)
        if step > 1:
            states, _ = attend_step(step - 1, 1, everyone[:1], False, states, rest)
            theirs, first = lax.optimization_barrier((theirs, states[0]))
            states = (first, *states[1:])
            states, _ = attend_step(step - 1, 1, everyone[1:], False, states, rest)
        if step < steps:
            states, made = attend_step(step, 0, everyone, step == 1, states, mine)
            keep_weight = made[0] if step == 1 else keep_weight

    def attend_last(cont, state):
        pieces = swap_pieces[cont]
        made = pl.pallas_call(
            functools.partial(last_kernel, steps, sources, conts, cont, pieces),
            out_shape=(array((length, width), jnp.bfloat16),)
            + (array((chips - 1, length // pieces, share), jnp.bfloat16),) * pieces,
            in_specs=[smem, smem] + [vmem] * 8,
            out_specs=(vmem,) * (1 + pieces),
            scratch_shapes=[pltpu.VMEM(a.shape, a.dtype) for a in state_shape]
            + [flipped],
            compiler_params=params,
            cost_estimate=cost(),
            name="attend_last",
        )(
            lists,
            counts,
            qs[cont],
            *mine,
            *theirs,
            *state,
            give_weight,
        )
        return made[0], made[1:]

    def onward(attended, got):
        parts = pl.pallas_call(
            functools.partial(onward_kernel, len(got)),
            out_shape=(array((length, share), jnp.bfloat16),) * (chips - 1),
            in_specs=[vmem] * (2 + len(got)),
            out_specs=(vmem,) * (chips - 1),
            compiler_params=params,
            cost_estimate=cost(),
            name="project_onward",
        )(attended, keep_weight, *got)
        far = []
        for k in range(1, chips):
            to_chip = [
                (t, (t // CORES + k) % chips * CORES + t % CORES) for t in range(members)
            ]
            far.append(lax.ppermute(parts[k - 1], "tp", to_chip))
        return parts, far

    def give_near(attended, pieces):
        return pl.pallas_call(
            functools.partial(give_near_kernel, conts),
            out_shape=(array((conts * length // pieces, share), jnp.bfloat16),) * pieces,
            in_specs=[vmem] * (conts + 1),
            out_specs=(vmem,) * pieces,
            compiler_params=params,
            cost_estimate=cost(2**35),
            name="give_near",
        )(*attended, give_weight)

    def near(attended, got):
        return pl.pallas_call(
            functools.partial(near_kernel, conts, len(got)),
            out_shape=(array((length, share), jnp.float32),) * conts,
            in_specs=[vmem] * (conts + 1) + [hbm] + [vmem] * len(got),
            out_specs=(vmem,) * conts,
            scratch_shapes=[
                pltpu.VMEM((conts, length, share), jnp.bfloat16),
                pltpu.SemaphoreType.DMA((1,)),
            ],
            compiler_params=params,
            cost_estimate=cost(),
            name="project_near",
        )(*attended, keep_weight, in_hbm(residual), *got)

    swap_pieces = [1] + [2] * (conts - 1)
    attended, give = attend_last(0, states[0])
    all_attended, fars = [], []
    for cont in range(conts):
        got = [lax.ppermute(x, "tp", sibling) for x in give]
        if cont + 1 < conts:
            got, state = lax.optimization_barrier((got, states[cont + 1]))
        parts, far = onward(attended, got)
        all_attended.append(attended)
        fars.append(far)
        if cont + 1 < conts:
            state, parts = lax.optimization_barrier((state, parts))
            attended, give = attend_last(cont + 1, state)
    all_attended, fars[:-1], _ = lax.optimization_barrier((all_attended, fars[:-1], parts))
    got = [lax.ppermute(x, "tp", sibling) for x in give_near(all_attended, 2 * conts)]
    nears = near(all_attended, got)

    totals, squares = [], []
    for cont in range(conts):
        total, square = pl.pallas_call(
            sum_kernel,
            out_shape=(array((length, share), jnp.float32), array((8, length), jnp.float32)),
            in_specs=[vmem] * (1 + len(fars[cont])),
            out_specs=(vmem,) * 2,
            compiler_params=params,
            cost_estimate=cost(),
            name="add_up",
        )(nears[cont], *fars[cont])
        totals.append(total)
        squares.append(square)
    squares = jnp.concatenate(squares, axis=0)
    squares = squares + lax.ppermute(squares, "tp", sibling)
    all_squares = [squares] + [
        lax.ppermute(
            squares,
            "tp",
            [(t, (t // CORES + k) % chips * CORES + t % CORES) for t in range(members)],
        )
        for k in range(1, chips)
    ]
    out = array((conts, length, share), jnp.bfloat16)
    stream = pl.pallas_call(
        functools.partial(stream_kernel, conts),
        out_shape=out,
        in_specs=[vmem] * conts,
        out_specs=vmem,
        compiler_params=params,
        cost_estimate=cost(),
        name="stream",
    )(*totals)
    normed = pl.pallas_call(
        functools.partial(norm_kernel, conts, model_width),
        out_shape=out,
        in_specs=[vmem] * (conts + chips + 1),
        out_specs=vmem,
        compiler_params=params,
        cost_estimate=cost(),
        name="norm",
    )(*totals, *all_squares, norm_gain.reshape(1, share))
    return stream, normed


def solution(mesh):
    placed = (
        P(("grp", "ctx"), None, "tp"),
        P(("grp", "ctx"), None, None),
        P(("grp", "ctx"), None, None),
        P(("grp", "ctx"), None),
        P(("grp", "ctx"), None),
        P("tp", ("grp", "ctx"), None, None),
        P("tp", ("grp", "ctx"), None),
        P("tp", None),
        P(("grp", "ctx"), None, None),
        P("tp"),
    )
    return jax.shard_map(
        functools.partial(
            shards, sources=mesh.shape["ctx"], members=mesh.shape["tp"]
        ),
        mesh=mesh,
        in_specs=placed,
        out_specs=(P(("grp", "ctx"), None, "tp"), P(("grp", "ctx"), None, "tp")),
        check_vma=False,
    )
```

```python
import functools
import math

import jax
import jax.numpy as jnp
from jax import lax
from jax.experimental import pallas as pl
from jax.experimental.pallas import tpu as pltpu
from jax.sharding import PartitionSpec as P

HEADS = 32
KVH = 2
HD = 128
BLK = 64
TILES = 8
CORES = 2
TOGETHER = 8

VERY_LOW = -1e30
TO_LOG2 = math.log2(math.e) / math.sqrt(HD)

VMEM_LIMIT = 24 * 1024 * 1024


def key_group(heads):
    return lax.axis_index("tp") * heads // (HEADS // KVH)


def group_lanes(heads):
    return pl.ds(pl.multiple_of(key_group(heads) * HD, HD), HD)


def pack_keys_kernel(heads, keys_ref, packed_ref, sems):
    copy = pltpu.make_async_copy(keys_ref.at[:, group_lanes(heads)], packed_ref, sems.at[0])
    copy.start()
    copy.wait()


def pack_values_kernel(heads, values_ref, packed_ref, values_buf, sems):
    copy = pltpu.make_async_copy(values_ref.at[:, group_lanes(heads)], values_buf, sems.at[0])
    copy.start()
    copy.wait()
    for p in range(packed_ref.shape[0] // HD):
        rows = slice(p * HD, (p + 1) * HD)
        packed_ref[rows, :] = values_buf[rows, :].T


def both_ways(values_refs, flipped_ref):
    total = flipped_ref.shape[0] // 2
    for part, values_ref in enumerate(values_refs):
        rows = values_ref.shape[0]
        for p in range(rows // HD):
            pair = values_ref[p * HD : (p + 1) * HD, :]
            at = part * rows + p * HD
            flipped_ref[at : at + HD, :] = pair
            flipped_ref[total + at : total + at + HD, :] = jnp.concatenate(
                [pair[:, BLK:], pair[:, :BLK]], axis=1
            )


def shard_scores(lists_ref, counts_ref, q_refs, keys_ref, flipped_ref, place, head, cont):
    pairs = keys_ref.shape[0] // HD
    conts, sources, source = place
    at = (head * conts + cont) * sources + source
    count = counts_ref[at]
    blocks = [lists_ref[at * TILES + t] for t in range(TILES)]
    keys = jnp.concatenate(
        [keys_ref[pl.ds(pl.multiple_of(b * BLK, BLK), BLK), :] for b in blocks], axis=0
    )
    scores = jnp.dot(keys, q_refs[cont][head], preferred_element_type=jnp.float32)
    lane = lax.broadcasted_iota(jnp.int32, (HD, HD), 1)
    halves = []
    for t, b in enumerate(blocks):
        spot = ((b + t) % 2 * pairs + b // 2) * HD
        halves.append(flipped_ref[pl.ds(pl.multiple_of(spot, HD), HD), :])
    values = jnp.concatenate(
        [jnp.where(lane < BLK, a, b) for a, b in zip(halves[::2], halves[1::2])], axis=1
    )
    tiles = [
        (scores[t * BLK : (t + 1) * BLK], t < count) for t in range(TILES)
    ]
    return tiles, values


def fold(op, tile):
    return functools.reduce(op, [tile[i : i + 8] for i in range(0, tile.shape[0], 8)])


def absorb(state, tiles, values):
    top, total, acc = state
    tops = [
        jnp.where(live, fold(jnp.maximum, tile), VERY_LOW) for tile, live in tiles
    ]
    best = jnp.max(functools.reduce(jnp.maximum, tops), axis=0, keepdims=True)
    new_top = jnp.maximum(top, best)
    weights = [
        jnp.exp2((tile - jnp.where(live, new_top, -VERY_LOW)) * TO_LOG2) for tile, live in tiles
    ]
    factor = jnp.exp2((top - new_top) * TO_LOG2)
    sums = functools.reduce(jnp.add, [fold(jnp.add, w) for w in weights])
    total = total * factor + jnp.sum(sums, axis=0, keepdims=True)
    rounded = jnp.concatenate([w.astype(jnp.bfloat16) for w in weights], axis=0)
    acc = acc * factor + jnp.dot(values, rounded, preferred_element_type=jnp.float32)
    return new_top, total, acc


def load_state(acc_ref, stat_ref, index):
    both = stat_ref[index]
    return both[0:1], both[1:2], acc_ref[index]


def store_state(acc_ref, stat_ref, index, state):
    top, total, acc = state
    stat_ref[index] = jnp.concatenate([top, total] + [total] * 6, axis=0)
    acc_ref[index] = acc


def start_all(copies):
    for copy in copies:
        copy.start()
    return copies


def weight_copies(weight_ref, target, sems, sibling):
    count, _, share = target.shape
    chips = weight_ref.shape[1] // (CORES * share)
    place = lax.axis_index("tp")
    chip, core = place // CORES, place % CORES
    held = 1 - core if sibling else core
    copies = []
    for k in range(count):
        start = (lax.rem(chip + k, chips) * CORES + held) * share
        copies.append(
            pltpu.make_async_copy(
                weight_ref.at[:, pl.ds(pl.multiple_of(start, HD), share)],
                target.at[k],
                sems.at[k],
            )
        )
    return copies


def first_kernel(
    sources,
    conts,
    lists_ref,
    counts_ref,
    keys_ref,
    values_ref,
    queries_ref,
    cont_keys_ref,
    cont_values_ref,
    weight_ref,
    *refs,
):
    states, refs = by_cont(refs[: 2 * conts]), refs[2 * conts :]
    q_refs, refs = refs[:conts], refs[conts:]
    (give_ref, keep_ref), weight_sems, refs = refs[:2], refs[-1], refs[2:-1]
    flipped_ref, rows_ref, ck_ref, cv_ref, own_ref, sems = refs
    heads, _, length = q_refs[0].shape
    lanes = group_lanes(heads)
    copies = start_all(
        [
            pltpu.make_async_copy(cont_values_ref.at[:, :, lanes], cv_ref, sems.at[0]),
            pltpu.make_async_copy(queries_ref, rows_ref, sems.at[1]),
            pltpu.make_async_copy(cont_keys_ref.at[:, :, lanes], ck_ref, sems.at[2]),
        ]
    )
    fetched = start_all(
        weight_copies(weight_ref, give_ref, weight_sems.at[0], True)
        + weight_copies(weight_ref, keep_ref, weight_sems.at[1], False)
    )
    place = conts, sources, lax.axis_index("ctx")
    both_ways([values_ref], flipped_ref)
    copies[0].wait()
    for cont in range(conts):
        own_ref[cont] = cv_ref[cont].T
    copies[1].wait()
    for cont in range(conts):
        for head in range(heads):
            q_refs[cont][head] = rows_ref[cont, :, head * HD : (head + 1) * HD].T
    for copy in copies[2:]:
        copy.wait()
    together = TOGETHER // conts

    def some_heads(index, carry):
        work = [(index * together + j, cont) for j in range(together) for cont in range(conts)]
        made = []
        for head, cont in work:
            scores = jnp.dot(
                ck_ref[cont], q_refs[cont][head], preferred_element_type=jnp.float32
            )
            key = lax.broadcasted_iota(jnp.int32, scores.shape, 0)
            row = lax.broadcasted_iota(jnp.int32, scores.shape, 1)
            scores = jnp.where(key <= row, scores, VERY_LOW)
            tiles, values = shard_scores(
                lists_ref, counts_ref, q_refs, keys_ref, flipped_ref, place, head, cont
            )
            made.append(
                ([(scores, True)] + tiles, jnp.concatenate([own_ref[cont], values], axis=1))
            )
        after = []
        for got in made:
            start = (
                jnp.full((1, length), VERY_LOW, jnp.float32),
                jnp.zeros((1, length), jnp.float32),
                jnp.zeros((HD, length), jnp.float32),
            )
            after.append(absorb(start, *got))
        for (head, cont), state in zip(work, after):
            store_state(*states[cont], head, state)
        return carry

    lax.fori_loop(0, heads // together, some_heads, 0)
    for copy in fetched:
        copy.wait()


def arrivals(step, sources):
    spot = lax.axis_index("ctx")
    core = lax.axis_index("tp") % CORES
    if sources == 4:
        if step == 1:
            mine = jnp.bitwise_xor(spot, 1 + core)
            return ((mine, True), (jnp.bitwise_xor(mine, 3), True))
        far = jnp.bitwise_xor(spot, 3)
        return ((far, core == 1), (far, core == 0))
    mine = jnp.where(core == 0, spot - step, spot + step)
    theirs = jnp.where(core == 0, spot + step, spot - step)
    return tuple((s, (s >= 0) & (s < sources)) for s in (mine, theirs))


def steps_of(sources):
    return 2 if sources == 4 else sources - 1


def absorb_shard(place, lists_ref, counts_ref, q_refs, held, flipped_ref, before, after):
    keys_ref, *values_refs = held
    heads = next(iter(q_refs.values())).shape[0]
    together = min(heads, TOGETHER // len(q_refs))
    both_ways(values_refs, flipped_ref)

    def some_heads(index, carry):
        work = [(index * together + j, cont) for j in range(together) for cont in q_refs]
        states = [load_state(*before[cont], head) for head, cont in work]
        made = [
            shard_scores(lists_ref, counts_ref, q_refs, keys_ref, flipped_ref, place, head, cont)
            for head, cont in work
        ]
        states = [absorb(state, *got) for state, got in zip(states, made)]
        for (head, cont), state in zip(work, states):
            store_state(*after[cont], head, state)
        return carry

    lax.fori_loop(0, heads // together, some_heads, 0)


def hand_on(before, after):
    for source_ref, target_ref in zip(before, after):
        target_ref[...] = source_ref[...]


def by_cont(refs, chosen=None):
    chosen = range(len(refs) // 2) if chosen is None else chosen
    return {cont: refs[2 * i : 2 * i + 2] for i, cont in enumerate(chosen)}


def middle_kernel(
    step, part, sources, conts, chosen, pieces, with_weight, lists_ref, counts_ref, *refs
):
    count = len(chosen)
    q_refs, refs = dict(zip(chosen, refs)), refs[count:]
    held, refs = refs[:pieces], refs[pieces:]
    before, refs = refs[: 2 * count], refs[2 * count :]
    if with_weight:
        weight_ref, *refs = refs
    after, refs = refs[: 2 * count], refs[2 * count :]
    if with_weight:
        keep_ref, flipped_ref, sems = refs
        copies = start_all(weight_copies(weight_ref, keep_ref, sems, False))
    else:
        (flipped_ref,) = refs
    source, valid = arrivals(step, sources)[part]

    def absorb_part():
        shard = ((conts, sources, source), lists_ref, counts_ref, q_refs, held, flipped_ref)
        absorb_shard(*shard, by_cont(before, chosen), by_cont(after, chosen))

    if valid is True:
        absorb_part()
    else:
        pl.when(valid)(absorb_part)
        pl.when(jnp.logical_not(valid))(lambda: hand_on(before, after))
    if with_weight:
        for copy in copies:
            copy.wait()


def finish_and_give(acc_ref, stat_ref, weight_ref, attended_ref, give_refs):
    for head in range(attended_ref.shape[1] // HD):
        _, total, acc = load_state(acc_ref, stat_ref, head)
        attended_ref[:, head * HD : (head + 1) * HD] = (acc * (1.0 / total)).T.astype(
            jnp.bfloat16
        )
    rows = give_refs[0].shape[1]
    for k in range(1, weight_ref.shape[0]):
        made = jnp.dot(
            attended_ref[...], weight_ref[k], preferred_element_type=jnp.float32
        ).astype(jnp.bfloat16)
        for i, give_ref in enumerate(give_refs):
            give_ref[k - 1] = made[i * rows : (i + 1) * rows]


def last_kernel(
    step,
    sources,
    conts,
    cont,
    pieces,
    lists_ref,
    counts_ref,
    q_ref,
    mine_keys_ref,
    mine_values_ref,
    their_keys_ref,
    their_values_ref,
    acc_in,
    stat_in,
    give_weight_ref,
    *refs,
):
    attended_ref, give_refs, refs = refs[0], refs[1 : 1 + pieces], refs[1 + pieces :]
    acc_ref, stat_ref, flipped_ref = refs
    before, after = (acc_in, stat_in), (acc_ref, stat_ref)
    one_of_two = sources == 4
    for part, (source, valid) in enumerate(arrivals(step, sources)):

        def absorb_part():
            held = (
                (mine_keys_ref, mine_values_ref),
                (their_keys_ref, their_values_ref),
            )[part]
            shard = ((conts, sources, source), lists_ref, counts_ref, {cont: q_ref}, held)
            first = part == 0 or one_of_two
            absorb_shard(
                *shard, flipped_ref, {cont: before if first else after}, {cont: after}
            )

        pl.when(valid)(absorb_part)
        if part == 0 and not one_of_two:
            pl.when(jnp.logical_not(valid))(lambda: hand_on(before, after))
    finish_and_give(acc_ref, stat_ref, give_weight_ref, attended_ref, give_refs)


def from_sibling(got_refs, k):
    return jnp.concatenate([ref[k] for ref in got_refs], axis=0).astype(jnp.float32)


def onward_kernel(pieces, attended_ref, weight_ref, *refs):
    got_refs, onward_refs = refs[:pieces], refs[pieces:]
    for k, onward_ref in enumerate(onward_refs, 1):
        onward_ref[...] = (
            jnp.dot(attended_ref[...], weight_ref[k], preferred_element_type=jnp.float32)
            + from_sibling(got_refs, k - 1)
        ).astype(jnp.bfloat16)


def attended_rows(refs):
    return jnp.concatenate([ref[...] for ref in refs], axis=0)


def give_near_kernel(conts, *refs):
    attended_refs, weight_ref, give_refs = refs[:conts], refs[conts], refs[conts + 1 :]
    made = jnp.dot(
        attended_rows(attended_refs), weight_ref[0], preferred_element_type=jnp.float32
    ).astype(jnp.bfloat16)
    rows = give_refs[0].shape[0]
    for i, give_ref in enumerate(give_refs):
        give_ref[...] = made[i * rows : (i + 1) * rows]


def near_kernel(conts, pieces, *refs):
    attended_refs, weight_ref, residual_ref = refs[:conts], refs[conts], refs[conts + 1]
    got_refs, refs = refs[conts + 2 : conts + 2 + pieces], refs[conts + 2 + pieces :]
    near_refs, (own_ref, sem) = refs[:conts], refs[conts:]
    length, share = near_refs[0].shape
    start = pl.multiple_of(lax.axis_index("tp") * share, HD)
    copy = pltpu.make_async_copy(
        residual_ref.at[:, :, pl.ds(start, share)], own_ref, sem.at[0]
    )
    copy.start()
    made = jnp.dot(
        attended_rows(attended_refs), weight_ref[0], preferred_element_type=jnp.float32
    ) + attended_rows(got_refs).astype(jnp.float32)
    for cont, near_ref in enumerate(near_refs):
        near_ref[...] = made[cont * length : (cont + 1) * length]
    copy.wait()
    for cont, near_ref in enumerate(near_refs):
        near_ref[...] += own_ref[cont].astype(jnp.float32)


def sum_kernel(near_ref, *refs):
    far_refs, (total_ref, squares_ref) = refs[:-2], refs[-2:]
    total = near_ref[...]
    for far_ref in far_refs:
        total = total + far_ref[...].astype(jnp.float32)
    total_ref[...] = total
    sums = jnp.sum(total * total, axis=1, keepdims=True)
    squares_ref[...] = jnp.broadcast_to(sums, (sums.shape[0], HD)).T[:8]


def stream_kernel(conts, *refs):
    for cont in range(conts):
        refs[conts][cont] = refs[cont][...].astype(jnp.bfloat16)


def norm_kernel(conts, model_width, *refs):
    totals, squares = refs[:conts], refs[conts:-2]
    gain_ref, normed_ref = refs[-2:]
    gain = gain_ref[...].astype(jnp.float32)
    for cont in range(conts):
        row = functools.reduce(jnp.add, [ref[cont * 8 : cont * 8 + 1, :] for ref in squares])
        scale = lax.rsqrt(row / model_width + 1e-05)
        scale = jnp.broadcast_to(scale, (HD, scale.shape[1])).T[:, 0:1]
        total = totals[cont][...]
        normed_ref[cont] = (total * scale * gain).astype(jnp.bfloat16)


def shards(
    queries,
    cont_keys,
    cont_values,
    prompt_keys,
    prompt_values,
    block_lists,
    tile_counts,
    out_weight,
    residual,
    norm_gain,
    *,
    sources,
    members,
):
    conts, length, width = queries.shape
    heads = width // HD
    rows_dev = prompt_keys.shape[0]
    model_width = residual.shape[2]
    share = norm_gain.shape[0]
    chips = members // CORES
    place = lax.axis_index("tp")
    pairs = heads * conts
    params = pltpu.CompilerParams(vmem_limit_bytes=VMEM_LIMIT)
    vmem = pl.BlockSpec(memory_space=pltpu.VMEM)
    hbm = pl.BlockSpec(memory_space=pltpu.HBM)

    def array(shape, dtype):
        return jax.ShapeDtypeStruct(shape, dtype)

    def cost(flops=1024):
        return pl.CostEstimate(flops=flops, bytes_accessed=1024, transcendentals=0)

    def in_hbm(x):
        return pltpu.with_memory_space_constraint(x, pltpu.HBM)

    kept = array((rows_dev, HD), jnp.bfloat16)
    keys = pl.pallas_call(
        functools.partial(pack_keys_kernel, heads),
        out_shape=kept,
        in_specs=[hbm],
        out_specs=vmem,
        scratch_shapes=[pltpu.SemaphoreType.DMA((1,))],
        compiler_params=params,
        cost_estimate=cost(),
        name="pack_keys",
    )(in_hbm(prompt_keys))
    values = pl.pallas_call(
        functools.partial(pack_values_kernel, heads),
        out_shape=kept,
        in_specs=[hbm],
        out_specs=vmem,
        scratch_shapes=[
            pltpu.VMEM((rows_dev, HD), jnp.bfloat16),
            pltpu.SemaphoreType.DMA((1,)),
        ],
        compiler_params=params,
        cost_estimate=cost(),
        name="pack_values",
    )(in_hbm(prompt_values))

    def across(step):
        def target(z, t):
            if sources == 4 and step == 1:
                return z ^ (1 + t % CORES)
            if sources == 4:
                return z ^ 1 if t % CORES == 1 else None
            to = z + step if t % CORES == 0 else z - step
            return to if 0 <= to < sources else None

        return [
            (z * members + t, target(z, t) * members + t)
            for z in range(sources)
            for t in range(members)
            if target(z, t) is not None
        ]

    sibling = [(t, t ^ 1) for t in range(members)]
    steps = steps_of(sources)
    smem = pl.BlockSpec(memory_space=pltpu.SMEM)
    lists = block_lists.reshape(-1)
    counts = tile_counts.reshape(-1)
    state_shape = (
        array((heads, HD, length), jnp.float32),
        array((heads, 8, length), jnp.float32),
    )
    flipped = pltpu.VMEM((2 * rows_dev, HD), jnp.bfloat16)
    weight_shape = array((chips, width, share), jnp.bfloat16)

    made = pl.pallas_call(
        functools.partial(first_kernel, sources, conts),
        out_shape=state_shape * conts
        + (array((heads, HD, length), jnp.bfloat16),) * conts
        + (weight_shape,) * 2,
        in_specs=[smem, smem, vmem, vmem] + [hbm] * 4,
        out_specs=(vmem,) * (3 * conts + 2),
        scratch_shapes=[
            flipped,
            pltpu.VMEM(queries.shape, jnp.bfloat16),
            pltpu.VMEM((conts, length, HD), jnp.bfloat16),
            pltpu.VMEM((conts, length, HD), jnp.bfloat16),
            pltpu.VMEM((conts, HD, length), jnp.bfloat16),
            pltpu.SemaphoreType.DMA((3,)),
            pltpu.SemaphoreType.DMA((2, chips)),
        ],
        compiler_params=params,
        cost_estimate=cost(),
        name="attend_own",
    )(
        lists,
        counts,
        keys,
        values,
        in_hbm(queries),
        in_hbm(cont_keys),
        in_hbm(cont_values),
        in_hbm(out_weight),
    )
    states = tuple(made[2 * c : 2 * c + 2] for c in range(conts))
    *qs, give_weight, keep_weight = made[2 * conts :]

    def attend_step(step, part, chosen, with_weight, states, held):
        flat = [x for cont in chosen for x in states[cont]]
        count = len(chosen)
        made = pl.pallas_call(
            functools.partial(
                middle_kernel, step, part, sources, conts, chosen, len(held), with_weight
            ),
            out_shape=state_shape * count + (weight_shape,) * with_weight,
            in_specs=[smem, smem] + [vmem] * (3 * count + len(held)) + [hbm] * with_weight,
            out_specs=(vmem,) * (2 * count + with_weight),
            scratch_shapes=[flipped] + [pltpu.SemaphoreType.DMA((chips,))] * with_weight,
            compiler_params=params,
            cost_estimate=cost(),
            name="attend_step",
        )(
            lists,
            counts,
            *[qs[cont] for cont in chosen],
            *held,
            *flat,
            *([in_hbm(out_weight)] * with_weight),
        )
        states = list(states)
        for i, cont in enumerate(chosen):
            states[cont] = tuple(made[2 * i : 2 * i + 2])
        return tuple(states), made[2 * count :]

    everyone = tuple(range(conts))
    mine, theirs = (keys, values), None
    for step in range(1, steps + 1):
        sent = mine if sources == 4 and step == 2 else (keys, values)
        mine_keys, mine_values = [lax.ppermute(x, ("ctx", "tp"), across(step)) for x in sent]
        mine_keys, states, theirs = lax.optimization_barrier((mine_keys, states, theirs))
        their_keys = lax.ppermute(mine_keys, "tp", sibling)
        mine_values, states = lax.optimization_barrier((mine_values, states))
        their_values = [
            lax.ppermute(x, "tp", sibling)
            for x in jnp.split(mine_values, 2 if step < steps else 1)
        ]
        before, mine = mine, (mine_keys, mine_values)
        rest, theirs = theirs, (their_keys, *their_values)
        if step > 1:
            states, _ = attend_step(step - 1, 0, everyone[1:], False, states, before)
            theirs, states = lax.optimization_barrier((theirs, states))
            states, _ = attend_step(step - 1, 1, everyone[1:], False, states, rest)
        if step < steps:
            states, _ = attend_step(step, 0, everyone[:1], False, states, mine)
            states, _ = attend_step(step, 1, everyone[:1], False, states, theirs)

    def attend_last(cont, state):
        pieces = swap_pieces[cont]
        made = pl.pallas_call(
            functools.partial(last_kernel, steps, sources, conts, cont, pieces),
            out_shape=(array((length, width), jnp.bfloat16),)
            + (array((chips - 1, length // pieces, share), jnp.bfloat16),) * pieces,
            in_specs=[smem, smem] + [vmem] * 8,
            out_specs=(vmem,) * (1 + pieces),
            scratch_shapes=[pltpu.VMEM(a.shape, a.dtype) for a in state_shape]
            + [flipped],
            compiler_params=params,
            cost_estimate=cost(),
            name="attend_last",
        )(
            lists,
            counts,
            qs[cont],
            *mine,
            *theirs,
            *state,
            give_weight,
        )
        return made[0], made[1:]

    def onward(attended, got):
        parts = pl.pallas_call(
            functools.partial(onward_kernel, len(got)),
            out_shape=(array((length, share), jnp.bfloat16),) * (chips - 1),
            in_specs=[vmem] * (2 + len(got)),
            out_specs=(vmem,) * (chips - 1),
            compiler_params=params,
            cost_estimate=cost(),
            name="project_onward",
        )(attended, keep_weight, *got)
        far = []
        for k in range(1, chips):
            to_chip = [
                (t, (t // CORES + k) % chips * CORES + t % CORES) for t in range(members)
            ]
            far.append(lax.ppermute(parts[k - 1], "tp", to_chip))
        return parts, far

    def give_near(attended, pieces):
        return pl.pallas_call(
            functools.partial(give_near_kernel, conts),
            out_shape=(array((conts * length // pieces, share), jnp.bfloat16),) * pieces,
            in_specs=[vmem] * (conts + 1),
            out_specs=(vmem,) * pieces,
            compiler_params=params,
            cost_estimate=cost(2**35),
            name="give_near",
        )(*attended, give_weight)

    def near(attended, got):
        return pl.pallas_call(
            functools.partial(near_kernel, conts, len(got)),
            out_shape=(array((length, share), jnp.float32),) * conts,
            in_specs=[vmem] * (conts + 1) + [hbm] + [vmem] * len(got),
            out_specs=(vmem,) * conts,
            scratch_shapes=[
                pltpu.VMEM((conts, length, share), jnp.bfloat16),
                pltpu.SemaphoreType.DMA((1,)),
            ],
            compiler_params=params,
            cost_estimate=cost(),
            name="project_near",
        )(*attended, keep_weight, in_hbm(residual), *got)

    swap_pieces = [1] + [2] * (conts - 1)
    attended, give = attend_last(0, states[0])
    all_attended, fars = [], []
    for cont in range(conts):
        got = [lax.ppermute(x, "tp", sibling) for x in give]
        if cont + 1 < conts:
            got, state = lax.optimization_barrier((got, states[cont + 1]))
        parts, far = onward(attended, got)
        all_attended.append(attended)
        fars.append(far)
        if cont + 1 < conts:
            state, parts = lax.optimization_barrier((state, parts))
            attended, give = attend_last(cont + 1, state)
    all_attended, fars[:-1], _ = lax.optimization_barrier((all_attended, fars[:-1], parts))
    got = [lax.ppermute(x, "tp", sibling) for x in give_near(all_attended, 2 * conts)]
    nears = near(all_attended, got)

    totals, squares = [], []
    for cont in range(conts):
        total, square = pl.pallas_call(
            sum_kernel,
            out_shape=(array((length, share), jnp.float32), array((8, length), jnp.float32)),
            in_specs=[vmem] * (1 + len(fars[cont])),
            out_specs=(vmem,) * 2,
            compiler_params=params,
            cost_estimate=cost(),
            name="add_up",
        )(nears[cont], *fars[cont])
        totals.append(total)
        squares.append(square)
    squares = jnp.concatenate(squares, axis=0)
    squares = squares + lax.ppermute(squares, "tp", sibling)
    all_squares = [squares] + [
        lax.ppermute(
            squares,
            "tp",
            [(t, (t // CORES + k) % chips * CORES + t % CORES) for t in range(members)],
        )
        for k in range(1, chips)
    ]
    out = array((conts, length, share), jnp.bfloat16)
    stream = pl.pallas_call(
        functools.partial(stream_kernel, conts),
        out_shape=out,
        in_specs=[vmem] * conts,
        out_specs=vmem,
        compiler_params=params,
        cost_estimate=cost(),
        name="stream",
    )(*totals)
    normed = pl.pallas_call(
        functools.partial(norm_kernel, conts, model_width),
        out_shape=out,
        in_specs=[vmem] * (conts + chips + 1),
        out_specs=vmem,
        compiler_params=params,
        cost_estimate=cost(),
        name="norm",
    )(*totals, *all_squares, norm_gain.reshape(1, share))
    return stream, normed


def solution(mesh):
    placed = (
        P(("grp", "ctx"), None, "tp"),
        P(("grp", "ctx"), None, None),
        P(("grp", "ctx"), None, None),
        P(("grp", "ctx"), None),
        P(("grp", "ctx"), None),
        P("tp", ("grp", "ctx"), None, None),
        P("tp", ("grp", "ctx"), None),
        P("tp", None),
        P(("grp", "ctx"), None, None),
        P("tp"),
    )
    return jax.shard_map(
        functools.partial(
            shards, sources=mesh.shape["ctx"], members=mesh.shape["tp"]
        ),
        mesh=mesh,
        in_specs=placed,
        out_specs=(P(("grp", "ctx"), None, "tp"), P(("grp", "ctx"), None, "tp")),
        check_vma=False,
    )
```
